32 devices in a mesh: dp: 8 (over z, x), group: 4 (over y, core).
Axes of the slice: x: 2, y: 2, z: 4, core: 2. Of those that a mesh axis runs over, the one named last changes fastest.
Arguments:
- tokens: bfloat16 [8, 1024, 1536], P('dp', 'group'), may hold values from -6 to 6
- cotangent: bfloat16 [8, 1024, 1536], P('dp', 'group'), may hold values from -6 to 6
- lengths: int32 [8], P('dp'), may hold values from 256 to 1024, as said below
- intake_weight: float32 [7077888], P(('dp', 'group')), may hold values from -0.15625 to 0.15625
- intake_first: float32 [7077888], P(('dp', 'group')), may hold values from -320 to 320
- intake_second: float32 [7077888], P(('dp', 'group')), may hold values from 2508.8 to 10035.2
- output_weight: float32 [2359296], P(('dp', 'group')), may hold values from -0.15625 to 0.15625
- output_first: float32 [2359296], P(('dp', 'group')), may hold values from -320 to 320
- output_second: float32 [2359296], P(('dp', 'group')), may hold values from 2508.8 to 10035.2
- swiglu_weight: float32 [21233664], P(('dp', 'group')), may hold values from -0.15625 to 0.15625
- swiglu_first: float32 [21233664], P(('dp', 'group')), may hold values from -320 to 320
- swiglu_second: float32 [21233664], P(('dp', 'group')), may hold values from 2508.8 to 10035.2
- down_weight: float32 [10616832], P(('dp', 'group')), may hold values from -0.078125 to 0.078125
- down_first: float32 [10616832], P(('dp', 'group')), may hold values from -320 to 320
- down_second: float32 [10616832], P(('dp', 'group')), may hold values from 2508.8 to 10035.2
- norm_gains: float32 [3072], P(('dp', 'group')), may hold values from 0.5 to 1.5
- gains_first: float32 [3072], P(('dp', 'group')), may hold values from -448 to 448
- gains_second: float32 [3072], P(('dp', 'group')), may hold values from 5120 to 20480
- conv_kernel: float32 [4608], P(('dp', 'group')), may hold values from -3.5 to 3.5
- kernel_first: float32 [4608], P(('dp', 'group')), may hold values from -448 to 448
- kernel_second: float32 [4608], P(('dp', 'group')), may hold values from 5120 to 20480
Outputs:
- block_out: bfloat16 [8, 1024, 1536], P('dp', 'group')
- input_grad: bfloat16 [8, 1024, 1536], P('dp', 'group')
- intake_first_new: float32 [7077888], P(('dp', 'group'))
- intake_second_new: float32 [7077888], P(('dp', 'group'))
- intake_weight_new: float32 [7077888], P(('dp', 'group'))
- output_first_new: float32 [2359296], P(('dp', 'group'))
- output_second_new: float32 [2359296], P(('dp', 'group'))
- output_weight_new: float32 [2359296], P(('dp', 'group'))
- swiglu_first_new: float32 [21233664], P(('dp', 'group'))
- swiglu_second_new: float32 [21233664], P(('dp', 'group'))
- swiglu_weight_new: float32 [21233664], P(('dp', 'group'))
- down_first_new: float32 [10616832], P(('dp', 'group'))
- down_second_new: float32 [10616832], P(('dp', 'group'))
- down_weight_new: float32 [10616832], P(('dp', 'group'))
- gains_first_new: float32 [3072], P(('dp', 'group'))
- gains_second_new: float32 [3072], P(('dp', 'group'))
- norm_gains_new: float32 [3072], P(('dp', 'group'))
- kernel_first_new: float32 [4608], P(('dp', 'group'))
- kernel_second_new: float32 [4608], P(('dp', 'group'))
- conv_kernel_new: float32 [4608], P(('dp', 'group'))
The draws below stay inside these ranges and needn't reach their ends.
Inputs may be any that keep to these rules, and one draw needn't show every extreme that they name: `lengths`: each row's valid positions are a prefix of its 1024 slots; some row is full and some row holds exactly 256.
All inputs are finite; a program needn't handle non-finite values.
Results may differ from the reference program's by a relative error of at most 0.018.
Values may be sent and summed in bfloat16 or wider, within the bound.
A program may use at most 256 MiB of HBM per device.

```python
import math
import jax
import jax.numpy as jnp
from jax import lax

D = 1536
FF = 6912
SLOTS = 1024
STEP = 5
ROWS = 8
N_DP = 8


def draw_lengths(key, part):
    key = jax.random.fold_in(key, 7)
    first, second = jax.random.split(key)
    values = jax.random.randint(first, (ROWS,), SLOTS // 4, SLOTS + 1)
    order = jax.random.permutation(second, ROWS)
    places = jnp.arange(ROWS)
    values = jnp.where(places == order[0], SLOTS, values)
    values = jnp.where(places == order[1], SLOTS // 4, values)
    return values.astype(jnp.int32)


def block_scale(key, dims, shards, smallest, top_value):
    def one(position, blocks):
        steps = jax.random.uniform(jax.random.fold_in(jax.random.fold_in(key, 6), position), (blocks,), jnp.float32, smallest / len(shards), top_value / len(shards))
        return jnp.repeat(jnp.exp(steps), dims[position] // blocks).reshape((-1,) + (1,) * (len(dims) - position - 1))

    level = one(*shards[0])
    for cut in shards[1:]:
        level = level * one(*cut)
    return level


def normal_values(key, extent, scale, most, cuts=(), held_as=jnp.bfloat16):
    values = scale * jax.random.normal(key, extent, jnp.float32)
    if cuts:
        values = values * block_scale(key, extent, cuts, -0.22, 0.18)
    return jnp.clip(values, -most, most).astype(held_as)


def setup_inputs(seed: int = 0) -> dict:
    key_of = jax.random.split(jax.random.key(seed), 22)
    tokens = normal_values(key_of[0], (ROWS, SLOTS, D), 1.0, 6.0, ((0, 8), (1, 4)))
    cotangent = normal_values(key_of[1], (ROWS, SLOTS, D), 1.0, 6.0, ((0, 8), (1, 4)))
    lengths = draw_lengths(jax.random.fold_in(key_of[21], 71), 0)
    intake_weight = normal_values(key_of[3], (D * 3 * D,), D ** -0.5, 0.15625, ((0, 32),), jnp.float32)
    intake_first = normal_values(key_of[4], (D * 3 * D,), (0.7 * (N_DP * SLOTS * 5 // 8) ** 0.5), 320.0, ((0, 32),), jnp.float32)
    intake_second = jnp.clip(jnp.exp(math.log(10035.2) - 1.3862944 * jax.random.uniform(key_of[5], (D * 3 * D,), jnp.float32) ** block_scale(key_of[5], (D * 3 * D,), ((0, 32),), -0.2, 0.2)), 2508.8, 10035.2)
    output_weight = normal_values(key_of[6], (D * D,), D ** -0.5, 0.15625, ((0, 32),), jnp.float32)
    output_first = normal_values(key_of[7], (D * D,), (0.7 * (N_DP * SLOTS * 5 // 8) ** 0.5), 320.0, ((0, 32),), jnp.float32)
    output_second = jnp.clip(jnp.exp(math.log(10035.2) - 1.3862944 * jax.random.uniform(key_of[8], (D * D,), jnp.float32) ** block_scale(key_of[8], (D * D,), ((0, 32),), -0.2, 0.2)), 2508.8, 10035.2)
    swiglu_weight = normal_values(key_of[9], (D * 2 * FF,), D ** -0.5, 0.15625, ((0, 32),), jnp.float32)
    swiglu_first = normal_values(key_of[10], (D * 2 * FF,), (0.7 * (N_DP * SLOTS * 5 // 8) ** 0.5), 320.0, ((0, 32),), jnp.float32)
    swiglu_second = jnp.clip(jnp.exp(math.log(10035.2) - 1.3862944 * jax.random.uniform(key_of[11], (D * 2 * FF,), jnp.float32) ** block_scale(key_of[11], (D * 2 * FF,), ((0, 32),), -0.2, 0.2)), 2508.8, 10035.2)
    down_weight = normal_values(key_of[12], (D * FF,), FF ** -0.5, 0.078125, ((0, 32),), jnp.float32)
    down_first = normal_values(key_of[13], (D * FF,), (0.7 * (N_DP * SLOTS * 5 // 8) ** 0.5), 320.0, ((0, 32),), jnp.float32)
    down_second = jnp.clip(jnp.exp(math.log(10035.2) - 1.3862944 * jax.random.uniform(key_of[14], (D * FF,), jnp.float32) ** block_scale(key_of[14], (D * FF,), ((0, 32),), -0.2, 0.2)), 2508.8, 10035.2)
    norm_gains = jnp.clip(1.0 + 0.1 * jax.random.normal(key_of[15], (2 * D,), jnp.float32), 0.5, 1.5)
    gains_first = normal_values(key_of[16], (2 * D,), ((N_DP * SLOTS * 5 // 8) ** 0.5), 448.0, ((0, 32),), jnp.float32)
    gains_second = jnp.clip(jnp.exp(math.log(20480.0) - 1.3862944 * jax.random.uniform(key_of[17], (2 * D,), jnp.float32) ** block_scale(key_of[17], (2 * D,), ((0, 32),), -0.2, 0.2)), 5120.0, 20480.0)
    conv_kernel = normal_values(key_of[18], (3 * D,), 3 ** -0.5, 3.5, ((0, 32),), jnp.float32)
    kernel_first = normal_values(key_of[19], (3 * D,), ((N_DP * SLOTS * 5 // 8) ** 0.5), 448.0, ((0, 32),), jnp.float32)
    kernel_second = jnp.clip(jnp.exp(math.log(20480.0) - 1.3862944 * jax.random.uniform(key_of[20], (3 * D,), jnp.float32) ** block_scale(key_of[20], (3 * D,), ((0, 32),), -0.2, 0.2)), 5120.0, 20480.0)
    return {"tokens": tokens, "cotangent": cotangent, "lengths": lengths, "intake_weight": intake_weight, "intake_first": intake_first, "intake_second": intake_second, "output_weight": output_weight, "output_first": output_first, "output_second": output_second, "swiglu_weight": swiglu_weight, "swiglu_first": swiglu_first, "swiglu_second": swiglu_second, "down_weight": down_weight, "down_first": down_first, "down_second": down_second, "norm_gains": norm_gains, "gains_first": gains_first, "gains_second": gains_second, "conv_kernel": conv_kernel, "kernel_first": kernel_first, "kernel_second": kernel_second}


EPS_NORM = 1e-05
BETA_ONE = 0.5
BETA_TWO = 0.5
ADAM_EPS = 1e-08
RATE_MATRIX = 0.02
RATE_VECTOR = 0.2
DECAY = 0.1
HIGH = lax.Precision.HIGHEST

@jax.custom_vjp
def low(v):
    return lax.optimization_barrier(v.astype(jnp.bfloat16)).astype(jnp.float32)

@jax.custom_vjp
def low_back(v):
    return v

def low_keep(v):
    return (low(v), None)

def low_pass(kept, grad):
    return (grad,)

def back_keep(v):
    return (v, None)

def back_low(kept, grad):
    return (low(grad),)
low.defvjp(low_keep, low_pass)
low_back.defvjp(back_keep, back_low)

def matmul(left, right):
    return jnp.dot(left, right, precision=HIGH, preferred_element_type=jnp.float32)

def rms_norm(values, gain):
    return values * lax.rsqrt(lax.optimization_barrier(jnp.mean(values * values, axis=-1, keepdims=True)) + EPS_NORM) * gain

def forward(rows, intake, output, swiglu, down, gains, kernel):
    intake = low(intake)
    output = low(output)
    swiglu = low(swiglu)
    down = low(down)
    gains = low(gains)
    kernel = low(kernel)
    normed = low(rms_norm(rows, gains[0]))
    mixed = low_back(matmul(normed, intake))
    part_b = mixed[..., :D]
    part_c = mixed[..., D:2 * D]
    part_x = mixed[..., 2 * D:]
    product = part_b * part_x
    padded = jnp.pad(product, ((0, 0), (2, 0), (0, 0)))
    conv = kernel[0] * padded[:, :-2] + kernel[1] * padded[:, 1:-1] + kernel[2] * padded[:, 2:]
    gated = low(part_c * conv)
    branch = low_back(matmul(gated, output))
    middle = rows + branch
    normed2 = low(rms_norm(middle, gains[1]))
    gate_up = low_back(matmul(normed2, swiglu))
    hidden = low(jax.nn.silu(gate_up[..., :FF]) * gate_up[..., FF:])
    return middle + low_back(matmul(hidden, down.T))

def update(weight, first, second, grad, rate, decay):
    first_new = BETA_ONE * first + (1.0 - BETA_ONE) * grad
    second_new = BETA_TWO * second + (1.0 - BETA_TWO) * grad * grad
    first_hat = first_new / (1.0 - BETA_ONE ** STEP)
    second_hat = second_new / (1.0 - BETA_TWO ** STEP)
    weight_new = weight - rate * (first_hat / (jnp.sqrt(second_hat) + ADAM_EPS) + decay * weight)
    return (first_new, second_new, weight_new)

def reference(tokens, cotangent, lengths, intake_weight, intake_first, intake_second, output_weight, output_first, output_second, swiglu_weight, swiglu_first, swiglu_second, down_weight, down_first, down_second, norm_gains, gains_first, gains_second, conv_kernel, kernel_first, kernel_second):
    rows = tokens.astype(jnp.float32)
    valid = (lax.iota(jnp.int32, SLOTS)[None, :] < lengths[:, None]).astype(jnp.float32)
    back = cotangent.astype(jnp.float32) * valid[:, :, None]
    masters = (intake_weight.reshape(D, 3 * D), output_weight.reshape(D, D), swiglu_weight.reshape(D, 2 * FF), down_weight.reshape(D, FF), norm_gains.reshape(2, D), conv_kernel.reshape(3, D))

    def one_row(totals, item):
        row, row_back = item

        def single(values, intake, output, swiglu, down, gains, kernel):
            return forward(values[None], intake, output, swiglu, down, gains, kernel)[0]
        result, pull = jax.vjp(single, row, *masters)
        grads = pull(row_back)
        summed = tuple((total + grad for total, grad in zip(totals, grads[1:])))
        return (summed, (result, grads[0]))
    zeros = tuple((jnp.zeros(master.shape, jnp.float32) for master in masters))
    sums, (results, row_grads) = lax.scan(one_row, zeros, (rows, back))
    intake_new = update(intake_weight, intake_first, intake_second, sums[0].reshape(-1), RATE_MATRIX, DECAY)
    output_new = update(output_weight, output_first, output_second, sums[1].reshape(-1), RATE_MATRIX, DECAY)
    swiglu_new = update(swiglu_weight, swiglu_first, swiglu_second, sums[2].reshape(-1), RATE_MATRIX, DECAY)
    down_new = update(down_weight, down_first, down_second, sums[3].reshape(-1), RATE_MATRIX, DECAY)
    gains_new = update(norm_gains, gains_first, gains_second, sums[4].reshape(-1), RATE_VECTOR, 0.0)
    kernel_new = update(conv_kernel, kernel_first, kernel_second, sums[5].reshape(-1), RATE_VECTOR, DECAY)
    return (results.astype(jnp.bfloat16), row_grads.astype(jnp.bfloat16), intake_new[0], intake_new[1], intake_new[2], output_new[0], output_new[1], output_new[2], swiglu_new[0], swiglu_new[1], swiglu_new[2], down_new[0], down_new[1], down_new[2], gains_new[0], gains_new[1], gains_new[2], kernel_new[0], kernel_new[1], kernel_new[2])
```

```python
import functools

import jax
import jax.numpy as jnp
from jax import lax
from jax.experimental import pallas as pl
from jax.experimental.pallas import tpu as pltpu
from jax.sharding import PartitionSpec as P

D = 1536
FF = 6912
STEP = 5
WIDTH = 256
ROW_TILE = 16

EPS_NORM = 1e-05
BETA_ONE = 0.5
BETA_TWO = 0.5
ADAM_EPS = 1e-08
RATE_MATRIX = 0.02
RATE_VECTOR = 0.2
DECAY = 0.1

MESH = pl.DeviceIdType.MESH
BF = jnp.bfloat16
F32 = jnp.float32


def update(weight, first, second, grad, rate, decay):
    first_new = BETA_ONE * first + (1.0 - BETA_ONE) * grad
    second_new = BETA_TWO * second + (1.0 - BETA_TWO) * grad * grad
    first_hat = first_new / (1.0 - BETA_ONE**STEP)
    second_hat = second_new / (1.0 - BETA_TWO**STEP)
    weight_new = weight - rate * (first_hat / (jnp.sqrt(second_hat) + ADAM_EPS) + decay * weight)
    return (first_new, second_new, weight_new)


def dot(left, right):
    return lax.dot_general(left, right, (((1,), (0,)), ((), ())), preferred_element_type=F32)


def dot_t(left, right):
    return lax.dot_general(left, right, (((1,), (1,)), ((), ())), preferred_element_type=F32)


def await_bytes(ref, sem):
    pltpu.make_async_copy(ref, ref, sem).wait()


def block_kernel(
    sizes,
    tok, nrm_own, bck_own, wi_own, wo_own, ff_own, taps, gains,
    block_out, input_grad, g_ff, g_wi, g_wo, g_gains, g_taps,
    wf_all, wi_all, wo_all, nrm_all, bck_all, n2_all, dbr_all,
    rs_br, rs_y, rs_n2, rs_n1,
    sib_f, sib_i, sib_o, z_f, z_i, z_o, mixed_far,
    ws, wi, wo, act, act_t, bck, bck_t, acc_y, acc_n, grad, sibv, part, stage,
    prod, conv, gated, dmix, mid, dmid, low, sibo, parto, outv,
    ag_ssem, ag_rsem, rs_ssem, rs_rsem, z_ssem, z_rsem, f_ssem, f_rsem,
    gs_ssem, gs_rsem, gz_ssem, gz_rsem, keep_sem, own_sem, wsem, lsem,
):
    (out_n, group, rows_n, seg, ch, cblk, chunks) = sizes
    blocks = ch // 128
    seq = group * seg
    dp = lax.axis_index("dp")
    g = lax.axis_index("group")
    o, a = dp // 2, lax.rem(dp, 2)
    y, b = g // 2, lax.rem(g, 2)
    t = 2 * y + a
    mate = (dp, g + 1 - 2 * b)

    def peer(k):
        o2 = lax.rem(o + k, out_n)
        return o2, (2 * o2 + a, g)

    barrier = pltpu.get_barrier_semaphore()
    for x2 in range(2):
        for g2 in range(group):
            @pl.when((x2 != a) | (g2 != g))
            def _():
                pl.semaphore_signal(barrier, inc=1, device_id=(2 * o + x2, g2), device_id_type=MESH)

    def greet(k, carry):
        pl.semaphore_signal(barrier, inc=1, device_id=peer(k)[1], device_id_type=MESH)
        return carry

    lax.fori_loop(1, out_n, greet, 0)
    pl.semaphore_wait(barrier, 2 * group - 1 + out_n - 1)

    def remote(src, dst, ssem, rsem, dev):
        return pltpu.make_async_remote_copy(
            src_ref=src, dst_ref=dst, send_sem=ssem, recv_sem=rsem, device_id=dev, device_id_type=MESH
        )

    def spread(src, dst, n, op):
        for t2 in range(group):
            ty, tx = t2 // 2, t2 % 2
            alone = (tx == a) & (ty == y) & (a == b)
            copy = remote(
                src, dst.at[g], ag_ssem.at[n, t2], ag_rsem.at[n, g], (2 * o + tx, 2 * ty + a)
            )
            if op == "start":
                @pl.when(alone)
                def _():
                    pltpu.make_async_copy(src, dst.at[g], ag_rsem.at[n, g]).start()

                @pl.when(jnp.logical_not(alone))
                def _():
                    copy.start()
            else:
                @pl.when(jnp.logical_not(alone))
                def _():
                    copy.wait_send()

    def give(src, dst, n, q, op):
        alone = (a == b) & (q == g)
        copy = remote(src, dst.at[t], rs_ssem.at[n, q], rs_rsem.at[n, t], (2 * o + b, q))
        if op == "start":
            @pl.when(alone)
            def _():
                pltpu.make_async_copy(src, dst.at[t], rs_rsem.at[n, t]).start()

            @pl.when(jnp.logical_not(alone))
            def _():
                copy.start()
        else:
            @pl.when(jnp.logical_not(alone))
            def _():
                copy.wait_send()

    def own_of(i):
        if isinstance(i, int) and i == 0:
            return wi_own
        if isinstance(i, int) and i == 1:
            return wo_own
        return ff_own.at[i - 2]

    def slot_of(i, o2, p):
        if isinstance(i, int) and i == 0:
            return wi_all.at[o2, p]
        if isinstance(i, int) and i == 1:
            return wo_all.at[o2, p]
        return wf_all.at[i - 2, :, o2, p]

    def half_of(i, p):
        if isinstance(i, int) and i == 0:
            return wi_all.at[:, p]
        if isinstance(i, int) and i == 1:
            return wo_all.at[:, p]
        return wf_all.at[i - 2, :, :, p]

    def gather_send(i):
        pltpu.make_async_copy(own_of(i), slot_of(i, o, b), own_sem.at[i]).start()

        def one(k, carry):
            remote(own_of(i), slot_of(i, o, b), z_ssem.at[i, k], z_rsem.at[i, o], peer(k)[1]).start()
            return carry

        lax.fori_loop(1, out_n, one, 0)

    def gather_pass(i):
        await_bytes(own_of(i), own_sem.at[i])

        def one(k, carry):
            o2, _ = peer(k)
            await_bytes(own_of(i), z_rsem.at[i, o2])
            return carry

        lax.fori_loop(1, out_n, one, 0)
        remote(half_of(i, b), half_of(i, b), f_ssem.at[i], f_rsem.at[i], mate).start()

    def gather_wait(i):
        await_bytes(half_of(i, 1 - b), f_rsem.at[i])

    def gather_close(i):
        def one(k, carry):
            await_bytes(own_of(i), z_ssem.at[i, k])
            return carry

        lax.fori_loop(1, out_n, one, 0)
        await_bytes(half_of(i, b), f_ssem.at[i])

    def fetch(src, dst, n):
        copy = pltpu.make_async_copy(src, dst, lsem.at[n])
        copy.start()
        copy.wait()

    def span(q):
        return pl.ds(q * seg, seg)

    def rows16(i):
        return pl.ds(pl.multiple_of(i * ROW_TILE, ROW_TILE), ROW_TILE)

    def lanes(k, j):
        return pl.ds(k * 384 + j * 128, 128)

    spread(nrm_own, nrm_all, 0, "start")
    gather_send(0)
    spread(bck_own, bck_all, 1, "start")
    gather_send(1)
    gather_send(2)
    prod[pl.ds(0, 8), :] = jnp.zeros((8, ch), F32)
    gather_pass(0)
    gather_send(3)
    gather_pass(1)
    gather_wait(0)
    fetch(wi_all, wi, 0)
    gather_wait(1)
    fetch(wo_all, wo, 0)

    for q in range(group):
        await_bytes(nrm_all.at[q], ag_rsem.at[0, q])
        fetch(nrm_all.at[q], act.at[span(q)], 0)
        for k in range(blocks):
            acc_y[span(q), pl.ds(k * 384, 384)] = dot(
                act[span(q), :], wi[:, :, :, pl.ds(k * 384, 384)].reshape(D, 384)
            )
        for k in range(blocks):
            col = pl.ds(k * 128, 128)
            prod[pl.ds(q * seg + 8, seg), col] = acc_y[span(q), lanes(k, 0)] * acc_y[span(q), lanes(k, 2)]
            cv = (
                taps[0:1, col] * prod[pl.ds(q * seg + 6, seg), col]
                + taps[1:2, col] * prod[pl.ds(q * seg + 7, seg), col]
                + taps[2:3, col] * prod[pl.ds(q * seg + 8, seg), col]
            )
            conv[span(q), col] = cv
            gated[span(q), col] = (acc_y[span(q), lanes(k, 1)] * cv).astype(BF)
        for n in range(4):
            col = pl.ds(n * 384, 384)
            stage[q, :, col] = dot(gated[span(q), :], wo[:, :, :, col].reshape(ch, 384)).astype(BF)
        give(stage.at[q], rs_br, 0, q, "start")

    spill = pltpu.make_async_copy(acc_y.at[:, pl.ds(0, 3 * ch)], mixed_far, lsem.at[2])
    spill.start()
    gather_pass(2)
    gather_send(4)

    for q in range(group):
        await_bytes(bck_all.at[q], ag_rsem.at[1, q])
        fetch(bck_all.at[q], bck.at[span(q)], 0)
        bck_t[:, span(q)] = bck[span(q), :].T

    for q in range(group):
        await_bytes(rs_br.at[q], rs_rsem.at[0, q])
    for q in range(group):
        give(stage.at[q], rs_br, 0, q, "end")
    fetch(rs_br, stage, 0)

    def arrived(here):
        total = stage[0, here, :].astype(F32)
        for q in range(1, group):
            total = total + stage[q, here, :].astype(F32)
        return total

    def middle_rows(i, carry):
        here = rows16(i)
        mi = tok[here, :].astype(F32) + arrived(here)
        mid[here, :] = mi
        s2 = lax.rsqrt(jnp.mean(mi * mi, axis=-1, keepdims=True) + EPS_NORM)
        low[here, :] = (mi * s2 * gains[1:2, :]).astype(BF)
        return carry

    lax.fori_loop(0, seg // ROW_TILE, middle_rows, 0)
    spread(low, n2_all, 2, "start")
    gather_pass(3)
    gather_send(5)
    gather_wait(2)
    pltpu.make_async_copy(wf_all.at[0], ws.at[0], wsem.at[0]).start()
    spill.wait()

    def clear(i, carry):
        here = rows16(i)
        acc_y[here, :] = jnp.zeros((ROW_TILE, D), F32)
        acc_n[here, :] = jnp.zeros((ROW_TILE, D), F32)
        return carry

    lax.fori_loop(0, seq // ROW_TILE, clear, 0)
    for q in range(group):
        await_bytes(n2_all.at[q], ag_rsem.at[2, q])
        fetch(n2_all.at[q], act.at[span(q)], 0)
        act_t[:, span(q)] = act[span(q), :].T

    def chunk_refs(kind, c):
        if kind == "f":
            return lax.rem(c, 2), c, sib_f.at[c], z_f.at[c], pl.ds(0, WIDTH), g_ff.at[c]
        n = chunks + c
        return n % 2, n, sib_i.at[c], z_i.at[c], pl.ds(0, 128), g_wi.at[c]

    def pair_send(kind, c, op):
        s, n, sib, _, cols, _ = chunk_refs(kind, c)
        copy = remote(grad.at[s, :, :, 1 - b, :, cols], sib, gs_ssem.at[n], gs_rsem.at[n], mate)
        if op == "start":
            copy.start()
        else:
            copy.wait_send()

    def part_sends(kind, c, op):
        s, n, _, z, cols, _ = chunk_refs(kind, c)

        def one(k, carry):
            o2, dev = peer(k)
            copy = remote(
                part.at[s, :, o2, :, cols], z.at[:, o], gz_ssem.at[n, k], gz_rsem.at[n, o], dev
            )
            if op == "start":
                copy.start()
            else:
                copy.wait_send()
            return carry

        lax.fori_loop(1, out_n, one, 0)
        keep = pltpu.make_async_copy(part.at[s, :, o, :, cols], z.at[:, o], keep_sem.at[n])
        if op == "start":
            keep.start()
        else:
            keep.wait()

    def pair_sum(kind, c):
        s, n, sib, _, cols, _ = chunk_refs(kind, c)
        await_bytes(sib, gs_rsem.at[n])
        fetch(sib, sibv.at[:, :, :, cols], 1)

        def one(i, carry):
            j, o2 = i // out_n, lax.rem(i, out_n)
            part[s, j, o2, :, cols] = (
                grad[s, j, o2, b, :, cols].astype(F32) + sibv[j, o2, :, cols].astype(F32)
            ).astype(BF)
            return carry

        lax.fori_loop(0, 3 * out_n, one, 0)
        part_sends(kind, c, "start")

    def total(kind, c):
        s, n, _, z, cols, dst = chunk_refs(kind, c)

        def one(k, carry):
            await_bytes(z.at[:, o], gz_rsem.at[n, peer(k)[0]])
            return carry

        lax.fori_loop(1, out_n, one, 0)
        fetch(z, sibv.at[:, :, :, cols], 1)

        def add(i, carry):
            j = i // (rows_n // 48)
            here = pl.ds(pl.multiple_of(lax.rem(i, rows_n // 48) * 48, 16), 48)
            value = sibv[j, 0, here, cols].astype(F32)
            for o2 in range(1, out_n):
                value = value + sibv[j, o2, here, cols].astype(F32)
            outv[j, here, cols] = value.astype(BF)
            return carry

        lax.fori_loop(0, 3 * (rows_n // 48), add, 0)
        fetch(outv.at[:, :, cols], dst, 1)

    half = out_n // 2

    def grad_rows(h):
        return pl.ds(pl.multiple_of(h * (D // 2), D // 2), D // 2), pl.ds(h * half, half)

    def hidden_chunk(c, carry):
        s = lax.rem(c, 2)
        await_bytes(ws.at[s], wsem.at[s])
        hid, dgt, dup = (pl.ds(j * WIDTH, WIDTH) for j in range(3))

        def token_tile(m, carry):
            here = pl.ds(pl.multiple_of(m * seg, seg), seg)
            n2 = act[here, :]
            gate = dot(n2, ws[s, 0].reshape(D, WIDTH))
            upper = dot(n2, ws[s, 1].reshape(D, WIDTH))
            d_hidden = dot(bck[here, :], ws[s, 2].reshape(D, WIDTH))
            sigma = jax.nn.sigmoid(gate)
            active = gate * sigma
            dmix[here, hid] = (active * upper).astype(BF)
            dmix[here, dgt] = (d_hidden * upper * (sigma * (1.0 + gate * (1.0 - sigma)))).astype(BF)
            dmix[here, dup] = (d_hidden * active).astype(BF)
            acc_y[here, :] += dot_t(dmix[here, hid], ws[s, 2].reshape(D, WIDTH))
            acc_n[here, :] += dot_t(dmix[here, dgt], ws[s, 0].reshape(D, WIDTH))
            acc_n[here, :] += dot_t(dmix[here, dup], ws[s, 1].reshape(D, WIDTH))
            return carry

        lax.fori_loop(0, group, token_tile, 0)

        @pl.when(c >= 2)
        def _():
            pair_send("f", c - 2, "end")

        def grad_tile(h, carry):
            rows, os = grad_rows(h)
            shape = (half, 2, rows_n, WIDTH)
            grad[s, 0, os] = dot(act_t[rows, :], dmix[:, dgt]).astype(BF).reshape(shape)
            grad[s, 1, os] = dot(act_t[rows, :], dmix[:, dup]).astype(BF).reshape(shape)
            grad[s, 2, os] = dot(bck_t[rows, :], dmix[:, hid]).astype(BF).reshape(shape)
            return carry

        lax.fori_loop(0, 2, grad_tile, 0)
        pair_send("f", c, "start")

        @pl.when(c >= 3)
        def _():
            part_sends("f", c - 3, "end")

        @pl.when(c >= 1)
        def _():
            pair_sum("f", c - 1)

        @pl.when(c + 2 < chunks)
        def _():
            gather_pass(c + 4)

        @pl.when(c + 4 < chunks)
        def _():
            gather_send(c + 6)

        @pl.when(c + 1 < chunks)
        def _():
            gather_wait(c + 3)
            pltpu.make_async_copy(wf_all.at[c + 1], ws.at[1 - s], wsem.at[1 - s]).start()

        return carry

    lax.fori_loop(0, chunks, hidden_chunk, 0)

    for q in range(group):
        stage[q] = acc_n[span(q), :].astype(BF)
        give(stage.at[q], rs_n2, 1, q, "start")
    part_sends("f", chunks - 3, "end")
    pair_sum("f", chunks - 1)
    for q in range(group):
        give(stage.at[q], rs_n2, 1, q, "end")
    for q in range(group):
        await_bytes(rs_n2.at[q], rs_rsem.at[1, q])
    spread(low, n2_all, 2, "end")
    fetch(rs_n2, stage, 0)
    fetch(bck_own, act.at[span(0)], 0)
    g_gains[...] = jnp.zeros_like(g_gains)

    def d_middle_rows(i, carry):
        here = rows16(i)
        dn = arrived(here)
        mi = mid[here, :]
        s2 = lax.rsqrt(jnp.mean(mi * mi, axis=-1, keepdims=True) + EPS_NORM)
        e2 = gains[1:2, :] * dn
        back = act[here, :].astype(F32)
        dm = back + s2 * e2 - mi * (s2 * s2 * s2) * jnp.mean(e2 * mi, axis=-1, keepdims=True)
        dmid[here, :] = dm
        low[here, :] = dm.astype(BF)
        g_gains[1] += jnp.sum((dn * mi * s2).reshape(ROW_TILE // 8, 8, D), axis=0)
        return carry

    lax.fori_loop(0, seg // ROW_TILE, d_middle_rows, 0)
    spread(low, dbr_all, 3, "start")

    for q in range(group):
        stage[q] = acc_y[span(q), :].astype(BF)
        give(stage.at[q], rs_y, 2, q, "start")
    spill_back = pltpu.make_async_copy(mixed_far, acc_y.at[:, pl.ds(0, 3 * ch)], lsem.at[2])
    spill_back.start()

    for q in range(group):
        bck_t[pl.ds(0, ch), span(q)] = gated[span(q), :].T
        fetch(nrm_all.at[q], act.at[span(q)], 0)
        act_t[:, span(q)] = act[span(q), :].T
    spill_back.wait()

    acc_n[pl.ds(seq, 8), pl.ds(0, ch)] = jnp.zeros((8, ch), F32)
    for q in range(group):
        await_bytes(dbr_all.at[q], ag_rsem.at[3, q])
        fetch(dbr_all.at[q], bck.at[span(q)], 0)
        acc_n[span(q), pl.ds(ch, ch)] = dot_t(bck[span(q), :], wo[...].reshape(ch, D))
        for k in range(blocks):
            col = pl.ds(k * 128, 128)
            d_gated = acc_n[span(q), pl.ds(ch + k * 128, 128)]
            acc_n[span(q), col] = d_gated * acc_y[span(q), lanes(k, 1)]
            dmix[span(q), lanes(k, 1)] = (d_gated * conv[span(q), col]).astype(BF)
    g_taps[...] = jnp.zeros_like(g_taps)
    for q in range(group):
        for k in range(blocks):
            col = pl.ds(k * 128, 128)
            d0 = acc_n[span(q), col]
            for n in range(3):
                g_taps[n, :, col] += jnp.sum(
                    (d0 * prod[pl.ds(q * seg + 6 + n, seg), col]).reshape(seg // 8, 8, 128), axis=0
                )
            d_product = (
                taps[2:3, col] * d0
                + taps[1:2, col] * acc_n[pl.ds(q * seg + 1, seg), col]
                + taps[0:1, col] * acc_n[pl.ds(q * seg + 2, seg), col]
            )
            dmix[span(q), lanes(k, 0)] = (d_product * acc_y[span(q), lanes(k, 2)]).astype(BF)
            dmix[span(q), lanes(k, 2)] = (d_product * acc_y[span(q), lanes(k, 0)]).astype(BF)

    for k in range(blocks):
        s = (chunks + k) % 2
        if k < 2:
            pair_send("f", chunks - 2 + k, "end")
        else:
            pair_send("i", k - 2, "end")

        def intake_tile(h, carry, k=k, s=s):
            rows, os = grad_rows(h)
            value = dot(act_t[rows, :], dmix[:, pl.ds(k * 384, 384)]).astype(BF)
            for j in range(3):
                grad[s, j, os, :, :, pl.ds(0, 128)] = value[:, j * 128 : (j + 1) * 128].reshape(
                    half, 2, rows_n, 128
                )
            return carry

        lax.fori_loop(0, 2, intake_tile, 0)
        pair_send("i", k, "start")
        if k >= 1:
            if k <= 2:
                part_sends("f", chunks - 3 + k, "end")
            else:
                part_sends("i", k - 3, "end")
            pair_sum("i", k - 1)

    for n in range(4):
        col = pl.ds(n * 384, 384)
        wo[:, :, :, col] = dot(bck_t[pl.ds(0, ch), :], bck[:, col]).astype(BF).reshape(out_n, 2, cblk, 384)
    last = chunks + blocks
    pair_o = remote(wo.at[:, 1 - b], sib_o, gs_ssem.at[last], gs_rsem.at[last], mate)
    pair_o.start()
    if blocks <= 2:
        part_sends("f", chunks - 3 + blocks, "end")
    else:
        part_sends("i", blocks - 3, "end")
    pair_sum("i", blocks - 1)

    await_bytes(sib_o, gs_rsem.at[last])
    fetch(sib_o, sibo, 1)

    def add_o(o2, carry):
        parto[o2] = (wo[o2, b].astype(F32) + sibo[o2].astype(F32)).astype(BF)
        return carry

    lax.fori_loop(0, out_n, add_o, 0)

    def part_o(op):
        def one(k, carry):
            o2, dev = peer(k)
            copy = remote(parto.at[o2], z_o.at[o], gz_ssem.at[last, k], gz_rsem.at[last, o], dev)
            if op == "start":
                copy.start()
            else:
                copy.wait_send()
            return carry

        lax.fori_loop(1, out_n, one, 0)
        keep = pltpu.make_async_copy(parto.at[o], z_o.at[o], keep_sem.at[last])
        if op == "start":
            keep.start()
        else:
            keep.wait()

    part_o("start")

    for q in range(group):
        give(stage.at[q], rs_y, 2, q, "end")
    for q in range(group):
        await_bytes(rs_y.at[q], rs_rsem.at[2, q])
    for q in range(group):
        for n in range(4):
            stage[q, :, pl.ds(n * 384, 384)] = dot_t(
                dmix[span(q), :], wi[pl.ds(n * out_n // 4, out_n // 4)].reshape(384, 3 * ch)
            ).astype(BF)
        give(stage.at[q], rs_n1, 3, q, "start")

    spread(low, dbr_all, 3, "end")
    for q in range(group):
        fetch(rs_y.at[q], act.at[span(q)], 0)

    def out_rows(i, carry):
        here = rows16(i)
        value = act[here, :].astype(F32)
        for q in range(1, group):
            value = value + act[pl.ds(pl.multiple_of(q * seg + i * ROW_TILE, ROW_TILE), ROW_TILE), :].astype(F32)
        low[here, :] = (mid[here, :] + value).astype(BF)
        return carry

    lax.fori_loop(0, seg // ROW_TILE, out_rows, 0)
    fetch(low, block_out, 0)

    for c in range(chunks):
        if c >= chunks - 2 and blocks < 2 - (chunks - 1 - c):
            part_sends("f", c, "end")
    for q in range(group):
        give(stage.at[q], rs_n1, 3, q, "end")
    for q in range(group):
        await_bytes(rs_n1.at[q], rs_rsem.at[3, q])
    fetch(rs_n1, stage, 0)

    def d_rows(i, carry):
        here = rows16(i)
        dn = arrived(here)
        row = tok[here, :].astype(F32)
        s1 = lax.rsqrt(jnp.mean(row * row, axis=-1, keepdims=True) + EPS_NORM)
        e1 = gains[0:1, :] * dn
        low[here, :] = (
            dmid[here, :] + s1 * e1 - row * (s1 * s1 * s1) * jnp.mean(e1 * row, axis=-1, keepdims=True)
        ).astype(BF)
        g_gains[0] += jnp.sum((dn * row * s1).reshape(ROW_TILE // 8, 8, D), axis=0)
        return carry

    lax.fori_loop(0, seg // ROW_TILE, d_rows, 0)
    fetch(low, input_grad, 0)

    def total_f(c, carry):
        total("f", c)
        return carry

    lax.fori_loop(0, chunks, total_f, 0)
    for k in range(max(0, blocks - 2), blocks):
        part_sends("i", k, "end")
        pair_send("i", k, "end")
    for k in range(blocks):
        total("i", k)
    part_o("end")
    pair_o.wait_send()

    def last_one(k, carry):
        await_bytes(z_o.at[o], gz_rsem.at[last, peer(k)[0]])
        return carry

    lax.fori_loop(1, out_n, last_one, 0)
    fetch(z_o, sibo, 1)
    value = sibo[0].astype(F32)
    for o2 in range(1, out_n):
        value = value + sibo[o2].astype(F32)
    outo = parto.at[0]
    outo[...] = value.astype(BF)
    fetch(outo, g_wo, 1)

    spread(nrm_own, nrm_all, 0, "end")
    spread(bck_own, bck_all, 1, "end")
    gather_close(0)
    gather_close(1)

    def close(c, carry):
        gather_close(c + 2)
        return carry

    lax.fori_loop(0, chunks, close, 0)


def forward_backward(sizes, tok, nrm, bck, wi_own, wo_own, ff_own, taps, gains):
    (out_n, group, rows_n, seg, ch, cblk, chunks) = sizes
    blocks = ch // 128
    seq = group * seg
    items = 2 + chunks
    sums = chunks + blocks + 1
    vm = pltpu.VMEM
    dma = pltpu.SemaphoreType.DMA

    def shape(*dims, dtype=BF):
        return jax.ShapeDtypeStruct(dims, dtype)

    any_spec = pl.BlockSpec(memory_space=pl.ANY)
    vmem_spec = pl.BlockSpec(memory_space=pltpu.VMEM)
    outs = [
        shape(seg, D), shape(seg, D),
        shape(chunks, 3, rows_n, WIDTH), shape(blocks, 3, rows_n, 128), shape(cblk, D),
        shape(2, 8, D, dtype=F32), shape(3, 8, ch, dtype=F32),
        shape(chunks, 3, out_n, 2, rows_n, WIDTH), shape(out_n, 2, rows_n, 3 * ch), shape(out_n, 2, cblk, D),
        shape(group, seg, D), shape(group, seg, D), shape(group, seg, D), shape(group, seg, D),
        shape(group, seg, D), shape(group, seg, D), shape(group, seg, D), shape(group, seg, D),
        shape(chunks, 3, out_n, rows_n, WIDTH), shape(blocks, 3, out_n, rows_n, 128), shape(out_n, cblk, D),
        shape(chunks, 3, out_n, rows_n, WIDTH), shape(blocks, 3, out_n, rows_n, 128), shape(out_n, cblk, D),
        shape(seq, 3 * ch, dtype=F32),
    ]
    out_specs = [any_spec] * 5 + [vmem_spec] * 2 + [any_spec] * (len(outs) - 7)
    scratch = [
        vm((2, 3, out_n, 2, rows_n, WIDTH), BF),
        vm((out_n, 2, rows_n, 3 * ch), BF),
        vm((out_n, 2, cblk, D), BF),
        vm((seq, D), BF), vm((D, seq), BF), vm((seq, D), BF), vm((D, seq), BF),
        vm((seq, D), F32), vm((seq + 8, D), F32),
        vm((2, 3, out_n, 2, rows_n, WIDTH), BF),
        vm((3, out_n, rows_n, WIDTH), BF),
        vm((2, 3, out_n, rows_n, WIDTH), BF),
        vm((group, seg, D), BF),
        vm((seq + 8, ch), F32), vm((seq, ch), F32), vm((seq, ch), BF), vm((seq, 3 * ch), BF),
        vm((seg, D), F32), vm((seg, D), F32), vm((seg, D), BF),
        vm((out_n, cblk, D), BF), vm((out_n, cblk, D), BF), vm((3, rows_n, WIDTH), BF),
        dma((4, group)), dma((4, group)), dma((4, group)), dma((4, group)),
        dma((items, out_n)), dma((items, out_n)), dma((items,)), dma((items,)),
        dma((sums,)), dma((sums,)), dma((sums, out_n)), dma((sums, out_n)), dma((sums,)),
        dma((items,)), dma((2,)), dma((3,)),
    ]
    results = pl.pallas_call(
        functools.partial(block_kernel, sizes),
        out_shape=outs,
        in_specs=[vmem_spec] + [any_spec] * 5 + [vmem_spec] * 2,
        out_specs=out_specs,
        scratch_shapes=scratch,
        compiler_params=pltpu.CompilerParams(
            collective_id=0, has_side_effects=True, vmem_limit_bytes=63 * 1024 * 1024
        ),
        cost_estimate=pl.CostEstimate(
            flops=6 * seq * D * (4 * ch + 3 * chunks * WIDTH),
            bytes_accessed=200_000_000,
            transcendentals=seq * chunks * WIDTH,
        ),
    )(tok, nrm, bck, wi_own, wo_own, ff_own, taps, gains)
    return results[:7]


def body(
    tokens,
    cotangent,
    lengths,
    intake_weight,
    intake_first,
    intake_second,
    output_weight,
    output_first,
    output_second,
    swiglu_weight,
    swiglu_first,
    swiglu_second,
    down_weight,
    down_first,
    down_second,
    norm_gains,
    gains_first,
    gains_second,
    conv_kernel,
    kernel_first,
    kernel_second,
):
    data_count = lax.axis_size("dp")
    group_count = lax.axis_size("group")
    dp = lax.axis_index("dp")
    member = lax.axis_index("group")
    block = D // (data_count * group_count)
    cblk = -(-block // 16) * 16
    ch = data_count * cblk
    blocks = ch // 128
    hidden_part = FF // group_count
    chunks = -(-hidden_part // WIDTH)
    hidden_full = chunks * WIDTH
    rows_n = D // data_count
    swap = []
    for one in range(data_count):
        for two in range(group_count):
            there = (2 * (one // 2) + two % 2) * group_count + 2 * (two // 2) + one % 2
            swap.append((one * group_count + two, there))
    work_part = 2 * (member // 2) + lax.rem(dp, 2)

    def cross(value):
        return lax.ppermute(value, ("dp", "group"), swap)

    intake_local = (
        intake_weight.astype(BF)
        .reshape(block, 3, data_count, group_count, block)
        .transpose(3, 0, 1, 2, 4)
    )
    intake_local = jnp.pad(intake_local, ((0, 0),) * 4 + ((0, cblk - block),))
    intake_local = (
        intake_local.reshape(group_count, block, 3, blocks, 128)
        .transpose(0, 1, 3, 2, 4)
        .reshape(group_count, block, 3 * ch)
    )
    ff_local = jnp.concatenate(
        [
            swiglu_weight.astype(BF).reshape(block, 2, group_count, hidden_part),
            down_weight.astype(BF).reshape(block, 1, group_count, hidden_part),
        ],
        axis=1,
    )
    ff_local = jnp.pad(ff_local, ((0, 0),) * 3 + ((0, hidden_full - hidden_part),))
    ff_local = ff_local.reshape(block, 3, group_count, chunks, WIDTH).transpose(2, 3, 1, 0, 4)
    wi_own = lax.all_to_all(intake_local, "group", split_axis=0, concat_axis=0, tiled=True)
    wi_own = cross(wi_own.reshape(rows_n, 3 * ch))
    ff_own = lax.all_to_all(ff_local, "group", split_axis=0, concat_axis=0, tiled=True)
    ff_own = cross(ff_own.transpose(1, 2, 0, 3, 4).reshape(chunks, 3, rows_n, WIDTH))
    wo_own = cross(
        jnp.pad(output_weight.astype(BF).reshape(block, D), ((0, cblk - block), (0, 0)))
    )
    gains_all = lax.all_gather(norm_gains.astype(BF), ("dp", "group"), axis=0, tiled=True)
    kernel_all = lax.all_gather(conv_kernel.astype(BF), ("dp", "group"), axis=0, tiled=True)
    gains = gains_all.astype(F32).reshape(2, D)
    taps = lax.dynamic_index_in_dim(
        kernel_all.astype(F32).reshape(3, data_count, group_count, block), work_part, 2, False
    )
    taps = jnp.pad(taps, ((0, 0), (0, 0), (0, cblk - block))).reshape(3, ch)

    rows = tokens[0].astype(F32)
    seg_len = rows.shape[0]
    positions = member * seg_len + lax.iota(jnp.int32, seg_len)
    valid = (positions < lengths[0]).astype(F32)[:, None]
    back_low = (cotangent[0].astype(F32) * valid).astype(BF)
    scale_one = lax.rsqrt(jnp.mean(rows * rows, axis=-1, keepdims=True) + EPS_NORM)
    normed = (rows * scale_one * gains[0]).astype(BF)

    sizes = (data_count // 2, group_count, rows_n, seg_len, ch, cblk, chunks)
    block_out, input_grad, g_ff, g_wi, g_wo, g_gains, g_taps = forward_backward(
        sizes, tokens[0], normed, back_low, wi_own, wo_own, ff_own, taps, gains
    )

    g_wi = cross(g_wi).reshape(blocks, 3, group_count, block, 128).transpose(2, 3, 1, 0, 4)
    g_wi = g_wi.reshape(group_count, block, 3, data_count, cblk)[..., :block]
    g_wi = lax.all_to_all(g_wi, "group", split_axis=0, concat_axis=0, tiled=True)
    intake_grad_flat = g_wi.transpose(1, 2, 3, 0, 4).reshape(-1).astype(F32)
    g_ff = cross(g_ff).reshape(chunks, 3, group_count, block, WIDTH).transpose(2, 3, 1, 0, 4)
    g_ff = g_ff.reshape(group_count, block, 3, hidden_full)
    g_ff = lax.all_to_all(g_ff, "group", split_axis=0, concat_axis=0, tiled=True)
    g_ff = g_ff[..., :hidden_part].transpose(1, 2, 0, 3)
    swiglu_grad_flat = g_ff[:, :2].reshape(-1).astype(F32)
    down_grad_flat = g_ff[:, 2].reshape(-1).astype(F32)
    output_grad_flat = cross(g_wo)[:block].reshape(-1).astype(F32)

    member_mask = (
        (lax.iota(jnp.int32, group_count) == work_part).astype(F32).reshape(1, 1, group_count, 1)
    )
    grad_taps = jnp.sum(g_taps, axis=1).reshape(3, data_count, cblk)[:, :, :block]
    kernel_placed = (grad_taps.reshape(3, data_count, 1, block) * member_mask).reshape(-1)
    small_shards = (
        lax.psum_scatter(
            jnp.sum(g_gains, axis=1).reshape(-1), ("dp", "group"), scatter_dimension=0, tiled=True
        ),
        lax.psum_scatter(kernel_placed, ("dp", "group"), scatter_dimension=0, tiled=True),
    )
    intake_new = update(
        intake_weight, intake_first, intake_second, intake_grad_flat, RATE_MATRIX, DECAY
    )
    output_new = update(
        output_weight, output_first, output_second, output_grad_flat, RATE_MATRIX, DECAY
    )
    swiglu_new = update(
        swiglu_weight, swiglu_first, swiglu_second, swiglu_grad_flat, RATE_MATRIX, DECAY
    )
    down_new = update(down_weight, down_first, down_second, down_grad_flat, RATE_MATRIX, DECAY)
    gains_new = update(norm_gains, gains_first, gains_second, small_shards[0], RATE_VECTOR, 0.0)
    kernel_new = update(
        conv_kernel, kernel_first, kernel_second, small_shards[1], RATE_VECTOR, DECAY
    )
    return (
        block_out[None],
        input_grad[None],
        intake_new[0],
        intake_new[1],
        intake_new[2],
        output_new[0],
        output_new[1],
        output_new[2],
        swiglu_new[0],
        swiglu_new[1],
        swiglu_new[2],
        down_new[0],
        down_new[1],
        down_new[2],
        gains_new[0],
        gains_new[1],
        gains_new[2],
        kernel_new[0],
        kernel_new[1],
        kernel_new[2],
    )


def solution(mesh):
    in_specs = (
        P("dp", "group", None),
        P("dp", "group", None),
        P("dp"),
        P(("dp", "group")),
        P(("dp", "group")),
        P(("dp", "group")),
        P(("dp", "group")),
        P(("dp", "group")),
        P(("dp", "group")),
        P(("dp", "group")),
        P(("dp", "group")),
        P(("dp", "group")),
        P(("dp", "group")),
        P(("dp", "group")),
        P(("dp", "group")),
        P(("dp", "group")),
        P(("dp", "group")),
        P(("dp", "group")),
        P(("dp", "group")),
        P(("dp", "group")),
        P(("dp", "group")),
    )
    out_specs = (
        P("dp", "group", None),
        P("dp", "group", None),
        P(("dp", "group")),
        P(("dp", "group")),
        P(("dp", "group")),
        P(("dp", "group")),
        P(("dp", "group")),
        P(("dp", "group")),
        P(("dp", "group")),
        P(("dp", "group")),
        P(("dp", "group")),
        P(("dp", "group")),
        P(("dp", "group")),
        P(("dp", "group")),
        P(("dp", "group")),
        P(("dp", "group")),
        P(("dp", "group")),
        P(("dp", "group")),
        P(("dp", "group")),
        P(("dp", "group")),
    )
    return jax.shard_map(body, mesh=mesh, in_specs=in_specs, out_specs=out_specs, check_vma=False)
```

```python
import functools

import jax
import jax.numpy as jnp
from jax import lax
from jax.experimental import pallas as pl
from jax.experimental.pallas import tpu as pltpu
from jax.sharding import PartitionSpec as P

D = 1536
FF = 6912
STEP = 5
WIDTH = 256
ROW_TILE = 16

EPS_NORM = 1e-05
BETA_ONE = 0.5
BETA_TWO = 0.5
ADAM_EPS = 1e-08
RATE_MATRIX = 0.02
RATE_VECTOR = 0.2
DECAY = 0.1

MESH = pl.DeviceIdType.MESH
BF = jnp.bfloat16
F32 = jnp.float32


def update(weight, first, second, grad, rate, decay):
    first_new = BETA_ONE * first + (1.0 - BETA_ONE) * grad
    second_new = BETA_TWO * second + (1.0 - BETA_TWO) * grad * grad
    first_hat = first_new / (1.0 - BETA_ONE**STEP)
    second_hat = second_new / (1.0 - BETA_TWO**STEP)
    weight_new = weight - rate * (first_hat / (jnp.sqrt(second_hat) + ADAM_EPS) + decay * weight)
    return (first_new, second_new, weight_new)


def dot(left, right):
    return lax.dot_general(left, right, (((1,), (0,)), ((), ())), preferred_element_type=F32)


def dot_t(left, right):
    return lax.dot_general(left, right, (((1,), (1,)), ((), ())), preferred_element_type=F32)


def await_bytes(ref, sem):
    pltpu.make_async_copy(ref, ref, sem).wait()


def block_kernel(
    sizes,
    tok, bck_own, wi_own, wo_own, ff_own, small_own,
    block_out, input_grad, g_ff, g_wi, g_wo, g_small,
    wf_all, wi_all, wo_all, tok_all, nrm_far, bck_all, n2_all, dbr_all,
    rs_br, rs_y, rs_n2, rs_n1,
    sib_f, sib_i, sib_o, z_f, z_i, z_o, mixed_far,
    ws, wi, wo, act, act_t, bck, bck_t, acc_y, acc_n, grad, sibv, part, stage,
    prod, conv, gated, dmix, mid, dmid, low, sibo, parto,
    small_all, gains, taps, g_gains, g_taps, sm_mine, sm_plane, sm_sum, sm_z,
    ag_ssem, ag_rsem, rs_ssem, rs_rsem, z_ssem, z_rsem, f_ssem, f_rsem,
    gs_ssem, gs_rsem, gz_ssem, gz_rsem, keep_sem, own_ssem, own_rsem, back_ssem, back_rsem,
    sa_ssem, sa_rsem, sz_ssem, sz_rsem, ta_ssem, ta_rsem, tz_ssem, tz_rsem, wsem, lsem,
):
    (out_n, group, rows_n, seg, ch, cblk, chunks) = sizes
    block = rows_n // group
    direct = block % 16 == 0
    count = 2 * out_n * group
    blocks = ch // 128
    seq = group * seg
    dp = lax.axis_index("dp")
    g = lax.axis_index("group")
    o, a = dp // 2, lax.rem(dp, 2)
    y, b = g // 2, lax.rem(g, 2)
    t = 2 * y + a
    mate = (dp, g + 1 - 2 * b)

    def peer(k):
        o2 = lax.rem(o + k, out_n)
        return o2, (2 * o2 + a, g)

    barrier = pltpu.get_barrier_semaphore()
    for x2 in range(2):
        for g2 in range(group):
            @pl.when((x2 != a) | (g2 != g))
            def _():
                pl.semaphore_signal(barrier, inc=1, device_id=(2 * o + x2, g2), device_id_type=MESH)

    def greet(k, carry):
        pl.semaphore_signal(barrier, inc=1, device_id=peer(k)[1], device_id_type=MESH)
        return carry

    lax.fori_loop(1, out_n, greet, 0)
    pl.semaphore_wait(barrier, 2 * group - 1 + out_n - 1)

    def remote(src, dst, ssem, rsem, dev):
        return pltpu.make_async_remote_copy(
            src_ref=src, dst_ref=dst, send_sem=ssem, recv_sem=rsem, device_id=dev, device_id_type=MESH
        )

    def spread(src, dst, n, op):
        for t2 in range(group):
            ty, tx = t2 // 2, t2 % 2
            alone = (tx == a) & (ty == y) & (a == b)
            copy = remote(
                src, dst.at[g], ag_ssem.at[n, t2], ag_rsem.at[n, g], (2 * o + tx, 2 * ty + a)
            )
            if op == "start":
                @pl.when(alone)
                def _():
                    pltpu.make_async_copy(src, dst.at[g], ag_rsem.at[n, g]).start()

                @pl.when(jnp.logical_not(alone))
                def _():
                    copy.start()
            else:
                @pl.when(jnp.logical_not(alone))
                def _():
                    copy.wait_send()

    def give(src, dst, n, q, op):
        alone = (a == b) & (q == g)
        copy = remote(src, dst.at[t], rs_ssem.at[n, q], rs_rsem.at[n, t], (2 * o + b, q))
        if op == "start":
            @pl.when(alone)
            def _():
                pltpu.make_async_copy(src, dst.at[t], rs_rsem.at[n, t]).start()

            @pl.when(jnp.logical_not(alone))
            def _():
                copy.start()
        else:
            @pl.when(jnp.logical_not(alone))
            def _():
                copy.wait_send()

    def slot_of(i, o2, p):
        if isinstance(i, int) and i == 0:
            return wi_all.at[o2, p]
        if isinstance(i, int) and i == 1:
            return wo_all.at[o2, p]
        return wf_all.at[i - 2, :, o2, p]

    def half_of(i, p):
        if isinstance(i, int) and i == 0:
            return wi_all.at[:, p]
        if isinstance(i, int) and i == 1:
            return wo_all.at[:, p]
        return wf_all.at[i - 2, :, :, p]

    my_rows = pl.ds(pl.multiple_of(g * block, 4), block)

    def switch(alone, local, copy, op):
        if op == "start":
            @pl.when(alone)
            def _():
                local.start()

            @pl.when(jnp.logical_not(alone))
            def _():
                copy.start()
        else:
            @pl.when(jnp.logical_not(alone))
            def _():
                copy.wait_send()

    def own_send(i, op):
        if isinstance(i, int) and i == 1:
            dst = wo_all.at[o, a]
            switch(
                a == b,
                pltpu.make_async_copy(wo_own, dst, own_rsem.at[1, 0]),
                remote(wo_own, dst, own_ssem.at[1, 0], own_rsem.at[1, 0], (2 * o + b, 2 * y + a)),
                op,
            )
            return
        if not direct:
            src = wi_own if isinstance(i, int) and i == 0 else ff_own.at[i - 2]
            if op == "start":
                pltpu.make_async_copy(src, slot_of(i, o, b), own_rsem.at[i, 0]).start()
            return
        for t2 in range(group):
            ty, tx = t2 // 2, t2 % 2
            if isinstance(i, int) and i == 0:
                src, dst = wi_own.at[t2], wi_all.at[o, a, my_rows]
            else:
                src, dst = ff_own.at[t2, i - 2], wf_all.at[i - 2, :, o, a, my_rows]
            switch(
                (tx == a) & (ty == y) & (a == b),
                pltpu.make_async_copy(src, dst, own_rsem.at[i, g]),
                remote(src, dst, own_ssem.at[i, t2], own_rsem.at[i, g], (2 * o + tx, 2 * ty + a)),
                op,
            )

    def own_wait(i):
        if not direct or isinstance(i, int) and i == 1:
            await_bytes(slot_of(i, o, b), own_rsem.at[i, 0])
            return
        for q in range(group):
            if isinstance(i, int) and i == 0:
                await_bytes(wi_all.at[o, b, pl.ds(q * block, block)], own_rsem.at[i, q])
            else:
                await_bytes(wf_all.at[i - 2, :, o, b, pl.ds(q * block, block)], own_rsem.at[i, q])

    def gather_send(i):
        own_wait(i)

        def one(k, carry):
            remote(
                slot_of(i, o, b), slot_of(i, o, b), z_ssem.at[i, k], z_rsem.at[i, o], peer(k)[1]
            ).start()
            return carry

        lax.fori_loop(1, out_n, one, 0)

    def gather_pass(i):
        def one(k, carry):
            o2, _ = peer(k)
            await_bytes(slot_of(i, o2, b), z_rsem.at[i, o2])
            return carry

        lax.fori_loop(1, out_n, one, 0)
        remote(half_of(i, b), half_of(i, b), f_ssem.at[i], f_rsem.at[i], mate).start()

    def gather_wait(i):
        await_bytes(half_of(i, 1 - b), f_rsem.at[i])

    def gather_close(i):
        def one(k, carry):
            await_bytes(slot_of(i, o, b), z_ssem.at[i, k])
            return carry

        lax.fori_loop(1, out_n, one, 0)
        await_bytes(half_of(i, b), f_ssem.at[i])
        own_send(i, "end")

    def fetch(src, dst, n):
        copy = pltpu.make_async_copy(src, dst, lsem.at[n])
        copy.start()
        copy.wait()

    def span(q):
        return pl.ds(q * seg, seg)

    def rows16(i):
        return pl.ds(pl.multiple_of(i * ROW_TILE, ROW_TILE), ROW_TILE)

    def lanes(k, j):
        return pl.ds(k * 384 + j * 128, 128)

    place = a * group + g
    mine = o * (2 * group) + place

    def plane(src, dst, ssem, rsem, op):
        for x2 in range(2):
            for g2 in range(group):
                @pl.when((x2 != a) | (g2 != g))
                def _():
                    copy = remote(src, dst, ssem.at[x2 * group + g2], rsem.at[place], (2 * o + x2, g2))
                    if op == "start":
                        copy.start()
                    else:
                        copy.wait_send()

    def plane_wait(ref, rsem):
        for x2 in range(2):
            for g2 in range(group):
                @pl.when((x2 != a) | (g2 != g))
                def _():
                    await_bytes(ref, rsem.at[x2 * group + g2])

    def far(src, dst, ssem, rsem, op):
        def one(k, carry):
            copy = remote(src, dst, ssem.at[k], rsem.at[o], peer(k)[1])
            if op == "start":
                copy.start()
            else:
                copy.wait_send()
            return carry

        lax.fori_loop(1, out_n, one, 0)

    def far_wait(ref, rsem):
        def one(k, carry):
            await_bytes(ref, rsem.at[peer(k)[0]])
            return carry

        lax.fori_loop(1, out_n, one, 0)

    planes = small_all.at[pl.ds(o * 2 * group, 2 * group)]
    pltpu.make_async_copy(small_own, small_all.at[mine], lsem.at[2]).start()
    plane(small_own, small_all.at[mine], sa_ssem, sa_rsem, "start")

    own_send(0, "start")
    own_send(1, "start")
    spread(tok, tok_all, 0, "start")
    own_send(2, "start")
    prod[pl.ds(0, 8), :] = jnp.zeros((8, ch), F32)
    await_bytes(small_own, lsem.at[2])
    plane_wait(small_own, sa_rsem)
    far(planes, planes, sz_ssem, sz_rsem, "start")
    gather_send(0)
    gather_send(1)
    gather_send(2)
    own_send(3, "start")
    own_send(4, "start")
    far_wait(planes, sz_rsem)

    share = 2 * D // count
    rows_of = {}
    for n in range(count):
        first = n * share // 128
        rows_of.setdefault(first, []).append((n, 0))
        if (n * share + share - 1) // 128 > first:
            rows_of.setdefault(first + 1, []).append((n, 1))
    for tile, pieces in rows_of.items():
        value = sum(small_all[n, r : r + 1, :] for n, r in pieces)
        i, j = tile // (D // 128), tile % (D // 128)
        gains[i : i + 1, j * 128 : (j + 1) * 128] = value
    rows_of = {}
    for m in range(3 * count):
        n, piece = m // 3, m % 3
        tap, rest = m // count, m % count
        lane = rest // group * cblk
        rows_of.setdefault((tap, lane // 128), []).append((n, 2 + 2 * piece, rest % group))
        if (lane + block - 1) // 128 > lane // 128:
            rows_of.setdefault((tap, lane // 128 + 1), []).append((n, 3 + 2 * piece, rest % group))
    for (tap, tile), pieces in rows_of.items():
        value = jnp.zeros((1, 128), F32)
        for t2 in range(group):
            value = value + jnp.where(t == t2, sum(small_all[n, r : r + 1, :] for n, r, p in pieces if p == t2), 0.0)
        taps[tap : tap + 1, tile * 128 : (tile + 1) * 128] = value

    for q in range(group):
        await_bytes(tok_all.at[q], ag_rsem.at[0, q])
        fetch(tok_all.at[q], act.at[span(q)], 0)

        def normed_rows(i, carry, q=q):
            here = pl.ds(pl.multiple_of(q * seg + i * ROW_TILE, ROW_TILE), ROW_TILE)
            row = act[here, :].astype(F32)
            s1 = lax.rsqrt(jnp.mean(row * row, axis=-1, keepdims=True) + EPS_NORM)
            act[here, :] = (row * s1 * gains[0:1, :]).astype(BF)
            return carry

        lax.fori_loop(0, seg // ROW_TILE, normed_rows, 0, unroll=2)
        if q == 0:
            spread(bck_own, bck_all, 1, "start")
    keep_normed = pltpu.make_async_copy(act, nrm_far, lsem.at[2])
    keep_normed.start()
    own_send(5, "start")
    gather_pass(0)
    gather_send(3)
    own_send(6, "start")
    gather_pass(1)
    gather_wait(0)
    fetch(wi_all, wi, 0)
    gather_wait(1)
    fetch(wo_all, wo, 0)
    keep_normed.wait()

    for q in range(group):
        for k in range(blocks):
            acc_y[span(q), pl.ds(k * 384, 384)] = dot(
                act[span(q), :], wi[:, :, :, pl.ds(k * 384, 384)].reshape(D, 384)
            )
        for k in range(blocks):
            col = pl.ds(k * 128, 128)
            prod[pl.ds(q * seg + 8, seg), col] = acc_y[span(q), lanes(k, 0)] * acc_y[span(q), lanes(k, 2)]
            cv = (
                taps[0:1, col] * prod[pl.ds(q * seg + 6, seg), col]
                + taps[1:2, col] * prod[pl.ds(q * seg + 7, seg), col]
                + taps[2:3, col] * prod[pl.ds(q * seg + 8, seg), col]
            )
            conv[span(q), col] = cv
            gated[span(q), col] = (acc_y[span(q), lanes(k, 1)] * cv).astype(BF)
        for n in range(4):
            col = pl.ds(n * 384, 384)
            stage[q, :, col] = dot(gated[span(q), :], wo[:, :, :, col].reshape(ch, 384)).astype(BF)
        give(stage.at[q], rs_br, 0, q, "start")

    spill = pltpu.make_async_copy(acc_y.at[:, pl.ds(0, 3 * ch)], mixed_far, lsem.at[2])
    spill.start()
    gather_pass(2)
    gather_send(4)
    for i in range(7, 2 + chunks):
        own_send(i, "start")

    for q in range(group):
        await_bytes(bck_all.at[q], ag_rsem.at[1, q])
        fetch(bck_all.at[q], bck.at[span(q)], 0)
        bck_t[:, span(q)] = bck[span(q), :].T

    for q in range(group):
        await_bytes(rs_br.at[q], rs_rsem.at[0, q])
    for q in range(group):
        give(stage.at[q], rs_br, 0, q, "end")
    fetch(rs_br, stage, 0)

    def arrived(here):
        total = stage[0, here, :].astype(F32)
        for q in range(1, group):
            total = total + stage[q, here, :].astype(F32)
        return total

    def middle_rows(i, carry):
        here = rows16(i)
        mi = tok[here, :].astype(F32) + arrived(here)
        mid[here, :] = mi
        s2 = lax.rsqrt(jnp.mean(mi * mi, axis=-1, keepdims=True) + EPS_NORM)
        low[here, :] = (mi * s2 * gains[1:2, :]).astype(BF)
        return carry

    lax.fori_loop(0, seg // ROW_TILE, middle_rows, 0)
    spread(low, n2_all, 2, "start")
    gather_pass(3)
    gather_send(5)
    gather_wait(2)
    pltpu.make_async_copy(wf_all.at[0], ws.at[0], wsem.at[0]).start()
    spill.wait()

    def clear(i, carry):
        here = rows16(i)
        acc_y[here, :] = jnp.zeros((ROW_TILE, D), F32)
        acc_n[here, :] = jnp.zeros((ROW_TILE, D), F32)
        return carry

    lax.fori_loop(0, seq // ROW_TILE, clear, 0)
    for q in range(group):
        await_bytes(n2_all.at[q], ag_rsem.at[2, q])
        fetch(n2_all.at[q], act.at[span(q)], 0)
        act_t[:, span(q)] = act[span(q), :].T

    def chunk_refs(kind, c):
        if kind == "f":
            return lax.rem(c, 2), c, sib_f.at[c], z_f.at[c], pl.ds(0, WIDTH), None
        n = chunks + c
        return n % 2, n, sib_i.at[c], z_i.at[c], pl.ds(0, 128), None

    def pair_send(kind, c, op):
        s, n, sib, _, cols, _ = chunk_refs(kind, c)
        copy = remote(grad.at[s, :, :, 1 - b, :, cols], sib, gs_ssem.at[n], gs_rsem.at[n], mate)
        if op == "start":
            copy.start()
        else:
            copy.wait_send()

    def part_sends(kind, c, op):
        s, n, _, z, cols, _ = chunk_refs(kind, c)

        def one(k, carry):
            o2, dev = peer(k)
            copy = remote(
                part.at[s, :, o2, :, cols], z.at[:, o], gz_ssem.at[n, k], gz_rsem.at[n, o], dev
            )
            if op == "start":
                copy.start()
            else:
                copy.wait_send()
            return carry

        lax.fori_loop(1, out_n, one, 0)
        keep = pltpu.make_async_copy(part.at[s, :, o, :, cols], z.at[:, o], keep_sem.at[n])
        if op == "start":
            keep.start()
        else:
            keep.wait()

    def pair_sum(kind, c):
        s, n, sib, _, cols, _ = chunk_refs(kind, c)
        await_bytes(sib, gs_rsem.at[n])
        fetch(sib, sibv.at[:, :, :, cols], 1)

        def one(i, carry):
            j, o2 = i // out_n, lax.rem(i, out_n)
            part[s, j, o2, :, cols] = (
                grad[s, j, o2, b, :, cols].astype(F32) + sibv[j, o2, :, cols].astype(F32)
            ).astype(BF)
            return carry

        lax.fori_loop(0, 3 * out_n, one, 0)
        part_sends(kind, c, "start")

    def out_slot(n):
        return (n // (2 * out_n), slice(None), lax.rem(n, 2 * out_n) // 2, lax.rem(n, 2))

    def hand_back(kind, c, op):
        _, n, _, _, cols, _ = chunk_refs(kind, c)
        dst = (g_ff if kind == "f" else g_wi)
        if not direct:
            if op == "start":
                h, _, o2, p = out_slot(n)
                fetch(ws.at[h, :, o2, p, :, cols], dst.at[c], 1)
            return
        h, _, o2, p = out_slot(n)
        for q in range(group):
            src = ws.at[h, :, o2, p, pl.ds(q * block, block), cols]
            switch(
                (a == b) & (q == g),
                pltpu.make_async_copy(src, dst.at[t, c], back_rsem.at[n, t]),
                remote(src, dst.at[t, c], back_ssem.at[n, q], back_rsem.at[n, t], (2 * o + b, q)),
                op,
            )

    def hand_wait(kind, c):
        if direct:
            _, n, _, _, _, _ = chunk_refs(kind, c)
            for t2 in range(group):
                await_bytes((g_ff if kind == "f" else g_wi).at[t2, c], back_rsem.at[n, t2])

    def total(kind, c):
        s, n, _, z, cols, _ = chunk_refs(kind, c)
        h, _, place_o, place_p = out_slot(n)

        def one(k, carry):
            await_bytes(z.at[:, o], gz_rsem.at[n, peer(k)[0]])
            return carry

        lax.fori_loop(1, out_n, one, 0)
        fetch(z, sibv.at[:, :, :, cols], 1)

        def add(i, carry):
            j = i // (rows_n // 48)
            here = pl.ds(pl.multiple_of(lax.rem(i, rows_n // 48) * 48, 16), 48)
            value = sibv[j, 0, here, cols].astype(F32)
            for o2 in range(1, out_n):
                value = value + sibv[j, o2, here, cols].astype(F32)
            ws[h, j, place_o, place_p, here, cols] = value.astype(BF)
            return carry

        lax.fori_loop(0, 3 * (rows_n // 48), add, 0)
        hand_back(kind, c, "start")

    half = out_n // 2

    def grad_rows(h):
        return pl.ds(pl.multiple_of(h * (D // 2), D // 2), D // 2), pl.ds(h * half, half)

    def hidden_chunk(c, carry):
        s = lax.rem(c, 2)
        await_bytes(ws.at[s], wsem.at[s])
        hid, dgt, dup = (pl.ds(j * WIDTH, WIDTH) for j in range(3))

        def token_tile(m, carry):
            here = pl.ds(pl.multiple_of(m * seg, seg), seg)
            n2 = act[here, :]
            gate = dot(n2, ws[s, 0].reshape(D, WIDTH))
            upper = dot(n2, ws[s, 1].reshape(D, WIDTH))
            d_hidden = dot(bck[here, :], ws[s, 2].reshape(D, WIDTH))
            sigma = jax.nn.sigmoid(gate)
            active = gate * sigma
            dmix[here, hid] = (active * upper).astype(BF)
            dmix[here, dgt] = (d_hidden * upper * (sigma * (1.0 + gate * (1.0 - sigma)))).astype(BF)
            dmix[here, dup] = (d_hidden * active).astype(BF)
            acc_y[here, :] += dot_t(dmix[here, hid], ws[s, 2].reshape(D, WIDTH))
            acc_n[here, :] += dot_t(dmix[here, dgt], ws[s, 0].reshape(D, WIDTH))
            acc_n[here, :] += dot_t(dmix[here, dup], ws[s, 1].reshape(D, WIDTH))
            return carry

        lax.fori_loop(0, group, token_tile, 0)

        @pl.when(c >= 2)
        def _():
            pair_send("f", c - 2, "end")

        def grad_tile(h, carry):
            rows, os = grad_rows(h)
            shape = (half, 2, rows_n, WIDTH)
            grad[s, 0, os] = dot(act_t[rows, :], dmix[:, dgt]).astype(BF).reshape(shape)
            grad[s, 1, os] = dot(act_t[rows, :], dmix[:, dup]).astype(BF).reshape(shape)
            grad[s, 2, os] = dot(bck_t[rows, :], dmix[:, hid]).astype(BF).reshape(shape)
            return carry

        lax.fori_loop(0, 2, grad_tile, 0)
        pair_send("f", c, "start")

        @pl.when(c >= 3)
        def _():
            part_sends("f", c - 3, "end")

        @pl.when(c >= 1)
        def _():
            pair_sum("f", c - 1)

        @pl.when(c + 2 < chunks)
        def _():
            gather_pass(c + 4)

        @pl.when(c + 4 < chunks)
        def _():
            gather_send(c + 6)

        @pl.when(c + 1 < chunks)
        def _():
            gather_wait(c + 3)
            pltpu.make_async_copy(wf_all.at[c + 1], ws.at[1 - s], wsem.at[1 - s]).start()

        return carry

    lax.fori_loop(0, chunks, hidden_chunk, 0)

    for q in range(group):
        stage[q] = acc_n[span(q), :].astype(BF)
        give(stage.at[q], rs_n2, 1, q, "start")
    part_sends("f", chunks - 3, "end")
    pair_sum("f", chunks - 1)
    total("f", 0)
    total("f", 1)
    for q in range(group):
        give(stage.at[q], rs_n2, 1, q, "end")
    for q in range(group):
        await_bytes(rs_n2.at[q], rs_rsem.at[1, q])
    spread(low, n2_all, 2, "end")
    fetch(rs_n2, stage, 0)
    fetch(bck_own, act.at[span(0)], 0)
    g_gains[...] = jnp.zeros_like(g_gains)

    def d_middle_rows(i, carry):
        here = rows16(i)
        dn = arrived(here)
        mi = mid[here, :]
        s2 = lax.rsqrt(jnp.mean(mi * mi, axis=-1, keepdims=True) + EPS_NORM)
        e2 = gains[1:2, :] * dn
        back = act[here, :].astype(F32)
        dm = back + s2 * e2 - mi * (s2 * s2 * s2) * jnp.mean(e2 * mi, axis=-1, keepdims=True)
        dmid[here, :] = dm
        low[here, :] = dm.astype(BF)
        g_gains[1] += jnp.sum((dn * mi * s2).reshape(ROW_TILE // 8, 8, D), axis=0)
        return carry

    lax.fori_loop(0, seg // ROW_TILE, d_middle_rows, 0)
    spread(low, dbr_all, 3, "start")

    for q in range(group):
        stage[q] = acc_y[span(q), :].astype(BF)
        give(stage.at[q], rs_y, 2, q, "start")
    spill_back = pltpu.make_async_copy(mixed_far, acc_y.at[:, pl.ds(0, 3 * ch)], lsem.at[2])
    spill_back.start()

    for q in range(group):
        bck_t[pl.ds(0, ch), span(q)] = gated[span(q), :].T
        fetch(nrm_far.at[span(q)], act.at[span(q)], 0)
        act_t[:, span(q)] = act[span(q), :].T
    spill_back.wait()
    total("f", 2)
    total("f", 3)

    acc_n[pl.ds(seq, 8), pl.ds(0, ch)] = jnp.zeros((8, ch), F32)
    for q in range(group):
        await_bytes(dbr_all.at[q], ag_rsem.at[3, q])
        fetch(dbr_all.at[q], bck.at[span(q)], 0)
        acc_n[span(q), pl.ds(ch, ch)] = dot_t(bck[span(q), :], wo[...].reshape(ch, D))
        for k in range(blocks):
            col = pl.ds(k * 128, 128)
            d_gated = acc_n[span(q), pl.ds(ch + k * 128, 128)]
            acc_n[span(q), col] = d_gated * acc_y[span(q), lanes(k, 1)]
            dmix[span(q), lanes(k, 1)] = (d_gated * conv[span(q), col]).astype(BF)
    g_taps[...] = jnp.zeros_like(g_taps)
    for q in range(group):
        for k in range(blocks):
            col = pl.ds(k * 128, 128)
            d0 = acc_n[span(q), col]
            for n in range(3):
                g_taps[n, :, col] += jnp.sum(
                    (d0 * prod[pl.ds(q * seg + 6 + n, seg), col]).reshape(seg // 8, 8, 128), axis=0
                )
            d_product = (
                taps[2:3, col] * d0
                + taps[1:2, col] * acc_n[pl.ds(q * seg + 1, seg), col]
                + taps[0:1, col] * acc_n[pl.ds(q * seg + 2, seg), col]
            )
            dmix[span(q), lanes(k, 0)] = (d_product * acc_y[span(q), lanes(k, 2)]).astype(BF)
            dmix[span(q), lanes(k, 2)] = (d_product * acc_y[span(q), lanes(k, 0)]).astype(BF)

    for k in range(blocks):
        s = (chunks + k) % 2
        if k < 2:
            pair_send("f", chunks - 2 + k, "end")
        else:
            pair_send("i", k - 2, "end")

        def intake_tile(h, carry, k=k, s=s):
            rows, os = grad_rows(h)
            value = dot(act_t[rows, :], dmix[:, pl.ds(k * 384, 384)]).astype(BF)
            for j in range(3):
                grad[s, j, os, :, :, pl.ds(0, 128)] = value[:, j * 128 : (j + 1) * 128].reshape(
                    half, 2, rows_n, 128
                )
            return carry

        lax.fori_loop(0, 2, intake_tile, 0)
        pair_send("i", k, "start")
        if k >= 1:
            if k <= 2:
                part_sends("f", chunks - 3 + k, "end")
            else:
                part_sends("i", k - 3, "end")
            pair_sum("i", k - 1)

    for n in range(4):
        col = pl.ds(n * 384, 384)
        wo[:, :, :, col] = dot(bck_t[pl.ds(0, ch), :], bck[:, col]).astype(BF).reshape(out_n, 2, cblk, 384)
    last = chunks + blocks
    pair_o = remote(wo.at[:, 1 - b], sib_o, gs_ssem.at[last], gs_rsem.at[last], mate)
    pair_o.start()
    if blocks <= 2:
        part_sends("f", chunks - 3 + blocks, "end")
    else:
        part_sends("i", blocks - 3, "end")
    pair_sum("i", blocks - 1)

    await_bytes(sib_o, gs_rsem.at[last])
    fetch(sib_o, sibo, 1)

    def add_o(o2, carry):
        parto[o2] = (wo[o2, b].astype(F32) + sibo[o2].astype(F32)).astype(BF)
        return carry

    lax.fori_loop(0, out_n, add_o, 0)

    def part_o(op):
        def one(k, carry):
            o2, dev = peer(k)
            copy = remote(parto.at[o2], z_o.at[o], gz_ssem.at[last, k], gz_rsem.at[last, o], dev)
            if op == "start":
                copy.start()
            else:
                copy.wait_send()
            return carry

        lax.fori_loop(1, out_n, one, 0)
        keep = pltpu.make_async_copy(parto.at[o], z_o.at[o], keep_sem.at[last])
        if op == "start":
            keep.start()
        else:
            keep.wait()

    part_o("start")

    for q in range(group):
        give(stage.at[q], rs_y, 2, q, "end")
    for q in range(group):
        await_bytes(rs_y.at[q], rs_rsem.at[2, q])
    for q in range(group):
        for n in range(4):
            stage[q, :, pl.ds(n * 384, 384)] = dot_t(
                dmix[span(q), :], wi[pl.ds(n * out_n // 4, out_n // 4)].reshape(384, 3 * ch)
            ).astype(BF)
        give(stage.at[q], rs_n1, 3, q, "start")

    spread(low, dbr_all, 3, "end")
    for q in range(group):
        fetch(rs_y.at[q], act.at[span(q)], 0)

    def out_rows(i, carry):
        here = rows16(i)
        value = act[here, :].astype(F32)
        for q in range(1, group):
            value = value + act[pl.ds(pl.multiple_of(q * seg + i * ROW_TILE, ROW_TILE), ROW_TILE), :].astype(F32)
        low[here, :] = (mid[here, :] + value).astype(BF)
        return carry

    lax.fori_loop(0, seg // ROW_TILE, out_rows, 0)
    fetch(low, block_out, 0)

    def total_f(c, carry):
        total("f", c)
        return carry

    lax.fori_loop(4, chunks, total_f, 0)
    for q in range(group):
        give(stage.at[q], rs_n1, 3, q, "end")
    for q in range(group):
        await_bytes(rs_n1.at[q], rs_rsem.at[3, q])
    fetch(rs_n1, stage, 0)

    def d_rows(i, carry):
        here = rows16(i)
        dn = arrived(here)
        row = tok[here, :].astype(F32)
        s1 = lax.rsqrt(jnp.mean(row * row, axis=-1, keepdims=True) + EPS_NORM)
        e1 = gains[0:1, :] * dn
        low[here, :] = (
            dmid[here, :] + s1 * e1 - row * (s1 * s1 * s1) * jnp.mean(e1 * row, axis=-1, keepdims=True)
        ).astype(BF)
        g_gains[0] += jnp.sum((dn * row * s1).reshape(ROW_TILE // 8, 8, D), axis=0)
        return carry

    lax.fori_loop(0, seg // ROW_TILE, d_rows, 0)
    fetch(low, input_grad, 0)

    sm_mine[...] = jnp.zeros_like(sm_mine)
    for i in range(2):
        value = jnp.sum(g_gains[i], axis=0, keepdims=True)
        for j in range(D // 128):
            row = i * (D // 128) + j
            sm_mine[row : row + 1, :] = value[:, j * 128 : (j + 1) * 128]
    for n in range(3):
        value = jnp.sum(g_taps[n], axis=0, keepdims=True)
        for k in range(blocks):
            for t2 in range(group):
                row = 2 * (D // 128) + (t2 * 3 + n) * blocks + k
                sm_mine[row : row + 1, :] = jnp.where(t == t2, value[:, k * 128 : (k + 1) * 128], 0.0)
    sm_plane[place] = sm_mine[...]
    plane(sm_mine, sm_plane.at[place], ta_ssem, ta_rsem, "start")

    for k in range(max(0, blocks - 2), blocks):
        part_sends("i", k, "end")
        pair_send("i", k, "end")
    total("i", 0)
    plane_wait(sm_mine, ta_rsem)
    value = sm_plane[0]
    for i in range(1, 2 * group):
        value = value + sm_plane[i]
    sm_sum[...] = value
    sm_z[o] = value
    far(sm_sum, sm_z.at[o], tz_ssem, tz_rsem, "start")
    for k in range(1, blocks):
        total("i", k)
    part_o("end")
    pair_o.wait_send()

    def last_one(k, carry):
        await_bytes(z_o.at[o], gz_rsem.at[last, peer(k)[0]])
        return carry

    lax.fori_loop(1, out_n, last_one, 0)
    fetch(z_o, sibo, 1)
    value = sibo[0].astype(F32)
    for o2 in range(1, out_n):
        value = value + sibo[o2].astype(F32)
    outo = parto.at[0]
    outo[...] = value.astype(BF)

    def back_o(op):
        switch(
            a == b,
            pltpu.make_async_copy(outo, g_wo, back_rsem.at[last, 0]),
            remote(outo, g_wo, back_ssem.at[last, 0], back_rsem.at[last, 0], (2 * o + b, 2 * y + a)),
            op,
        )

    back_o("start")
    far_wait(sm_sum, tz_rsem)
    value = sm_z[0]
    for i in range(1, out_n):
        value = value + sm_z[i]
    g_small[...] = value

    plane(small_own, small_all.at[mine], sa_ssem, sa_rsem, "end")
    far(planes, planes, sz_ssem, sz_rsem, "end")
    plane(sm_mine, sm_plane.at[place], ta_ssem, ta_rsem, "end")
    far(sm_sum, sm_z.at[o], tz_ssem, tz_rsem, "end")
    spread(tok, tok_all, 0, "end")
    spread(bck_own, bck_all, 1, "end")
    gather_close(0)
    gather_close(1)

    def close(c, carry):
        gather_close(c + 2)
        hand_back("f", c, "end")
        hand_wait("f", c)
        return carry

    lax.fori_loop(0, chunks, close, 0)
    for k in range(blocks):
        hand_back("i", k, "end")
        hand_wait("i", k)
    back_o("end")
    await_bytes(g_wo, back_rsem.at[last, 0])


def forward_backward(sizes, tok, bck, wi_own, wo_own, ff_own, small_own):
    (out_n, group, rows_n, seg, ch, cblk, chunks) = sizes
    blocks = ch // 128
    seq = group * seg
    block = rows_n // group
    places = 2 * group
    small_rows = -(-(2 * D // 128 + group * 3 * blocks) // 8) * 8
    items = 2 + chunks
    sums = chunks + blocks + 1
    vm = pltpu.VMEM
    dma = pltpu.SemaphoreType.DMA

    def shape(*dims, dtype=BF):
        return jax.ShapeDtypeStruct(dims, dtype)

    any_spec = pl.BlockSpec(memory_space=pl.ANY)
    vmem_spec = pl.BlockSpec(memory_space=pltpu.VMEM)
    if block % 16 == 0:
        given = [shape(group, chunks, 3, block, WIDTH), shape(group, blocks, 3, block, 128)]
    else:
        given = [shape(chunks, 3, rows_n, WIDTH), shape(blocks, 3, rows_n, 128)]
    outs = [
        shape(seg, D), shape(seg, D), *given, shape(cblk, D), shape(small_rows, 128, dtype=F32),
        shape(chunks, 3, out_n, 2, rows_n, WIDTH), shape(out_n, 2, rows_n, 3 * ch), shape(out_n, 2, cblk, D),
        shape(group, seg, D), shape(seq, D), shape(group, seg, D), shape(group, seg, D), shape(group, seg, D),
        shape(group, seg, D), shape(group, seg, D), shape(group, seg, D), shape(group, seg, D),
        shape(chunks, 3, out_n, rows_n, WIDTH), shape(blocks, 3, out_n, rows_n, 128), shape(out_n, cblk, D),
        shape(chunks, 3, out_n, rows_n, WIDTH), shape(blocks, 3, out_n, rows_n, 128), shape(out_n, cblk, D),
        shape(seq, 3 * ch, dtype=F32),
    ]
    out_specs = [any_spec] * 5 + [vmem_spec] + [any_spec] * (len(outs) - 6)
    scratch = [
        vm((2, 3, out_n, 2, rows_n, WIDTH), BF),
        vm((out_n, 2, rows_n, 3 * ch), BF),
        vm((out_n, 2, cblk, D), BF),
        vm((seq, D), BF), vm((D, seq), BF), vm((seq, D), BF), vm((D, seq), BF),
        vm((seq, D), F32), vm((seq + 8, D), F32),
        vm((2, 3, out_n, 2, rows_n, WIDTH), BF),
        vm((3, out_n, rows_n, WIDTH), BF),
        vm((2, 3, out_n, rows_n, WIDTH), BF),
        vm((group, seg, D), BF),
        vm((seq + 8, ch), F32), vm((seq, ch), F32), vm((seq, ch), BF), vm((seq, 3 * ch), BF),
        vm((seg, D), F32), vm((seg, D), F32), vm((seg, D), BF),
        vm((out_n, cblk, D), BF), vm((out_n, cblk, D), BF),
        vm((places * out_n, 8, 128), F32), vm((2, D), F32), vm((3, ch), F32),
        vm((2, 8, D), F32), vm((3, 8, ch), F32),
        vm((small_rows, 128), F32), vm((places, small_rows, 128), F32),
        vm((small_rows, 128), F32), vm((out_n, small_rows, 128), F32),
        dma((4, group)), dma((4, group)), dma((4, group)), dma((4, group)),
        dma((items, out_n)), dma((items, out_n)), dma((items,)), dma((items,)),
        dma((sums,)), dma((sums,)), dma((sums, out_n)), dma((sums, out_n)), dma((sums,)),
        dma((items, group)), dma((items, group)), dma((sums, group)), dma((sums, group)),
        dma((places,)), dma((places,)), dma((out_n,)), dma((out_n,)),
        dma((places,)), dma((places,)), dma((out_n,)), dma((out_n,)), dma((2,)), dma((3,)),
    ]
    results = pl.pallas_call(
        functools.partial(block_kernel, sizes),
        out_shape=outs,
        in_specs=[vmem_spec] + [any_spec] * 4 + [vmem_spec],
        out_specs=out_specs,
        scratch_shapes=scratch,
        compiler_params=pltpu.CompilerParams(
            collective_id=0, has_side_effects=True, vmem_limit_bytes=63 * 1024 * 1024
        ),
        cost_estimate=pl.CostEstimate(
            flops=6 * seq * D * (4 * ch + 3 * chunks * WIDTH),
            bytes_accessed=200_000_000,
            transcendentals=seq * chunks * WIDTH,
        ),
    )(tok, bck, wi_own, wo_own, ff_own, small_own)
    return results[:6]


def body(
    tokens,
    cotangent,
    lengths,
    intake_weight,
    intake_first,
    intake_second,
    output_weight,
    output_first,
    output_second,
    swiglu_weight,
    swiglu_first,
    swiglu_second,
    down_weight,
    down_first,
    down_second,
    norm_gains,
    gains_first,
    gains_second,
    conv_kernel,
    kernel_first,
    kernel_second,
):
    data_count = lax.axis_size("dp")
    group_count = lax.axis_size("group")
    dp = lax.axis_index("dp")
    member = lax.axis_index("group")
    block = D // (data_count * group_count)
    cblk = -(-block // 16) * 16
    ch = data_count * cblk
    blocks = ch // 128
    hidden_part = FF // group_count
    chunks = -(-hidden_part // WIDTH)
    hidden_full = chunks * WIDTH
    rows_n = D // data_count
    swap = []
    for one in range(data_count):
        for two in range(group_count):
            there = (2 * (one // 2) + two % 2) * group_count + 2 * (two // 2) + one % 2
            swap.append((one * group_count + two, there))

    def cross(value):
        return lax.ppermute(value, ("dp", "group"), swap)

    intake_local = (
        intake_weight.astype(BF)
        .reshape(block, 3, data_count, group_count, block)
        .transpose(3, 0, 1, 2, 4)
    )
    intake_local = jnp.pad(intake_local, ((0, 0),) * 4 + ((0, cblk - block),))
    intake_local = (
        intake_local.reshape(group_count, block, 3, blocks, 128)
        .transpose(0, 1, 3, 2, 4)
        .reshape(group_count, block, 3 * ch)
    )
    ff_local = jnp.concatenate(
        [
            swiglu_weight.astype(BF).reshape(block, 2, group_count, hidden_part),
            down_weight.astype(BF).reshape(block, 1, group_count, hidden_part),
        ],
        axis=1,
    )
    ff_local = jnp.pad(ff_local, ((0, 0),) * 3 + ((0, hidden_full - hidden_part),))
    ff_local = ff_local.reshape(block, 3, group_count, chunks, WIDTH).transpose(2, 3, 1, 0, 4)
    wo_own = jnp.pad(output_weight.astype(BF).reshape(block, D), ((0, cblk - block), (0, 0)))
    if block % 16 == 0:
        wi_own, ff_own = intake_local, ff_local
    else:
        wi_own = lax.all_to_all(intake_local, "group", split_axis=0, concat_axis=0, tiled=True)
        wi_own = cross(wi_own.reshape(rows_n, 3 * ch))
        ff_own = lax.all_to_all(ff_local, "group", split_axis=0, concat_axis=0, tiled=True)
        ff_own = cross(ff_own.transpose(1, 2, 0, 3, 4).reshape(chunks, 3, rows_n, WIDTH))

    number = dp * group_count + member
    share = norm_gains.shape[0]

    def placed(values, lane):
        line = lax.dynamic_update_slice(jnp.zeros((256,), F32), lax.reduce_precision(values, 8, 7), (lane,))
        return line.reshape(2, 128)

    runs = [placed(norm_gains, lax.rem(number * share, 128))]
    for piece in range(3):
        rest = lax.rem(3 * number + piece, data_count * group_count)
        lane = lax.rem(rest // group_count * cblk, 128)
        runs.append(placed(conv_kernel[piece * block : (piece + 1) * block], lane))
    small_own = jnp.concatenate(runs)

    seg_len = tokens.shape[1]
    positions = member * seg_len + lax.iota(jnp.int32, seg_len)
    valid = (positions < lengths[0]).astype(F32)[:, None]
    back_low = (cotangent[0].astype(F32) * valid).astype(BF)

    sizes = (data_count // 2, group_count, rows_n, seg_len, ch, cblk, chunks)
    block_out, input_grad, g_ff, g_wi, g_wo, g_small = forward_backward(
        sizes, tokens[0], back_low, wi_own, wo_own, ff_own, small_own
    )

    if block % 16:
        g_wi = cross(g_wi).reshape(blocks, 3, group_count, block, 128).transpose(2, 0, 1, 3, 4)
        g_wi = lax.all_to_all(g_wi, "group", split_axis=0, concat_axis=0, tiled=True)
        g_ff = cross(g_ff).reshape(chunks, 3, group_count, block, WIDTH).transpose(2, 0, 1, 3, 4)
        g_ff = lax.all_to_all(g_ff, "group", split_axis=0, concat_axis=0, tiled=True)
    g_wi = g_wi.transpose(0, 3, 2, 1, 4).reshape(group_count, block, 3, data_count, cblk)
    intake_grad_flat = g_wi[..., :block].transpose(1, 2, 3, 0, 4).reshape(-1).astype(F32)
    g_ff = g_ff.transpose(3, 2, 0, 1, 4).reshape(block, 3, group_count, hidden_full)
    g_ff = g_ff[..., :hidden_part]
    swiglu_grad_flat = g_ff[:, :2].reshape(-1).astype(F32)
    down_grad_flat = g_ff[:, 2].reshape(-1).astype(F32)
    output_grad_flat = g_wo[:block].reshape(-1).astype(F32)

    gain_rows = 2 * D // 128
    taps_grad = g_small[gain_rows : gain_rows + group_count * 3 * blocks]
    taps_grad = taps_grad.reshape(group_count, 3, data_count, cblk)[..., :block]
    taps_grad = taps_grad.transpose(1, 2, 0, 3).reshape(-1)
    small_shards = (
        lax.dynamic_slice(g_small[:gain_rows].reshape(-1), (number * share,), (share,)),
        lax.dynamic_slice(taps_grad, (number * 3 * block,), (3 * block,)),
    )
    intake_new = update(
        intake_weight, intake_first, intake_second, intake_grad_flat, RATE_MATRIX, DECAY
    )
    output_new = update(
        output_weight, output_first, output_second, output_grad_flat, RATE_MATRIX, DECAY
    )
    swiglu_new = update(
        swiglu_weight, swiglu_first, swiglu_second, swiglu_grad_flat, RATE_MATRIX, DECAY
    )
    down_new = update(down_weight, down_first, down_second, down_grad_flat, RATE_MATRIX, DECAY)
    gains_new = update(norm_gains, gains_first, gains_second, small_shards[0], RATE_VECTOR, 0.0)
    kernel_new = update(
        conv_kernel, kernel_first, kernel_second, small_shards[1], RATE_VECTOR, DECAY
    )
    return (
        block_out[None],
        input_grad[None],
        intake_new[0],
        intake_new[1],
        intake_new[2],
        output_new[0],
        output_new[1],
        output_new[2],
        swiglu_new[0],
        swiglu_new[1],
        swiglu_new[2],
        down_new[0],
        down_new[1],
        down_new[2],
        gains_new[0],
        gains_new[1],
        gains_new[2],
        kernel_new[0],
        kernel_new[1],
        kernel_new[2],
    )


def solution(mesh):
    in_specs = (
        P("dp", "group", None),
        P("dp", "group", None),
        P("dp"),
        P(("dp", "group")),
        P(("dp", "group")),
        P(("dp", "group")),
        P(("dp", "group")),
        P(("dp", "group")),
        P(("dp", "group")),
        P(("dp", "group")),
        P(("dp", "group")),
        P(("dp", "group")),
        P(("dp", "group")),
        P(("dp", "group")),
        P(("dp", "group")),
        P(("dp", "group")),
        P(("dp", "group")),
        P(("dp", "group")),
        P(("dp", "group")),
        P(("dp", "group")),
        P(("dp", "group")),
    )
    out_specs = (
        P("dp", "group", None),
        P("dp", "group", None),
        P(("dp", "group")),
        P(("dp", "group")),
        P(("dp", "group")),
        P(("dp", "group")),
        P(("dp", "group")),
        P(("dp", "group")),
        P(("dp", "group")),
        P(("dp", "group")),
        P(("dp", "group")),
        P(("dp", "group")),
        P(("dp", "group")),
        P(("dp", "group")),
        P(("dp", "group")),
        P(("dp", "group")),
        P(("dp", "group")),
        P(("dp", "group")),
        P(("dp", "group")),
        P(("dp", "group")),
    )
    return jax.shard_map(body, mesh=mesh, in_specs=in_specs, out_specs=out_specs, check_vma=False)
```

```python
import functools

import jax
import jax.numpy as jnp
from jax import lax
from jax.experimental import pallas as pl
from jax.experimental.pallas import tpu as pltpu
from jax.sharding import PartitionSpec as P

D = 1536
FF = 6912
STEP = 5
WIDTH = 256
ROW_TILE = 16

EPS_NORM = 1e-05
BETA_ONE = 0.5
BETA_TWO = 0.5
ADAM_EPS = 1e-08
RATE_MATRIX = 0.02
RATE_VECTOR = 0.2
DECAY = 0.1

MESH = pl.DeviceIdType.MESH
BF = jnp.bfloat16
F32 = jnp.float32


def update(weight, first, second, grad, rate, decay):
    first_new = BETA_ONE * first + (1.0 - BETA_ONE) * grad
    second_new = BETA_TWO * second + (1.0 - BETA_TWO) * grad * grad
    first_hat = first_new / (1.0 - BETA_ONE**STEP)
    second_hat = second_new / (1.0 - BETA_TWO**STEP)
    weight_new = weight - rate * (first_hat / (jnp.sqrt(second_hat) + ADAM_EPS) + decay * weight)
    return (first_new, second_new, weight_new)


def dot(left, right):
    return lax.dot_general(left, right, (((1,), (0,)), ((), ())), preferred_element_type=F32)


def dot_t(left, right):
    return lax.dot_general(left, right, (((1,), (1,)), ((), ())), preferred_element_type=F32)


def await_bytes(ref, sem):
    pltpu.make_async_copy(ref, ref, sem).wait()


def block_kernel(
    sizes,
    tok, bck_own, wi_own, wo_own, ff_own, small_own,
    block_out, input_grad, g_ff, g_wi, g_wo, g_small,
    wf_all, wi_all, wo_all, tok_all, nrm_far, bck_all, n2_all, dbr_all,
    rs_br, rs_y, rs_n2, rs_n1,
    sib_f, sib_i, sib_o, up_f, up_i, down_f, down_i, far_f, far_i, z_o, mixed_far,
    ws, wi, wo, act, act_t, bck, bck_t, acc_y, acc_n, grad, sibv, part, stage,
    prod, conv, gated, dmix, mid, dmid, low, sibo, parto,
    small_all, gains, taps, g_gains, g_taps, sm_mine, sm_plane, sm_sum, sm_z,
    ag_ssem, ag_rsem, rs_ssem, rs_rsem, z_ssem, z_rsem, f_ssem, f_rsem,
    gs_ssem, gs_rsem, gz_ssem, up_sem, down_sem, own_ssem, own_rsem, back_ssem, back_rsem, osem,
    sa_ssem, sa_rsem, sz_ssem, sz_rsem, ta_ssem, ta_rsem, tz_ssem, tz_rsem, wsem, lsem,
):
    (out_n, group, rows_n, seg, ch, cblk, chunks) = sizes
    block = rows_n // group
    direct = block % 16 == 0
    count = 2 * out_n * group
    blocks = ch // 128
    seq = group * seg
    dp = lax.axis_index("dp")
    g = lax.axis_index("group")
    o, a = dp // 2, lax.rem(dp, 2)
    y, b = g // 2, lax.rem(g, 2)
    t = 2 * y + a
    mate = (dp, g + 1 - 2 * b)

    def peer(k):
        o2 = lax.rem(o + k, out_n)
        return o2, (2 * o2 + a, g)

    barrier = pltpu.get_barrier_semaphore()
    for x2 in range(2):
        for g2 in range(group):
            @pl.when((x2 != a) | (g2 != g))
            def _():
                pl.semaphore_signal(barrier, inc=1, device_id=(2 * o + x2, g2), device_id_type=MESH)

    def greet(k, carry):
        pl.semaphore_signal(barrier, inc=1, device_id=peer(k)[1], device_id_type=MESH)
        return carry

    lax.fori_loop(1, out_n, greet, 0)
    pl.semaphore_wait(barrier, 2 * group - 1 + out_n - 1)

    def remote(src, dst, ssem, rsem, dev):
        return pltpu.make_async_remote_copy(
            src_ref=src, dst_ref=dst, send_sem=ssem, recv_sem=rsem, device_id=dev, device_id_type=MESH
        )

    def spread(src, dst, n, op):
        for t2 in range(group):
            ty, tx = t2 // 2, t2 % 2
            alone = (tx == a) & (ty == y) & (a == b)
            copy = remote(
                src, dst.at[g], ag_ssem.at[n, t2], ag_rsem.at[n, g], (2 * o + tx, 2 * ty + a)
            )
            if op == "start":
                @pl.when(alone)
                def _():
                    pltpu.make_async_copy(src, dst.at[g], ag_rsem.at[n, g]).start()

                @pl.when(jnp.logical_not(alone))
                def _():
                    copy.start()
            else:
                @pl.when(jnp.logical_not(alone))
                def _():
                    copy.wait_send()

    def give(src, dst, n, q, op):
        alone = (a == b) & (q == g)
        copy = remote(src, dst.at[t], rs_ssem.at[n, q], rs_rsem.at[n, t], (2 * o + b, q))
        if op == "start":
            @pl.when(alone)
            def _():
                pltpu.make_async_copy(src, dst.at[t], rs_rsem.at[n, t]).start()

            @pl.when(jnp.logical_not(alone))
            def _():
                copy.start()
        else:
            @pl.when(jnp.logical_not(alone))
            def _():
                copy.wait_send()

    def slot_of(i, o2, p):
        if isinstance(i, int) and i == 0:
            return wi_all.at[o2, p]
        if isinstance(i, int) and i == 1:
            return wo_all.at[o2, p]
        return wf_all.at[i - 2, :, o2, p]

    def half_of(i, p):
        if isinstance(i, int) and i == 0:
            return wi_all.at[:, p]
        if isinstance(i, int) and i == 1:
            return wo_all.at[:, p]
        return wf_all.at[i - 2, :, :, p]

    my_rows = pl.ds(pl.multiple_of(g * block, 4), block)

    def switch(alone, local, copy, op):
        if op == "start":
            @pl.when(alone)
            def _():
                local.start()

            @pl.when(jnp.logical_not(alone))
            def _():
                copy.start()
        else:
            @pl.when(jnp.logical_not(alone))
            def _():
                copy.wait_send()

    def own_send(i, op):
        if isinstance(i, int) and i == 1:
            dst = wo_all.at[o, a]
            switch(
                a == b,
                pltpu.make_async_copy(wo_own, dst, own_rsem.at[1, 0]),
                remote(wo_own, dst, own_ssem.at[1, 0], own_rsem.at[1, 0], (2 * o + b, 2 * y + a)),
                op,
            )
            return
        if not direct:
            src = wi_own if isinstance(i, int) and i == 0 else ff_own.at[i - 2]
            if op == "start":
                pltpu.make_async_copy(src, slot_of(i, o, b), own_rsem.at[i, 0]).start()
            return
        for t2 in range(group):
            ty, tx = t2 // 2, t2 % 2
            if isinstance(i, int) and i == 0:
                src, dst = wi_own.at[t2], wi_all.at[o, a, my_rows]
            else:
                src, dst = ff_own.at[t2, i - 2], wf_all.at[i - 2, :, o, a, my_rows]
            switch(
                (tx == a) & (ty == y) & (a == b),
                pltpu.make_async_copy(src, dst, own_rsem.at[i, g]),
                remote(src, dst, own_ssem.at[i, t2], own_rsem.at[i, g], (2 * o + tx, 2 * ty + a)),
                op,
            )

    def own_wait(i):
        if not direct or isinstance(i, int) and i == 1:
            await_bytes(slot_of(i, o, b), own_rsem.at[i, 0])
            return
        for q in range(group):
            if isinstance(i, int) and i == 0:
                await_bytes(wi_all.at[o, b, pl.ds(q * block, block)], own_rsem.at[i, q])
            else:
                await_bytes(wf_all.at[i - 2, :, o, b, pl.ds(q * block, block)], own_rsem.at[i, q])

    first, final = o == 0, o == out_n - 1

    def piece_send(i, src, side):
        ref = slot_of(i, src, b)
        dev = (2 * (o + 1 - 2 * side) + a, g)
        remote(ref, ref, z_ssem.at[i, side, src], z_rsem.at[i, src], dev).start()

    def when(condition, call, *args):
        @pl.when(condition)
        def _():
            call(*args)

    def hop(i, h):
        if h == 0:
            own_wait(i)
            when(jnp.logical_not(final), piece_send, i, o, 0)
            when(jnp.logical_not(first), piece_send, i, o, 1)
            return

        @pl.when(o - h >= 0)
        def _():
            await_bytes(slot_of(i, o - h, b), z_rsem.at[i, o - h])
            when(jnp.logical_not(final), piece_send, i, o - h, 0)

        @pl.when(o + h < out_n)
        def _():
            await_bytes(slot_of(i, o + h, b), z_rsem.at[i, o + h])
            when(jnp.logical_not(first), piece_send, i, o + h, 1)

        if h == out_n - 1:
            remote(half_of(i, b), half_of(i, b), f_ssem.at[i], f_rsem.at[i], mate).start()

    items = 2 + chunks
    sent = set()

    def own_start(*which):
        for i in which:
            if i < items and i not in sent:
                sent.add(i)
                own_send(i, "start")

    def pump(time):
        if isinstance(time, int):
            own_start(*range(time + 1))
        for h in range(out_n - 1, -1, -1):
            if isinstance(time, int):
                if 0 <= time - h < items:
                    hop(time - h, h)
            else:
                when(time - h < items, hop, time - h, h)

    def gather_wait(i):
        await_bytes(half_of(i, 1 - b), f_rsem.at[i])

    def gather_close(i):
        def sent(src, side):
            await_bytes(slot_of(i, src, b), z_ssem.at[i, side, src])

        @pl.when(jnp.logical_not(final))
        def _():
            lax.fori_loop(0, o + 1, lambda src, carry: (sent(src, 0), carry)[1], 0)

        @pl.when(jnp.logical_not(first))
        def _():
            lax.fori_loop(o, out_n, lambda src, carry: (sent(src, 1), carry)[1], 0)

        await_bytes(half_of(i, b), f_ssem.at[i])
        own_send(i, "end")

    def fetch(src, dst, n):
        copy = pltpu.make_async_copy(src, dst, lsem.at[n])
        copy.start()
        copy.wait()

    def span(q):
        return pl.ds(q * seg, seg)

    def rows16(i):
        return pl.ds(pl.multiple_of(i * ROW_TILE, ROW_TILE), ROW_TILE)

    def lanes(k, j):
        return pl.ds(k * 384 + j * 128, 128)

    place = a * group + g
    mine = o * (2 * group) + place

    def plane(src, dst, ssem, rsem, op):
        for x2 in range(2):
            for g2 in range(group):
                @pl.when((x2 != a) | (g2 != g))
                def _():
                    copy = remote(src, dst, ssem.at[x2 * group + g2], rsem.at[place], (2 * o + x2, g2))
                    if op == "start":
                        copy.start()
                    else:
                        copy.wait_send()

    def plane_wait(ref, rsem):
        for x2 in range(2):
            for g2 in range(group):
                @pl.when((x2 != a) | (g2 != g))
                def _():
                    await_bytes(ref, rsem.at[x2 * group + g2])

    def far(src, dst, ssem, rsem, op):
        def one(k, carry):
            copy = remote(src, dst, ssem.at[k], rsem.at[o], peer(k)[1])
            if op == "start":
                copy.start()
            else:
                copy.wait_send()
            return carry

        lax.fori_loop(1, out_n, one, 0)

    def far_wait(ref, rsem):
        def one(k, carry):
            await_bytes(ref, rsem.at[peer(k)[0]])
            return carry

        lax.fori_loop(1, out_n, one, 0)

    planes = small_all.at[pl.ds(o * 2 * group, 2 * group)]
    pltpu.make_async_copy(small_own, small_all.at[mine], lsem.at[2]).start()
    plane(small_own, small_all.at[mine], sa_ssem, sa_rsem, "start")

    own_start(0)
    own_start(1)
    own_start(2)
    spread(tok, tok_all, 0, "start")
    own_start(3)
    prod[pl.ds(0, 8), :] = jnp.zeros((8, ch), F32)
    pump(0)
    await_bytes(small_own, lsem.at[2])
    plane_wait(small_own, sa_rsem)
    far(planes, planes, sz_ssem, sz_rsem, "start")
    pump(1)
    far_wait(planes, sz_rsem)

    share = 2 * D // count
    rows_of = {}
    for n in range(count):
        row = n * share // 128
        rows_of.setdefault(row, []).append((n, 0))
        if (n * share + share - 1) // 128 > row:
            rows_of.setdefault(row + 1, []).append((n, 1))
    for tile, pieces in rows_of.items():
        value = sum(small_all[n, r : r + 1, :] for n, r in pieces)
        i, j = tile // (D // 128), tile % (D // 128)
        gains[i : i + 1, j * 128 : (j + 1) * 128] = value
    rows_of = {}
    for m in range(3 * count):
        n, piece = m // 3, m % 3
        tap, rest = m // count, m % count
        lane = rest // group * cblk
        rows_of.setdefault((tap, lane // 128), []).append((n, 2 + 2 * piece, rest % group))
        if (lane + block - 1) // 128 > lane // 128:
            rows_of.setdefault((tap, lane // 128 + 1), []).append((n, 3 + 2 * piece, rest % group))
    for (tap, tile), pieces in rows_of.items():
        value = jnp.zeros((1, 128), F32)
        for t2 in range(group):
            value = value + jnp.where(t == t2, sum(small_all[n, r : r + 1, :] for n, r, p in pieces if p == t2), 0.0)
        taps[tap : tap + 1, tile * 128 : (tile + 1) * 128] = value

    pump(2)
    for q in range(group):
        await_bytes(tok_all.at[q], ag_rsem.at[0, q])
        fetch(tok_all.at[q], act.at[span(q)], 0)

        def normed_rows(i, carry, q=q):
            here = pl.ds(pl.multiple_of(q * seg + i * ROW_TILE, ROW_TILE), ROW_TILE)
            row = act[here, :].astype(F32)
            s1 = lax.rsqrt(jnp.mean(row * row, axis=-1, keepdims=True) + EPS_NORM)
            act[here, :] = (row * s1 * gains[0:1, :]).astype(BF)
            return carry

        lax.fori_loop(0, seg // ROW_TILE, normed_rows, 0, unroll=2)
    own_start(4)
    spread(bck_own, bck_all, 1, "start")
    own_start(5)
    keep_normed = pltpu.make_async_copy(act, nrm_far, lsem.at[2])
    keep_normed.start()
    for time in range(3, out_n):
        pump(time)
    gather_wait(0)
    fetch(wi_all, wi, 0)
    keep_normed.wait()

    for q in range(group):
        for k in range(blocks):
            acc_y[span(q), pl.ds(k * 384, 384)] = dot(
                act[span(q), :], wi[:, :, :, pl.ds(k * 384, 384)].reshape(D, 384)
            )
        for k in range(blocks):
            col = pl.ds(k * 128, 128)
            prod[pl.ds(q * seg + 8, seg), col] = acc_y[span(q), lanes(k, 0)] * acc_y[span(q), lanes(k, 2)]
            cv = (
                taps[0:1, col] * prod[pl.ds(q * seg + 6, seg), col]
                + taps[1:2, col] * prod[pl.ds(q * seg + 7, seg), col]
                + taps[2:3, col] * prod[pl.ds(q * seg + 8, seg), col]
            )
            conv[span(q), col] = cv
            gated[span(q), col] = (acc_y[span(q), lanes(k, 1)] * cv).astype(BF)
    pump(out_n)
    gather_wait(1)
    fetch(wo_all, wo, 0)
    for q in range(group):
        for n in range(4):
            col = pl.ds(n * 384, 384)
            stage[q, :, col] = dot(gated[span(q), :], wo[:, :, :, col].reshape(ch, 384)).astype(BF)
        give(stage.at[q], rs_br, 0, q, "start")

    spill = pltpu.make_async_copy(acc_y.at[:, pl.ds(0, 3 * ch)], mixed_far, lsem.at[2])
    spill.start()
    own_start(6)
    pump(out_n + 1)
    for q in range(group):
        await_bytes(bck_all.at[q], ag_rsem.at[1, q])
        fetch(bck_all.at[q], bck.at[span(q)], 0)
        bck_t[:, span(q)] = bck[span(q), :].T

    pump(out_n + 2)
    for q in range(group):
        await_bytes(rs_br.at[q], rs_rsem.at[0, q])
    for q in range(group):
        give(stage.at[q], rs_br, 0, q, "end")
    fetch(rs_br, stage, 0)

    def arrived(here):
        total = stage[0, here, :].astype(F32)
        for q in range(1, group):
            total = total + stage[q, here, :].astype(F32)
        return total

    def middle_rows(i, carry):
        here = rows16(i)
        mi = tok[here, :].astype(F32) + arrived(here)
        mid[here, :] = mi
        s2 = lax.rsqrt(jnp.mean(mi * mi, axis=-1, keepdims=True) + EPS_NORM)
        low[here, :] = (mi * s2 * gains[1:2, :]).astype(BF)
        return carry

    lax.fori_loop(0, seg // ROW_TILE, middle_rows, 0)
    spread(low, n2_all, 2, "start")
    own_start(*range(items))
    pump(out_n + 3)
    pump(out_n + 4)
    gather_wait(2)
    pltpu.make_async_copy(wf_all.at[0], ws.at[0], wsem.at[0]).start()
    spill.wait()

    def clear(i, carry):
        here = rows16(i)
        acc_y[here, :] = jnp.zeros((ROW_TILE, D), F32)
        acc_n[here, :] = jnp.zeros((ROW_TILE, D), F32)
        return carry

    lax.fori_loop(0, seq // ROW_TILE, clear, 0)
    for q in range(group):
        await_bytes(n2_all.at[q], ag_rsem.at[2, q])
        fetch(n2_all.at[q], act.at[span(q)], 0)
        act_t[:, span(q)] = act[span(q), :].T

    def chunk_refs(kind, c):
        if kind == "f":
            return lax.rem(c, 2), c, sib_f.at[c], pl.ds(0, WIDTH)
        n = chunks + c
        return n % 2, n, sib_i.at[c], pl.ds(0, 128)

    def pair_send(kind, c, op):
        s, n, sib, cols = chunk_refs(kind, c)
        copy = remote(grad.at[s, :, :, 1 - b, :, cols], sib, gs_ssem.at[n], gs_rsem.at[n], mate)
        if op == "start":
            copy.start()
        else:
            copy.wait_send()

    def line_refs(kind, c, side):
        if kind == "f":
            return (down_f if side else up_f).at[c], far_f.at[c]
        return (down_i if side else up_i).at[c], far_i.at[c]

    def line_range(side):
        return (0, o) if side else (o + 1, out_n)

    def line_send(kind, c, side, op="start"):
        _, n, _, _ = chunk_refs(kind, c)
        come, mine_far = line_refs(kind, c, side)
        rsem = (down_sem if side else up_sem)
        dev = (2 * (o + 1 - 2 * side) + a, g)

        def one(d, carry):
            copy = remote(mine_far.at[:, d], come.at[:, d], gz_ssem.at[n, d], rsem.at[n, d], dev)
            if op == "start":
                copy.start()
            else:
                copy.wait_send()
            return carry

        lax.fori_loop(*line_range(side), one, 0)

    def pair_sum(kind, c):
        s, n, sib, cols = chunk_refs(kind, c)
        _, mine_far = line_refs(kind, c, 0)
        await_bytes(sib, gs_rsem.at[n])
        fetch(sib, sibv.at[:, :, :, cols], 1)

        def one(i, carry):
            j, o2 = i // out_n, lax.rem(i, out_n)
            part[0, j, o2, :, cols] = (
                grad[s, j, o2, b, :, cols].astype(F32) + sibv[j, o2, :, cols].astype(F32)
            ).astype(BF)
            return carry

        lax.fori_loop(0, 3 * out_n, one, 0)
        fetch(part.at[0, :, :, :, cols], mine_far, 1)
        when(first, line_send, kind, c, 0)
        when(final, line_send, kind, c, 1)

    def line_step(kind, c, side):
        _, n, _, cols = chunk_refs(kind, c)
        come, mine_far = line_refs(kind, c, side)
        rsem = (down_sem if side else up_sem)
        low_d, high_d = line_range(side)
        await_bytes(come.at[:, o], rsem.at[n, o])

        def ask(d, carry):
            await_bytes(come.at[:, d], rsem.at[n, d])
            pltpu.make_async_copy(come.at[:, d], part.at[1, :, d, :, cols], lsem.at[3]).start()
            pltpu.make_async_copy(mine_far.at[:, d], sibv.at[:, d, :, cols], lsem.at[4]).start()
            pltpu.make_async_copy(come.at[:, d], part.at[1, :, d, :, cols], lsem.at[3]).wait()
            pltpu.make_async_copy(mine_far.at[:, d], sibv.at[:, d, :, cols], lsem.at[4]).wait()
            for j in range(3):
                sibv[j, d, :, cols] = (
                    sibv[j, d, :, cols].astype(F32) + part[1, j, d, :, cols].astype(F32)
                ).astype(BF)
            fetch(sibv.at[:, d, :, cols], mine_far.at[:, d], 1)
            return carry

        lax.fori_loop(low_d, high_d, ask, 0)
        when(jnp.logical_not(first if side else final), line_send, kind, c, side)

    def line_time(kind, time, number):
        for side, at in ((0, o), (1, out_n - 1 - o)):
            for c in [time - at] if kind == "f" else range(number):
                if kind == "f":
                    @pl.when((at > 0) & (c >= 0) & (c < number))
                    def _():
                        line_step(kind, c, side)
                else:
                    @pl.when((at > 0) & (c == time - at))
                    def _():
                        line_step(kind, c, side)

    def line_close(kind, c):
        when(jnp.logical_not(final), line_send, kind, c, 0, "end")
        when(jnp.logical_not(first), line_send, kind, c, 1, "end")

    def out_slot(n):
        return (n // (2 * out_n), slice(None), lax.rem(n, 2 * out_n) // 2, lax.rem(n, 2))

    def hand_back(kind, c, op):
        _, n, _, cols = chunk_refs(kind, c)
        dst = (g_ff if kind == "f" else g_wi)
        if not direct:
            if op == "start":
                h, _, o2, p = out_slot(n)
                fetch(ws.at[h, :, o2, p, :, cols], dst.at[c], 1)
            return
        h, _, o2, p = out_slot(n)
        for q in range(group):
            src = ws.at[h, :, o2, p, pl.ds(q * block, block), cols]
            switch(
                (a == b) & (q == g),
                pltpu.make_async_copy(src, dst.at[t, c], back_rsem.at[n, t]),
                remote(src, dst.at[t, c], back_ssem.at[n, q], back_rsem.at[n, t], (2 * o + b, q)),
                op,
            )

    def hand_wait(kind, c):
        if direct:
            _, n, _, _ = chunk_refs(kind, c)
            for t2 in range(group):
                await_bytes((g_ff if kind == "f" else g_wi).at[t2, c], back_rsem.at[n, t2])

    def total(kind, c):
        s, n, _, cols = chunk_refs(kind, c)
        h, _, place_o, place_p = out_slot(n)
        come_up, mine_far = line_refs(kind, c, 0)
        come_down, _ = line_refs(kind, c, 1)
        fetch(mine_far.at[:, o], sibv.at[:, 0, :, cols], 1)
        for m, (missing, come) in enumerate(((first, come_up), (final, come_down))):
            @pl.when(missing)
            def _(m=m):
                for j in range(3):
                    part[1, j, m, :, cols] = jnp.zeros((rows_n, 128 if kind == "i" else WIDTH), BF)

            @pl.when(jnp.logical_not(missing))
            def _(m=m, come=come):
                fetch(come.at[:, o], part.at[1, :, m, :, cols], 1)

        def add(i, carry):
            j = i // (rows_n // 48)
            here = pl.ds(pl.multiple_of(lax.rem(i, rows_n // 48) * 48, 16), 48)
            value = sibv[j, 0, here, cols].astype(F32)
            for m in range(2):
                value = value + part[1, j, m, here, cols].astype(F32)
            ws[h, j, place_o, place_p, here, cols] = value.astype(BF)
            return carry

        lax.fori_loop(0, 3 * (rows_n // 48), add, 0)
        hand_back(kind, c, "start")

    half = out_n // 2

    def grad_rows(h):
        return pl.ds(pl.multiple_of(h * (D // 2), D // 2), D // 2), pl.ds(h * half, half)

    loop_pump = out_n + 5

    def hidden_chunk(c, carry):
        s = lax.rem(c, 2)
        await_bytes(ws.at[s], wsem.at[s])
        hid, dgt, dup = (pl.ds(j * WIDTH, WIDTH) for j in range(3))

        def token_tile(m, carry):
            here = pl.ds(pl.multiple_of(m * seg, seg), seg)
            n2 = act[here, :]
            gate = dot(n2, ws[s, 0].reshape(D, WIDTH))
            upper = dot(n2, ws[s, 1].reshape(D, WIDTH))
            d_hidden = dot(bck[here, :], ws[s, 2].reshape(D, WIDTH))
            sigma = jax.nn.sigmoid(gate)
            active = gate * sigma
            dmix[here, hid] = (active * upper).astype(BF)
            dmix[here, dgt] = (d_hidden * upper * (sigma * (1.0 + gate * (1.0 - sigma)))).astype(BF)
            dmix[here, dup] = (d_hidden * active).astype(BF)
            acc_y[here, :] += dot_t(dmix[here, hid], ws[s, 2].reshape(D, WIDTH))
            acc_n[here, :] += dot_t(dmix[here, dgt], ws[s, 0].reshape(D, WIDTH))
            acc_n[here, :] += dot_t(dmix[here, dup], ws[s, 1].reshape(D, WIDTH))
            return carry

        lax.fori_loop(0, group, token_tile, 0)

        @pl.when(c >= 2)
        def _():
            pair_send("f", c - 2, "end")

        def grad_tile(h, carry):
            rows, os = grad_rows(h)
            shape = (half, 2, rows_n, WIDTH)
            grad[s, 0, os] = dot(act_t[rows, :], dmix[:, dgt]).astype(BF).reshape(shape)
            grad[s, 1, os] = dot(act_t[rows, :], dmix[:, dup]).astype(BF).reshape(shape)
            grad[s, 2, os] = dot(bck_t[rows, :], dmix[:, hid]).astype(BF).reshape(shape)
            return carry

        lax.fori_loop(0, 2, grad_tile, 0)
        pair_send("f", c, "start")

        @pl.when(c >= 1)
        def _():
            pair_sum("f", c - 1)

        pump(c + loop_pump)

        @pl.when(c + 1 < chunks)
        def _():
            gather_wait(c + 3)
            pltpu.make_async_copy(wf_all.at[c + 1], ws.at[1 - s], wsem.at[1 - s]).start()

        return carry

    lax.fori_loop(0, chunks, hidden_chunk, 0)

    for q in range(group):
        stage[q] = acc_n[span(q), :].astype(BF)
        give(stage.at[q], rs_n2, 1, q, "start")
    pair_sum("f", chunks - 1)
    for time in range(1, 4):
        line_time("f", time, chunks)
    for q in range(group):
        give(stage.at[q], rs_n2, 1, q, "end")
    for q in range(group):
        await_bytes(rs_n2.at[q], rs_rsem.at[1, q])
    spread(low, n2_all, 2, "end")
    fetch(rs_n2, stage, 0)
    fetch(bck_own, act.at[span(0)], 0)
    g_gains[...] = jnp.zeros_like(g_gains)

    def d_middle_rows(i, carry):
        here = rows16(i)
        dn = arrived(here)
        mi = mid[here, :]
        s2 = lax.rsqrt(jnp.mean(mi * mi, axis=-1, keepdims=True) + EPS_NORM)
        e2 = gains[1:2, :] * dn
        back = act[here, :].astype(F32)
        dm = back + s2 * e2 - mi * (s2 * s2 * s2) * jnp.mean(e2 * mi, axis=-1, keepdims=True)
        dmid[here, :] = dm
        low[here, :] = dm.astype(BF)
        g_gains[1] += jnp.sum((dn * mi * s2).reshape(ROW_TILE // 8, 8, D), axis=0)
        return carry

    lax.fori_loop(0, seg // ROW_TILE, d_middle_rows, 0)
    spread(low, dbr_all, 3, "start")

    for q in range(group):
        stage[q] = acc_y[span(q), :].astype(BF)
        give(stage.at[q], rs_y, 2, q, "start")
    spill_back = pltpu.make_async_copy(mixed_far, acc_y.at[:, pl.ds(0, 3 * ch)], lsem.at[2])
    spill_back.start()

    for q in range(group):
        bck_t[pl.ds(0, ch), span(q)] = gated[span(q), :].T
        fetch(nrm_far.at[span(q)], act.at[span(q)], 0)
        act_t[:, span(q)] = act[span(q), :].T
    spill_back.wait()
    for time in range(4, 7):
        line_time("f", time, chunks)

    acc_n[pl.ds(seq, 8), pl.ds(0, ch)] = jnp.zeros((8, ch), F32)
    for q in range(group):
        await_bytes(dbr_all.at[q], ag_rsem.at[3, q])
        fetch(dbr_all.at[q], bck.at[span(q)], 0)
        acc_n[span(q), pl.ds(ch, ch)] = dot_t(bck[span(q), :], wo[...].reshape(ch, D))
        for k in range(blocks):
            col = pl.ds(k * 128, 128)
            d_gated = acc_n[span(q), pl.ds(ch + k * 128, 128)]
            acc_n[span(q), col] = d_gated * acc_y[span(q), lanes(k, 1)]
            dmix[span(q), lanes(k, 1)] = (d_gated * conv[span(q), col]).astype(BF)
    g_taps[...] = jnp.zeros_like(g_taps)
    for q in range(group):
        for k in range(blocks):
            col = pl.ds(k * 128, 128)
            d0 = acc_n[span(q), col]
            for n in range(3):
                g_taps[n, :, col] += jnp.sum(
                    (d0 * prod[pl.ds(q * seg + 6 + n, seg), col]).reshape(seg // 8, 8, 128), axis=0
                )
            d_product = (
                taps[2:3, col] * d0
                + taps[1:2, col] * acc_n[pl.ds(q * seg + 1, seg), col]
                + taps[0:1, col] * acc_n[pl.ds(q * seg + 2, seg), col]
            )
            dmix[span(q), lanes(k, 0)] = (d_product * acc_y[span(q), lanes(k, 2)]).astype(BF)
            dmix[span(q), lanes(k, 2)] = (d_product * acc_y[span(q), lanes(k, 0)]).astype(BF)

    for k in range(blocks):
        s = (chunks + k) % 2
        if k < 2:
            pair_send("f", chunks - 2 + k, "end")
        else:
            pair_send("i", k - 2, "end")

        def intake_tile(h, carry, k=k, s=s):
            rows, os = grad_rows(h)
            value = dot(act_t[rows, :], dmix[:, pl.ds(k * 384, 384)]).astype(BF)
            for j in range(3):
                grad[s, j, os, :, :, pl.ds(0, 128)] = value[:, j * 128 : (j + 1) * 128].reshape(
                    half, 2, rows_n, 128
                )
            return carry

        lax.fori_loop(0, 2, intake_tile, 0)
        pair_send("i", k, "start")
        if k >= 1:
            pair_sum("i", k - 1)

    for n in range(4):
        col = pl.ds(n * 384, 384)
        wo[:, :, :, col] = dot(bck_t[pl.ds(0, ch), :], bck[:, col]).astype(BF).reshape(out_n, 2, cblk, 384)
    last = chunks + blocks
    pair_o = remote(wo.at[:, 1 - b], sib_o, gs_ssem.at[last], gs_rsem.at[last], mate)
    pair_o.start()
    pair_sum("i", blocks - 1)

    await_bytes(sib_o, gs_rsem.at[last])
    fetch(sib_o, sibo, 1)

    def add_o(o2, carry):
        parto[o2] = (wo[o2, b].astype(F32) + sibo[o2].astype(F32)).astype(BF)
        return carry

    lax.fori_loop(0, out_n, add_o, 0)

    def part_o(op):
        def one(k, carry):
            o2, dev = peer(k)
            copy = remote(parto.at[o2], z_o.at[o], gz_ssem.at[last, k], up_sem.at[last, o], dev)
            if op == "start":
                copy.start()
            else:
                copy.wait_send()
            return carry

        lax.fori_loop(1, out_n, one, 0)
        keep = pltpu.make_async_copy(parto.at[o], z_o.at[o], osem.at[0])
        if op == "start":
            keep.start()
        else:
            keep.wait()

    part_o("start")

    for q in range(group):
        give(stage.at[q], rs_y, 2, q, "end")
    for q in range(group):
        await_bytes(rs_y.at[q], rs_rsem.at[2, q])
    for q in range(group):
        for n in range(4):
            stage[q, :, pl.ds(n * 384, 384)] = dot_t(
                dmix[span(q), :], wi[pl.ds(n * out_n // 4, out_n // 4)].reshape(384, 3 * ch)
            ).astype(BF)
        give(stage.at[q], rs_n1, 3, q, "start")

    spread(low, dbr_all, 3, "end")
    for q in range(group):
        fetch(rs_y.at[q], act.at[span(q)], 0)

    def out_rows(i, carry):
        here = rows16(i)
        value = act[here, :].astype(F32)
        for q in range(1, group):
            value = value + act[pl.ds(pl.multiple_of(q * seg + i * ROW_TILE, ROW_TILE), ROW_TILE), :].astype(F32)
        low[here, :] = (mid[here, :] + value).astype(BF)
        return carry

    lax.fori_loop(0, seg // ROW_TILE, out_rows, 0)
    fetch(low, block_out, 0)

    for time in range(7, chunks + out_n - 1):
        line_time("f", time, chunks)

    def total_f(c, carry):
        total("f", c)
        return carry

    lax.fori_loop(0, chunks, total_f, 0)
    for q in range(group):
        give(stage.at[q], rs_n1, 3, q, "end")
    for q in range(group):
        await_bytes(rs_n1.at[q], rs_rsem.at[3, q])
    fetch(rs_n1, stage, 0)

    def d_rows(i, carry):
        here = rows16(i)
        dn = arrived(here)
        row = tok[here, :].astype(F32)
        s1 = lax.rsqrt(jnp.mean(row * row, axis=-1, keepdims=True) + EPS_NORM)
        e1 = gains[0:1, :] * dn
        low[here, :] = (
            dmid[here, :] + s1 * e1 - row * (s1 * s1 * s1) * jnp.mean(e1 * row, axis=-1, keepdims=True)
        ).astype(BF)
        g_gains[0] += jnp.sum((dn * row * s1).reshape(ROW_TILE // 8, 8, D), axis=0)
        return carry

    lax.fori_loop(0, seg // ROW_TILE, d_rows, 0)
    fetch(low, input_grad, 0)

    sm_mine[...] = jnp.zeros_like(sm_mine)
    for i in range(2):
        value = jnp.sum(g_gains[i], axis=0, keepdims=True)
        for j in range(D // 128):
            row = i * (D // 128) + j
            sm_mine[row : row + 1, :] = value[:, j * 128 : (j + 1) * 128]
    for n in range(3):
        value = jnp.sum(g_taps[n], axis=0, keepdims=True)
        for k in range(blocks):
            for t2 in range(group):
                row = 2 * (D // 128) + (t2 * 3 + n) * blocks + k
                sm_mine[row : row + 1, :] = jnp.where(t == t2, value[:, k * 128 : (k + 1) * 128], 0.0)
    sm_plane[place] = sm_mine[...]
    plane(sm_mine, sm_plane.at[place], ta_ssem, ta_rsem, "start")

    for k in range(max(0, blocks - 2), blocks):
        pair_send("i", k, "end")

    def lines(time, carry):
        line_time("i", time, blocks)
        return carry

    lax.fori_loop(1, out_n - 1, lines, 0)
    plane_wait(sm_mine, ta_rsem)
    value = sm_plane[0]
    for i in range(1, 2 * group):
        value = value + sm_plane[i]
    sm_sum[...] = value
    sm_z[o] = value
    far(sm_sum, sm_z.at[o], tz_ssem, tz_rsem, "start")
    lax.fori_loop(out_n - 1, blocks + out_n - 1, lines, 0)
    for k in range(blocks):
        total("i", k)
    part_o("end")
    pair_o.wait_send()

    def last_one(k, carry):
        await_bytes(z_o.at[o], up_sem.at[last, peer(k)[0]])
        return carry

    lax.fori_loop(1, out_n, last_one, 0)
    fetch(z_o, sibo, 1)
    value = sibo[0].astype(F32)
    for o2 in range(1, out_n):
        value = value + sibo[o2].astype(F32)
    outo = parto.at[0]
    outo[...] = value.astype(BF)

    def back_o(op):
        switch(
            a == b,
            pltpu.make_async_copy(outo, g_wo, back_rsem.at[last, 0]),
            remote(outo, g_wo, back_ssem.at[last, 0], back_rsem.at[last, 0], (2 * o + b, 2 * y + a)),
            op,
        )

    back_o("start")
    far_wait(sm_sum, tz_rsem)
    value = sm_z[0]
    for i in range(1, out_n):
        value = value + sm_z[i]
    g_small[...] = value

    plane(small_own, small_all.at[mine], sa_ssem, sa_rsem, "end")
    far(planes, planes, sz_ssem, sz_rsem, "end")
    plane(sm_mine, sm_plane.at[place], ta_ssem, ta_rsem, "end")
    far(sm_sum, sm_z.at[o], tz_ssem, tz_rsem, "end")
    spread(tok, tok_all, 0, "end")
    spread(bck_own, bck_all, 1, "end")
    gather_close(0)
    gather_close(1)

    def close(c, carry):
        gather_close(c + 2)
        line_close("f", c)
        hand_back("f", c, "end")
        hand_wait("f", c)
        return carry

    lax.fori_loop(0, chunks, close, 0)
    for k in range(blocks):
        line_close("i", k)
        hand_back("i", k, "end")
        hand_wait("i", k)
    back_o("end")
    await_bytes(g_wo, back_rsem.at[last, 0])


def forward_backward(sizes, tok, bck, wi_own, wo_own, ff_own, small_own):
    (out_n, group, rows_n, seg, ch, cblk, chunks) = sizes
    blocks = ch // 128
    seq = group * seg
    block = rows_n // group
    places = 2 * group
    small_rows = -(-(2 * D // 128 + group * 3 * blocks) // 8) * 8
    items = 2 + chunks
    sums = chunks + blocks + 1
    vm = pltpu.VMEM
    dma = pltpu.SemaphoreType.DMA

    def shape(*dims, dtype=BF):
        return jax.ShapeDtypeStruct(dims, dtype)

    any_spec = pl.BlockSpec(memory_space=pl.ANY)
    vmem_spec = pl.BlockSpec(memory_space=pltpu.VMEM)
    if block % 16 == 0:
        given = [shape(group, chunks, 3, block, WIDTH), shape(group, blocks, 3, block, 128)]
    else:
        given = [shape(chunks, 3, rows_n, WIDTH), shape(blocks, 3, rows_n, 128)]
    outs = [
        shape(seg, D), shape(seg, D), *given, shape(cblk, D), shape(small_rows, 128, dtype=F32),
        shape(chunks, 3, out_n, 2, rows_n, WIDTH), shape(out_n, 2, rows_n, 3 * ch), shape(out_n, 2, cblk, D),
        shape(group, seg, D), shape(seq, D), shape(group, seg, D), shape(group, seg, D), shape(group, seg, D),
        shape(group, seg, D), shape(group, seg, D), shape(group, seg, D), shape(group, seg, D),
        shape(chunks, 3, out_n, rows_n, WIDTH), shape(blocks, 3, out_n, rows_n, 128), shape(out_n, cblk, D),
        *[shape(chunks, 3, out_n, rows_n, WIDTH), shape(blocks, 3, out_n, rows_n, 128)] * 3, shape(out_n, cblk, D),
        shape(seq, 3 * ch, dtype=F32),
    ]
    out_specs = [any_spec] * 5 + [vmem_spec] + [any_spec] * (len(outs) - 6)
    scratch = [
        vm((2, 3, out_n, 2, rows_n, WIDTH), BF),
        vm((out_n, 2, rows_n, 3 * ch), BF),
        vm((out_n, 2, cblk, D), BF),
        vm((seq, D), BF), vm((D, seq), BF), vm((seq, D), BF), vm((D, seq), BF),
        vm((seq, D), F32), vm((seq + 8, D), F32),
        vm((2, 3, out_n, 2, rows_n, WIDTH), BF),
        vm((3, out_n, rows_n, WIDTH), BF),
        vm((2, 3, out_n, rows_n, WIDTH), BF),
        vm((group, seg, D), BF),
        vm((seq + 8, ch), F32), vm((seq, ch), F32), vm((seq, ch), BF), vm((seq, 3 * ch), BF),
        vm((seg, D), F32), vm((seg, D), F32), vm((seg, D), BF),
        vm((out_n, cblk, D), BF), vm((out_n, cblk, D), BF),
        vm((places * out_n, 8, 128), F32), vm((2, D), F32), vm((3, ch), F32),
        vm((2, 8, D), F32), vm((3, 8, ch), F32),
        vm((small_rows, 128), F32), vm((places, small_rows, 128), F32),
        vm((small_rows, 128), F32), vm((out_n, small_rows, 128), F32),
        dma((4, group)), dma((4, group)), dma((4, group)), dma((4, group)),
        dma((items, 2, out_n)), dma((items, out_n)), dma((items,)), dma((items,)),
        dma((sums,)), dma((sums,)), dma((sums, out_n)), dma((sums, out_n)), dma((sums, out_n)),
        dma((items, group)), dma((items, group)), dma((sums, group)), dma((sums, group)), dma((1,)),
        dma((places,)), dma((places,)), dma((out_n,)), dma((out_n,)),
        dma((places,)), dma((places,)), dma((out_n,)), dma((out_n,)), dma((2,)), dma((5,)),
    ]
    results = pl.pallas_call(
        functools.partial(block_kernel, sizes),
        out_shape=outs,
        in_specs=[vmem_spec] + [any_spec] * 4 + [vmem_spec],
        out_specs=out_specs,
        scratch_shapes=scratch,
        compiler_params=pltpu.CompilerParams(
            collective_id=0, has_side_effects=True, vmem_limit_bytes=63 * 1024 * 1024
        ),
        cost_estimate=pl.CostEstimate(
            flops=6 * seq * D * (4 * ch + 3 * chunks * WIDTH),
            bytes_accessed=200_000_000,
            transcendentals=seq * chunks * WIDTH,
        ),
    )(tok, bck, wi_own, wo_own, ff_own, small_own)
    return results[:6]


def body(
    tokens,
    cotangent,
    lengths,
    intake_weight,
    intake_first,
    intake_second,
    output_weight,
    output_first,
    output_second,
    swiglu_weight,
    swiglu_first,
    swiglu_second,
    down_weight,
    down_first,
    down_second,
    norm_gains,
    gains_first,
    gains_second,
    conv_kernel,
    kernel_first,
    kernel_second,
):
    data_count = lax.axis_size("dp")
    group_count = lax.axis_size("group")
    dp = lax.axis_index("dp")
    member = lax.axis_index("group")
    block = D // (data_count * group_count)
    cblk = -(-block // 16) * 16
    ch = data_count * cblk
    blocks = ch // 128
    hidden_part = FF // group_count
    chunks = -(-hidden_part // WIDTH)
    hidden_full = chunks * WIDTH
    rows_n = D // data_count
    swap = []
    for one in range(data_count):
        for two in range(group_count):
            there = (2 * (one // 2) + two % 2) * group_count + 2 * (two // 2) + one % 2
            swap.append((one * group_count + two, there))

    def cross(value):
        return lax.ppermute(value, ("dp", "group"), swap)

    intake_local = (
        intake_weight.astype(BF)
        .reshape(block, 3, data_count, group_count, block)
        .transpose(3, 0, 1, 2, 4)
    )
    intake_local = jnp.pad(intake_local, ((0, 0),) * 4 + ((0, cblk - block),))
    intake_local = (
        intake_local.reshape(group_count, block, 3, blocks, 128)
        .transpose(0, 1, 3, 2, 4)
        .reshape(group_count, block, 3 * ch)
    )
    ff_local = jnp.concatenate(
        [
            swiglu_weight.astype(BF).reshape(block, 2, group_count, hidden_part),
            down_weight.astype(BF).reshape(block, 1, group_count, hidden_part),
        ],
        axis=1,
    )
    ff_local = jnp.pad(ff_local, ((0, 0),) * 3 + ((0, hidden_full - hidden_part),))
    ff_local = ff_local.reshape(block, 3, group_count, chunks, WIDTH).transpose(2, 3, 1, 0, 4)
    wo_own = jnp.pad(output_weight.astype(BF).reshape(block, D), ((0, cblk - block), (0, 0)))
    if block % 16 == 0:
        wi_own, ff_own = intake_local, ff_local
    else:
        wi_own = lax.all_to_all(intake_local, "group", split_axis=0, concat_axis=0, tiled=True)
        wi_own = cross(wi_own.reshape(rows_n, 3 * ch))
        ff_own = lax.all_to_all(ff_local, "group", split_axis=0, concat_axis=0, tiled=True)
        ff_own = cross(ff_own.transpose(1, 2, 0, 3, 4).reshape(chunks, 3, rows_n, WIDTH))

    number = dp * group_count + member
    share = norm_gains.shape[0]

    def placed(values, lane):
        line = lax.dynamic_update_slice(jnp.zeros((256,), F32), lax.reduce_precision(values, 8, 7), (lane,))
        return line.reshape(2, 128)

    runs = [placed(norm_gains, lax.rem(number * share, 128))]
    for piece in range(3):
        rest = lax.rem(3 * number + piece, data_count * group_count)
        lane = lax.rem(rest // group_count * cblk, 128)
        runs.append(placed(conv_kernel[piece * block : (piece + 1) * block], lane))
    small_own = jnp.concatenate(runs)

    seg_len = tokens.shape[1]
    positions = member * seg_len + lax.iota(jnp.int32, seg_len)
    valid = (positions < lengths[0]).astype(F32)[:, None]
    back_low = (cotangent[0].astype(F32) * valid).astype(BF)

    sizes = (data_count // 2, group_count, rows_n, seg_len, ch, cblk, chunks)
    block_out, input_grad, g_ff, g_wi, g_wo, g_small = forward_backward(
        sizes, tokens[0], back_low, wi_own, wo_own, ff_own, small_own
    )

    if block % 16:
        g_wi = cross(g_wi).reshape(blocks, 3, group_count, block, 128).transpose(2, 0, 1, 3, 4)
        g_wi = lax.all_to_all(g_wi, "group", split_axis=0, concat_axis=0, tiled=True)
        g_ff = cross(g_ff).reshape(chunks, 3, group_count, block, WIDTH).transpose(2, 0, 1, 3, 4)
        g_ff = lax.all_to_all(g_ff, "group", split_axis=0, concat_axis=0, tiled=True)
    g_wi = g_wi.transpose(0, 3, 2, 1, 4).reshape(group_count, block, 3, data_count, cblk)
    intake_grad_flat = g_wi[..., :block].transpose(1, 2, 3, 0, 4).reshape(-1).astype(F32)
    g_ff = g_ff.transpose(3, 2, 0, 1, 4).reshape(block, 3, group_count, hidden_full)
    g_ff = g_ff[..., :hidden_part]
    swiglu_grad_flat = g_ff[:, :2].reshape(-1).astype(F32)
    down_grad_flat = g_ff[:, 2].reshape(-1).astype(F32)
    output_grad_flat = g_wo[:block].reshape(-1).astype(F32)

    gain_rows = 2 * D // 128
    taps_grad = g_small[gain_rows : gain_rows + group_count * 3 * blocks]
    taps_grad = taps_grad.reshape(group_count, 3, data_count, cblk)[..., :block]
    taps_grad = taps_grad.transpose(1, 2, 0, 3).reshape(-1)
    small_shards = (
        lax.dynamic_slice(g_small[:gain_rows].reshape(-1), (number * share,), (share,)),
        lax.dynamic_slice(taps_grad, (number * 3 * block,), (3 * block,)),
    )
    intake_new = update(
        intake_weight, intake_first, intake_second, intake_grad_flat, RATE_MATRIX, DECAY
    )
    output_new = update(
        output_weight, output_first, output_second, output_grad_flat, RATE_MATRIX, DECAY
    )
    swiglu_new = update(
        swiglu_weight, swiglu_first, swiglu_second, swiglu_grad_flat, RATE_MATRIX, DECAY
    )
    down_new = update(down_weight, down_first, down_second, down_grad_flat, RATE_MATRIX, DECAY)
    gains_new = update(norm_gains, gains_first, gains_second, small_shards[0], RATE_VECTOR, 0.0)
    kernel_new = update(
        conv_kernel, kernel_first, kernel_second, small_shards[1], RATE_VECTOR, DECAY
    )
    return (
        block_out[None],
        input_grad[None],
        intake_new[0],
        intake_new[1],
        intake_new[2],
        output_new[0],
        output_new[1],
        output_new[2],
        swiglu_new[0],
        swiglu_new[1],
        swiglu_new[2],
        down_new[0],
        down_new[1],
        down_new[2],
        gains_new[0],
        gains_new[1],
        gains_new[2],
        kernel_new[0],
        kernel_new[1],
        kernel_new[2],
    )


def solution(mesh):
    in_specs = (
        P("dp", "group", None),
        P("dp", "group", None),
        P("dp"),
        P(("dp", "group")),
        P(("dp", "group")),
        P(("dp", "group")),
        P(("dp", "group")),
        P(("dp", "group")),
        P(("dp", "group")),
        P(("dp", "group")),
        P(("dp", "group")),
        P(("dp", "group")),
        P(("dp", "group")),
        P(("dp", "group")),
        P(("dp", "group")),
        P(("dp", "group")),
        P(("dp", "group")),
        P(("dp", "group")),
        P(("dp", "group")),
        P(("dp", "group")),
        P(("dp", "group")),
    )
    out_specs = (
        P("dp", "group", None),
        P("dp", "group", None),
        P(("dp", "group")),
        P(("dp", "group")),
        P(("dp", "group")),
        P(("dp", "group")),
        P(("dp", "group")),
        P(("dp", "group")),
        P(("dp", "group")),
        P(("dp", "group")),
        P(("dp", "group")),
        P(("dp", "group")),
        P(("dp", "group")),
        P(("dp", "group")),
        P(("dp", "group")),
        P(("dp", "group")),
        P(("dp", "group")),
        P(("dp", "group")),
        P(("dp", "group")),
        P(("dp", "group")),
    )
    return jax.shard_map(body, mesh=mesh, in_specs=in_specs, out_specs=out_specs, check_vma=False)
```

```python
import functools

import jax
import jax.numpy as jnp
from jax import lax
from jax.experimental import pallas as pl
from jax.experimental.pallas import tpu as pltpu
from jax.sharding import PartitionSpec as P

D = 1536
FF = 6912
STEP = 5
WIDTH = 256
ROW_TILE = 16

EPS_NORM = 1e-05
BETA_ONE = 0.5
BETA_TWO = 0.5
ADAM_EPS = 1e-08
RATE_MATRIX = 0.02
RATE_VECTOR = 0.2
DECAY = 0.1

MESH = pl.DeviceIdType.MESH
BF = jnp.bfloat16
F32 = jnp.float32


def update(weight, first, second, grad, rate, decay):
    first_new = BETA_ONE * first + (1.0 - BETA_ONE) * grad
    second_new = BETA_TWO * second + (1.0 - BETA_TWO) * grad * grad
    first_hat = first_new / (1.0 - BETA_ONE**STEP)
    second_hat = second_new / (1.0 - BETA_TWO**STEP)
    weight_new = weight - rate * (first_hat / (jnp.sqrt(second_hat) + ADAM_EPS) + decay * weight)
    return (first_new, second_new, weight_new)


def dot(left, right):
    return lax.dot_general(left, right, (((1,), (0,)), ((), ())), preferred_element_type=F32)


def dot_t(left, right):
    return lax.dot_general(left, right, (((1,), (1,)), ((), ())), preferred_element_type=F32)


def await_bytes(ref, sem):
    pltpu.make_async_copy(ref, ref, sem).wait()


def block_kernel(
    sizes,
    tok, bck_own, wi_own, wo_own, ff_own, small_own,
    block_out, input_grad, g_ff, g_wi, g_wo, g_small,
    wf_all, wi_all, wo_all, tok_all, nrm_far, bck_all, n2_all, dbr_all,
    rs_br, rs_y, rs_n2, rs_n1, via,
    sib_f, sib_i, sib_o, up_f, up_i, down_f, down_i, far_f, far_i, z_o, mixed_far,
    ws, wi, wo, act, act_t, bck, bck_t, acc_y, acc_n, grad, sibv, part, stage,
    prod, gated, dmix, mid, dmid, low, sibo, parto,
    small_all, gains, taps, g_gains, g_taps, sm_mine, sm_plane, sm_sum, sm_z,
    extra, ag_ssem, ag_rsem, ag_fsem, rs_ssem, rs_rsem, via_ssem, via_rsem, z_ssem, z_rsem, f_ssem, f_rsem,
    gs_ssem, gs_rsem, gz_ssem, up_sem, down_sem, own_ssem, own_rsem, back_ssem, back_rsem, osem,
    sa_ssem, sa_rsem, sz_ssem, sz_rsem, ta_ssem, ta_rsem, tz_ssem, tz_rsem, wsem, lsem,
):
    (out_n, group, rows_n, seg, ch, cblk, chunks) = sizes
    block = rows_n // group
    direct = block % 16 == 0
    count = 2 * out_n * group
    blocks = ch // 128
    seq = group * seg
    dp = lax.axis_index("dp")
    g = lax.axis_index("group")
    o, a = dp // 2, lax.rem(dp, 2)
    y, b = g // 2, lax.rem(g, 2)
    t = 2 * y + a
    mate = (dp, g + 1 - 2 * b)

    def peer(k):
        o2 = lax.rem(o + k, out_n)
        return o2, (2 * o2 + a, g)

    barrier = pltpu.get_barrier_semaphore()
    for x2 in range(2):
        for g2 in range(group):
            @pl.when((x2 != a) | (g2 != g))
            def _():
                pl.semaphore_signal(barrier, inc=1, device_id=(2 * o + x2, g2), device_id_type=MESH)

    def greet(k, carry):
        pl.semaphore_signal(barrier, inc=1, device_id=peer(k)[1], device_id_type=MESH)
        return carry

    lax.fori_loop(1, out_n, greet, 0)
    pl.semaphore_wait(barrier, 2 * group - 1 + out_n - 1)

    def remote(src, dst, ssem, rsem, dev):
        return pltpu.make_async_remote_copy(
            src_ref=src, dst_ref=dst, send_sem=ssem, recv_sem=rsem, device_id=dev, device_id_type=MESH
        )

    def switch(alone, local, copy, op):
        if op == "start":
            @pl.when(alone)
            def _():
                local.start()

            @pl.when(jnp.logical_not(alone))
            def _():
                copy.start()
        else:
            @pl.when(jnp.logical_not(alone))
            def _():
                copy.wait_send()

    odd = lax.rem(a + b, 2)
    size = seg // 2
    y_via = odd * y + (1 - odd) * (1 - y)
    h_via = 1 - odd
    partner = (2 * o + odd * a + (1 - odd) * (1 - a), 2 * (odd * (1 - y) + (1 - odd) * y) + b)

    def part_of(h):
        return pl.ds(h * size, size) if isinstance(h, int) else pl.ds(pl.multiple_of(h * size, size), size)

    def spread(src, dst, n, op):
        for d, h in ((1, 0), (2, 1), (1, 1), (2, 0), (0, 0), (0, 1)):
            x2, y2 = (1 - a if d == 1 else a), (1 - y if d == 2 else y)
            one, two = src.at[part_of(h)], dst.at[g, part_of(h)]
            copy = remote(one, two, ag_ssem.at[n, d, h], ag_rsem.at[n, g, h], (2 * o + x2, 2 * y2 + a))
            if d == 0:
                switch(a == b, pltpu.make_async_copy(one, two, ag_rsem.at[n, g, h]), copy, op)
            elif op == "start":
                copy.start()
            else:
                copy.wait_send()
        if op == "end":
            for k in range(2):
                ref = dst.at[2 * y_via + k, part_of(h_via)]
                await_bytes(ref, ag_fsem.at[n, k])

    def spread_on(dst, n):
        for k in range(2):
            q = 2 * y_via + k
            ref = dst.at[q, part_of(h_via)]
            await_bytes(ref, ag_rsem.at[n, q, h_via])
            remote(ref, ref, ag_fsem.at[n, k], ag_rsem.at[n, q, h_via], partner).start()

    def spread_wait(dst, n, q):
        for h in range(2):
            @pl.when((q // 2 != y_via) | (h != h_via))
            def _():
                await_bytes(dst.at[q, part_of(h)], ag_rsem.at[n, q, h])

    def give(terms, dst, n, at, q, h, slot, op="start"):
        one, two = terms(q).at[part_of(h)], dst.at[slot, part_of(h)]
        copy = remote(one, two, rs_ssem.at[n, at, h], rs_rsem.at[n, slot, h], (2 * o + b, q))
        if slot == 0:
            switch(q == g, pltpu.make_async_copy(one, two, rs_rsem.at[n, 0, h]), copy, op)
        elif op == "start":
            copy.start()
        else:
            copy.wait_send()

    def give_half(terms, n, k, h, op):
        q = 2 * (1 - y) + k
        dev = (2 * o + 1 - a, g) if h == 0 else (dp, 2 * (1 - y) + b)
        copy = remote(terms(q).at[part_of(h)], via.at[n, k], via_ssem.at[n, k, h], via_rsem.at[n, k], dev)
        if op == "start":
            copy.start()
        else:
            copy.wait_send()

    def scatter(terms, dst, n, produce):
        for k in range(2):
            q = 2 * (1 - y) + k
            produce(q)

            @pl.when(odd == 1)
            def _():
                give_half(terms, n, k, 0, "start")
                give_half(terms, n, k, 1, "start")

            @pl.when(odd == 0)
            def _():
                give(terms, dst, n, k, q, 1, 1)

        for k in range(2):
            q = 2 * y + k
            produce(q)

            @pl.when(odd == 1)
            def _():
                give(terms, dst, n, 2 + k, q, 0, 2)

            @pl.when(odd == 0)
            def _():
                give(terms, dst, n, 2 + k, q, 0, 0)
                give(terms, dst, n, 2 + k, q, 1, 0)

    def scatter_on(terms, dst, n):
        for k in range(2):
            q = 2 * y_via + k
            await_bytes(via.at[n, k], via_rsem.at[n, k])
            fetch(via.at[n, k], extra, 0)

            def add_rows(i, carry):
                here = pl.ds(pl.multiple_of(odd * size + i * ROW_TILE, ROW_TILE), ROW_TILE)
                ref = terms(q)
                ref[here, :] = (ref[here, :].astype(F32) + extra[rows16(i), :].astype(F32)).astype(BF)
                return carry

            lax.fori_loop(0, size // ROW_TILE, add_rows, 0)

            @pl.when(odd == 1)
            def _():
                give(terms, dst, n, 2 + k, q, 1, 2)

            @pl.when(odd == 0)
            def _():
                give(terms, dst, n, k, q, 0, 1)

    def scatter_end(terms, dst, n):
        @pl.when(odd == 1)
        def _():
            for k in range(2):
                for h in range(2):
                    give_half(terms, n, k, h, "end")
                    give(terms, dst, n, 2 + k, 2 * y + k, h, 2, "end")

        @pl.when(odd == 0)
        def _():
            for k in range(2):
                for h in range(2):
                    give(terms, dst, n, k, 2 * (1 - y) + k, h, 1, "end")
                    give(terms, dst, n, 2 + k, 2 * y + k, h, 0, "end")

    def scatter_wait(dst, n):
        for slot in range(3):
            for h in range(2):
                await_bytes(dst.at[slot, part_of(h)], rs_rsem.at[n, slot, h])

    def staged(q):
        return stage.at[q]

    def any_span(q):
        return pl.ds(pl.multiple_of(q * seg, seg), seg)

    def slot_of(i, o2, p):
        if isinstance(i, int) and i == 0:
            return wi_all.at[o2, p]
        if isinstance(i, int) and i == 1:
            return wo_all.at[o2, p]
        return wf_all.at[i - 2, :, o2, p]

    def half_of(i, p):
        if isinstance(i, int) and i == 0:
            return wi_all.at[:, p]
        if isinstance(i, int) and i == 1:
            return wo_all.at[:, p]
        return wf_all.at[i - 2, :, :, p]

    my_rows = pl.ds(pl.multiple_of(g * block, 4), block)

    def own_send(i, op):
        if isinstance(i, int) and i == 1:
            dst = wo_all.at[o, a]
            switch(
                a == b,
                pltpu.make_async_copy(wo_own, dst, own_rsem.at[1, 0]),
                remote(wo_own, dst, own_ssem.at[1, 0], own_rsem.at[1, 0], (2 * o + b, 2 * y + a)),
                op,
            )
            return
        if not direct:
            src = wi_own if isinstance(i, int) and i == 0 else ff_own.at[i - 2]
            if op == "start":
                pltpu.make_async_copy(src, slot_of(i, o, b), own_rsem.at[i, 0]).start()
            return
        for t2 in range(group):
            ty, tx = t2 // 2, t2 % 2
            if isinstance(i, int) and i == 0:
                src, dst = wi_own.at[t2], wi_all.at[o, a, my_rows]
            else:
                src, dst = ff_own.at[t2, i - 2], wf_all.at[i - 2, :, o, a, my_rows]
            switch(
                (tx == a) & (ty == y) & (a == b),
                pltpu.make_async_copy(src, dst, own_rsem.at[i, g]),
                remote(src, dst, own_ssem.at[i, t2], own_rsem.at[i, g], (2 * o + tx, 2 * ty + a)),
                op,
            )

    def own_wait(i):
        if not direct or isinstance(i, int) and i == 1:
            await_bytes(slot_of(i, o, b), own_rsem.at[i, 0])
            return
        for q in range(group):
            if isinstance(i, int) and i == 0:
                await_bytes(wi_all.at[o, b, pl.ds(q * block, block)], own_rsem.at[i, q])
            else:
                await_bytes(wf_all.at[i - 2, :, o, b, pl.ds(q * block, block)], own_rsem.at[i, q])

    first, final = o == 0, o == out_n - 1

    def piece_send(i, src, side):
        ref = slot_of(i, src, b)
        dev = (2 * (o + 1 - 2 * side) + a, g)
        remote(ref, ref, z_ssem.at[i, side, src], z_rsem.at[i, src], dev).start()

    def when(condition, call, *args):
        @pl.when(condition)
        def _():
            call(*args)

    def hop(i, h):
        if h == 0:
            own_wait(i)
            when(jnp.logical_not(final), piece_send, i, o, 0)
            when(jnp.logical_not(first), piece_send, i, o, 1)
            return

        @pl.when(o - h >= 0)
        def _():
            await_bytes(slot_of(i, o - h, b), z_rsem.at[i, o - h])
            when(jnp.logical_not(final), piece_send, i, o - h, 0)

        @pl.when(o + h < out_n)
        def _():
            await_bytes(slot_of(i, o + h, b), z_rsem.at[i, o + h])
            when(jnp.logical_not(first), piece_send, i, o + h, 1)

        if h == out_n - 1:
            remote(half_of(i, b), half_of(i, b), f_ssem.at[i], f_rsem.at[i], mate).start()

    items = 2 + chunks
    sent = set()

    def own_start(*which):
        for i in which:
            if i < items and i not in sent:
                sent.add(i)
                own_send(i, "start")

    def pump(time):
        if isinstance(time, int):
            own_start(*range(time + 1))
        for h in range(out_n - 1, -1, -1):
            if isinstance(time, int):
                if 0 <= time - h < items:
                    hop(time - h, h)
            else:
                when(time - h < items, hop, time - h, h)

    def gather_wait(i):
        await_bytes(half_of(i, 1 - b), f_rsem.at[i])

    def gather_close(i):
        def sent(src, side):
            await_bytes(slot_of(i, src, b), z_ssem.at[i, side, src])

        @pl.when(jnp.logical_not(final))
        def _():
            lax.fori_loop(0, o + 1, lambda src, carry: (sent(src, 0), carry)[1], 0)

        @pl.when(jnp.logical_not(first))
        def _():
            lax.fori_loop(o, out_n, lambda src, carry: (sent(src, 1), carry)[1], 0)

        await_bytes(half_of(i, b), f_ssem.at[i])
        own_send(i, "end")

    def fetch(src, dst, n):
        copy = pltpu.make_async_copy(src, dst, lsem.at[n])
        copy.start()
        copy.wait()

    def span(q):
        return pl.ds(q * seg, seg)

    def rows16(i):
        return pl.ds(pl.multiple_of(i * ROW_TILE, ROW_TILE), ROW_TILE)

    def lanes(k, j):
        return pl.ds(k * 384 + j * 128, 128)

    place = a * group + g
    mine = o * (2 * group) + place

    def plane(src, dst, ssem, rsem, op):
        for x2 in range(2):
            for g2 in range(group):
                @pl.when((x2 != a) | (g2 != g))
                def _():
                    copy = remote(src, dst, ssem.at[x2 * group + g2], rsem.at[place], (2 * o + x2, g2))
                    if op == "start":
                        copy.start()
                    else:
                        copy.wait_send()

    def plane_wait(ref, rsem):
        for x2 in range(2):
            for g2 in range(group):
                @pl.when((x2 != a) | (g2 != g))
                def _():
                    await_bytes(ref, rsem.at[x2 * group + g2])

    def far(src, dst, ssem, rsem, op):
        def one(k, carry):
            copy = remote(src, dst, ssem.at[k], rsem.at[o], peer(k)[1])
            if op == "start":
                copy.start()
            else:
                copy.wait_send()
            return carry

        lax.fori_loop(1, out_n, one, 0)

    def far_wait(ref, rsem):
        def one(k, carry):
            await_bytes(ref, rsem.at[peer(k)[0]])
            return carry

        lax.fori_loop(1, out_n, one, 0)

    planes = small_all.at[pl.ds(o * 2 * group, 2 * group)]
    pltpu.make_async_copy(small_own, small_all.at[mine], lsem.at[2]).start()
    plane(small_own, small_all.at[mine], sa_ssem, sa_rsem, "start")

    def convolved(q, col):
        return (
            taps[0:1, col] * prod[pl.ds(q * seg + 6, seg), col]
            + taps[1:2, col] * prod[pl.ds(q * seg + 7, seg), col]
            + taps[2:3, col] * prod[pl.ds(q * seg + 8, seg), col]
        )

    own_start(0)
    own_start(1)
    own_start(2)
    spread(tok, tok_all, 0, "start")
    own_start(3)
    prod[pl.ds(0, 8), :] = jnp.zeros((8, ch), F32)
    pump(0)
    await_bytes(small_own, lsem.at[2])
    plane_wait(small_own, sa_rsem)
    far(planes, planes, sz_ssem, sz_rsem, "start")
    pump(1)
    far_wait(planes, sz_rsem)
    spread_on(tok_all, 0)

    share = 2 * D // count
    rows_of = {}
    for n in range(count):
        row = n * share // 128
        rows_of.setdefault(row, []).append((n, 0))
        if (n * share + share - 1) // 128 > row:
            rows_of.setdefault(row + 1, []).append((n, 1))
    for tile, pieces in rows_of.items():
        value = sum(small_all[n, r : r + 1, :] for n, r in pieces)
        i, j = tile // (D // 128), tile % (D // 128)
        gains[i : i + 1, j * 128 : (j + 1) * 128] = value
    rows_of = {}
    for m in range(3 * count):
        n, piece = m // 3, m % 3
        tap, rest = m // count, m % count
        lane = rest // group * cblk
        rows_of.setdefault((tap, lane // 128), []).append((n, 2 + 2 * piece, rest % group))
        if (lane + block - 1) // 128 > lane // 128:
            rows_of.setdefault((tap, lane // 128 + 1), []).append((n, 3 + 2 * piece, rest % group))
    for (tap, tile), pieces in rows_of.items():
        value = jnp.zeros((1, 128), F32)
        for t2 in range(group):
            value = value + jnp.where(t == t2, sum(small_all[n, r : r + 1, :] for n, r, p in pieces if p == t2), 0.0)
        taps[tap : tap + 1, tile * 128 : (tile + 1) * 128] = value

    pump(2)
    for q in range(group):
        spread_wait(tok_all, 0, q)
        fetch(tok_all.at[q], act.at[span(q)], 0)

        def normed_rows(i, carry, q=q):
            here = pl.ds(pl.multiple_of(q * seg + i * ROW_TILE, ROW_TILE), ROW_TILE)
            row = act[here, :].astype(F32)
            s1 = lax.rsqrt(jnp.mean(row * row, axis=-1, keepdims=True) + EPS_NORM)
            act[here, :] = (row * s1 * gains[0:1, :]).astype(BF)
            return carry

        lax.fori_loop(0, seg // ROW_TILE, normed_rows, 0, unroll=2)
    own_start(4)
    spread(bck_own, bck_all, 1, "start")
    own_start(5)
    keep_normed = pltpu.make_async_copy(act, nrm_far, lsem.at[2])
    keep_normed.start()
    for time in range(3, out_n):
        pump(time)
    gather_wait(0)
    fetch(wi_all, wi, 0)
    keep_normed.wait()

    for q in range(group):
        for k in range(blocks):
            acc_y[span(q), pl.ds(k * 384, 384)] = dot(
                act[span(q), :], wi[:, :, :, pl.ds(k * 384, 384)].reshape(D, 384)
            )
        for k in range(blocks):
            col = pl.ds(k * 128, 128)
            prod[pl.ds(q * seg + 8, seg), col] = acc_y[span(q), lanes(k, 0)] * acc_y[span(q), lanes(k, 2)]
            gated[span(q), col] = (acc_y[span(q), lanes(k, 1)] * convolved(q, col)).astype(BF)
    spread_on(bck_all, 1)
    pump(out_n)
    gather_wait(1)
    fetch(wo_all, wo, 0)

    def branch(q):
        for n in range(4):
            col = pl.ds(n * 384, 384)
            stage[q, :, col] = dot(gated[any_span(q), :], wo[:, :, :, col].reshape(ch, 384)).astype(BF)

    scatter(staged, rs_br, 0, branch)
    scatter_on(staged, rs_br, 0)
    spill = pltpu.make_async_copy(acc_y.at[:, pl.ds(0, 3 * ch)], mixed_far, lsem.at[2])
    spill.start()
    own_start(6)
    pump(out_n + 1)
    for q in range(group):
        spread_wait(bck_all, 1, q)
        fetch(bck_all.at[q], bck.at[span(q)], 0)
        bck_t[:, span(q)] = bck[span(q), :].T

    pump(out_n + 2)
    scatter_wait(rs_br, 0)
    scatter_end(staged, rs_br, 0)
    fetch(rs_br, stage.at[pl.ds(0, 3)], 0)

    def arrived(here):
        total = stage[0, here, :].astype(F32)
        for q in range(1, 3):
            total = total + stage[q, here, :].astype(F32)
        return total

    def middle_rows(i, carry):
        here = rows16(i)
        mi = tok[here, :].astype(F32) + arrived(here)
        mid[here, :] = mi
        s2 = lax.rsqrt(jnp.mean(mi * mi, axis=-1, keepdims=True) + EPS_NORM)
        low[here, :] = (mi * s2 * gains[1:2, :]).astype(BF)
        return carry

    lax.fori_loop(0, seg // ROW_TILE, middle_rows, 0)
    spread(low, n2_all, 2, "start")
    own_start(*range(items))
    pump(out_n + 3)
    spread_on(n2_all, 2)
    pump(out_n + 4)
    gather_wait(2)
    pltpu.make_async_copy(wf_all.at[0], ws.at[0], wsem.at[0]).start()
    spill.wait()

    def clear(i, carry):
        here = rows16(i)
        acc_y[here, :] = jnp.zeros((ROW_TILE, D), F32)
        acc_n[here, :] = jnp.zeros((ROW_TILE, D), F32)
        return carry

    lax.fori_loop(0, seq // ROW_TILE, clear, 0)
    for q in range(group):
        spread_wait(n2_all, 2, q)
        fetch(n2_all.at[q], act.at[span(q)], 0)
        act_t[:, span(q)] = act[span(q), :].T

    def chunk_refs(kind, c):
        if kind == "f":
            return lax.rem(c, 2), c, sib_f.at[c], pl.ds(0, WIDTH)
        n = chunks + c
        return n % 2, n, sib_i.at[c], pl.ds(0, 128)

    def pair_send(kind, c, op):
        s, n, sib, cols = chunk_refs(kind, c)
        copy = remote(grad.at[s, :, :, 1 - b, :, cols], sib, gs_ssem.at[n], gs_rsem.at[n], mate)
        if op == "start":
            copy.start()
        else:
            copy.wait_send()

    def line_refs(kind, c, side):
        if kind == "f":
            return (down_f if side else up_f).at[c], far_f.at[c]
        return (down_i if side else up_i).at[c], far_i.at[c]

    def line_range(side):
        return (0, o) if side else (o + 1, out_n)

    def line_send(kind, c, side, op="start"):
        _, n, _, _ = chunk_refs(kind, c)
        come, mine_far = line_refs(kind, c, side)
        rsem = (down_sem if side else up_sem)
        dev = (2 * (o + 1 - 2 * side) + a, g)

        def one(d, carry):
            copy = remote(mine_far.at[:, d], come.at[:, d], gz_ssem.at[n, d], rsem.at[n, d], dev)
            if op == "start":
                copy.start()
            else:
                copy.wait_send()
            return carry

        lax.fori_loop(*line_range(side), one, 0)

    def pair_sum(kind, c):
        s, n, sib, cols = chunk_refs(kind, c)
        _, mine_far = line_refs(kind, c, 0)
        await_bytes(sib, gs_rsem.at[n])
        fetch(sib, sibv.at[:, :, :, cols], 1)

        def one(i, carry):
            j, o2 = i // out_n, lax.rem(i, out_n)
            part[0, j, o2, :, cols] = (
                grad[s, j, o2, b, :, cols].astype(F32) + sibv[j, o2, :, cols].astype(F32)
            ).astype(BF)
            return carry

        lax.fori_loop(0, 3 * out_n, one, 0)
        fetch(part.at[0, :, :, :, cols], mine_far, 1)
        when(first, line_send, kind, c, 0)
        when(final, line_send, kind, c, 1)

    def line_step(kind, c, side):
        _, n, _, cols = chunk_refs(kind, c)
        come, mine_far = line_refs(kind, c, side)
        rsem = (down_sem if side else up_sem)
        low_d, high_d = line_range(side)
        await_bytes(come.at[:, o], rsem.at[n, o])

        def ask(d, carry):
            await_bytes(come.at[:, d], rsem.at[n, d])
            pltpu.make_async_copy(come.at[:, d], part.at[1, :, d, :, cols], lsem.at[3]).start()
            pltpu.make_async_copy(mine_far.at[:, d], sibv.at[:, d, :, cols], lsem.at[4]).start()
            pltpu.make_async_copy(come.at[:, d], part.at[1, :, d, :, cols], lsem.at[3]).wait()
            pltpu.make_async_copy(mine_far.at[:, d], sibv.at[:, d, :, cols], lsem.at[4]).wait()
            for j in range(3):
                sibv[j, d, :, cols] = (
                    sibv[j, d, :, cols].astype(F32) + part[1, j, d, :, cols].astype(F32)
                ).astype(BF)
            fetch(sibv.at[:, d, :, cols], mine_far.at[:, d], 1)
            return carry

        lax.fori_loop(low_d, high_d, ask, 0)
        when(jnp.logical_not(first if side else final), line_send, kind, c, side)

    def line_time(kind, time, number):
        for side, at in ((0, o), (1, out_n - 1 - o)):
            for c in [time - at] if kind == "f" else range(number):
                if kind == "f":
                    @pl.when((at > 0) & (c >= 0) & (c < number))
                    def _():
                        line_step(kind, c, side)
                else:
                    @pl.when((at > 0) & (c == time - at))
                    def _():
                        line_step(kind, c, side)

    def line_close(kind, c):
        when(jnp.logical_not(final), line_send, kind, c, 0, "end")
        when(jnp.logical_not(first), line_send, kind, c, 1, "end")

    def out_slot(n):
        return (n // (2 * out_n), slice(None), lax.rem(n, 2 * out_n) // 2, lax.rem(n, 2))

    def hand_back(kind, c, op):
        _, n, _, cols = chunk_refs(kind, c)
        dst = (g_ff if kind == "f" else g_wi)
        if not direct:
            if op == "start":
                h, _, o2, p = out_slot(n)
                fetch(ws.at[h, :, o2, p, :, cols], dst.at[c], 1)
            return
        h, _, o2, p = out_slot(n)
        for q in range(group):
            src = ws.at[h, :, o2, p, pl.ds(q * block, block), cols]
            switch(
                (a == b) & (q == g),
                pltpu.make_async_copy(src, dst.at[t, c], back_rsem.at[n, t]),
                remote(src, dst.at[t, c], back_ssem.at[n, q], back_rsem.at[n, t], (2 * o + b, q)),
                op,
            )

    def hand_wait(kind, c):
        if direct:
            _, n, _, _ = chunk_refs(kind, c)
            for t2 in range(group):
                await_bytes((g_ff if kind == "f" else g_wi).at[t2, c], back_rsem.at[n, t2])

    def total(kind, c):
        s, n, _, cols = chunk_refs(kind, c)
        h, _, place_o, place_p = out_slot(n)
        come_up, mine_far = line_refs(kind, c, 0)
        come_down, _ = line_refs(kind, c, 1)
        fetch(mine_far.at[:, o], sibv.at[:, 0, :, cols], 1)
        for m, (missing, come) in enumerate(((first, come_up), (final, come_down))):
            @pl.when(missing)
            def _(m=m):
                for j in range(3):
                    part[1, j, m, :, cols] = jnp.zeros((rows_n, 128 if kind == "i" else WIDTH), BF)

            @pl.when(jnp.logical_not(missing))
            def _(m=m, come=come):
                fetch(come.at[:, o], part.at[1, :, m, :, cols], 1)

        def add(i, carry):
            j = i // (rows_n // 48)
            here = pl.ds(pl.multiple_of(lax.rem(i, rows_n // 48) * 48, 16), 48)
            value = sibv[j, 0, here, cols].astype(F32)
            for m in range(2):
                value = value + part[1, j, m, here, cols].astype(F32)
            ws[h, j, place_o, place_p, here, cols] = value.astype(BF)
            return carry

        lax.fori_loop(0, 3 * (rows_n // 48), add, 0)
        hand_back(kind, c, "start")

    half = out_n // 2

    def grad_rows(h):
        return pl.ds(pl.multiple_of(h * (D // 2), D // 2), D // 2), pl.ds(h * half, half)

    loop_pump = out_n + 5

    def hidden_chunk(c, carry):
        s = lax.rem(c, 2)
        await_bytes(ws.at[s], wsem.at[s])
        hid, dgt, dup = (pl.ds(j * WIDTH, WIDTH) for j in range(3))

        def token_tile(m, carry):
            here = pl.ds(pl.multiple_of(m * (seq // 2), seq // 2), seq // 2)
            n2 = act[here, :]
            gate = dot(n2, ws[s, 0].reshape(D, WIDTH))
            upper = dot(n2, ws[s, 1].reshape(D, WIDTH))
            d_hidden = dot(bck[here, :], ws[s, 2].reshape(D, WIDTH))
            sigma = jax.nn.sigmoid(gate)
            active = gate * sigma
            dmix[here, hid] = (active * upper).astype(BF)
            dmix[here, dgt] = (d_hidden * upper * (sigma * (1.0 + gate * (1.0 - sigma)))).astype(BF)
            dmix[here, dup] = (d_hidden * active).astype(BF)
            acc_y[here, :] += dot_t(dmix[here, hid], ws[s, 2].reshape(D, WIDTH))
            acc_n[here, :] += dot_t(dmix[here, dgt], ws[s, 0].reshape(D, WIDTH))
            acc_n[here, :] += dot_t(dmix[here, dup], ws[s, 1].reshape(D, WIDTH))
            return carry

        lax.fori_loop(0, 2, token_tile, 0)

        @pl.when(c >= 2)
        def _():
            pair_send("f", c - 2, "end")

        def grad_tile(h, carry):
            rows, os = grad_rows(h)
            shape = (half, 2, rows_n, WIDTH)
            grad[s, 0, os] = dot(act_t[rows, :], dmix[:, dgt]).astype(BF).reshape(shape)
            grad[s, 1, os] = dot(act_t[rows, :], dmix[:, dup]).astype(BF).reshape(shape)
            grad[s, 2, os] = dot(bck_t[rows, :], dmix[:, hid]).astype(BF).reshape(shape)
            return carry

        lax.fori_loop(0, 2, grad_tile, 0)
        pair_send("f", c, "start")

        @pl.when(c >= 1)
        def _():
            pair_sum("f", c - 1)

        pump(c + loop_pump)

        @pl.when(c + 1 < chunks)
        def _():
            gather_wait(c + 3)
            pltpu.make_async_copy(wf_all.at[c + 1], ws.at[1 - s], wsem.at[1 - s]).start()

        return carry

    lax.fori_loop(0, chunks, hidden_chunk, 0)

    def d_normed_two(q):
        stage[q] = acc_n[any_span(q), :].astype(BF)

    scatter(staged, rs_n2, 1, d_normed_two)
    pair_sum("f", chunks - 1)
    scatter_on(staged, rs_n2, 1)
    for time in range(1, 4):
        line_time("f", time, chunks)
    scatter_wait(rs_n2, 1)
    scatter_end(staged, rs_n2, 1)
    spread(low, n2_all, 2, "end")
    fetch(rs_n2, stage.at[pl.ds(0, 3)], 0)
    fetch(bck_own, act.at[span(0)], 0)
    g_gains[...] = jnp.zeros_like(g_gains)

    def d_middle_rows(i, carry):
        here = rows16(i)
        dn = arrived(here)
        mi = mid[here, :]
        s2 = lax.rsqrt(jnp.mean(mi * mi, axis=-1, keepdims=True) + EPS_NORM)
        e2 = gains[1:2, :] * dn
        back = act[here, :].astype(F32)
        dm = back + s2 * e2 - mi * (s2 * s2 * s2) * jnp.mean(e2 * mi, axis=-1, keepdims=True)
        dmid[here, :] = dm
        low[here, :] = dm.astype(BF)
        g_gains[1] += jnp.sum((dn * mi * s2).reshape(ROW_TILE // 8, 8, D), axis=0)
        return carry

    lax.fori_loop(0, seg // ROW_TILE, d_middle_rows, 0)
    spread(low, dbr_all, 3, "start")

    for q in range(group):
        stage[q] = acc_y[span(q), :].astype(BF)
    spill_back = pltpu.make_async_copy(mixed_far, acc_y.at[:, pl.ds(0, 3 * ch)], lsem.at[2])
    spill_back.start()

    for q in range(group):
        bck_t[pl.ds(0, ch), span(q)] = gated[span(q), :].T
        fetch(nrm_far.at[span(q)], act.at[span(q)], 0)
        act_t[:, span(q)] = act[span(q), :].T
    spill_back.wait()
    spread_on(dbr_all, 3)
    for time in range(4, 7):
        line_time("f", time, chunks)

    acc_n[pl.ds(seq, 8), pl.ds(0, ch)] = jnp.zeros((8, ch), F32)
    for q in range(group):
        spread_wait(dbr_all, 3, q)
        fetch(dbr_all.at[q], bck.at[span(q)], 0)
        acc_n[span(q), pl.ds(ch, ch)] = dot_t(bck[span(q), :], wo[...].reshape(ch, D))
        for k in range(blocks):
            col = pl.ds(k * 128, 128)
            d_gated = acc_n[span(q), pl.ds(ch + k * 128, 128)]
            acc_n[span(q), col] = d_gated * acc_y[span(q), lanes(k, 1)]
            dmix[span(q), lanes(k, 1)] = (d_gated * convolved(q, col)).astype(BF)
    scatter(staged, rs_y, 2, lambda q: None)
    g_taps[...] = jnp.zeros_like(g_taps)
    for q in range(group):
        for k in range(blocks):
            col = pl.ds(k * 128, 128)
            d0 = acc_n[span(q), col]
            for n in range(3):
                g_taps[n, :, col] += jnp.sum(
                    (d0 * prod[pl.ds(q * seg + 6 + n, seg), col]).reshape(seg // 8, 8, 128), axis=0
                )
            d_product = (
                taps[2:3, col] * d0
                + taps[1:2, col] * acc_n[pl.ds(q * seg + 1, seg), col]
                + taps[0:1, col] * acc_n[pl.ds(q * seg + 2, seg), col]
            )
            dmix[span(q), lanes(k, 0)] = (d_product * acc_y[span(q), lanes(k, 2)]).astype(BF)
            dmix[span(q), lanes(k, 2)] = (d_product * acc_y[span(q), lanes(k, 0)]).astype(BF)

    for k in range(blocks):
        s = (chunks + k) % 2
        if k < 2:
            pair_send("f", chunks - 2 + k, "end")
        else:
            pair_send("i", k - 2, "end")

        def intake_tile(h, carry, k=k, s=s):
            rows, os = grad_rows(h)
            value = dot(act_t[rows, :], dmix[:, pl.ds(k * 384, 384)]).astype(BF)
            for j in range(3):
                grad[s, j, os, :, :, pl.ds(0, 128)] = value[:, j * 128 : (j + 1) * 128].reshape(
                    half, 2, rows_n, 128
                )
            return carry

        lax.fori_loop(0, 2, intake_tile, 0)
        pair_send("i", k, "start")
        if k >= 1:
            pair_sum("i", k - 1)

    for n in range(4):
        col = pl.ds(n * 384, 384)
        wo[:, :, :, col] = dot(bck_t[pl.ds(0, ch), :], bck[:, col]).astype(BF).reshape(out_n, 2, cblk, 384)
    last = chunks + blocks
    pair_o = remote(wo.at[:, 1 - b], sib_o, gs_ssem.at[last], gs_rsem.at[last], mate)
    pair_o.start()
    pair_sum("i", blocks - 1)

    await_bytes(sib_o, gs_rsem.at[last])
    fetch(sib_o, sibo, 1)

    def add_o(o2, carry):
        parto[o2] = (wo[o2, b].astype(F32) + sibo[o2].astype(F32)).astype(BF)
        return carry

    lax.fori_loop(0, out_n, add_o, 0)

    def part_o(op):
        def one(k, carry):
            o2, dev = peer(k)
            copy = remote(parto.at[o2], z_o.at[o], gz_ssem.at[last, k], up_sem.at[last, o], dev)
            if op == "start":
                copy.start()
            else:
                copy.wait_send()
            return carry

        lax.fori_loop(1, out_n, one, 0)
        keep = pltpu.make_async_copy(parto.at[o], z_o.at[o], osem.at[0])
        if op == "start":
            keep.start()
        else:
            keep.wait()

    part_o("start")

    def lent(q):
        return bck.at[any_span(q)]

    def d_normed(q):
        for n in range(4):
            bck[any_span(q), pl.ds(n * 384, 384)] = dot_t(
                dmix[any_span(q), :], wi[pl.ds(n * out_n // 4, out_n // 4)].reshape(384, 3 * ch)
            ).astype(BF)

    scatter(lent, rs_n1, 3, d_normed)
    scatter_on(staged, rs_y, 2)
    scatter_on(lent, rs_n1, 3)
    scatter_wait(rs_y, 2)
    scatter_end(staged, rs_y, 2)
    spread(low, dbr_all, 3, "end")
    for q in range(3):
        fetch(rs_y.at[q], act.at[span(q)], 0)

    def out_rows(i, carry):
        here = rows16(i)
        value = act[here, :].astype(F32)
        for q in range(1, 3):
            value = value + act[pl.ds(pl.multiple_of(q * seg + i * ROW_TILE, ROW_TILE), ROW_TILE), :].astype(F32)
        low[here, :] = (mid[here, :] + value).astype(BF)
        return carry

    lax.fori_loop(0, seg // ROW_TILE, out_rows, 0)
    fetch(low, block_out, 0)

    for time in range(7, chunks + out_n - 1):
        line_time("f", time, chunks)

    def total_f(c, carry):
        total("f", c)
        return carry

    lax.fori_loop(0, chunks, total_f, 0)
    scatter_wait(rs_n1, 3)
    scatter_end(lent, rs_n1, 3)
    fetch(rs_n1, stage.at[pl.ds(0, 3)], 0)

    def d_rows(i, carry):
        here = rows16(i)
        dn = arrived(here)
        row = tok[here, :].astype(F32)
        s1 = lax.rsqrt(jnp.mean(row * row, axis=-1, keepdims=True) + EPS_NORM)
        e1 = gains[0:1, :] * dn
        low[here, :] = (
            dmid[here, :] + s1 * e1 - row * (s1 * s1 * s1) * jnp.mean(e1 * row, axis=-1, keepdims=True)
        ).astype(BF)
        g_gains[0] += jnp.sum((dn * row * s1).reshape(ROW_TILE // 8, 8, D), axis=0)
        return carry

    lax.fori_loop(0, seg // ROW_TILE, d_rows, 0)
    fetch(low, input_grad, 0)

    sm_mine[...] = jnp.zeros_like(sm_mine)
    for i in range(2):
        value = jnp.sum(g_gains[i], axis=0, keepdims=True)
        for j in range(D // 128):
            row = i * (D // 128) + j
            sm_mine[row : row + 1, :] = value[:, j * 128 : (j + 1) * 128]
    for n in range(3):
        value = jnp.sum(g_taps[n], axis=0, keepdims=True)
        for k in range(blocks):
            for t2 in range(group):
                row = 2 * (D // 128) + (t2 * 3 + n) * blocks + k
                sm_mine[row : row + 1, :] = jnp.where(t == t2, value[:, k * 128 : (k + 1) * 128], 0.0)
    sm_plane[place] = sm_mine[...]
    plane(sm_mine, sm_plane.at[place], ta_ssem, ta_rsem, "start")

    for k in range(max(0, blocks - 2), blocks):
        pair_send("i", k, "end")

    def lines(time, carry):
        line_time("i", time, blocks)
        return carry

    lax.fori_loop(1, out_n - 1, lines, 0)
    plane_wait(sm_mine, ta_rsem)
    value = sm_plane[0]
    for i in range(1, 2 * group):
        value = value + sm_plane[i]
    sm_sum[...] = value
    sm_z[o] = value
    far(sm_sum, sm_z.at[o], tz_ssem, tz_rsem, "start")
    lax.fori_loop(out_n - 1, blocks + out_n - 1, lines, 0)
    for k in range(blocks):
        total("i", k)
    part_o("end")
    pair_o.wait_send()

    def last_one(k, carry):
        await_bytes(z_o.at[o], up_sem.at[last, peer(k)[0]])
        return carry

    lax.fori_loop(1, out_n, last_one, 0)
    fetch(z_o, sibo, 1)
    value = sibo[0].astype(F32)
    for o2 in range(1, out_n):
        value = value + sibo[o2].astype(F32)
    outo = parto.at[0]
    outo[...] = value.astype(BF)

    def back_o(op):
        switch(
            a == b,
            pltpu.make_async_copy(outo, g_wo, back_rsem.at[last, 0]),
            remote(outo, g_wo, back_ssem.at[last, 0], back_rsem.at[last, 0], (2 * o + b, 2 * y + a)),
            op,
        )

    back_o("start")
    far_wait(sm_sum, tz_rsem)
    value = sm_z[0]
    for i in range(1, out_n):
        value = value + sm_z[i]
    g_small[...] = value

    plane(small_own, small_all.at[mine], sa_ssem, sa_rsem, "end")
    far(planes, planes, sz_ssem, sz_rsem, "end")
    plane(sm_mine, sm_plane.at[place], ta_ssem, ta_rsem, "end")
    far(sm_sum, sm_z.at[o], tz_ssem, tz_rsem, "end")
    spread(tok, tok_all, 0, "end")
    spread(bck_own, bck_all, 1, "end")
    gather_close(0)
    gather_close(1)

    def close(c, carry):
        gather_close(c + 2)
        line_close("f", c)
        hand_back("f", c, "end")
        hand_wait("f", c)
        return carry

    lax.fori_loop(0, chunks, close, 0)
    for k in range(blocks):
        line_close("i", k)
        hand_back("i", k, "end")
        hand_wait("i", k)
    back_o("end")
    await_bytes(g_wo, back_rsem.at[last, 0])


def forward_backward(sizes, tok, bck, wi_own, wo_own, ff_own, small_own):
    (out_n, group, rows_n, seg, ch, cblk, chunks) = sizes
    blocks = ch // 128
    seq = group * seg
    block = rows_n // group
    places = 2 * group
    small_rows = -(-(2 * D // 128 + group * 3 * blocks) // 8) * 8
    items = 2 + chunks
    sums = chunks + blocks + 1
    vm = pltpu.VMEM
    dma = pltpu.SemaphoreType.DMA

    def shape(*dims, dtype=BF):
        return jax.ShapeDtypeStruct(dims, dtype)

    any_spec = pl.BlockSpec(memory_space=pl.ANY)
    vmem_spec = pl.BlockSpec(memory_space=pltpu.VMEM)
    if block % 16 == 0:
        given = [shape(group, chunks, 3, block, WIDTH), shape(group, blocks, 3, block, 128)]
    else:
        given = [shape(chunks, 3, rows_n, WIDTH), shape(blocks, 3, rows_n, 128)]
    outs = [
        shape(seg, D), shape(seg, D), *given, shape(cblk, D), shape(small_rows, 128, dtype=F32),
        shape(chunks, 3, out_n, 2, rows_n, WIDTH), shape(out_n, 2, rows_n, 3 * ch), shape(out_n, 2, cblk, D),
        shape(group, seg, D), shape(seq, D), shape(group, seg, D), shape(group, seg, D), shape(group, seg, D),
        shape(3, seg, D), shape(3, seg, D), shape(3, seg, D), shape(3, seg, D), shape(4, 2, seg // 2, D),
        shape(chunks, 3, out_n, rows_n, WIDTH), shape(blocks, 3, out_n, rows_n, 128), shape(out_n, cblk, D),
        *[shape(chunks, 3, out_n, rows_n, WIDTH), shape(blocks, 3, out_n, rows_n, 128)] * 3, shape(out_n, cblk, D),
        shape(seq, 3 * ch, dtype=F32),
    ]
    out_specs = [any_spec] * 5 + [vmem_spec] + [any_spec] * (len(outs) - 6)
    scratch = [
        vm((2, 3, out_n, 2, rows_n, WIDTH), BF),
        vm((out_n, 2, rows_n, 3 * ch), BF),
        vm((out_n, 2, cblk, D), BF),
        vm((seq, D), BF), vm((D, seq), BF), vm((seq, D), BF), vm((D, seq), BF),
        vm((seq, D), F32), vm((seq + 8, D), F32),
        vm((2, 3, out_n, 2, rows_n, WIDTH), BF),
        vm((3, out_n, rows_n, WIDTH), BF),
        vm((2, 3, out_n, rows_n, WIDTH), BF),
        vm((group, seg, D), BF),
        vm((seq + 8, ch), F32), vm((seq, ch), BF), vm((seq, 3 * ch), BF),
        vm((seg, D), F32), vm((seg, D), F32), vm((seg, D), BF),
        vm((out_n, cblk, D), BF), vm((out_n, cblk, D), BF),
        vm((places * out_n, 8, 128), F32), vm((2, D), F32), vm((3, ch), F32),
        vm((2, 8, D), F32), vm((3, 8, ch), F32),
        vm((small_rows, 128), F32), vm((places, small_rows, 128), F32),
        vm((small_rows, 128), F32), vm((out_n, small_rows, 128), F32),
        vm((seg // 2, D), BF),
        dma((4, 3, 2)), dma((4, group, 2)), dma((4, 2)), dma((4, 4, 2)), dma((4, 3, 2)), dma((4, 2, 2)), dma((4, 2)),
        dma((items, 2, out_n)), dma((items, out_n)), dma((items,)), dma((items,)),
        dma((sums,)), dma((sums,)), dma((sums, out_n)), dma((sums, out_n)), dma((sums, out_n)),
        dma((items, group)), dma((items, group)), dma((sums, group)), dma((sums, group)), dma((1,)),
        dma((places,)), dma((places,)), dma((out_n,)), dma((out_n,)),
        dma((places,)), dma((places,)), dma((out_n,)), dma((out_n,)), dma((2,)), dma((5,)),
    ]
    results = pl.pallas_call(
        functools.partial(block_kernel, sizes),
        out_shape=outs,
        in_specs=[vmem_spec] + [any_spec] * 4 + [vmem_spec],
        out_specs=out_specs,
        scratch_shapes=scratch,
        compiler_params=pltpu.CompilerParams(
            collective_id=0, has_side_effects=True, vmem_limit_bytes=63 * 1024 * 1024
        ),
        cost_estimate=pl.CostEstimate(
            flops=6 * seq * D * (4 * ch + 3 * chunks * WIDTH),
            bytes_accessed=200_000_000,
            transcendentals=seq * chunks * WIDTH,
        ),
    )(tok, bck, wi_own, wo_own, ff_own, small_own)
    return results[:6]


def body(
    tokens,
    cotangent,
    lengths,
    intake_weight,
    intake_first,
    intake_second,
    output_weight,
    output_first,
    output_second,
    swiglu_weight,
    swiglu_first,
    swiglu_second,
    down_weight,
    down_first,
    down_second,
    norm_gains,
    gains_first,
    gains_second,
    conv_kernel,
    kernel_first,
    kernel_second,
):
    data_count = lax.axis_size("dp")
    group_count = lax.axis_size("group")
    dp = lax.axis_index("dp")
    member = lax.axis_index("group")
    block = D // (data_count * group_count)
    cblk = -(-block // 16) * 16
    ch = data_count * cblk
    blocks = ch // 128
    hidden_part = FF // group_count
    chunks = -(-hidden_part // WIDTH)
    hidden_full = chunks * WIDTH
    rows_n = D // data_count
    swap = []
    for one in range(data_count):
        for two in range(group_count):
            there = (2 * (one // 2) + two % 2) * group_count + 2 * (two // 2) + one % 2
            swap.append((one * group_count + two, there))

    def cross(value):
        return lax.ppermute(value, ("dp", "group"), swap)

    intake_local = (
        intake_weight.astype(BF)
        .reshape(block, 3, data_count, group_count, block)
        .transpose(3, 0, 1, 2, 4)
    )
    intake_local = jnp.pad(intake_local, ((0, 0),) * 4 + ((0, cblk - block),))
    intake_local = (
        intake_local.reshape(group_count, block, 3, blocks, 128)
        .transpose(0, 1, 3, 2, 4)
        .reshape(group_count, block, 3 * ch)
    )
    ff_local = jnp.concatenate(
        [
            swiglu_weight.astype(BF).reshape(block, 2, group_count, hidden_part),
            down_weight.astype(BF).reshape(block, 1, group_count, hidden_part),
        ],
        axis=1,
    )
    ff_local = jnp.pad(ff_local, ((0, 0),) * 3 + ((0, hidden_full - hidden_part),))
    ff_local = ff_local.reshape(block, 3, group_count, chunks, WIDTH).transpose(2, 3, 1, 0, 4)
    wo_own = jnp.pad(output_weight.astype(BF).reshape(block, D), ((0, cblk - block), (0, 0)))
    if block % 16 == 0:
        wi_own, ff_own = intake_local, ff_local
    else:
        wi_own = lax.all_to_all(intake_local, "group", split_axis=0, concat_axis=0, tiled=True)
        wi_own = cross(wi_own.reshape(rows_n, 3 * ch))
        ff_own = lax.all_to_all(ff_local, "group", split_axis=0, concat_axis=0, tiled=True)
        ff_own = cross(ff_own.transpose(1, 2, 0, 3, 4).reshape(chunks, 3, rows_n, WIDTH))

    number = dp * group_count + member
    share = norm_gains.shape[0]

    def placed(values, lane):
        line = lax.dynamic_update_slice(jnp.zeros((256,), F32), lax.reduce_precision(values, 8, 7), (lane,))
        return line.reshape(2, 128)

    runs = [placed(norm_gains, lax.rem(number * share, 128))]
    for piece in range(3):
        rest = lax.rem(3 * number + piece, data_count * group_count)
        lane = lax.rem(rest // group_count * cblk, 128)
        runs.append(placed(conv_kernel[piece * block : (piece + 1) * block], lane))
    small_own = jnp.concatenate(runs)

    seg_len = tokens.shape[1]
    positions = member * seg_len + lax.iota(jnp.int32, seg_len)
    valid = (positions < lengths[0]).astype(F32)[:, None]
    back_low = (cotangent[0].astype(F32) * valid).astype(BF)

    sizes = (data_count // 2, group_count, rows_n, seg_len, ch, cblk, chunks)
    block_out, input_grad, g_ff, g_wi, g_wo, g_small = forward_backward(
        sizes, tokens[0], back_low, wi_own, wo_own, ff_own, small_own
    )

    if block % 16:
        g_wi = cross(g_wi).reshape(blocks, 3, group_count, block, 128).transpose(2, 0, 1, 3, 4)
        g_wi = lax.all_to_all(g_wi, "group", split_axis=0, concat_axis=0, tiled=True)
        g_ff = cross(g_ff).reshape(chunks, 3, group_count, block, WIDTH).transpose(2, 0, 1, 3, 4)
        g_ff = lax.all_to_all(g_ff, "group", split_axis=0, concat_axis=0, tiled=True)
    g_wi = g_wi.transpose(0, 3, 2, 1, 4).reshape(group_count, block, 3, data_count, cblk)
    intake_grad_flat = g_wi[..., :block].transpose(1, 2, 3, 0, 4).reshape(-1).astype(F32)
    g_ff = g_ff.transpose(3, 2, 0, 1, 4).reshape(block, 3, group_count, hidden_full)
    g_ff = g_ff[..., :hidden_part]
    swiglu_grad_flat = g_ff[:, :2].reshape(-1).astype(F32)
    down_grad_flat = g_ff[:, 2].reshape(-1).astype(F32)
    output_grad_flat = g_wo[:block].reshape(-1).astype(F32)

    gain_rows = 2 * D // 128
    taps_grad = g_small[gain_rows : gain_rows + group_count * 3 * blocks]
    taps_grad = taps_grad.reshape(group_count, 3, data_count, cblk)[..., :block]
    taps_grad = taps_grad.transpose(1, 2, 0, 3).reshape(-1)
    small_shards = (
        lax.dynamic_slice(g_small[:gain_rows].reshape(-1), (number * share,), (share,)),
        lax.dynamic_slice(taps_grad, (number * 3 * block,), (3 * block,)),
    )
    intake_new = update(
        intake_weight, intake_first, intake_second, intake_grad_flat, RATE_MATRIX, DECAY
    )
    output_new = update(
        output_weight, output_first, output_second, output_grad_flat, RATE_MATRIX, DECAY
    )
    swiglu_new = update(
        swiglu_weight, swiglu_first, swiglu_second, swiglu_grad_flat, RATE_MATRIX, DECAY
    )
    down_new = update(down_weight, down_first, down_second, down_grad_flat, RATE_MATRIX, DECAY)
    gains_new = update(norm_gains, gains_first, gains_second, small_shards[0], RATE_VECTOR, 0.0)
    kernel_new = update(
        conv_kernel, kernel_first, kernel_second, small_shards[1], RATE_VECTOR, DECAY
    )
    return (
        block_out[None],
        input_grad[None],
        intake_new[0],
        intake_new[1],
        intake_new[2],
        output_new[0],
        output_new[1],
        output_new[2],
        swiglu_new[0],
        swiglu_new[1],
        swiglu_new[2],
        down_new[0],
        down_new[1],
        down_new[2],
        gains_new[0],
        gains_new[1],
        gains_new[2],
        kernel_new[0],
        kernel_new[1],
        kernel_new[2],
    )


def solution(mesh):
    in_specs = (
        P("dp", "group", None),
        P("dp", "group", None),
        P("dp"),
        P(("dp", "group")),
        P(("dp", "group")),
        P(("dp", "group")),
        P(("dp", "group")),
        P(("dp", "group")),
        P(("dp", "group")),
        P(("dp", "group")),
        P(("dp", "group")),
        P(("dp", "group")),
        P(("dp", "group")),
        P(("dp", "group")),
        P(("dp", "group")),
        P(("dp", "group")),
        P(("dp", "group")),
        P(("dp", "group")),
        P(("dp", "group")),
        P(("dp", "group")),
        P(("dp", "group")),
    )
    out_specs = (
        P("dp", "group", None),
        P("dp", "group", None),
        P(("dp", "group")),
        P(("dp", "group")),
        P(("dp", "group")),
        P(("dp", "group")),
        P(("dp", "group")),
        P(("dp", "group")),
        P(("dp", "group")),
        P(("dp", "group")),
        P(("dp", "group")),
        P(("dp", "group")),
        P(("dp", "group")),
        P(("dp", "group")),
        P(("dp", "group")),
        P(("dp", "group")),
        P(("dp", "group")),
        P(("dp", "group")),
        P(("dp", "group")),
        P(("dp", "group")),
    )
    return jax.shard_map(body, mesh=mesh, in_specs=in_specs, out_specs=out_specs, check_vma=False)
```

```python
import functools

import jax
import jax.numpy as jnp
from jax import lax
from jax.experimental import pallas as pl
from jax.experimental.pallas import tpu as pltpu
from jax.sharding import PartitionSpec as P

D = 1536
FF = 6912
STEP = 5
WIDTH = 256
ROW_TILE = 16

EPS_NORM = 1e-05
BETA_ONE = 0.5
BETA_TWO = 0.5
ADAM_EPS = 1e-08
RATE_MATRIX = 0.02
RATE_VECTOR = 0.2
DECAY = 0.1

MESH = pl.DeviceIdType.MESH
BF = jnp.bfloat16
F32 = jnp.float32


def update(weight, first, second, grad, rate, decay):
    first_new = BETA_ONE * first + (1.0 - BETA_ONE) * grad
    second_new = BETA_TWO * second + (1.0 - BETA_TWO) * grad * grad
    first_hat = first_new / (1.0 - BETA_ONE**STEP)
    second_hat = second_new / (1.0 - BETA_TWO**STEP)
    weight_new = weight - rate * (first_hat / (jnp.sqrt(second_hat) + ADAM_EPS) + decay * weight)
    return (first_new, second_new, weight_new)


def dot(left, right):
    return lax.dot_general(left, right, (((1,), (0,)), ((), ())), preferred_element_type=F32)


def dot_t(left, right):
    return lax.dot_general(left, right, (((1,), (1,)), ((), ())), preferred_element_type=F32)


def await_bytes(ref, sem):
    pltpu.make_async_copy(ref, ref, sem).wait()


def block_kernel(
    sizes,
    tok, bck_own, wi_own, wo_own, ff_own, small_own,
    block_out, input_grad, g_ff, g_wi, g_wo, g_small,
    wf_all, wi_all, wo_all, tok_all, nrm_far, bck_all, n2_all, dbr_all,
    rs_br, rs_y, rs_n2, rs_n1, via,
    sib_f, sib_i, sib_o, come_f, come_i, far_f, far_i, z_o, mixed_far,
    ws, wi, wo, act, act_t, bck, bck_t, acc_y, acc_n, grad, sibv, part, stage,
    prod, gated, dmix, mid, dmid, low, sibo, parto,
    small_all, gains, taps, g_gains, g_taps, sm_mine, sm_plane, sm_sum, sm_z,
    extra, ag_ssem, ag_rsem, ag_fsem, rs_ssem, rs_rsem, via_ssem, via_rsem, z_ssem, z_rsem, f_ssem, f_rsem,
    gs_ssem, gs_rsem, gz_ssem, come_sem, far_sem, buf_sem, own_ssem, own_rsem, back_ssem, back_rsem, osem,
    sa_ssem, sa_rsem, sz_ssem, sz_rsem, ta_ssem, ta_rsem, tz_ssem, tz_rsem, wsem, lsem,
):
    (out_n, group, rows_n, seg, ch, cblk, chunks) = sizes
    block = rows_n // group
    direct = block % 16 == 0
    count = 2 * out_n * group
    blocks = ch // 128
    seq = group * seg
    dp = lax.axis_index("dp")
    g = lax.axis_index("group")
    o, a = dp // 2, lax.rem(dp, 2)
    y, b = g // 2, lax.rem(g, 2)
    t = 2 * y + a
    mate = (dp, g + 1 - 2 * b)

    def peer(k):
        o2 = lax.rem(o + k, out_n)
        return o2, (2 * o2 + a, g)

    barrier = pltpu.get_barrier_semaphore()
    for x2 in range(2):
        for g2 in range(group):
            @pl.when((x2 != a) | (g2 != g))
            def _():
                pl.semaphore_signal(barrier, inc=1, device_id=(2 * o + x2, g2), device_id_type=MESH)

    def greet(k, carry):
        pl.semaphore_signal(barrier, inc=1, device_id=peer(k)[1], device_id_type=MESH)
        return carry

    lax.fori_loop(1, out_n, greet, 0)
    pl.semaphore_wait(barrier, 2 * group - 1 + out_n - 1)

    def remote(src, dst, ssem, rsem, dev):
        return pltpu.make_async_remote_copy(
            src_ref=src, dst_ref=dst, send_sem=ssem, recv_sem=rsem, device_id=dev, device_id_type=MESH
        )

    def switch(alone, local, copy, op):
        if op == "start":
            @pl.when(alone)
            def _():
                local.start()

            @pl.when(jnp.logical_not(alone))
            def _():
                copy.start()
        else:
            @pl.when(jnp.logical_not(alone))
            def _():
                copy.wait_send()

    odd = lax.rem(a + b, 2)
    size = seg // 2
    y_via = odd * y + (1 - odd) * (1 - y)
    h_via = 1 - odd
    partner = (2 * o + odd * a + (1 - odd) * (1 - a), 2 * (odd * (1 - y) + (1 - odd) * y) + b)

    def part_of(h):
        return pl.ds(h * size, size) if isinstance(h, int) else pl.ds(pl.multiple_of(h * size, size), size)

    def spread(src, dst, n, op):
        for d, h in ((1, 0), (2, 1), (1, 1), (2, 0), (0, 0), (0, 1)):
            x2, y2 = (1 - a if d == 1 else a), (1 - y if d == 2 else y)
            one, two = src.at[part_of(h)], dst.at[g, part_of(h)]
            copy = remote(one, two, ag_ssem.at[n, d, h], ag_rsem.at[n, g, h], (2 * o + x2, 2 * y2 + a))
            if d == 0:
                switch(a == b, pltpu.make_async_copy(one, two, ag_rsem.at[n, g, h]), copy, op)
            elif op == "start":
                copy.start()
            else:
                copy.wait_send()
        if op == "end":
            for k in range(2):
                ref = dst.at[2 * y_via + k, part_of(h_via)]
                await_bytes(ref, ag_fsem.at[n, k])

    def spread_on(dst, n):
        for k in range(2):
            q = 2 * y_via + k
            ref = dst.at[q, part_of(h_via)]
            await_bytes(ref, ag_rsem.at[n, q, h_via])
            remote(ref, ref, ag_fsem.at[n, k], ag_rsem.at[n, q, h_via], partner).start()

    def spread_wait(dst, n, q):
        for h in range(2):
            @pl.when((q // 2 != y_via) | (h != h_via))
            def _():
                await_bytes(dst.at[q, part_of(h)], ag_rsem.at[n, q, h])

    def give(terms, dst, n, at, q, h, slot, op="start"):
        one, two = terms(q).at[part_of(h)], dst.at[slot, part_of(h)]
        copy = remote(one, two, rs_ssem.at[n, at, h], rs_rsem.at[n, slot, h], (2 * o + b, q))
        if slot == 0:
            switch(q == g, pltpu.make_async_copy(one, two, rs_rsem.at[n, 0, h]), copy, op)
        elif op == "start":
            copy.start()
        else:
            copy.wait_send()

    def give_half(terms, n, k, h, op):
        q = 2 * (1 - y) + k
        dev = (2 * o + 1 - a, g) if h == 0 else (dp, 2 * (1 - y) + b)
        copy = remote(terms(q).at[part_of(h)], via.at[n, k], via_ssem.at[n, k, h], via_rsem.at[n, k], dev)
        if op == "start":
            copy.start()
        else:
            copy.wait_send()

    def scatter(terms, dst, n, produce):
        for k in range(2):
            q = 2 * (1 - y) + k
            produce(q)

            @pl.when(odd == 1)
            def _():
                give_half(terms, n, k, 0, "start")
                give_half(terms, n, k, 1, "start")

            @pl.when(odd == 0)
            def _():
                give(terms, dst, n, k, q, 1, 1)

        for k in range(2):
            q = 2 * y + k
            produce(q)

            @pl.when(odd == 1)
            def _():
                give(terms, dst, n, 2 + k, q, 0, 2)

            @pl.when(odd == 0)
            def _():
                give(terms, dst, n, 2 + k, q, 0, 0)
                give(terms, dst, n, 2 + k, q, 1, 0)

    def scatter_on(terms, dst, n):
        for k in range(2):
            q = 2 * y_via + k
            await_bytes(via.at[n, k], via_rsem.at[n, k])
            fetch(via.at[n, k], extra, 0)

            def add_rows(i, carry):
                here = pl.ds(pl.multiple_of(odd * size + i * ROW_TILE, ROW_TILE), ROW_TILE)
                ref = terms(q)
                ref[here, :] = (ref[here, :].astype(F32) + extra[rows16(i), :].astype(F32)).astype(BF)
                return carry

            lax.fori_loop(0, size // ROW_TILE, add_rows, 0)

            @pl.when(odd == 1)
            def _():
                give(terms, dst, n, 2 + k, q, 1, 2)

            @pl.when(odd == 0)
            def _():
                give(terms, dst, n, k, q, 0, 1)

    def scatter_end(terms, dst, n):
        @pl.when(odd == 1)
        def _():
            for k in range(2):
                for h in range(2):
                    give_half(terms, n, k, h, "end")
                    give(terms, dst, n, 2 + k, 2 * y + k, h, 2, "end")

        @pl.when(odd == 0)
        def _():
            for k in range(2):
                for h in range(2):
                    give(terms, dst, n, k, 2 * (1 - y) + k, h, 1, "end")
                    give(terms, dst, n, 2 + k, 2 * y + k, h, 0, "end")

    def scatter_wait(dst, n):
        for slot in range(3):
            for h in range(2):
                await_bytes(dst.at[slot, part_of(h)], rs_rsem.at[n, slot, h])

    def staged(q):
        return stage.at[q]

    def any_span(q):
        return pl.ds(pl.multiple_of(q * seg, seg), seg)

    def slot_of(i, o2, p):
        if isinstance(i, int) and i == 0:
            return wi_all.at[o2, p]
        if isinstance(i, int) and i == 1:
            return wo_all.at[o2, p]
        return wf_all.at[i - 2, :, o2, p]

    def half_of(i, p):
        if isinstance(i, int) and i == 0:
            return wi_all.at[:, p]
        if isinstance(i, int) and i == 1:
            return wo_all.at[:, p]
        return wf_all.at[i - 2, :, :, p]

    my_rows = pl.ds(pl.multiple_of(g * block, 4), block)

    def own_send(i, op):
        if isinstance(i, int) and i == 1:
            dst = wo_all.at[o, a]
            switch(
                a == b,
                pltpu.make_async_copy(wo_own, dst, own_rsem.at[1, 0]),
                remote(wo_own, dst, own_ssem.at[1, 0], own_rsem.at[1, 0], (2 * o + b, 2 * y + a)),
                op,
            )
            return
        if not direct:
            src = wi_own if isinstance(i, int) and i == 0 else ff_own.at[i - 2]
            if op == "start":
                pltpu.make_async_copy(src, slot_of(i, o, b), own_rsem.at[i, 0]).start()
            return
        for t2 in range(group):
            ty, tx = t2 // 2, t2 % 2
            if isinstance(i, int) and i == 0:
                src, dst = wi_own.at[t2], wi_all.at[o, a, my_rows]
            else:
                src, dst = ff_own.at[t2, i - 2], wf_all.at[i - 2, :, o, a, my_rows]
            switch(
                (tx == a) & (ty == y) & (a == b),
                pltpu.make_async_copy(src, dst, own_rsem.at[i, g]),
                remote(src, dst, own_ssem.at[i, t2], own_rsem.at[i, g], (2 * o + tx, 2 * ty + a)),
                op,
            )

    def own_wait(i):
        if not direct or isinstance(i, int) and i == 1:
            await_bytes(slot_of(i, o, b), own_rsem.at[i, 0])
            return
        for q in range(group):
            if isinstance(i, int) and i == 0:
                await_bytes(wi_all.at[o, b, pl.ds(q * block, block)], own_rsem.at[i, q])
            else:
                await_bytes(wf_all.at[i - 2, :, o, b, pl.ds(q * block, block)], own_rsem.at[i, q])

    first, final = o == 0, o == out_n - 1

    def piece_send(i, src, side):
        ref = slot_of(i, src, b)
        dev = (2 * (o + 1 - 2 * side) + a, g)
        remote(ref, ref, z_ssem.at[i, side, src], z_rsem.at[i, src], dev).start()

    def when(condition, call, *args):
        @pl.when(condition)
        def _():
            call(*args)

    def hop(i, h):
        if h == 0:
            own_wait(i)
            when(jnp.logical_not(final), piece_send, i, o, 0)
            when(jnp.logical_not(first), piece_send, i, o, 1)
            return

        @pl.when(o - h >= 0)
        def _():
            await_bytes(slot_of(i, o - h, b), z_rsem.at[i, o - h])
            when(jnp.logical_not(final), piece_send, i, o - h, 0)

        @pl.when(o + h < out_n)
        def _():
            await_bytes(slot_of(i, o + h, b), z_rsem.at[i, o + h])
            when(jnp.logical_not(first), piece_send, i, o + h, 1)

        if h == out_n - 1:
            remote(half_of(i, b), half_of(i, b), f_ssem.at[i], f_rsem.at[i], mate).start()

    items = 2 + chunks
    sent = set()

    def own_start(*which):
        for i in which:
            if i < items and i not in sent:
                sent.add(i)
                own_send(i, "start")

    def pump(time):
        if isinstance(time, int):
            own_start(*range(time + 1))
        for h in range(out_n - 1, -1, -1):
            if isinstance(time, int):
                if 0 <= time - h < items:
                    hop(time - h, h)
            else:
                when(time - h < items, hop, time - h, h)

    def gather_wait(i):
        await_bytes(half_of(i, 1 - b), f_rsem.at[i])

    def gather_close(i):
        def sent(src, side):
            await_bytes(slot_of(i, src, b), z_ssem.at[i, side, src])

        @pl.when(jnp.logical_not(final))
        def _():
            lax.fori_loop(0, o + 1, lambda src, carry: (sent(src, 0), carry)[1], 0)

        @pl.when(jnp.logical_not(first))
        def _():
            lax.fori_loop(o, out_n, lambda src, carry: (sent(src, 1), carry)[1], 0)

        await_bytes(half_of(i, b), f_ssem.at[i])
        own_send(i, "end")

    def fetch(src, dst, n):
        copy = pltpu.make_async_copy(src, dst, lsem.at[n])
        copy.start()
        copy.wait()

    def span(q):
        return pl.ds(q * seg, seg)

    def rows16(i):
        return pl.ds(pl.multiple_of(i * ROW_TILE, ROW_TILE), ROW_TILE)

    def lanes(k, j):
        return pl.ds(k * 384 + j * 128, 128)

    place = a * group + g
    mine = o * (2 * group) + place

    def plane(src, dst, ssem, rsem, op):
        for x2 in range(2):
            for g2 in range(group):
                @pl.when((x2 != a) | (g2 != g))
                def _():
                    copy = remote(src, dst, ssem.at[x2 * group + g2], rsem.at[place], (2 * o + x2, g2))
                    if op == "start":
                        copy.start()
                    else:
                        copy.wait_send()

    def plane_wait(ref, rsem):
        for x2 in range(2):
            for g2 in range(group):
                @pl.when((x2 != a) | (g2 != g))
                def _():
                    await_bytes(ref, rsem.at[x2 * group + g2])

    def far(src, dst, ssem, rsem, op):
        def one(k, carry):
            copy = remote(src, dst, ssem.at[k], rsem.at[o], peer(k)[1])
            if op == "start":
                copy.start()
            else:
                copy.wait_send()
            return carry

        lax.fori_loop(1, out_n, one, 0)

    def far_wait(ref, rsem):
        def one(k, carry):
            await_bytes(ref, rsem.at[peer(k)[0]])
            return carry

        lax.fori_loop(1, out_n, one, 0)

    planes = small_all.at[pl.ds(o * 2 * group, 2 * group)]
    pltpu.make_async_copy(small_own, small_all.at[mine], lsem.at[2]).start()
    plane(small_own, small_all.at[mine], sa_ssem, sa_rsem, "start")

    def convolved(q, col):
        return (
            taps[0:1, col] * prod[pl.ds(q * seg + 6, seg), col]
            + taps[1:2, col] * prod[pl.ds(q * seg + 7, seg), col]
            + taps[2:3, col] * prod[pl.ds(q * seg + 8, seg), col]
        )

    own_start(0)
    own_start(1)
    own_start(2)
    spread(tok, tok_all, 0, "start")
    own_start(3)
    prod[pl.ds(0, 8), :] = jnp.zeros((8, ch), F32)
    pump(0)
    await_bytes(small_own, lsem.at[2])
    plane_wait(small_own, sa_rsem)
    far(planes, planes, sz_ssem, sz_rsem, "start")
    pump(1)
    far_wait(planes, sz_rsem)
    spread_on(tok_all, 0)

    share = 2 * D // count
    rows_of = {}
    for n in range(count):
        row = n * share // 128
        rows_of.setdefault(row, []).append((n, 0))
        if (n * share + share - 1) // 128 > row:
            rows_of.setdefault(row + 1, []).append((n, 1))
    for tile, pieces in rows_of.items():
        value = sum(small_all[n, r : r + 1, :] for n, r in pieces)
        i, j = tile // (D // 128), tile % (D // 128)
        gains[i : i + 1, j * 128 : (j + 1) * 128] = value
    rows_of = {}
    for m in range(3 * count):
        n, piece = m // 3, m % 3
        tap, rest = m // count, m % count
        lane = rest // group * cblk
        rows_of.setdefault((tap, lane // 128), []).append((n, 2 + 2 * piece, rest % group))
        if (lane + block - 1) // 128 > lane // 128:
            rows_of.setdefault((tap, lane // 128 + 1), []).append((n, 3 + 2 * piece, rest % group))
    for (tap, tile), pieces in rows_of.items():
        value = jnp.zeros((1, 128), F32)
        for t2 in range(group):
            value = value + jnp.where(t == t2, sum(small_all[n, r : r + 1, :] for n, r, p in pieces if p == t2), 0.0)
        taps[tap : tap + 1, tile * 128 : (tile + 1) * 128] = value

    pump(2)
    for q in range(group):
        spread_wait(tok_all, 0, q)
        fetch(tok_all.at[q], act.at[span(q)], 0)

        def normed_rows(i, carry, q=q):
            here = pl.ds(pl.multiple_of(q * seg + i * ROW_TILE, ROW_TILE), ROW_TILE)
            row = act[here, :].astype(F32)
            s1 = lax.rsqrt(jnp.mean(row * row, axis=-1, keepdims=True) + EPS_NORM)
            act[here, :] = (row * s1 * gains[0:1, :]).astype(BF)
            return carry

        lax.fori_loop(0, seg // ROW_TILE, normed_rows, 0, unroll=2)
    own_start(4)
    spread(bck_own, bck_all, 1, "start")
    own_start(5)
    keep_normed = pltpu.make_async_copy(act, nrm_far, lsem.at[2])
    keep_normed.start()
    for time in range(3, out_n):
        pump(time)
    gather_wait(0)
    fetch(wi_all, wi, 0)
    keep_normed.wait()

    for q in range(group):
        for k in range(blocks):
            acc_y[span(q), pl.ds(k * 384, 384)] = dot(
                act[span(q), :], wi[:, :, :, pl.ds(k * 384, 384)].reshape(D, 384)
            )
        for k in range(blocks):
            col = pl.ds(k * 128, 128)
            prod[pl.ds(q * seg + 8, seg), col] = acc_y[span(q), lanes(k, 0)] * acc_y[span(q), lanes(k, 2)]
            gated[span(q), col] = (acc_y[span(q), lanes(k, 1)] * convolved(q, col)).astype(BF)
    spread_on(bck_all, 1)
    pump(out_n)
    gather_wait(1)
    fetch(wo_all, wo, 0)

    def branch(q):
        for n in range(4):
            col = pl.ds(n * 384, 384)
            stage[q, :, col] = dot(gated[any_span(q), :], wo[:, :, :, col].reshape(ch, 384)).astype(BF)

    scatter(staged, rs_br, 0, branch)
    scatter_on(staged, rs_br, 0)
    spill = pltpu.make_async_copy(acc_y.at[:, pl.ds(0, 3 * ch)], mixed_far, lsem.at[2])
    spill.start()
    own_start(6)
    pump(out_n + 1)
    for q in range(group):
        spread_wait(bck_all, 1, q)
        fetch(bck_all.at[q], bck.at[span(q)], 0)
        bck_t[:, span(q)] = bck[span(q), :].T

    pump(out_n + 2)
    scatter_wait(rs_br, 0)
    scatter_end(staged, rs_br, 0)
    fetch(rs_br, stage.at[pl.ds(0, 3)], 0)

    def arrived(here):
        total = stage[0, here, :].astype(F32)
        for q in range(1, 3):
            total = total + stage[q, here, :].astype(F32)
        return total

    def middle_rows(i, carry):
        here = rows16(i)
        mi = tok[here, :].astype(F32) + arrived(here)
        mid[here, :] = mi
        s2 = lax.rsqrt(jnp.mean(mi * mi, axis=-1, keepdims=True) + EPS_NORM)
        low[here, :] = (mi * s2 * gains[1:2, :]).astype(BF)
        return carry

    lax.fori_loop(0, seg // ROW_TILE, middle_rows, 0)
    spread(low, n2_all, 2, "start")
    own_start(*range(items))
    pump(out_n + 3)
    spread_on(n2_all, 2)
    pump(out_n + 4)
    gather_wait(2)
    pltpu.make_async_copy(wf_all.at[0], ws.at[0], wsem.at[0]).start()
    spill.wait()

    def clear(i, carry):
        here = rows16(i)
        acc_y[here, :] = jnp.zeros((ROW_TILE, D), F32)
        acc_n[here, :] = jnp.zeros((ROW_TILE, D), F32)
        return carry

    lax.fori_loop(0, seq // ROW_TILE, clear, 0)
    for q in range(group):
        spread_wait(n2_all, 2, q)
        fetch(n2_all.at[q], act.at[span(q)], 0)
        act_t[:, span(q)] = act[span(q), :].T

    def chunk_refs(kind, c):
        if kind == "f":
            return lax.rem(c, 2), c, sib_f.at[c], pl.ds(0, WIDTH)
        n = chunks + c
        return n % 2, n, sib_i.at[c], pl.ds(0, 128)

    def pair_send(kind, c, op):
        s, n, sib, cols = chunk_refs(kind, c)
        copy = remote(grad.at[s, :, :, 1 - b, :, cols], sib, gs_ssem.at[n], gs_rsem.at[n], mate)
        if op == "start":
            copy.start()
        else:
            copy.wait_send()

    steps = out_n.bit_length() - 1

    def halves_refs(kind, c):
        return (come_f if kind == "f" else come_i).at[c], (far_f if kind == "f" else far_i).at[c]

    def flipped(k):
        m = 1 << k
        return o + m - 2 * m * lax.rem(o // m, 2)

    def kept(device, k, i):
        return lax.rem(device, 2 << k) + (2 << k) * i

    def step_at(k):
        return out_n - (out_n >> k), out_n >> (k + 1)

    def step_send(kind, c, k, op="start"):
        _, n, _, _ = chunk_refs(kind, c)
        come, mine_far = halves_refs(kind, c)
        at, number = step_at(k)
        there = flipped(k)
        for i in range(number):
            copy = remote(
                mine_far.at[:, kept(there, k, i)], come.at[:, at + i],
                gz_ssem.at[n, at + i], come_sem.at[n, at + i], (2 * there + a, g),
            )
            if op == "start":
                copy.start()
            else:
                copy.wait_send()

    def pair_fetch(kind, c, op):
        s, n, sib, cols = chunk_refs(kind, c)
        if op == "start":
            await_bytes(sib, gs_rsem.at[n])
        copy = pltpu.make_async_copy(sib, sibv.at[:, :, :, cols], lsem.at[1])
        copy.start() if op == "start" else copy.wait()

    def pair_far(kind, c):
        s, n, _, cols = chunk_refs(kind, c)
        return pltpu.make_async_copy(part.at[s, :, :, :, cols], halves_refs(kind, c)[1], far_sem.at[s])

    def pair_add(kind, c):
        s, n, _, cols = chunk_refs(kind, c)
        pair_fetch(kind, c, "end")

        def one(i, carry):
            j, o2 = i // out_n, lax.rem(i, out_n)
            part[s, j, o2, :, cols] = (
                grad[s, j, o2, b, :, cols].astype(F32) + sibv[j, o2, :, cols].astype(F32)
            ).astype(BF)
            return carry

        lax.fori_loop(0, 3 * out_n, one, 0)
        pair_far(kind, c).start()

    def first_send(kind, c):
        pair_far(kind, c).wait()
        step_send(kind, c, 0)

    def stage_ask(job, buf, op):
        kind, c, k = job
        _, n, _, cols = chunk_refs(kind, c)
        come, mine_far = halves_refs(kind, c)
        at, number = step_at(k)
        for i in range(number):
            if op == "start":
                await_bytes(come.at[:, at + i], come_sem.at[n, at + i])
            for m, src in ((i, come.at[:, at + i]), (number + i, mine_far.at[:, kept(o, k, i)])):
                copy = pltpu.make_async_copy(src, part.at[buf, :, m, :, cols], buf_sem.at[buf, m])
                copy.start() if op == "start" else copy.wait()

    def stage_back(job, buf, op):
        kind, c, k = job
        _, n, _, cols = chunk_refs(kind, c)
        mine_far = halves_refs(kind, c)[1]
        at, number = step_at(k)
        for i in range(number):
            m = number + i
            copy = pltpu.make_async_copy(
                part.at[buf, :, m, :, cols], mine_far.at[:, kept(o, k, i)], buf_sem.at[buf, m]
            )
            copy.start() if op == "start" else copy.wait()

    def stage_add(job, buf):
        kind, c, k = job
        _, n, _, cols = chunk_refs(kind, c)
        h, _, place_o, place_p = out_slot(n)
        at, number = step_at(k)

        def add(i, carry):
            j, r = i // (rows_n // 48), lax.rem(i, rows_n // 48)
            here = pl.ds(pl.multiple_of(r * 48, 16), 48)
            for m in range(number):
                value = (
                    part[buf, j, m, here, cols].astype(F32) + part[buf, j, number + m, here, cols].astype(F32)
                ).astype(BF)
                if k == steps - 1:
                    ws[h, j, place_o, place_p, here, cols] = value
                else:
                    part[buf, j, number + m, here, cols] = value
            return carry

        lax.fori_loop(0, 3 * (rows_n // 48), add, 0)
        if k == steps - 1:
            hand_back(kind, c, "start")
        else:
            stage_back(job, buf, "start")

    def stage_on(job, buf):
        kind, c, k = job
        if k < steps - 1:
            stage_back(job, buf, "end")
            step_send(kind, c, k + 1)

    def sums_of(jobs):
        for i, job in enumerate(jobs):
            if i == 0:
                stage_ask(job, 0, "start")
            if i >= 1:
                stage_on(jobs[i - 1], (i - 1) % 2)
            if i + 1 < len(jobs):
                stage_ask(jobs[i + 1], (i + 1) % 2, "start")
            stage_ask(job, i % 2, "end")
            stage_add(job, i % 2)
        stage_on(jobs[-1], (len(jobs) - 1) % 2)

    def out_slot(n):
        return (n // (2 * out_n), slice(None), lax.rem(n, 2 * out_n) // 2, lax.rem(n, 2))

    def hand_back(kind, c, op):
        _, n, _, cols = chunk_refs(kind, c)
        dst = (g_ff if kind == "f" else g_wi)
        if not direct:
            if op == "start":
                h, _, o2, p = out_slot(n)
                fetch(ws.at[h, :, o2, p, :, cols], dst.at[c], 1)
            return
        h, _, o2, p = out_slot(n)
        for q in range(group):
            src = ws.at[h, :, o2, p, pl.ds(q * block, block), cols]
            switch(
                (a == b) & (q == g),
                pltpu.make_async_copy(src, dst.at[t, c], back_rsem.at[n, t]),
                remote(src, dst.at[t, c], back_ssem.at[n, q], back_rsem.at[n, t], (2 * o + b, q)),
                op,
            )

    def hand_wait(kind, c):
        if direct:
            _, n, _, _ = chunk_refs(kind, c)
            for t2 in range(group):
                await_bytes((g_ff if kind == "f" else g_wi).at[t2, c], back_rsem.at[n, t2])

    half = out_n // 2

    def grad_rows(h):
        return pl.ds(pl.multiple_of(h * (D // 2), D // 2), D // 2), pl.ds(h * half, half)

    loop_pump = out_n + 5

    def hidden_chunk(c, carry):
        s = lax.rem(c, 2)
        await_bytes(ws.at[s], wsem.at[s])
        hid, dgt, dup = (pl.ds(j * WIDTH, WIDTH) for j in range(3))

        def token_tile(m, carry):
            here = pl.ds(pl.multiple_of(m * (seq // 2), seq // 2), seq // 2)
            n2 = act[here, :]
            gate = dot(n2, ws[s, 0].reshape(D, WIDTH))
            upper = dot(n2, ws[s, 1].reshape(D, WIDTH))
            d_hidden = dot(bck[here, :], ws[s, 2].reshape(D, WIDTH))
            sigma = jax.nn.sigmoid(gate)
            active = gate * sigma
            dmix[here, hid] = (active * upper).astype(BF)
            dmix[here, dgt] = (d_hidden * upper * (sigma * (1.0 + gate * (1.0 - sigma)))).astype(BF)
            dmix[here, dup] = (d_hidden * active).astype(BF)
            acc_y[here, :] += dot_t(dmix[here, hid], ws[s, 2].reshape(D, WIDTH))
            acc_n[here, :] += dot_t(dmix[here, dgt], ws[s, 0].reshape(D, WIDTH))
            acc_n[here, :] += dot_t(dmix[here, dup], ws[s, 1].reshape(D, WIDTH))
            return carry

        lax.fori_loop(0, 2, token_tile, 0)

        @pl.when(c >= 1)
        def _():
            pair_fetch("f", c - 1, "start")

        @pl.when(c >= 2)
        def _():
            first_send("f", c - 2)

        @pl.when(c >= 2)
        def _():
            pair_send("f", c - 2, "end")

        def grad_tile(h, carry):
            rows, os = grad_rows(h)
            shape = (half, 2, rows_n, WIDTH)
            grad[s, 0, os] = dot(act_t[rows, :], dmix[:, dgt]).astype(BF).reshape(shape)
            grad[s, 1, os] = dot(act_t[rows, :], dmix[:, dup]).astype(BF).reshape(shape)
            grad[s, 2, os] = dot(bck_t[rows, :], dmix[:, hid]).astype(BF).reshape(shape)
            return carry

        lax.fori_loop(0, 2, grad_tile, 0)
        pair_send("f", c, "start")

        @pl.when(c >= 1)
        def _():
            pair_add("f", c - 1)

        pump(c + loop_pump)

        @pl.when(c + 1 < chunks)
        def _():
            gather_wait(c + 3)
            pltpu.make_async_copy(wf_all.at[c + 1], ws.at[1 - s], wsem.at[1 - s]).start()

        return carry

    lax.fori_loop(0, chunks, hidden_chunk, 0)

    def d_normed_two(q):
        stage[q] = acc_n[any_span(q), :].astype(BF)

    scatter(staged, rs_n2, 1, d_normed_two)
    first_send("f", chunks - 2)
    pair_fetch("f", chunks - 1, "start")
    pair_add("f", chunks - 1)
    scatter_on(staged, rs_n2, 1)
    first_send("f", chunks - 1)
    for k in range(steps - 1):
        sums_of([("f", c, k) for c in range(chunks - 2)])
    scatter_wait(rs_n2, 1)
    scatter_end(staged, rs_n2, 1)
    spread(low, n2_all, 2, "end")
    fetch(rs_n2, stage.at[pl.ds(0, 3)], 0)
    fetch(bck_own, act.at[span(0)], 0)
    g_gains[...] = jnp.zeros_like(g_gains)

    def d_middle_rows(i, carry):
        here = rows16(i)
        dn = arrived(here)
        mi = mid[here, :]
        s2 = lax.rsqrt(jnp.mean(mi * mi, axis=-1, keepdims=True) + EPS_NORM)
        e2 = gains[1:2, :] * dn
        back = act[here, :].astype(F32)
        dm = back + s2 * e2 - mi * (s2 * s2 * s2) * jnp.mean(e2 * mi, axis=-1, keepdims=True)
        dmid[here, :] = dm
        low[here, :] = dm.astype(BF)
        g_gains[1] += jnp.sum((dn * mi * s2).reshape(ROW_TILE // 8, 8, D), axis=0)
        return carry

    lax.fori_loop(0, seg // ROW_TILE, d_middle_rows, 0)
    spread(low, dbr_all, 3, "start")

    for q in range(group):
        stage[q] = acc_y[span(q), :].astype(BF)
    spill_back = pltpu.make_async_copy(mixed_far, acc_y.at[:, pl.ds(0, 3 * ch)], lsem.at[2])
    spill_back.start()

    for q in range(group):
        bck_t[pl.ds(0, ch), span(q)] = gated[span(q), :].T
        fetch(nrm_far.at[span(q)], act.at[span(q)], 0)
        act_t[:, span(q)] = act[span(q), :].T
    spill_back.wait()
    spread_on(dbr_all, 3)
    for k in range(steps - 1):
        sums_of([("f", c, k) for c in range(chunks - 2, chunks)])
    sums_of([("f", c, steps - 1) for c in range(chunks - 3)])

    acc_n[pl.ds(seq, 8), pl.ds(0, ch)] = jnp.zeros((8, ch), F32)
    for q in range(group):
        spread_wait(dbr_all, 3, q)
        fetch(dbr_all.at[q], bck.at[span(q)], 0)
        acc_n[span(q), pl.ds(ch, ch)] = dot_t(bck[span(q), :], wo[...].reshape(ch, D))
        for k in range(blocks):
            col = pl.ds(k * 128, 128)
            d_gated = acc_n[span(q), pl.ds(ch + k * 128, 128)]
            acc_n[span(q), col] = d_gated * acc_y[span(q), lanes(k, 1)]
            dmix[span(q), lanes(k, 1)] = (d_gated * convolved(q, col)).astype(BF)
    scatter(staged, rs_y, 2, lambda q: None)
    g_taps[...] = jnp.zeros_like(g_taps)
    for q in range(group):
        for k in range(blocks):
            col = pl.ds(k * 128, 128)
            d0 = acc_n[span(q), col]
            for n in range(3):
                g_taps[n, :, col] += jnp.sum(
                    (d0 * prod[pl.ds(q * seg + 6 + n, seg), col]).reshape(seg // 8, 8, 128), axis=0
                )
            d_product = (
                taps[2:3, col] * d0
                + taps[1:2, col] * acc_n[pl.ds(q * seg + 1, seg), col]
                + taps[0:1, col] * acc_n[pl.ds(q * seg + 2, seg), col]
            )
            dmix[span(q), lanes(k, 0)] = (d_product * acc_y[span(q), lanes(k, 2)]).astype(BF)
            dmix[span(q), lanes(k, 2)] = (d_product * acc_y[span(q), lanes(k, 0)]).astype(BF)

    for k in range(blocks):
        s = (chunks + k) % 2
        if k < 2:
            pair_send("f", chunks - 2 + k, "end")
        else:
            pair_send("i", k - 2, "end")

        def intake_tile(h, carry, k=k, s=s):
            rows, os = grad_rows(h)
            value = dot(act_t[rows, :], dmix[:, pl.ds(k * 384, 384)]).astype(BF)
            for j in range(3):
                grad[s, j, os, :, :, pl.ds(0, 128)] = value[:, j * 128 : (j + 1) * 128].reshape(
                    half, 2, rows_n, 128
                )
            return carry

        lax.fori_loop(0, 2, intake_tile, 0)
        pair_send("i", k, "start")
        if k >= 1:
            pair_fetch("i", k - 1, "start")
            if k >= 2:
                first_send("i", k - 2)
            pair_add("i", k - 1)

    for n in range(4):
        col = pl.ds(n * 384, 384)
        wo[:, :, :, col] = dot(bck_t[pl.ds(0, ch), :], bck[:, col]).astype(BF).reshape(out_n, 2, cblk, 384)
    last = chunks + blocks
    pair_o = remote(wo.at[:, 1 - b], sib_o, gs_ssem.at[last], gs_rsem.at[last], mate)
    pair_o.start()
    if blocks >= 2:
        first_send("i", blocks - 2)
    pair_fetch("i", blocks - 1, "start")
    pair_add("i", blocks - 1)
    first_send("i", blocks - 1)

    await_bytes(sib_o, gs_rsem.at[last])
    fetch(sib_o, sibo, 1)

    def add_o(o2, carry):
        parto[o2] = (wo[o2, b].astype(F32) + sibo[o2].astype(F32)).astype(BF)
        return carry

    lax.fori_loop(0, out_n, add_o, 0)

    def part_o(op):
        def one(k, carry):
            o2, dev = peer(k)
            copy = remote(parto.at[o2], z_o.at[o], gz_ssem.at[last, k], come_sem.at[last, o], dev)
            if op == "start":
                copy.start()
            else:
                copy.wait_send()
            return carry

        lax.fori_loop(1, out_n, one, 0)
        keep = pltpu.make_async_copy(parto.at[o], z_o.at[o], osem.at[0])
        if op == "start":
            keep.start()
        else:
            keep.wait()

    part_o("start")

    def lent(q):
        return bck.at[any_span(q)]

    def d_normed(q):
        for n in range(4):
            bck[any_span(q), pl.ds(n * 384, 384)] = dot_t(
                dmix[any_span(q), :], wi[pl.ds(n * out_n // 4, out_n // 4)].reshape(384, 3 * ch)
            ).astype(BF)

    scatter(lent, rs_n1, 3, d_normed)
    scatter_on(staged, rs_y, 2)
    scatter_on(lent, rs_n1, 3)
    scatter_wait(rs_y, 2)
    scatter_end(staged, rs_y, 2)
    spread(low, dbr_all, 3, "end")
    for q in range(3):
        fetch(rs_y.at[q], act.at[span(q)], 0)

    def out_rows(i, carry):
        here = rows16(i)
        value = act[here, :].astype(F32)
        for q in range(1, 3):
            value = value + act[pl.ds(pl.multiple_of(q * seg + i * ROW_TILE, ROW_TILE), ROW_TILE), :].astype(F32)
        low[here, :] = (mid[here, :] + value).astype(BF)
        return carry

    lax.fori_loop(0, seg // ROW_TILE, out_rows, 0)
    fetch(low, block_out, 0)

    sums_of([("f", c, steps - 1) for c in range(chunks - 3, chunks)])
    scatter_wait(rs_n1, 3)
    scatter_end(lent, rs_n1, 3)
    fetch(rs_n1, stage.at[pl.ds(0, 3)], 0)

    def d_rows(i, carry):
        here = rows16(i)
        dn = arrived(here)
        row = tok[here, :].astype(F32)
        s1 = lax.rsqrt(jnp.mean(row * row, axis=-1, keepdims=True) + EPS_NORM)
        e1 = gains[0:1, :] * dn
        low[here, :] = (
            dmid[here, :] + s1 * e1 - row * (s1 * s1 * s1) * jnp.mean(e1 * row, axis=-1, keepdims=True)
        ).astype(BF)
        g_gains[0] += jnp.sum((dn * row * s1).reshape(ROW_TILE // 8, 8, D), axis=0)
        return carry

    lax.fori_loop(0, seg // ROW_TILE, d_rows, 0)
    fetch(low, input_grad, 0)

    sm_mine[...] = jnp.zeros_like(sm_mine)
    for i in range(2):
        value = jnp.sum(g_gains[i], axis=0, keepdims=True)
        for j in range(D // 128):
            row = i * (D // 128) + j
            sm_mine[row : row + 1, :] = value[:, j * 128 : (j + 1) * 128]
    for n in range(3):
        value = jnp.sum(g_taps[n], axis=0, keepdims=True)
        for k in range(blocks):
            for t2 in range(group):
                row = 2 * (D // 128) + (t2 * 3 + n) * blocks + k
                sm_mine[row : row + 1, :] = jnp.where(t == t2, value[:, k * 128 : (k + 1) * 128], 0.0)
    sm_plane[place] = sm_mine[...]
    plane(sm_mine, sm_plane.at[place], ta_ssem, ta_rsem, "start")

    for k in range(max(0, blocks - 2), blocks):
        pair_send("i", k, "end")

    for k in range(steps - 1):
        sums_of([("i", c, k) for c in range(blocks)])
    plane_wait(sm_mine, ta_rsem)
    value = sm_plane[0]
    for i in range(1, 2 * group):
        value = value + sm_plane[i]
    sm_sum[...] = value
    sm_z[o] = value
    far(sm_sum, sm_z.at[o], tz_ssem, tz_rsem, "start")
    sums_of([("i", c, steps - 1) for c in range(blocks)])
    part_o("end")
    pair_o.wait_send()

    def last_one(k, carry):
        await_bytes(z_o.at[o], come_sem.at[last, peer(k)[0]])
        return carry

    lax.fori_loop(1, out_n, last_one, 0)
    fetch(z_o, sibo, 1)
    value = sibo[0].astype(F32)
    for o2 in range(1, out_n):
        value = value + sibo[o2].astype(F32)
    outo = parto.at[0]
    outo[...] = value.astype(BF)

    def back_o(op):
        switch(
            a == b,
            pltpu.make_async_copy(outo, g_wo, back_rsem.at[last, 0]),
            remote(outo, g_wo, back_ssem.at[last, 0], back_rsem.at[last, 0], (2 * o + b, 2 * y + a)),
            op,
        )

    back_o("start")
    far_wait(sm_sum, tz_rsem)
    value = sm_z[0]
    for i in range(1, out_n):
        value = value + sm_z[i]
    g_small[...] = value

    plane(small_own, small_all.at[mine], sa_ssem, sa_rsem, "end")
    far(planes, planes, sz_ssem, sz_rsem, "end")
    plane(sm_mine, sm_plane.at[place], ta_ssem, ta_rsem, "end")
    far(sm_sum, sm_z.at[o], tz_ssem, tz_rsem, "end")
    spread(tok, tok_all, 0, "end")
    spread(bck_own, bck_all, 1, "end")
    gather_close(0)
    gather_close(1)

    def close(c, carry):
        gather_close(c + 2)
        for k in range(steps):
            step_send("f", c, k, "end")
        hand_back("f", c, "end")
        hand_wait("f", c)
        return carry

    lax.fori_loop(0, chunks, close, 0)
    for k in range(blocks):
        for step in range(steps):
            step_send("i", k, step, "end")
        hand_back("i", k, "end")
        hand_wait("i", k)
    back_o("end")
    await_bytes(g_wo, back_rsem.at[last, 0])


def forward_backward(sizes, tok, bck, wi_own, wo_own, ff_own, small_own):
    (out_n, group, rows_n, seg, ch, cblk, chunks) = sizes
    blocks = ch // 128
    seq = group * seg
    block = rows_n // group
    places = 2 * group
    small_rows = -(-(2 * D // 128 + group * 3 * blocks) // 8) * 8
    items = 2 + chunks
    sums = chunks + blocks + 1
    vm = pltpu.VMEM
    dma = pltpu.SemaphoreType.DMA

    def shape(*dims, dtype=BF):
        return jax.ShapeDtypeStruct(dims, dtype)

    any_spec = pl.BlockSpec(memory_space=pl.ANY)
    vmem_spec = pl.BlockSpec(memory_space=pltpu.VMEM)
    if block % 16 == 0:
        given = [shape(group, chunks, 3, block, WIDTH), shape(group, blocks, 3, block, 128)]
    else:
        given = [shape(chunks, 3, rows_n, WIDTH), shape(blocks, 3, rows_n, 128)]
    outs = [
        shape(seg, D), shape(seg, D), *given, shape(cblk, D), shape(small_rows, 128, dtype=F32),
        shape(chunks, 3, out_n, 2, rows_n, WIDTH), shape(out_n, 2, rows_n, 3 * ch), shape(out_n, 2, cblk, D),
        shape(group, seg, D), shape(seq, D), shape(group, seg, D), shape(group, seg, D), shape(group, seg, D),
        shape(3, seg, D), shape(3, seg, D), shape(3, seg, D), shape(3, seg, D), shape(4, 2, seg // 2, D),
        shape(chunks, 3, out_n, rows_n, WIDTH), shape(blocks, 3, out_n, rows_n, 128), shape(out_n, cblk, D),
        *[shape(chunks, 3, out_n, rows_n, WIDTH), shape(blocks, 3, out_n, rows_n, 128)] * 2, shape(out_n, cblk, D),
        shape(seq, 3 * ch, dtype=F32),
    ]
    out_specs = [any_spec] * 5 + [vmem_spec] + [any_spec] * (len(outs) - 6)
    scratch = [
        vm((2, 3, out_n, 2, rows_n, WIDTH), BF),
        vm((out_n, 2, rows_n, 3 * ch), BF),
        vm((out_n, 2, cblk, D), BF),
        vm((seq, D), BF), vm((D, seq), BF), vm((seq, D), BF), vm((D, seq), BF),
        vm((seq, D), F32), vm((seq + 8, D), F32),
        vm((2, 3, out_n, 2, rows_n, WIDTH), BF),
        vm((3, out_n, rows_n, WIDTH), BF),
        vm((2, 3, out_n, rows_n, WIDTH), BF),
        vm((group, seg, D), BF),
        vm((seq + 8, ch), F32), vm((seq, ch), BF), vm((seq, 3 * ch), BF),
        vm((seg, D), F32), vm((seg, D), F32), vm((seg, D), BF),
        vm((out_n, cblk, D), BF), vm((out_n, cblk, D), BF),
        vm((places * out_n, 8, 128), F32), vm((2, D), F32), vm((3, ch), F32),
        vm((2, 8, D), F32), vm((3, 8, ch), F32),
        vm((small_rows, 128), F32), vm((places, small_rows, 128), F32),
        vm((small_rows, 128), F32), vm((out_n, small_rows, 128), F32),
        vm((seg // 2, D), BF),
        dma((4, 3, 2)), dma((4, group, 2)), dma((4, 2)), dma((4, 4, 2)), dma((4, 3, 2)), dma((4, 2, 2)), dma((4, 2)),
        dma((items, 2, out_n)), dma((items, out_n)), dma((items,)), dma((items,)),
        dma((sums,)), dma((sums,)), dma((sums, out_n)), dma((sums, out_n)), dma((2,)), dma((2, out_n)),
        dma((items, group)), dma((items, group)), dma((sums, group)), dma((sums, group)), dma((1,)),
        dma((places,)), dma((places,)), dma((out_n,)), dma((out_n,)),
        dma((places,)), dma((places,)), dma((out_n,)), dma((out_n,)), dma((2,)), dma((5,)),
    ]
    results = pl.pallas_call(
        functools.partial(block_kernel, sizes),
        out_shape=outs,
        in_specs=[vmem_spec] + [any_spec] * 4 + [vmem_spec],
        out_specs=out_specs,
        scratch_shapes=scratch,
        compiler_params=pltpu.CompilerParams(
            collective_id=0, has_side_effects=True, vmem_limit_bytes=63 * 1024 * 1024
        ),
        cost_estimate=pl.CostEstimate(
            flops=6 * seq * D * (4 * ch + 3 * chunks * WIDTH),
            bytes_accessed=200_000_000,
            transcendentals=seq * chunks * WIDTH,
        ),
    )(tok, bck, wi_own, wo_own, ff_own, small_own)
    return results[:6]


def body(
    tokens,
    cotangent,
    lengths,
    intake_weight,
    intake_first,
    intake_second,
    output_weight,
    output_first,
    output_second,
    swiglu_weight,
    swiglu_first,
    swiglu_second,
    down_weight,
    down_first,
    down_second,
    norm_gains,
    gains_first,
    gains_second,
    conv_kernel,
    kernel_first,
    kernel_second,
):
    data_count = lax.axis_size("dp")
    group_count = lax.axis_size("group")
    dp = lax.axis_index("dp")
    member = lax.axis_index("group")
    block = D // (data_count * group_count)
    cblk = -(-block // 16) * 16
    ch = data_count * cblk
    blocks = ch // 128
    hidden_part = FF // group_count
    chunks = -(-hidden_part // WIDTH)
    hidden_full = chunks * WIDTH
    rows_n = D // data_count
    swap = []
    for one in range(data_count):
        for two in range(group_count):
            there = (2 * (one // 2) + two % 2) * group_count + 2 * (two // 2) + one % 2
            swap.append((one * group_count + two, there))

    def cross(value):
        return lax.ppermute(value, ("dp", "group"), swap)

    intake_local = (
        intake_weight.astype(BF)
        .reshape(block, 3, data_count, group_count, block)
        .transpose(3, 0, 1, 2, 4)
    )
    intake_local = jnp.pad(intake_local, ((0, 0),) * 4 + ((0, cblk - block),))
    intake_local = (
        intake_local.reshape(group_count, block, 3, blocks, 128)
        .transpose(0, 1, 3, 2, 4)
        .reshape(group_count, block, 3 * ch)
    )
    ff_local = jnp.concatenate(
        [
            swiglu_weight.astype(BF).reshape(block, 2, group_count, hidden_part),
            down_weight.astype(BF).reshape(block, 1, group_count, hidden_part),
        ],
        axis=1,
    )
    ff_local = jnp.pad(ff_local, ((0, 0),) * 3 + ((0, hidden_full - hidden_part),))
    ff_local = ff_local.reshape(block, 3, group_count, chunks, WIDTH).transpose(2, 3, 1, 0, 4)
    wo_own = jnp.pad(output_weight.astype(BF).reshape(block, D), ((0, cblk - block), (0, 0)))
    if block % 16 == 0:
        wi_own, ff_own = intake_local, ff_local
    else:
        wi_own = lax.all_to_all(intake_local, "group", split_axis=0, concat_axis=0, tiled=True)
        wi_own = cross(wi_own.reshape(rows_n, 3 * ch))
        ff_own = lax.all_to_all(ff_local, "group", split_axis=0, concat_axis=0, tiled=True)
        ff_own = cross(ff_own.transpose(1, 2, 0, 3, 4).reshape(chunks, 3, rows_n, WIDTH))

    number = dp * group_count + member
    share = norm_gains.shape[0]

    def placed(values, lane):
        line = lax.dynamic_update_slice(jnp.zeros((256,), F32), lax.reduce_precision(values, 8, 7), (lane,))
        return line.reshape(2, 128)

    runs = [placed(norm_gains, lax.rem(number * share, 128))]
    for piece in range(3):
        rest = lax.rem(3 * number + piece, data_count * group_count)
        lane = lax.rem(rest // group_count * cblk, 128)
        runs.append(placed(conv_kernel[piece * block : (piece + 1) * block], lane))
    small_own = jnp.concatenate(runs)

    seg_len = tokens.shape[1]
    positions = member * seg_len + lax.iota(jnp.int32, seg_len)
    valid = (positions < lengths[0]).astype(F32)[:, None]
    back_low = (cotangent[0].astype(F32) * valid).astype(BF)

    sizes = (data_count // 2, group_count, rows_n, seg_len, ch, cblk, chunks)
    block_out, input_grad, g_ff, g_wi, g_wo, g_small = forward_backward(
        sizes, tokens[0], back_low, wi_own, wo_own, ff_own, small_own
    )

    if block % 16:
        g_wi = cross(g_wi).reshape(blocks, 3, group_count, block, 128).transpose(2, 0, 1, 3, 4)
        g_wi = lax.all_to_all(g_wi, "group", split_axis=0, concat_axis=0, tiled=True)
        g_ff = cross(g_ff).reshape(chunks, 3, group_count, block, WIDTH).transpose(2, 0, 1, 3, 4)
        g_ff = lax.all_to_all(g_ff, "group", split_axis=0, concat_axis=0, tiled=True)
    g_wi = g_wi.transpose(0, 3, 2, 1, 4).reshape(group_count, block, 3, data_count, cblk)
    intake_grad_flat = g_wi[..., :block].transpose(1, 2, 3, 0, 4).reshape(-1).astype(F32)
    g_ff = g_ff.transpose(3, 2, 0, 1, 4).reshape(block, 3, group_count, hidden_full)
    g_ff = g_ff[..., :hidden_part]
    swiglu_grad_flat = g_ff[:, :2].reshape(-1).astype(F32)
    down_grad_flat = g_ff[:, 2].reshape(-1).astype(F32)
    output_grad_flat = g_wo[:block].reshape(-1).astype(F32)

    gain_rows = 2 * D // 128
    taps_grad = g_small[gain_rows : gain_rows + group_count * 3 * blocks]
    taps_grad = taps_grad.reshape(group_count, 3, data_count, cblk)[..., :block]
    taps_grad = taps_grad.transpose(1, 2, 0, 3).reshape(-1)
    small_shards = (
        lax.dynamic_slice(g_small[:gain_rows].reshape(-1), (number * share,), (share,)),
        lax.dynamic_slice(taps_grad, (number * 3 * block,), (3 * block,)),
    )
    intake_new = update(
        intake_weight, intake_first, intake_second, intake_grad_flat, RATE_MATRIX, DECAY
    )
    output_new = update(
        output_weight, output_first, output_second, output_grad_flat, RATE_MATRIX, DECAY
    )
    swiglu_new = update(
        swiglu_weight, swiglu_first, swiglu_second, swiglu_grad_flat, RATE_MATRIX, DECAY
    )
    down_new = update(down_weight, down_first, down_second, down_grad_flat, RATE_MATRIX, DECAY)
    gains_new = update(norm_gains, gains_first, gains_second, small_shards[0], RATE_VECTOR, 0.0)
    kernel_new = update(
        conv_kernel, kernel_first, kernel_second, small_shards[1], RATE_VECTOR, DECAY
    )
    return (
        block_out[None],
        input_grad[None],
        intake_new[0],
        intake_new[1],
        intake_new[2],
        output_new[0],
        output_new[1],
        output_new[2],
        swiglu_new[0],
        swiglu_new[1],
        swiglu_new[2],
        down_new[0],
        down_new[1],
        down_new[2],
        gains_new[0],
        gains_new[1],
        gains_new[2],
        kernel_new[0],
        kernel_new[1],
        kernel_new[2],
    )


def solution(mesh):
    in_specs = (
        P("dp", "group", None),
        P("dp", "group", None),
        P("dp"),
        P(("dp", "group")),
        P(("dp", "group")),
        P(("dp", "group")),
        P(("dp", "group")),
        P(("dp", "group")),
        P(("dp", "group")),
        P(("dp", "group")),
        P(("dp", "group")),
        P(("dp", "group")),
        P(("dp", "group")),
        P(("dp", "group")),
        P(("dp", "group")),
        P(("dp", "group")),
        P(("dp", "group")),
        P(("dp", "group")),
        P(("dp", "group")),
        P(("dp", "group")),
        P(("dp", "group")),
    )
    out_specs = (
        P("dp", "group", None),
        P("dp", "group", None),
        P(("dp", "group")),
        P(("dp", "group")),
        P(("dp", "group")),
        P(("dp", "group")),
        P(("dp", "group")),
        P(("dp", "group")),
        P(("dp", "group")),
        P(("dp", "group")),
        P(("dp", "group")),
        P(("dp", "group")),
        P(("dp", "group")),
        P(("dp", "group")),
        P(("dp", "group")),
        P(("dp", "group")),
        P(("dp", "group")),
        P(("dp", "group")),
        P(("dp", "group")),
        P(("dp", "group")),
    )
    return jax.shard_map(body, mesh=mesh, in_specs=in_specs, out_specs=out_specs, check_vma=False)
```

```python
import functools

import jax
import jax.numpy as jnp
from jax import lax
from jax.experimental import pallas as pl
from jax.experimental.pallas import tpu as pltpu
from jax.sharding import PartitionSpec as P

D = 1536
FF = 6912
STEP = 5
WIDTH = 256
ROW_TILE = 16

EPS_NORM = 1e-05
BETA_ONE = 0.5
BETA_TWO = 0.5
ADAM_EPS = 1e-08
RATE_MATRIX = 0.02
RATE_VECTOR = 0.2
DECAY = 0.1

MESH = pl.DeviceIdType.MESH
BF = jnp.bfloat16
F32 = jnp.float32


def update(weight, first, second, grad, rate, decay):
    first_new = BETA_ONE * first + (1.0 - BETA_ONE) * grad
    second_new = BETA_TWO * second + (1.0 - BETA_TWO) * grad * grad
    first_hat = first_new / (1.0 - BETA_ONE**STEP)
    second_hat = second_new / (1.0 - BETA_TWO**STEP)
    weight_new = weight - rate * (first_hat / (jnp.sqrt(second_hat) + ADAM_EPS) + decay * weight)
    return (first_new, second_new, weight_new)


def dot(left, right):
    return lax.dot_general(left, right, (((1,), (0,)), ((), ())), preferred_element_type=F32)


def dot_t(left, right):
    return lax.dot_general(left, right, (((1,), (1,)), ((), ())), preferred_element_type=F32)


def await_bytes(ref, sem):
    pltpu.make_async_copy(ref, ref, sem).wait()


def block_kernel(
    sizes,
    tok, bck_own, wi_own, wo_own, ff_own, small_own,
    block_out, input_grad, g_ff, g_wi, g_wo, g_small,
    wf_all, wi_all, wo_all, tok_all, nrm_far, bck_all, n2_all, dbr_all,
    rs_br, rs_y, rs_n2, rs_n1, via,
    sib_f, sib_i, sib_o, come_f, come_i, far_f, far_i, z_o, mixed_far,
    ws, wi, wo, act, act_t, bck, bck_t, acc_y, acc_n, grad, sibv, part, stage,
    prod, gated, dmix, mid, dmid, low, sibo, parto,
    small_all, gains, taps, g_gains, g_taps, sm_mine, sm_plane, sm_sum, sm_z,
    extra, ag_ssem, ag_rsem, ag_fsem, rs_ssem, rs_rsem, via_ssem, via_rsem, z_ssem, z_rsem, f_ssem, f_rsem,
    gs_ssem, gs_rsem, gz_ssem, come_sem, far_sem, buf_sem, own_ssem, own_rsem, back_ssem, back_rsem, osem,
    sa_ssem, sa_rsem, sz_ssem, sz_rsem, ta_ssem, ta_rsem, tz_ssem, tz_rsem, wsem, lsem,
):
    (out_n, group, rows_n, seg, ch, cblk, chunks) = sizes
    block = rows_n // group
    direct = block % 16 == 0
    count = 2 * out_n * group
    blocks = ch // 128
    seq = group * seg
    dp = lax.axis_index("dp")
    g = lax.axis_index("group")
    o, a = dp // 2, lax.rem(dp, 2)
    y, b = g // 2, lax.rem(g, 2)
    t = 2 * y + a
    mate = (dp, g + 1 - 2 * b)

    def peer(k):
        o2 = lax.rem(o + k, out_n)
        return o2, (2 * o2 + a, g)

    barrier = pltpu.get_barrier_semaphore()
    for x2 in range(2):
        for g2 in range(group):
            @pl.when((x2 != a) | (g2 != g))
            def _():
                pl.semaphore_signal(barrier, inc=1, device_id=(2 * o + x2, g2), device_id_type=MESH)

    def greet(k, carry):
        pl.semaphore_signal(barrier, inc=1, device_id=peer(k)[1], device_id_type=MESH)
        return carry

    lax.fori_loop(1, out_n, greet, 0)
    pl.semaphore_wait(barrier, 2 * group - 1 + out_n - 1)

    def remote(src, dst, ssem, rsem, dev):
        return pltpu.make_async_remote_copy(
            src_ref=src, dst_ref=dst, send_sem=ssem, recv_sem=rsem, device_id=dev, device_id_type=MESH
        )

    def switch(alone, local, copy, op):
        if op == "start":
            @pl.when(alone)
            def _():
                local.start()

            @pl.when(jnp.logical_not(alone))
            def _():
                copy.start()
        else:
            @pl.when(jnp.logical_not(alone))
            def _():
                copy.wait_send()

    odd = lax.rem(a + b, 2)
    size = seg // 2
    y_via = odd * y + (1 - odd) * (1 - y)
    h_via = 1 - odd
    partner = (2 * o + odd * a + (1 - odd) * (1 - a), 2 * (odd * (1 - y) + (1 - odd) * y) + b)

    def part_of(h):
        return pl.ds(h * size, size) if isinstance(h, int) else pl.ds(pl.multiple_of(h * size, size), size)

    def spread(src, dst, n, op):
        for d, h in ((1, 0), (2, 1), (1, 1), (2, 0), (0, 0), (0, 1)):
            x2, y2 = (1 - a if d == 1 else a), (1 - y if d == 2 else y)
            one, two = src.at[part_of(h)], dst.at[g, part_of(h)]
            copy = remote(one, two, ag_ssem.at[n, d, h], ag_rsem.at[n, g, h], (2 * o + x2, 2 * y2 + a))
            if d == 0:
                switch(a == b, pltpu.make_async_copy(one, two, ag_rsem.at[n, g, h]), copy, op)
            elif op == "start":
                copy.start()
            else:
                copy.wait_send()
        if op == "end":
            for k in range(2):
                ref = dst.at[2 * y_via + k, part_of(h_via)]
                await_bytes(ref, ag_fsem.at[n, k])

    def spread_on(dst, n):
        for k in range(2):
            q = 2 * y_via + k
            ref = dst.at[q, part_of(h_via)]
            await_bytes(ref, ag_rsem.at[n, q, h_via])
            remote(ref, ref, ag_fsem.at[n, k], ag_rsem.at[n, q, h_via], partner).start()

    def spread_wait(dst, n, q):
        for h in range(2):
            @pl.when((q // 2 != y_via) | (h != h_via))
            def _():
                await_bytes(dst.at[q, part_of(h)], ag_rsem.at[n, q, h])

    def give(terms, dst, n, at, q, h, slot, op="start"):
        one, two = terms(q).at[part_of(h)], dst.at[slot, part_of(h)]
        copy = remote(one, two, rs_ssem.at[n, at, h], rs_rsem.at[n, slot, h], (2 * o + b, q))
        if slot == 0:
            switch(q == g, pltpu.make_async_copy(one, two, rs_rsem.at[n, 0, h]), copy, op)
        elif op == "start":
            copy.start()
        else:
            copy.wait_send()

    def give_half(terms, n, k, h, op):
        q = 2 * (1 - y) + k
        dev = (2 * o + 1 - a, g) if h == 0 else (dp, 2 * (1 - y) + b)
        copy = remote(terms(q).at[part_of(h)], via.at[n, k], via_ssem.at[n, k, h], via_rsem.at[n, k], dev)
        if op == "start":
            copy.start()
        else:
            copy.wait_send()

    def scatter(terms, dst, n, produce):
        for k in range(2):
            q = 2 * (1 - y) + k
            produce(q)

            @pl.when(odd == 1)
            def _():
                give_half(terms, n, k, 0, "start")
                give_half(terms, n, k, 1, "start")

            @pl.when(odd == 0)
            def _():
                give(terms, dst, n, k, q, 1, 1)

        for k in range(2):
            q = 2 * y + k
            produce(q)

            @pl.when(odd == 1)
            def _():
                give(terms, dst, n, 2 + k, q, 0, 2)

            @pl.when(odd == 0)
            def _():
                give(terms, dst, n, 2 + k, q, 0, 0)
                give(terms, dst, n, 2 + k, q, 1, 0)

    def scatter_on(terms, dst, n):
        for k in range(2):
            q = 2 * y_via + k
            await_bytes(via.at[n, k], via_rsem.at[n, k])
            fetch(via.at[n, k], extra, 0)

            def add_rows(i, carry):
                here = pl.ds(pl.multiple_of(odd * size + i * ROW_TILE, ROW_TILE), ROW_TILE)
                ref = terms(q)
                ref[here, :] = (ref[here, :].astype(F32) + extra[rows16(i), :].astype(F32)).astype(BF)
                return carry

            lax.fori_loop(0, size // ROW_TILE, add_rows, 0)

            @pl.when(odd == 1)
            def _():
                give(terms, dst, n, 2 + k, q, 1, 2)

            @pl.when(odd == 0)
            def _():
                give(terms, dst, n, k, q, 0, 1)

    def scatter_end(terms, dst, n):
        @pl.when(odd == 1)
        def _():
            for k in range(2):
                for h in range(2):
                    give_half(terms, n, k, h, "end")
                    give(terms, dst, n, 2 + k, 2 * y + k, h, 2, "end")

        @pl.when(odd == 0)
        def _():
            for k in range(2):
                for h in range(2):
                    give(terms, dst, n, k, 2 * (1 - y) + k, h, 1, "end")
                    give(terms, dst, n, 2 + k, 2 * y + k, h, 0, "end")

    def scatter_wait(dst, n):
        for slot in range(3):
            for h in range(2):
                await_bytes(dst.at[slot, part_of(h)], rs_rsem.at[n, slot, h])

    arrivals = (2 * y, 2 * y + 1, 2 * (1 - y), 2 * (1 - y) + 1)

    def staged(q):
        return stage.at[q]

    def any_span(q):
        return pl.ds(pl.multiple_of(q * seg, seg), seg)

    def slot_of(i, o2, p):
        if isinstance(i, int) and i == 0:
            return wi_all.at[o2, p]
        if isinstance(i, int) and i == 1:
            return wo_all.at[o2, p]
        return wf_all.at[i - 2, :, o2, p]

    def half_of(i, p):
        if isinstance(i, int) and i == 0:
            return wi_all.at[:, p]
        if isinstance(i, int) and i == 1:
            return wo_all.at[:, p]
        return wf_all.at[i - 2, :, :, p]

    my_rows = pl.ds(pl.multiple_of(g * block, 4), block)

    def own_send(i, op):
        if isinstance(i, int) and i == 1:
            dst = wo_all.at[o, a]
            switch(
                a == b,
                pltpu.make_async_copy(wo_own, dst, own_rsem.at[1, 0]),
                remote(wo_own, dst, own_ssem.at[1, 0], own_rsem.at[1, 0], (2 * o + b, 2 * y + a)),
                op,
            )
            return
        if not direct:
            src = wi_own if isinstance(i, int) and i == 0 else ff_own.at[i - 2]
            if op == "start":
                pltpu.make_async_copy(src, slot_of(i, o, b), own_rsem.at[i, 0]).start()
            return
        for t2 in range(group):
            ty, tx = t2 // 2, t2 % 2
            if isinstance(i, int) and i == 0:
                src, dst = wi_own.at[t2], wi_all.at[o, a, my_rows]
            else:
                src, dst = ff_own.at[t2, i - 2], wf_all.at[i - 2, :, o, a, my_rows]
            switch(
                (tx == a) & (ty == y) & (a == b),
                pltpu.make_async_copy(src, dst, own_rsem.at[i, g]),
                remote(src, dst, own_ssem.at[i, t2], own_rsem.at[i, g], (2 * o + tx, 2 * ty + a)),
                op,
            )

    def own_wait(i):
        if not direct or isinstance(i, int) and i == 1:
            await_bytes(slot_of(i, o, b), own_rsem.at[i, 0])
            return
        for q in range(group):
            if isinstance(i, int) and i == 0:
                await_bytes(wi_all.at[o, b, pl.ds(q * block, block)], own_rsem.at[i, q])
            else:
                await_bytes(wf_all.at[i - 2, :, o, b, pl.ds(q * block, block)], own_rsem.at[i, q])

    first, final = o == 0, o == out_n - 1

    def piece_send(i, src, side):
        ref = slot_of(i, src, b)
        dev = (2 * (o + 1 - 2 * side) + a, g)
        remote(ref, ref, z_ssem.at[i, side, src], z_rsem.at[i, src], dev).start()

    def when(condition, call, *args):
        @pl.when(condition)
        def _():
            call(*args)

    def hop(i, h):
        if h == 0:
            own_wait(i)
            when(jnp.logical_not(final), piece_send, i, o, 0)
            when(jnp.logical_not(first), piece_send, i, o, 1)
            return

        @pl.when(o - h >= 0)
        def _():
            await_bytes(slot_of(i, o - h, b), z_rsem.at[i, o - h])
            when(jnp.logical_not(final), piece_send, i, o - h, 0)

        @pl.when(o + h < out_n)
        def _():
            await_bytes(slot_of(i, o + h, b), z_rsem.at[i, o + h])
            when(jnp.logical_not(first), piece_send, i, o + h, 1)

        if h == out_n - 1:
            remote(half_of(i, b), half_of(i, b), f_ssem.at[i], f_rsem.at[i], mate).start()

    items = 2 + chunks
    sent = set()

    def own_start(*which):
        for i in which:
            if i < items and i not in sent:
                sent.add(i)
                own_send(i, "start")

    def pump(time, hops=None):
        if isinstance(time, int):
            own_start(*range(time + 1))
        for h in hops or range(out_n - 1, -1, -1):
            if isinstance(time, int):
                if 0 <= time - h < items:
                    hop(time - h, h)
            else:
                when(time - h < items, hop, time - h, h)

    def gather_wait(i):
        await_bytes(half_of(i, 1 - b), f_rsem.at[i])

    def gather_close(i):
        def sent(src, side):
            await_bytes(slot_of(i, src, b), z_ssem.at[i, side, src])

        @pl.when(jnp.logical_not(final))
        def _():
            lax.fori_loop(0, o + 1, lambda src, carry: (sent(src, 0), carry)[1], 0)

        @pl.when(jnp.logical_not(first))
        def _():
            lax.fori_loop(o, out_n, lambda src, carry: (sent(src, 1), carry)[1], 0)

        await_bytes(half_of(i, b), f_ssem.at[i])
        own_send(i, "end")

    def fetch(src, dst, n):
        copy = pltpu.make_async_copy(src, dst, lsem.at[n])
        copy.start()
        copy.wait()

    def span(q):
        return pl.ds(q * seg, seg)

    def rows16(i):
        return pl.ds(pl.multiple_of(i * ROW_TILE, ROW_TILE), ROW_TILE)

    def lanes(k, j):
        return pl.ds(k * 384 + j * 128, 128)

    place = a * group + g
    mine = o * (2 * group) + place

    def plane(src, dst, ssem, rsem, op):
        for x2 in range(2):
            for g2 in range(group):
                @pl.when((x2 != a) | (g2 != g))
                def _():
                    copy = remote(src, dst, ssem.at[x2 * group + g2], rsem.at[place], (2 * o + x2, g2))
                    if op == "start":
                        copy.start()
                    else:
                        copy.wait_send()

    def plane_wait(ref, rsem):
        for x2 in range(2):
            for g2 in range(group):
                @pl.when((x2 != a) | (g2 != g))
                def _():
                    await_bytes(ref, rsem.at[x2 * group + g2])

    def far(src, dst, ssem, rsem, op):
        def one(k, carry):
            copy = remote(src, dst, ssem.at[k], rsem.at[o], peer(k)[1])
            if op == "start":
                copy.start()
            else:
                copy.wait_send()
            return carry

        lax.fori_loop(1, out_n, one, 0)

    def far_wait(ref, rsem):
        def one(k, carry):
            await_bytes(ref, rsem.at[peer(k)[0]])
            return carry

        lax.fori_loop(1, out_n, one, 0)

    planes = small_all.at[pl.ds(o * 2 * group, 2 * group)]
    pltpu.make_async_copy(small_own, small_all.at[mine], lsem.at[2]).start()
    plane(small_own, small_all.at[mine], sa_ssem, sa_rsem, "start")

    def convolved(q, col):
        return (
            taps[0:1, col] * prod[pl.ds(q * seg + 6, seg), col]
            + taps[1:2, col] * prod[pl.ds(q * seg + 7, seg), col]
            + taps[2:3, col] * prod[pl.ds(q * seg + 8, seg), col]
        )

    own_start(0)
    own_start(1)
    own_start(2)
    spread(tok, tok_all, 0, "start")
    own_start(3)
    prod[pl.ds(0, 8), :] = jnp.zeros((8, ch), F32)
    pump(0)
    await_bytes(small_own, lsem.at[2])
    plane_wait(small_own, sa_rsem)
    far(planes, planes, sz_ssem, sz_rsem, "start")
    pump(1)
    far_wait(planes, sz_rsem)
    spread_on(tok_all, 0)

    share = 2 * D // count
    rows_of = {}
    for n in range(count):
        row = n * share // 128
        rows_of.setdefault(row, []).append((n, 0))
        if (n * share + share - 1) // 128 > row:
            rows_of.setdefault(row + 1, []).append((n, 1))
    for tile, pieces in rows_of.items():
        value = sum(small_all[n, r : r + 1, :] for n, r in pieces)
        i, j = tile // (D // 128), tile % (D // 128)
        gains[i : i + 1, j * 128 : (j + 1) * 128] = value
    rows_of = {}
    for m in range(3 * count):
        n, piece = m // 3, m % 3
        tap, rest = m // count, m % count
        lane = rest // group * cblk
        rows_of.setdefault((tap, lane // 128), []).append((n, 2 + 2 * piece, rest % group))
        if (lane + block - 1) // 128 > lane // 128:
            rows_of.setdefault((tap, lane // 128 + 1), []).append((n, 3 + 2 * piece, rest % group))
    for (tap, tile), pieces in rows_of.items():
        value = jnp.zeros((1, 128), F32)
        for t2 in range(group):
            value = value + jnp.where(t == t2, sum(small_all[n, r : r + 1, :] for n, r, p in pieces if p == t2), 0.0)
        taps[tap : tap + 1, tile * 128 : (tile + 1) * 128] = value

    pump(2)
    for q in arrivals:
        spread_wait(tok_all, 0, q)
        fetch(tok_all.at[q], act.at[any_span(q)], 0)

        def normed_rows(i, carry, q=q):
            here = pl.ds(pl.multiple_of(q * seg + i * ROW_TILE, ROW_TILE), ROW_TILE)
            row = act[here, :].astype(F32)
            s1 = lax.rsqrt(jnp.mean(row * row, axis=-1, keepdims=True) + EPS_NORM)
            act[here, :] = (row * s1 * gains[0:1, :]).astype(BF)
            return carry

        lax.fori_loop(0, seg // ROW_TILE, normed_rows, 0, unroll=2)
    own_start(4)
    spread(bck_own, bck_all, 1, "start")
    own_start(5)
    keep_normed = pltpu.make_async_copy(act, nrm_far, lsem.at[2])
    keep_normed.start()
    for time in range(3, out_n - 1):
        pump(time)
    last_hop, other_hops = (out_n - 1,), tuple(range(out_n - 2, -1, -1))
    pump(out_n - 1, last_hop)
    gather_wait(0)
    fetch(wi_all, wi, 0)
    keep_normed.wait()

    for q in range(group):
        for k in range(blocks):
            acc_y[span(q), pl.ds(k * 384, 384)] = dot(
                act[span(q), :], wi[:, :, :, pl.ds(k * 384, 384)].reshape(D, 384)
            )
        for k in range(blocks):
            col = pl.ds(k * 128, 128)
            prod[pl.ds(q * seg + 8, seg), col] = acc_y[span(q), lanes(k, 0)] * acc_y[span(q), lanes(k, 2)]
            gated[span(q), col] = (acc_y[span(q), lanes(k, 1)] * convolved(q, col)).astype(BF)
    spread_on(bck_all, 1)
    pump(out_n - 1, other_hops)
    pump(out_n, last_hop)
    gather_wait(1)
    fetch(wo_all, wo, 0)

    def branch(q):
        for n in range(4):
            col = pl.ds(n * 384, 384)
            stage[q, :, col] = dot(gated[any_span(q), :], wo[:, :, :, col].reshape(ch, 384)).astype(BF)

    scatter(staged, rs_br, 0, branch)
    scatter_on(staged, rs_br, 0)
    pump(out_n, other_hops)
    spill = pltpu.make_async_copy(acc_y.at[:, pl.ds(0, 3 * ch)], mixed_far, lsem.at[2])
    spill.start()
    own_start(6)
    pump(out_n + 1)
    for q in arrivals:
        spread_wait(bck_all, 1, q)
        fetch(bck_all.at[q], bck.at[any_span(q)], 0)
        bck_t[:, any_span(q)] = bck[any_span(q), :].T

    scatter_wait(rs_br, 0)
    scatter_end(staged, rs_br, 0)
    fetch(rs_br, stage.at[pl.ds(0, 3)], 0)

    def arrived(here):
        total = stage[0, here, :].astype(F32)
        for q in range(1, 3):
            total = total + stage[q, here, :].astype(F32)
        return total

    def middle_rows(i, carry):
        here = rows16(i)
        mi = tok[here, :].astype(F32) + arrived(here)
        mid[here, :] = mi
        s2 = lax.rsqrt(jnp.mean(mi * mi, axis=-1, keepdims=True) + EPS_NORM)
        low[here, :] = (mi * s2 * gains[1:2, :]).astype(BF)
        return carry

    lax.fori_loop(0, seg // ROW_TILE, middle_rows, 0)
    spread(low, n2_all, 2, "start")
    own_start(*range(items))
    pump(out_n + 2)
    spread_on(n2_all, 2)
    gather_wait(2)
    pltpu.make_async_copy(wf_all.at[0], ws.at[0], wsem.at[0]).start()
    spill.wait()

    def clear(i, carry):
        here = rows16(i)
        acc_y[here, :] = jnp.zeros((ROW_TILE, D), F32)
        acc_n[here, :] = jnp.zeros((ROW_TILE, D), F32)
        return carry

    lax.fori_loop(0, seq // ROW_TILE, clear, 0)
    for q in arrivals:
        spread_wait(n2_all, 2, q)
        fetch(n2_all.at[q], act.at[any_span(q)], 0)
        act_t[:, any_span(q)] = act[any_span(q), :].T

    pump(out_n + 3)

    def chunk_refs(kind, c):
        if kind == "f":
            return lax.rem(c, 2), c, sib_f.at[c], pl.ds(0, WIDTH)
        n = chunks + c
        return n % 2, n, sib_i.at[c], pl.ds(0, 128)

    def pair_send(kind, c, op):
        s, n, sib, cols = chunk_refs(kind, c)
        copy = remote(grad.at[s, :, :, 1 - b, :, cols], sib, gs_ssem.at[n], gs_rsem.at[n], mate)
        if op == "start":
            copy.start()
        else:
            copy.wait_send()

    steps = out_n.bit_length() - 1

    def halves_refs(kind, c):
        return (come_f if kind == "f" else come_i).at[c], (far_f if kind == "f" else far_i).at[c]

    def flipped(k):
        m = 1 << k
        return o + m - 2 * m * lax.rem(o // m, 2)

    def kept(device, k, i):
        return lax.rem(device, 2 << k) + (2 << k) * i

    def step_at(k):
        return out_n - (out_n >> k), out_n >> (k + 1)

    def step_send(kind, c, k, op="start"):
        _, n, _, _ = chunk_refs(kind, c)
        come, mine_far = halves_refs(kind, c)
        at, number = step_at(k)
        there = flipped(k)
        for i in range(number):
            copy = remote(
                mine_far.at[:, kept(there, k, i)], come.at[:, at + i],
                gz_ssem.at[n, at + i], come_sem.at[n, at + i], (2 * there + a, g),
            )
            if op == "start":
                copy.start()
            else:
                copy.wait_send()

    def pair_fetch(kind, c, op):
        s, n, sib, cols = chunk_refs(kind, c)
        if op == "start":
            await_bytes(sib, gs_rsem.at[n])
        copy = pltpu.make_async_copy(sib, sibv.at[:, :, :, cols], lsem.at[1])
        copy.start() if op == "start" else copy.wait()

    def pair_far(kind, c):
        s, n, _, cols = chunk_refs(kind, c)
        return pltpu.make_async_copy(part.at[s, :, :, :, cols], halves_refs(kind, c)[1], far_sem.at[s])

    def pair_add(kind, c):
        s, n, _, cols = chunk_refs(kind, c)
        pair_fetch(kind, c, "end")

        def one(i, carry):
            j, o2 = i // out_n, lax.rem(i, out_n)
            part[s, j, o2, :, cols] = (
                grad[s, j, o2, b, :, cols].astype(F32) + sibv[j, o2, :, cols].astype(F32)
            ).astype(BF)
            return carry

        lax.fori_loop(0, 3 * out_n, one, 0)
        pair_far(kind, c).start()

    def first_send(kind, c):
        pair_far(kind, c).wait()
        step_send(kind, c, 0)

    def stage_ask(job, buf, op):
        kind, c, k = job
        _, n, _, cols = chunk_refs(kind, c)
        come, mine_far = halves_refs(kind, c)
        at, number = step_at(k)
        for i in range(number):
            if op == "start":
                await_bytes(come.at[:, at + i], come_sem.at[n, at + i])
            for m, src in ((i, come.at[:, at + i]), (number + i, mine_far.at[:, kept(o, k, i)])):
                copy = pltpu.make_async_copy(src, part.at[buf, :, m, :, cols], buf_sem.at[buf, m])
                copy.start() if op == "start" else copy.wait()

    def stage_back(job, buf, op):
        kind, c, k = job
        _, n, _, cols = chunk_refs(kind, c)
        mine_far = halves_refs(kind, c)[1]
        at, number = step_at(k)
        for i in range(number):
            m = number + i
            copy = pltpu.make_async_copy(
                part.at[buf, :, m, :, cols], mine_far.at[:, kept(o, k, i)], buf_sem.at[buf, m]
            )
            copy.start() if op == "start" else copy.wait()

    def stage_add(job, buf):
        kind, c, k = job
        _, n, _, cols = chunk_refs(kind, c)
        h, _, place_o, place_p = out_slot(n)
        at, number = step_at(k)

        def add(i, carry):
            j, r = i // (rows_n // 48), lax.rem(i, rows_n // 48)
            here = pl.ds(pl.multiple_of(r * 48, 16), 48)
            for m in range(number):
                value = (
                    part[buf, j, m, here, cols].astype(F32) + part[buf, j, number + m, here, cols].astype(F32)
                ).astype(BF)
                if k == steps - 1:
                    ws[h, j, place_o, place_p, here, cols] = value
                else:
                    part[buf, j, number + m, here, cols] = value
            return carry

        lax.fori_loop(0, 3 * (rows_n // 48), add, 0)
        if k == steps - 1:
            hand_back(kind, c, "start")
        else:
            stage_back(job, buf, "start")

    def stage_on(job, buf):
        kind, c, k = job
        if k < steps - 1:
            stage_back(job, buf, "end")
            step_send(kind, c, k + 1)

    def sums_of(jobs):
        for i, job in enumerate(jobs):
            if i == 0:
                stage_ask(job, 0, "start")
            if i >= 1:
                stage_on(jobs[i - 1], (i - 1) % 2)
            if i + 1 < len(jobs):
                stage_ask(jobs[i + 1], (i + 1) % 2, "start")
            stage_ask(job, i % 2, "end")
            stage_add(job, i % 2)
        stage_on(jobs[-1], (len(jobs) - 1) % 2)

    def out_slot(n):
        return (n // (2 * out_n), slice(None), lax.rem(n, 2 * out_n) // 2, lax.rem(n, 2))

    def hand_back(kind, c, op):
        _, n, _, cols = chunk_refs(kind, c)
        dst = (g_ff if kind == "f" else g_wi)
        if not direct:
            if op == "start":
                h, _, o2, p = out_slot(n)
                fetch(ws.at[h, :, o2, p, :, cols], dst.at[c], 1)
            return
        h, _, o2, p = out_slot(n)
        for q in range(group):
            src = ws.at[h, :, o2, p, pl.ds(q * block, block), cols]
            switch(
                (a == b) & (q == g),
                pltpu.make_async_copy(src, dst.at[t, c], back_rsem.at[n, t]),
                remote(src, dst.at[t, c], back_ssem.at[n, q], back_rsem.at[n, t], (2 * o + b, q)),
                op,
            )

    def hand_wait(kind, c):
        if direct:
            _, n, _, _ = chunk_refs(kind, c)
            for t2 in range(group):
                await_bytes((g_ff if kind == "f" else g_wi).at[t2, c], back_rsem.at[n, t2])

    half = out_n // 2

    def grad_rows(h):
        return pl.ds(pl.multiple_of(h * (D // 2), D // 2), D // 2), pl.ds(h * half, half)

    loop_pump = out_n + 4

    def d_normed_two(q):
        stage[q] = acc_n[any_span(q), :].astype(BF)

    def hidden_chunk(c, carry):
        s = lax.rem(c, 2)
        await_bytes(ws.at[s], wsem.at[s])
        hid, dgt, dup = (pl.ds(j * WIDTH, WIDTH) for j in range(3))

        def token_tile(m, carry):
            here = pl.ds(pl.multiple_of(m * (seq // 2), seq // 2), seq // 2)
            n2 = act[here, :]
            gate = dot(n2, ws[s, 0].reshape(D, WIDTH))
            upper = dot(n2, ws[s, 1].reshape(D, WIDTH))
            d_hidden = dot(bck[here, :], ws[s, 2].reshape(D, WIDTH))
            sigma = jax.nn.sigmoid(gate)
            active = gate * sigma
            dmix[here, hid] = (active * upper).astype(BF)
            dmix[here, dgt] = (d_hidden * upper * (sigma * (1.0 + gate * (1.0 - sigma)))).astype(BF)
            dmix[here, dup] = (d_hidden * active).astype(BF)
            acc_y[here, :] += dot_t(dmix[here, hid], ws[s, 2].reshape(D, WIDTH))
            acc_n[here, :] += dot_t(dmix[here, dgt], ws[s, 0].reshape(D, WIDTH))
            acc_n[here, :] += dot_t(dmix[here, dup], ws[s, 1].reshape(D, WIDTH))
            return carry

        lax.fori_loop(0, 2, token_tile, 0)

        @pl.when(c == chunks - 1)
        def _():
            scatter(staged, rs_n2, 1, d_normed_two)

        @pl.when(c >= 1)
        def _():
            pair_fetch("f", c - 1, "start")

        @pl.when(c >= 2)
        def _():
            first_send("f", c - 2)

        @pl.when(c >= 2)
        def _():
            pair_send("f", c - 2, "end")

        def grad_tile(h, carry):
            rows, os = grad_rows(h)
            shape = (half, 2, rows_n, WIDTH)
            grad[s, 0, os] = dot(act_t[rows, :], dmix[:, dgt]).astype(BF).reshape(shape)
            grad[s, 1, os] = dot(act_t[rows, :], dmix[:, dup]).astype(BF).reshape(shape)
            grad[s, 2, os] = dot(bck_t[rows, :], dmix[:, hid]).astype(BF).reshape(shape)
            return carry

        lax.fori_loop(0, 2, grad_tile, 0)
        pair_send("f", c, "start")

        @pl.when(c >= 1)
        def _():
            pair_add("f", c - 1)

        pump(c + loop_pump)

        @pl.when(c + 1 < chunks)
        def _():
            gather_wait(c + 3)
            pltpu.make_async_copy(wf_all.at[c + 1], ws.at[1 - s], wsem.at[1 - s]).start()

        return carry

    lax.fori_loop(0, chunks, hidden_chunk, 0)

    first_send("f", chunks - 2)
    pair_fetch("f", chunks - 1, "start")
    pair_add("f", chunks - 1)
    scatter_on(staged, rs_n2, 1)
    first_send("f", chunks - 1)
    for k in range(steps - 1):
        sums_of([("f", c, k) for c in range(chunks - 2)])
    scatter_wait(rs_n2, 1)
    scatter_end(staged, rs_n2, 1)
    spread(low, n2_all, 2, "end")
    fetch(rs_n2, stage.at[pl.ds(0, 3)], 0)
    fetch(bck_own, act.at[span(0)], 0)
    g_gains[...] = jnp.zeros_like(g_gains)

    def d_middle_rows(i, carry):
        here = rows16(i)
        dn = arrived(here)
        mi = mid[here, :]
        s2 = lax.rsqrt(jnp.mean(mi * mi, axis=-1, keepdims=True) + EPS_NORM)
        e2 = gains[1:2, :] * dn
        back = act[here, :].astype(F32)
        dm = back + s2 * e2 - mi * (s2 * s2 * s2) * jnp.mean(e2 * mi, axis=-1, keepdims=True)
        dmid[here, :] = dm
        low[here, :] = dm.astype(BF)
        g_gains[1] += jnp.sum((dn * mi * s2).reshape(ROW_TILE // 8, 8, D), axis=0)
        return carry

    lax.fori_loop(0, seg // ROW_TILE, d_middle_rows, 0)
    spread(low, dbr_all, 3, "start")

    for q in range(group):
        stage[q] = acc_y[span(q), :].astype(BF)
    spill_back = pltpu.make_async_copy(mixed_far, acc_y.at[:, pl.ds(0, 3 * ch)], lsem.at[2])
    spill_back.start()

    for q in range(group):
        bck_t[pl.ds(0, ch), span(q)] = gated[span(q), :].T
        fetch(nrm_far.at[span(q)], act.at[span(q)], 0)
        act_t[:, span(q)] = act[span(q), :].T
    spill_back.wait()
    spread_on(dbr_all, 3)
    for k in range(steps - 1):
        sums_of([("f", c, k) for c in range(chunks - 2, chunks)])
    sums_of([("f", c, steps - 1) for c in range(chunks - 3)])

    acc_n[pl.ds(seq, 8), pl.ds(0, ch)] = jnp.zeros((8, ch), F32)
    for q in arrivals:
        spread_wait(dbr_all, 3, q)
        fetch(dbr_all.at[q], bck.at[any_span(q)], 0)
        acc_n[any_span(q), pl.ds(ch, ch)] = dot_t(bck[any_span(q), :], wo[...].reshape(ch, D))
    for q in range(group):
        for k in range(blocks):
            col = pl.ds(k * 128, 128)
            d_gated = acc_n[span(q), pl.ds(ch + k * 128, 128)]
            acc_n[span(q), col] = d_gated * acc_y[span(q), lanes(k, 1)]
            dmix[span(q), lanes(k, 1)] = (d_gated * convolved(q, col)).astype(BF)
    scatter(staged, rs_y, 2, lambda q: None)
    g_taps[...] = jnp.zeros_like(g_taps)
    for q in range(group):
        for k in range(blocks):
            col = pl.ds(k * 128, 128)
            d0 = acc_n[span(q), col]
            for n in range(3):
                g_taps[n, :, col] += jnp.sum(
                    (d0 * prod[pl.ds(q * seg + 6 + n, seg), col]).reshape(seg // 8, 8, 128), axis=0
                )
            d_product = (
                taps[2:3, col] * d0
                + taps[1:2, col] * acc_n[pl.ds(q * seg + 1, seg), col]
                + taps[0:1, col] * acc_n[pl.ds(q * seg + 2, seg), col]
            )
            dmix[span(q), lanes(k, 0)] = (d_product * acc_y[span(q), lanes(k, 2)]).astype(BF)
            dmix[span(q), lanes(k, 2)] = (d_product * acc_y[span(q), lanes(k, 0)]).astype(BF)

    for k in range(blocks):
        s = (chunks + k) % 2
        if k < 2:
            pair_send("f", chunks - 2 + k, "end")
        else:
            pair_send("i", k - 2, "end")

        def intake_tile(h, carry, k=k, s=s):
            rows, os = grad_rows(h)
            value = dot(act_t[rows, :], dmix[:, pl.ds(k * 384, 384)]).astype(BF)
            for j in range(3):
                grad[s, j, os, :, :, pl.ds(0, 128)] = value[:, j * 128 : (j + 1) * 128].reshape(
                    half, 2, rows_n, 128
                )
            return carry

        lax.fori_loop(0, 2, intake_tile, 0)
        pair_send("i", k, "start")
        if k >= 1:
            pair_fetch("i", k - 1, "start")
            if k >= 2:
                first_send("i", k - 2)
            pair_add("i", k - 1)

    for n in range(4):
        col = pl.ds(n * 384, 384)
        wo[:, :, :, col] = dot(bck_t[pl.ds(0, ch), :], bck[:, col]).astype(BF).reshape(out_n, 2, cblk, 384)
    last = chunks + blocks
    pair_o = remote(wo.at[:, 1 - b], sib_o, gs_ssem.at[last], gs_rsem.at[last], mate)
    pair_o.start()
    if blocks >= 2:
        first_send("i", blocks - 2)
    pair_fetch("i", blocks - 1, "start")
    pair_add("i", blocks - 1)
    first_send("i", blocks - 1)

    await_bytes(sib_o, gs_rsem.at[last])
    fetch(sib_o, sibo, 1)

    def add_o(o2, carry):
        parto[o2] = (wo[o2, b].astype(F32) + sibo[o2].astype(F32)).astype(BF)
        return carry

    lax.fori_loop(0, out_n, add_o, 0)

    def part_o(op):
        def one(k, carry):
            o2, dev = peer(k)
            copy = remote(parto.at[o2], z_o.at[o], gz_ssem.at[last, k], come_sem.at[last, o], dev)
            if op == "start":
                copy.start()
            else:
                copy.wait_send()
            return carry

        lax.fori_loop(1, out_n, one, 0)
        keep = pltpu.make_async_copy(parto.at[o], z_o.at[o], osem.at[0])
        if op == "start":
            keep.start()
        else:
            keep.wait()

    part_o("start")

    def lent(q):
        return bck.at[any_span(q)]

    def d_normed(q):
        for n in range(4):
            bck[any_span(q), pl.ds(n * 384, 384)] = dot_t(
                dmix[any_span(q), :], wi[pl.ds(n * out_n // 4, out_n // 4)].reshape(384, 3 * ch)
            ).astype(BF)

    scatter(lent, rs_n1, 3, d_normed)
    scatter_on(staged, rs_y, 2)
    scatter_on(lent, rs_n1, 3)
    scatter_wait(rs_y, 2)
    scatter_end(staged, rs_y, 2)
    spread(low, dbr_all, 3, "end")
    for q in range(3):
        fetch(rs_y.at[q], act.at[span(q)], 0)

    def out_rows(i, carry):
        here = rows16(i)
        value = act[here, :].astype(F32)
        for q in range(1, 3):
            value = value + act[pl.ds(pl.multiple_of(q * seg + i * ROW_TILE, ROW_TILE), ROW_TILE), :].astype(F32)
        low[here, :] = (mid[here, :] + value).astype(BF)
        return carry

    lax.fori_loop(0, seg // ROW_TILE, out_rows, 0)
    fetch(low, block_out, 0)

    sums_of([("f", c, steps - 1) for c in range(chunks - 3, chunks)])
    scatter_wait(rs_n1, 3)
    scatter_end(lent, rs_n1, 3)
    fetch(rs_n1, stage.at[pl.ds(0, 3)], 0)

    def d_rows(i, carry):
        here = rows16(i)
        dn = arrived(here)
        row = tok[here, :].astype(F32)
        s1 = lax.rsqrt(jnp.mean(row * row, axis=-1, keepdims=True) + EPS_NORM)
        e1 = gains[0:1, :] * dn
        low[here, :] = (
            dmid[here, :] + s1 * e1 - row * (s1 * s1 * s1) * jnp.mean(e1 * row, axis=-1, keepdims=True)
        ).astype(BF)
        g_gains[0] += jnp.sum((dn * row * s1).reshape(ROW_TILE // 8, 8, D), axis=0)
        return carry

    lax.fori_loop(0, seg // ROW_TILE, d_rows, 0)
    fetch(low, input_grad, 0)

    sm_mine[...] = jnp.zeros_like(sm_mine)
    for i in range(2):
        value = jnp.sum(g_gains[i], axis=0, keepdims=True)
        for j in range(D // 128):
            row = i * (D // 128) + j
            sm_mine[row : row + 1, :] = value[:, j * 128 : (j + 1) * 128]
    for n in range(3):
        value = jnp.sum(g_taps[n], axis=0, keepdims=True)
        for k in range(blocks):
            for t2 in range(group):
                row = 2 * (D // 128) + (t2 * 3 + n) * blocks + k
                sm_mine[row : row + 1, :] = jnp.where(t == t2, value[:, k * 128 : (k + 1) * 128], 0.0)
    sm_plane[place] = sm_mine[...]
    plane(sm_mine, sm_plane.at[place], ta_ssem, ta_rsem, "start")

    for k in range(max(0, blocks - 2), blocks):
        pair_send("i", k, "end")

    for k in range(steps - 1):
        sums_of([("i", c, k) for c in range(blocks)])
    plane_wait(sm_mine, ta_rsem)
    value = sm_plane[0]
    for i in range(1, 2 * group):
        value = value + sm_plane[i]
    sm_sum[...] = value
    sm_z[o] = value
    far(sm_sum, sm_z.at[o], tz_ssem, tz_rsem, "start")
    sums_of([("i", c, steps - 1) for c in range(blocks)])
    part_o("end")
    pair_o.wait_send()

    def last_one(k, carry):
        await_bytes(z_o.at[o], come_sem.at[last, peer(k)[0]])
        return carry

    lax.fori_loop(1, out_n, last_one, 0)
    fetch(z_o, sibo, 1)
    value = sibo[0].astype(F32)
    for o2 in range(1, out_n):
        value = value + sibo[o2].astype(F32)
    outo = parto.at[0]
    outo[...] = value.astype(BF)

    def back_o(op):
        switch(
            a == b,
            pltpu.make_async_copy(outo, g_wo, back_rsem.at[last, 0]),
            remote(outo, g_wo, back_ssem.at[last, 0], back_rsem.at[last, 0], (2 * o + b, 2 * y + a)),
            op,
        )

    back_o("start")
    far_wait(sm_sum, tz_rsem)
    value = sm_z[0]
    for i in range(1, out_n):
        value = value + sm_z[i]
    g_small[...] = value

    plane(small_own, small_all.at[mine], sa_ssem, sa_rsem, "end")
    far(planes, planes, sz_ssem, sz_rsem, "end")
    plane(sm_mine, sm_plane.at[place], ta_ssem, ta_rsem, "end")
    far(sm_sum, sm_z.at[o], tz_ssem, tz_rsem, "end")
    spread(tok, tok_all, 0, "end")
    spread(bck_own, bck_all, 1, "end")
    gather_close(0)
    gather_close(1)

    def close(c, carry):
        gather_close(c + 2)
        for k in range(steps):
            step_send("f", c, k, "end")
        hand_back("f", c, "end")
        hand_wait("f", c)
        return carry

    lax.fori_loop(0, chunks, close, 0)
    for k in range(blocks):
        for step in range(steps):
            step_send("i", k, step, "end")
        hand_back("i", k, "end")
        hand_wait("i", k)
    back_o("end")
    await_bytes(g_wo, back_rsem.at[last, 0])


def forward_backward(sizes, tok, bck, wi_own, wo_own, ff_own, small_own):
    (out_n, group, rows_n, seg, ch, cblk, chunks) = sizes
    blocks = ch // 128
    seq = group * seg
    block = rows_n // group
    places = 2 * group
    small_rows = -(-(2 * D // 128 + group * 3 * blocks) // 8) * 8
    items = 2 + chunks
    sums = chunks + blocks + 1
    vm = pltpu.VMEM
    dma = pltpu.SemaphoreType.DMA

    def shape(*dims, dtype=BF):
        return jax.ShapeDtypeStruct(dims, dtype)

    any_spec = pl.BlockSpec(memory_space=pl.ANY)
    vmem_spec = pl.BlockSpec(memory_space=pltpu.VMEM)
    if block % 16 == 0:
        given = [shape(group, chunks, 3, block, WIDTH), shape(group, blocks, 3, block, 128)]
    else:
        given = [shape(chunks, 3, rows_n, WIDTH), shape(blocks, 3, rows_n, 128)]
    outs = [
        shape(seg, D), shape(seg, D), *given, shape(cblk, D), shape(small_rows, 128, dtype=F32),
        shape(chunks, 3, out_n, 2, rows_n, WIDTH), shape(out_n, 2, rows_n, 3 * ch), shape(out_n, 2, cblk, D),
        shape(group, seg, D), shape(seq, D), shape(group, seg, D), shape(group, seg, D), shape(group, seg, D),
        shape(3, seg, D), shape(3, seg, D), shape(3, seg, D), shape(3, seg, D), shape(4, 2, seg // 2, D),
        shape(chunks, 3, out_n, rows_n, WIDTH), shape(blocks, 3, out_n, rows_n, 128), shape(out_n, cblk, D),
        *[shape(chunks, 3, out_n, rows_n, WIDTH), shape(blocks, 3, out_n, rows_n, 128)] * 2, shape(out_n, cblk, D),
        shape(seq, 3 * ch, dtype=F32),
    ]
    out_specs = [any_spec] * 5 + [vmem_spec] + [any_spec] * (len(outs) - 6)
    scratch = [
        vm((2, 3, out_n, 2, rows_n, WIDTH), BF),
        vm((out_n, 2, rows_n, 3 * ch), BF),
        vm((out_n, 2, cblk, D), BF),
        vm((seq, D), BF), vm((D, seq), BF), vm((seq, D), BF), vm((D, seq), BF),
        vm((seq, D), F32), vm((seq + 8, D), F32),
        vm((2, 3, out_n, 2, rows_n, WIDTH), BF),
        vm((3, out_n, rows_n, WIDTH), BF),
        vm((2, 3, out_n, rows_n, WIDTH), BF),
        vm((group, seg, D), BF),
        vm((seq + 8, ch), F32), vm((seq, ch), BF), vm((seq, 3 * ch), BF),
        vm((seg, D), F32), vm((seg, D), F32), vm((seg, D), BF),
        vm((out_n, cblk, D), BF), vm((out_n, cblk, D), BF),
        vm((places * out_n, 8, 128), F32), vm((2, D), F32), vm((3, ch), F32),
        vm((2, 8, D), F32), vm((3, 8, ch), F32),
        vm((small_rows, 128), F32), vm((places, small_rows, 128), F32),
        vm((small_rows, 128), F32), vm((out_n, small_rows, 128), F32),
        vm((seg // 2, D), BF),
        dma((4, 3, 2)), dma((4, group, 2)), dma((4, 2)), dma((4, 4, 2)), dma((4, 3, 2)), dma((4, 2, 2)), dma((4, 2)),
        dma((items, 2, out_n)), dma((items, out_n)), dma((items,)), dma((items,)),
        dma((sums,)), dma((sums,)), dma((sums, out_n)), dma((sums, out_n)), dma((2,)), dma((2, out_n)),
        dma((items, group)), dma((items, group)), dma((sums, group)), dma((sums, group)), dma((1,)),
        dma((places,)), dma((places,)), dma((out_n,)), dma((out_n,)),
        dma((places,)), dma((places,)), dma((out_n,)), dma((out_n,)), dma((2,)), dma((5,)),
    ]
    results = pl.pallas_call(
        functools.partial(block_kernel, sizes),
        out_shape=outs,
        in_specs=[vmem_spec] + [any_spec] * 4 + [vmem_spec],
        out_specs=out_specs,
        scratch_shapes=scratch,
        compiler_params=pltpu.CompilerParams(
            collective_id=0, has_side_effects=True, vmem_limit_bytes=63 * 1024 * 1024
        ),
        cost_estimate=pl.CostEstimate(
            flops=6 * seq * D * (4 * ch + 3 * chunks * WIDTH),
            bytes_accessed=200_000_000,
            transcendentals=seq * chunks * WIDTH,
        ),
    )(tok, bck, wi_own, wo_own, ff_own, small_own)
    return results[:6]


def body(
    tokens,
    cotangent,
    lengths,
    intake_weight,
    intake_first,
    intake_second,
    output_weight,
    output_first,
    output_second,
    swiglu_weight,
    swiglu_first,
    swiglu_second,
    down_weight,
    down_first,
    down_second,
    norm_gains,
    gains_first,
    gains_second,
    conv_kernel,
    kernel_first,
    kernel_second,
):
    data_count = lax.axis_size("dp")
    group_count = lax.axis_size("group")
    dp = lax.axis_index("dp")
    member = lax.axis_index("group")
    block = D // (data_count * group_count)
    cblk = -(-block // 16) * 16
    ch = data_count * cblk
    blocks = ch // 128
    part_tiles = [FF // 128 // group_count + (n < FF // 128 % group_count) for n in range(group_count)]
    begins = [sum(part_tiles[:n]) for n in range(group_count)]
    chunks = -(-max(part_tiles) * 128 // WIDTH)
    hidden_full = chunks * WIDTH
    rows_n = D // data_count
    swap = []
    for one in range(data_count):
        for two in range(group_count):
            there = (2 * (one // 2) + two % 2) * group_count + 2 * (two // 2) + one % 2
            swap.append((one * group_count + two, there))

    def cross(value):
        return lax.ppermute(value, ("dp", "group"), swap)

    intake_local = (
        intake_weight.astype(BF)
        .reshape(block, 3, data_count, group_count, block)
        .transpose(3, 0, 1, 2, 4)
    )
    intake_local = jnp.pad(intake_local, ((0, 0),) * 4 + ((0, cblk - block),))
    intake_local = (
        intake_local.reshape(group_count, block, 3, blocks, 128)
        .transpose(0, 1, 3, 2, 4)
        .reshape(group_count, block, 3 * ch)
    )
    ff_local = jnp.concatenate(
        [swiglu_weight.astype(BF).reshape(block, 2, FF), down_weight.astype(BF).reshape(block, 1, FF)],
        axis=1,
    )
    pieces = []
    for begin, tiles in zip(begins, part_tiles):
        pieces.append(ff_local[:, :, begin * 128 : (begin + tiles) * 128])
        if tiles * 128 < hidden_full:
            pieces.append(jnp.zeros((block, 3, hidden_full - tiles * 128), BF))
    ff_local = jnp.concatenate(pieces, axis=-1)
    ff_local = ff_local.reshape(block, 3, group_count, chunks, WIDTH).transpose(2, 3, 1, 0, 4)
    wo_own = jnp.pad(output_weight.astype(BF).reshape(block, D), ((0, cblk - block), (0, 0)))
    if block % 16 == 0:
        wi_own, ff_own = intake_local, ff_local
    else:
        wi_own = lax.all_to_all(intake_local, "group", split_axis=0, concat_axis=0, tiled=True)
        wi_own = cross(wi_own.reshape(rows_n, 3 * ch))
        ff_own = lax.all_to_all(ff_local, "group", split_axis=0, concat_axis=0, tiled=True)
        ff_own = cross(ff_own.transpose(1, 2, 0, 3, 4).reshape(chunks, 3, rows_n, WIDTH))

    number = dp * group_count + member
    share = norm_gains.shape[0]

    def placed(values, lane):
        line = lax.dynamic_update_slice(jnp.zeros((256,), F32), lax.reduce_precision(values, 8, 7), (lane,))
        return line.reshape(2, 128)

    runs = [placed(norm_gains, lax.rem(number * share, 128))]
    for piece in range(3):
        rest = lax.rem(3 * number + piece, data_count * group_count)
        lane = lax.rem(rest // group_count * cblk, 128)
        runs.append(placed(conv_kernel[piece * block : (piece + 1) * block], lane))
    small_own = jnp.concatenate(runs)

    seg_len = tokens.shape[1]
    positions = member * seg_len + lax.iota(jnp.int32, seg_len)
    valid = (positions < lengths[0]).astype(F32)[:, None]
    back_low = (cotangent[0].astype(F32) * valid).astype(BF)

    sizes = (data_count // 2, group_count, rows_n, seg_len, ch, cblk, chunks)
    block_out, input_grad, g_ff, g_wi, g_wo, g_small = forward_backward(
        sizes, tokens[0], back_low, wi_own, wo_own, ff_own, small_own
    )

    if block % 16:
        g_wi = cross(g_wi).reshape(blocks, 3, group_count, block, 128).transpose(2, 0, 1, 3, 4)
        g_wi = lax.all_to_all(g_wi, "group", split_axis=0, concat_axis=0, tiled=True)
        g_ff = cross(g_ff).reshape(chunks, 3, group_count, block, WIDTH).transpose(2, 0, 1, 3, 4)
        g_ff = lax.all_to_all(g_ff, "group", split_axis=0, concat_axis=0, tiled=True)
    g_wi = g_wi.transpose(0, 3, 2, 1, 4).reshape(group_count, block, 3, data_count, cblk)
    intake_grad_flat = g_wi[..., :block].transpose(1, 2, 3, 0, 4).reshape(-1).astype(F32)
    g_ff = g_ff.transpose(3, 2, 0, 1, 4).reshape(block, 3, group_count, hidden_full)
    g_ff = jnp.concatenate([g_ff[:, :, n, : part_tiles[n] * 128] for n in range(group_count)], axis=-1)
    swiglu_grad_flat = g_ff[:, :2].reshape(-1).astype(F32)
    down_grad_flat = g_ff[:, 2].reshape(-1).astype(F32)
    output_grad_flat = g_wo[:block].reshape(-1).astype(F32)

    gain_rows = 2 * D // 128
    taps_grad = g_small[gain_rows : gain_rows + group_count * 3 * blocks]
    taps_grad = taps_grad.reshape(group_count, 3, data_count, cblk)[..., :block]
    taps_grad = taps_grad.transpose(1, 2, 0, 3).reshape(-1)
    small_shards = (
        lax.dynamic_slice(g_small[:gain_rows].reshape(-1), (number * share,), (share,)),
        lax.dynamic_slice(taps_grad, (number * 3 * block,), (3 * block,)),
    )
    intake_new = update(
        intake_weight, intake_first, intake_second, intake_grad_flat, RATE_MATRIX, DECAY
    )
    output_new = update(
        output_weight, output_first, output_second, output_grad_flat, RATE_MATRIX, DECAY
    )
    swiglu_new = update(
        swiglu_weight, swiglu_first, swiglu_second, swiglu_grad_flat, RATE_MATRIX, DECAY
    )
    down_new = update(down_weight, down_first, down_second, down_grad_flat, RATE_MATRIX, DECAY)
    gains_new = update(norm_gains, gains_first, gains_second, small_shards[0], RATE_VECTOR, 0.0)
    kernel_new = update(
        conv_kernel, kernel_first, kernel_second, small_shards[1], RATE_VECTOR, DECAY
    )
    return (
        block_out[None],
        input_grad[None],
        intake_new[0],
        intake_new[1],
        intake_new[2],
        output_new[0],
        output_new[1],
        output_new[2],
        swiglu_new[0],
        swiglu_new[1],
        swiglu_new[2],
        down_new[0],
        down_new[1],
        down_new[2],
        gains_new[0],
        gains_new[1],
        gains_new[2],
        kernel_new[0],
        kernel_new[1],
        kernel_new[2],
    )


def solution(mesh):
    in_specs = (
        P("dp", "group", None),
        P("dp", "group", None),
        P("dp"),
        P(("dp", "group")),
        P(("dp", "group")),
        P(("dp", "group")),
        P(("dp", "group")),
        P(("dp", "group")),
        P(("dp", "group")),
        P(("dp", "group")),
        P(("dp", "group")),
        P(("dp", "group")),
        P(("dp", "group")),
        P(("dp", "group")),
        P(("dp", "group")),
        P(("dp", "group")),
        P(("dp", "group")),
        P(("dp", "group")),
        P(("dp", "group")),
        P(("dp", "group")),
        P(("dp", "group")),
    )
    out_specs = (
        P("dp", "group", None),
        P("dp", "group", None),
        P(("dp", "group")),
        P(("dp", "group")),
        P(("dp", "group")),
        P(("dp", "group")),
        P(("dp", "group")),
        P(("dp", "group")),
        P(("dp", "group")),
        P(("dp", "group")),
        P(("dp", "group")),
        P(("dp", "group")),
        P(("dp", "group")),
        P(("dp", "group")),
        P(("dp", "group")),
        P(("dp", "group")),
        P(("dp", "group")),
        P(("dp", "group")),
        P(("dp", "group")),
        P(("dp", "group")),
    )
    return jax.shard_map(body, mesh=mesh, in_specs=in_specs, out_specs=out_specs, check_vma=False)
```

```python
import functools

import jax
import jax.numpy as jnp
from jax import lax
from jax.experimental import pallas as pl
from jax.experimental.pallas import tpu as pltpu
from jax.sharding import PartitionSpec as P

D = 1536
FF = 6912
STEP = 5
WIDTH = 256
ROW_TILE = 16

EPS_NORM = 1e-05
BETA_ONE = 0.5
BETA_TWO = 0.5
ADAM_EPS = 1e-08
RATE_MATRIX = 0.02
RATE_VECTOR = 0.2
DECAY = 0.1

MESH = pl.DeviceIdType.MESH
BF = jnp.bfloat16
F32 = jnp.float32


def update(weight, first, second, grad, rate, decay):
    first_new = BETA_ONE * first + (1.0 - BETA_ONE) * grad
    second_new = BETA_TWO * second + (1.0 - BETA_TWO) * grad * grad
    first_hat = first_new / (1.0 - BETA_ONE**STEP)
    second_hat = second_new / (1.0 - BETA_TWO**STEP)
    weight_new = weight - rate * (first_hat / (jnp.sqrt(second_hat) + ADAM_EPS) + decay * weight)
    return (first_new, second_new, weight_new)


def dot(left, right):
    return lax.dot_general(left, right, (((1,), (0,)), ((), ())), preferred_element_type=F32)


def dot_t(left, right):
    return lax.dot_general(left, right, (((1,), (1,)), ((), ())), preferred_element_type=F32)


def await_bytes(ref, sem):
    pltpu.make_async_copy(ref, ref, sem).wait()


def block_kernel(
    sizes,
    tok, bck_own, wi_own, wo_own, ff_own, small_own,
    block_out, input_grad, g_ff, g_wi, g_wo, g_small,
    wf_all, wi_all, wo_all, tok_all, nrm_far, bck_all, n2_all, dbr_all,
    rs_br, rs_y, rs_n2, rs_n1, via,
    sib_f, sib_i, sib_o, come_f, come_i, far_f, far_i, z_o, mixed_far,
    ws, wi, wo, act, act_t, bck, bck_t, acc_y, acc_n, grad, sibv, part, stage,
    prod, gated, dmix, mid, dmid, low, sibo, parto,
    small_all, gains, taps, g_gains, g_taps, sm_mine, sm_plane, sm_sum, sm_z,
    extra, ag_ssem, ag_rsem, ag_fsem, rs_ssem, rs_rsem, via_ssem, via_rsem, z_ssem, z_rsem, f_ssem, f_rsem,
    gs_ssem, gs_rsem, gz_ssem, come_sem, far_sem, buf_sem, own_ssem, own_rsem, back_ssem, back_rsem, osem,
    sa_ssem, sa_rsem, sz_ssem, sz_rsem, ta_ssem, ta_rsem, tz_ssem, tz_rsem, wsem, lsem,
):
    (out_n, group, rows_n, seg, ch, cblk, chunks) = sizes
    block = rows_n // group
    direct = block % 16 == 0
    count = 2 * out_n * group
    blocks = ch // 128
    seq = group * seg
    dp = lax.axis_index("dp")
    g = lax.axis_index("group")
    o, a = dp // 2, lax.rem(dp, 2)
    y, b = g // 2, lax.rem(g, 2)
    t = 2 * y + a
    mate = (dp, g + 1 - 2 * b)

    def peer(k):
        o2 = lax.rem(o + k, out_n)
        return o2, (2 * o2 + a, g)

    barrier = pltpu.get_barrier_semaphore()
    for x2 in range(2):
        for g2 in range(group):
            @pl.when((x2 != a) | (g2 != g))
            def _():
                pl.semaphore_signal(barrier, inc=1, device_id=(2 * o + x2, g2), device_id_type=MESH)

    def greet(k, carry):
        pl.semaphore_signal(barrier, inc=1, device_id=peer(k)[1], device_id_type=MESH)
        return carry

    lax.fori_loop(1, out_n, greet, 0)
    pl.semaphore_wait(barrier, 2 * group - 1 + out_n - 1)

    def remote(src, dst, ssem, rsem, dev):
        return pltpu.make_async_remote_copy(
            src_ref=src, dst_ref=dst, send_sem=ssem, recv_sem=rsem, device_id=dev, device_id_type=MESH
        )

    def switch(alone, local, copy, op):
        if op == "start":
            @pl.when(alone)
            def _():
                local.start()

            @pl.when(jnp.logical_not(alone))
            def _():
                copy.start()
        else:
            @pl.when(jnp.logical_not(alone))
            def _():
                copy.wait_send()

    odd = lax.rem(a + b, 2)
    size = seg // 2
    y_via = odd * y + (1 - odd) * (1 - y)
    h_via = 1 - odd
    partner = (2 * o + odd * a + (1 - odd) * (1 - a), 2 * (odd * (1 - y) + (1 - odd) * y) + b)

    def part_of(h):
        return pl.ds(h * size, size) if isinstance(h, int) else pl.ds(pl.multiple_of(h * size, size), size)

    def spread(src, dst, n, op):
        for d, h in ((1, 0), (2, 1), (1, 1), (2, 0), (0, 0), (0, 1)):
            x2, y2 = (1 - a if d == 1 else a), (1 - y if d == 2 else y)
            one, two = src.at[part_of(h)], dst.at[g, part_of(h)]
            copy = remote(one, two, ag_ssem.at[n, d, h], ag_rsem.at[n, g, h], (2 * o + x2, 2 * y2 + a))
            if d == 0:
                switch(a == b, pltpu.make_async_copy(one, two, ag_rsem.at[n, g, h]), copy, op)
            elif op == "start":
                copy.start()
            else:
                copy.wait_send()
        if op == "end":
            for k in range(2):
                ref = dst.at[2 * y_via + k, part_of(h_via)]
                await_bytes(ref, ag_fsem.at[n, k])

    def spread_on(dst, n):
        for k in range(2):
            q = 2 * y_via + k
            ref = dst.at[q, part_of(h_via)]
            await_bytes(ref, ag_rsem.at[n, q, h_via])
            remote(ref, ref, ag_fsem.at[n, k], ag_rsem.at[n, q, h_via], partner).start()

    def spread_wait(dst, n, q):
        for h in range(2):
            @pl.when((q // 2 != y_via) | (h != h_via))
            def _():
                await_bytes(dst.at[q, part_of(h)], ag_rsem.at[n, q, h])

    def give(terms, dst, n, at, q, h, slot, op="start"):
        one, two = terms(q).at[part_of(h)], dst.at[slot, part_of(h)]
        copy = remote(one, two, rs_ssem.at[n, at, h], rs_rsem.at[n, slot, h], (2 * o + b, q))
        if slot == 0:
            switch(q == g, pltpu.make_async_copy(one, two, rs_rsem.at[n, 0, h]), copy, op)
        elif op == "start":
            copy.start()
        else:
            copy.wait_send()

    def give_half(terms, n, k, h, op):
        q = 2 * (1 - y) + k
        dev = (2 * o + 1 - a, g) if h == 0 else (dp, 2 * (1 - y) + b)
        copy = remote(terms(q).at[part_of(h)], via.at[n, k], via_ssem.at[n, k, h], via_rsem.at[n, k], dev)
        if op == "start":
            copy.start()
        else:
            copy.wait_send()

    def scatter(terms, dst, n, produce):
        for k in range(2):
            q = 2 * (1 - y) + k
            produce(q)

            @pl.when(odd == 1)
            def _():
                give_half(terms, n, k, 0, "start")
                give_half(terms, n, k, 1, "start")

            @pl.when(odd == 0)
            def _():
                give(terms, dst, n, k, q, 1, 1)

        for k in range(2):
            q = 2 * y + k
            produce(q)

            @pl.when(odd == 1)
            def _():
                give(terms, dst, n, 2 + k, q, 0, 2)

            @pl.when(odd == 0)
            def _():
                give(terms, dst, n, 2 + k, q, 0, 0)
                give(terms, dst, n, 2 + k, q, 1, 0)

    def scatter_on(terms, dst, n):
        for k in range(2):
            q = 2 * y_via + k
            await_bytes(via.at[n, k], via_rsem.at[n, k])
            fetch(via.at[n, k], extra, 0)

            def add_rows(i, carry):
                here = pl.ds(pl.multiple_of(odd * size + i * ROW_TILE, ROW_TILE), ROW_TILE)
                ref = terms(q)
                ref[here, :] = (ref[here, :].astype(F32) + extra[rows16(i), :].astype(F32)).astype(BF)
                return carry

            lax.fori_loop(0, size // ROW_TILE, add_rows, 0)

            @pl.when(odd == 1)
            def _():
                give(terms, dst, n, 2 + k, q, 1, 2)

            @pl.when(odd == 0)
            def _():
                give(terms, dst, n, k, q, 0, 1)

    def scatter_end(terms, dst, n):
        @pl.when(odd == 1)
        def _():
            for k in range(2):
                for h in range(2):
                    give_half(terms, n, k, h, "end")
                    give(terms, dst, n, 2 + k, 2 * y + k, h, 2, "end")

        @pl.when(odd == 0)
        def _():
            for k in range(2):
                for h in range(2):
                    give(terms, dst, n, k, 2 * (1 - y) + k, h, 1, "end")
                    give(terms, dst, n, 2 + k, 2 * y + k, h, 0, "end")

    def scatter_wait(dst, n):
        for slot in range(3):
            for h in range(2):
                await_bytes(dst.at[slot, part_of(h)], rs_rsem.at[n, slot, h])

    arrivals = (2 * y, 2 * y + 1, 2 * (1 - y), 2 * (1 - y) + 1)

    def staged(q):
        return stage.at[q]

    def any_span(q):
        return pl.ds(pl.multiple_of(q * seg, seg), seg)

    def slot_of(i, o2, p):
        if isinstance(i, int) and i == 0:
            return wi_all.at[o2, p]
        if isinstance(i, int) and i == 1:
            return wo_all.at[o2, p]
        return wf_all.at[i - 2, :, o2, p]

    def half_of(i, p):
        if isinstance(i, int) and i == 0:
            return wi_all.at[:, p]
        if isinstance(i, int) and i == 1:
            return wo_all.at[:, p]
        return wf_all.at[i - 2, :, :, p]

    my_rows = pl.ds(pl.multiple_of(g * block, 4), block)

    def own_send(i, op):
        if isinstance(i, int) and i == 1:
            dst = wo_all.at[o, a]
            switch(
                a == b,
                pltpu.make_async_copy(wo_own, dst, own_rsem.at[1, 0]),
                remote(wo_own, dst, own_ssem.at[1, 0], own_rsem.at[1, 0], (2 * o + b, 2 * y + a)),
                op,
            )
            return
        if not direct:
            src = wi_own if isinstance(i, int) and i == 0 else ff_own.at[i - 2]
            if op == "start":
                pltpu.make_async_copy(src, slot_of(i, o, b), own_rsem.at[i, 0]).start()
            return
        for t2 in range(group):
            ty, tx = t2 // 2, t2 % 2
            if isinstance(i, int) and i == 0:
                src, dst = wi_own.at[t2], wi_all.at[o, a, my_rows]
            else:
                src, dst = ff_own.at[t2, i - 2], wf_all.at[i - 2, :, o, a, my_rows]
            switch(
                (tx == a) & (ty == y) & (a == b),
                pltpu.make_async_copy(src, dst, own_rsem.at[i, g]),
                remote(src, dst, own_ssem.at[i, t2], own_rsem.at[i, g], (2 * o + tx, 2 * ty + a)),
                op,
            )

    def own_wait(i):
        if not direct or isinstance(i, int) and i == 1:
            await_bytes(slot_of(i, o, b), own_rsem.at[i, 0])
            return
        for q in range(group):
            if isinstance(i, int) and i == 0:
                await_bytes(wi_all.at[o, b, pl.ds(q * block, block)], own_rsem.at[i, q])
            else:
                await_bytes(wf_all.at[i - 2, :, o, b, pl.ds(q * block, block)], own_rsem.at[i, q])

    first, final = o == 0, o == out_n - 1

    def piece_copy(i, src, side, far_by=1):
        ref = slot_of(i, src, b)
        dev = (2 * (o + far_by * (1 - 2 * side)) + a, g)
        return remote(ref, ref, z_ssem.at[i, 2 * side + far_by - 1, src], z_rsem.at[i, src], dev)

    def when(condition, call, *args):
        @pl.when(condition)
        def _():
            call(*args)

    def own_pieces(i, op):
        for side in range(2):
            for far_by in range(1, min(3, out_n)):
                copy = piece_copy(i, o, side, far_by)
                when((o >= far_by) if side else (o + far_by < out_n), copy.start if op == "start" else copy.wait_send)

    def pass_on(i, h, op="start"):
        for side in range(2):
            src = o + h if side else o - h
            there = (src < out_n) & (o > 0) if side else (src >= 0) & (o < out_n - 1)

            @pl.when((src < out_n) if side else (src >= 0))
            def _(src=src, side=side):
                if op == "start":
                    await_bytes(slot_of(i, src, b), z_rsem.at[i, src])

            @pl.when(there)
            def _(src=src, side=side):
                copy = piece_copy(i, src, side)
                copy.start() if op == "start" else copy.wait_send()

    def to_mate(i):
        for h in sorted({1, out_n - 1}):
            for side in range(2):
                src = o + h if side else o - h

                @pl.when((src < out_n) if side else (src >= 0))
                def _(src=src):
                    await_bytes(slot_of(i, src, b), z_rsem.at[i, src])

        remote(half_of(i, b), half_of(i, b), f_ssem.at[i], f_rsem.at[i], mate).start()

    items = 2 + chunks
    sent = set()

    def own_start(*which):
        for i in which:
            if i < items and i not in sent:
                sent.add(i)
                own_send(i, "start")

    def leave(i):
        own_wait(i)
        own_pieces(i, "start")

    def pump(time):
        work = [(time + 1, leave, ())]
        work += [(time - n, pass_on, (n + 1,)) for n in range(1, out_n - 2)]
        work += [(time - (out_n - 2), to_mate, ())]
        if isinstance(time, int):
            own_start(*range(time + 2))
        for i, call, args in work:
            if isinstance(i, int):
                if 0 <= i < items:
                    call(i, *args)
            else:
                when(i < items, call, i, *args)

    def gather_wait(i):
        await_bytes(half_of(i, 1 - b), f_rsem.at[i])

    def gather_close(i):
        own_pieces(i, "end")
        for h in range(2, out_n - 1):
            pass_on(i, h, "end")
        await_bytes(half_of(i, b), f_ssem.at[i])
        own_send(i, "end")

    def fetch(src, dst, n):
        copy = pltpu.make_async_copy(src, dst, lsem.at[n])
        copy.start()
        copy.wait()

    def span(q):
        return pl.ds(q * seg, seg)

    def rows16(i):
        return pl.ds(pl.multiple_of(i * ROW_TILE, ROW_TILE), ROW_TILE)

    def lanes(k, j):
        return pl.ds(k * 384 + j * 128, 128)

    place = a * group + g
    mine = o * (2 * group) + place

    def plane(src, dst, ssem, rsem, op):
        for x2 in range(2):
            for g2 in range(group):
                @pl.when((x2 != a) | (g2 != g))
                def _():
                    copy = remote(src, dst, ssem.at[x2 * group + g2], rsem.at[place], (2 * o + x2, g2))
                    if op == "start":
                        copy.start()
                    else:
                        copy.wait_send()

    def plane_wait(ref, rsem):
        for x2 in range(2):
            for g2 in range(group):
                @pl.when((x2 != a) | (g2 != g))
                def _():
                    await_bytes(ref, rsem.at[x2 * group + g2])

    def far(src, dst, ssem, rsem, op):
        def one(k, carry):
            copy = remote(src, dst, ssem.at[k], rsem.at[o], peer(k)[1])
            if op == "start":
                copy.start()
            else:
                copy.wait_send()
            return carry

        lax.fori_loop(1, out_n, one, 0)

    def far_wait(ref, rsem):
        def one(k, carry):
            await_bytes(ref, rsem.at[peer(k)[0]])
            return carry

        lax.fori_loop(1, out_n, one, 0)

    planes = small_all.at[pl.ds(o * 2 * group, 2 * group)]
    pltpu.make_async_copy(small_own, small_all.at[mine], lsem.at[2]).start()
    plane(small_own, small_all.at[mine], sa_ssem, sa_rsem, "start")

    def convolved(q, col):
        return (
            taps[0:1, col] * prod[pl.ds(q * seg + 6, seg), col]
            + taps[1:2, col] * prod[pl.ds(q * seg + 7, seg), col]
            + taps[2:3, col] * prod[pl.ds(q * seg + 8, seg), col]
        )

    own_start(0)
    own_start(1)
    own_start(2)
    spread(tok, tok_all, 0, "start")
    own_start(3)
    own_start(4)
    prod[pl.ds(0, 8), :] = jnp.zeros((8, ch), F32)
    leave(0)
    pump(0)
    await_bytes(small_own, lsem.at[2])
    plane_wait(small_own, sa_rsem)
    far(planes, planes, sz_ssem, sz_rsem, "start")
    pump(1)
    far_wait(planes, sz_rsem)
    spread_on(tok_all, 0)

    share = 2 * D // count
    rows_of = {}
    for n in range(count):
        row = n * share // 128
        rows_of.setdefault(row, []).append((n, 0))
        if (n * share + share - 1) // 128 > row:
            rows_of.setdefault(row + 1, []).append((n, 1))
    for tile, pieces in rows_of.items():
        value = sum(small_all[n, r : r + 1, :] for n, r in pieces)
        i, j = tile // (D // 128), tile % (D // 128)
        gains[i : i + 1, j * 128 : (j + 1) * 128] = value
    rows_of = {}
    for m in range(3 * count):
        n, piece = m // 3, m % 3
        tap, rest = m // count, m % count
        lane = rest // group * cblk
        rows_of.setdefault((tap, lane // 128), []).append((n, 2 + 2 * piece, rest % group))
        if (lane + block - 1) // 128 > lane // 128:
            rows_of.setdefault((tap, lane // 128 + 1), []).append((n, 3 + 2 * piece, rest % group))
    for (tap, tile), pieces in rows_of.items():
        value = jnp.zeros((1, 128), F32)
        for t2 in range(group):
            value = value + jnp.where(t == t2, sum(small_all[n, r : r + 1, :] for n, r, p in pieces if p == t2), 0.0)
        taps[tap : tap + 1, tile * 128 : (tile + 1) * 128] = value

    pump(2)
    for q in arrivals:
        spread_wait(tok_all, 0, q)
        fetch(tok_all.at[q], act.at[any_span(q)], 0)

        def normed_rows(i, carry, q=q):
            here = pl.ds(pl.multiple_of(q * seg + i * ROW_TILE, ROW_TILE), ROW_TILE)
            row = act[here, :].astype(F32)
            s1 = lax.rsqrt(jnp.mean(row * row, axis=-1, keepdims=True) + EPS_NORM)
            act[here, :] = (row * s1 * gains[0:1, :]).astype(BF)
            return carry

        lax.fori_loop(0, seg // ROW_TILE, normed_rows, 0, unroll=2)
    spread(bck_own, bck_all, 1, "start")
    own_start(5)
    keep_normed = pltpu.make_async_copy(act, nrm_far, lsem.at[2])
    keep_normed.start()
    for time in range(3, out_n):
        pump(time)
    gather_wait(0)
    fetch(wi_all, wi, 0)
    keep_normed.wait()

    for q in range(group):
        for k in range(blocks):
            acc_y[span(q), pl.ds(k * 384, 384)] = dot(
                act[span(q), :], wi[:, :, :, pl.ds(k * 384, 384)].reshape(D, 384)
            )
        for k in range(blocks):
            col = pl.ds(k * 128, 128)
            prod[pl.ds(q * seg + 8, seg), col] = acc_y[span(q), lanes(k, 0)] * acc_y[span(q), lanes(k, 2)]
            gated[span(q), col] = (acc_y[span(q), lanes(k, 1)] * convolved(q, col)).astype(BF)
    spread_on(bck_all, 1)
    gather_wait(1)
    fetch(wo_all, wo, 0)

    def branch(q):
        for n in range(4):
            col = pl.ds(n * 384, 384)
            stage[q, :, col] = dot(gated[any_span(q), :], wo[:, :, :, col].reshape(ch, 384)).astype(BF)

    scatter(staged, rs_br, 0, branch)
    pump(out_n)
    scatter_on(staged, rs_br, 0)
    spill = pltpu.make_async_copy(acc_y.at[:, pl.ds(0, 3 * ch)], mixed_far, lsem.at[2])
    spill.start()
    own_start(6)
    for q in arrivals:
        spread_wait(bck_all, 1, q)
        fetch(bck_all.at[q], bck.at[any_span(q)], 0)
        bck_t[:, any_span(q)] = bck[any_span(q), :].T

    pump(out_n + 1)
    scatter_wait(rs_br, 0)
    scatter_end(staged, rs_br, 0)
    fetch(rs_br, stage.at[pl.ds(0, 3)], 0)

    def arrived(here):
        total = stage[0, here, :].astype(F32)
        for q in range(1, 3):
            total = total + stage[q, here, :].astype(F32)
        return total

    def middle_rows(i, carry):
        here = rows16(i)
        mi = tok[here, :].astype(F32) + arrived(here)
        mid[here, :] = mi
        s2 = lax.rsqrt(jnp.mean(mi * mi, axis=-1, keepdims=True) + EPS_NORM)
        low[here, :] = (mi * s2 * gains[1:2, :]).astype(BF)
        return carry

    lax.fori_loop(0, seg // ROW_TILE, middle_rows, 0)
    spread(low, n2_all, 2, "start")
    own_start(*range(items))
    pump(out_n + 2)
    spread_on(n2_all, 2)
    gather_wait(2)
    pltpu.make_async_copy(wf_all.at[0], ws.at[0], wsem.at[0]).start()
    spill.wait()

    def clear(i, carry):
        here = rows16(i)
        acc_y[here, :] = jnp.zeros((ROW_TILE, D), F32)
        acc_n[here, :] = jnp.zeros((ROW_TILE, D), F32)
        return carry

    lax.fori_loop(0, seq // ROW_TILE, clear, 0)
    for q in arrivals:
        spread_wait(n2_all, 2, q)
        fetch(n2_all.at[q], act.at[any_span(q)], 0)
        act_t[:, any_span(q)] = act[any_span(q), :].T


    def chunk_refs(kind, c):
        if kind == "f":
            return lax.rem(c, 2), c, sib_f.at[c], pl.ds(0, WIDTH)
        n = chunks + c
        return n % 2, n, sib_i.at[c], pl.ds(0, 128)

    def pair_send(kind, c, op):
        s, n, sib, cols = chunk_refs(kind, c)
        copy = remote(grad.at[s, :, :, 1 - b, :, cols], sib, gs_ssem.at[n], gs_rsem.at[n], mate)
        if op == "start":
            copy.start()
        else:
            copy.wait_send()

    steps = out_n.bit_length() - 1

    def halves_refs(kind, c):
        return (come_f if kind == "f" else come_i).at[c], (far_f if kind == "f" else far_i).at[c]

    def flipped(k):
        m = 1 << k
        return o + m - 2 * m * lax.rem(o // m, 2)

    def kept(device, k, i):
        return lax.rem(device, 2 << k) + (2 << k) * i

    def step_at(k):
        return out_n - (out_n >> k), out_n >> (k + 1)

    def step_send(kind, c, k, op="start"):
        _, n, _, _ = chunk_refs(kind, c)
        come, mine_far = halves_refs(kind, c)
        at, number = step_at(k)
        there = flipped(k)
        for i in range(number):
            copy = remote(
                mine_far.at[:, kept(there, k, i)], come.at[:, at + i],
                gz_ssem.at[n, at + i], come_sem.at[n, at + i], (2 * there + a, g),
            )
            if op == "start":
                copy.start()
            else:
                copy.wait_send()

    def pair_fetch(kind, c, op):
        s, n, sib, cols = chunk_refs(kind, c)
        if op == "start":
            await_bytes(sib, gs_rsem.at[n])
        copy = pltpu.make_async_copy(sib, sibv.at[:, :, :, cols], lsem.at[1])
        copy.start() if op == "start" else copy.wait()

    def pair_far(kind, c):
        s, n, _, cols = chunk_refs(kind, c)
        return pltpu.make_async_copy(part.at[s, :, :, :, cols], halves_refs(kind, c)[1], far_sem.at[s])

    def pair_add(kind, c):
        s, n, _, cols = chunk_refs(kind, c)
        pair_fetch(kind, c, "end")

        def one(i, carry):
            j, o2 = i // out_n, lax.rem(i, out_n)
            part[s, j, o2, :, cols] = (
                grad[s, j, o2, b, :, cols].astype(F32) + sibv[j, o2, :, cols].astype(F32)
            ).astype(BF)
            return carry

        lax.fori_loop(0, 3 * out_n, one, 0)
        pair_far(kind, c).start()

    def first_send(kind, c):
        pair_far(kind, c).wait()
        step_send(kind, c, 0)

    def stage_ask(job, buf, op):
        kind, c, k = job
        _, n, _, cols = chunk_refs(kind, c)
        come, mine_far = halves_refs(kind, c)
        at, number = step_at(k)
        for i in range(number):
            if op == "start":
                await_bytes(come.at[:, at + i], come_sem.at[n, at + i])
            for m, src in ((i, come.at[:, at + i]), (number + i, mine_far.at[:, kept(o, k, i)])):
                copy = pltpu.make_async_copy(src, part.at[buf, :, m, :, cols], buf_sem.at[buf, m])
                copy.start() if op == "start" else copy.wait()

    def stage_back(job, buf, op):
        kind, c, k = job
        _, n, _, cols = chunk_refs(kind, c)
        mine_far = halves_refs(kind, c)[1]
        at, number = step_at(k)
        for i in range(number):
            m = number + i
            copy = pltpu.make_async_copy(
                part.at[buf, :, m, :, cols], mine_far.at[:, kept(o, k, i)], buf_sem.at[buf, m]
            )
            copy.start() if op == "start" else copy.wait()

    def stage_add(job, buf):
        kind, c, k = job
        _, n, _, cols = chunk_refs(kind, c)
        h, _, place_o, place_p = out_slot(n)
        at, number = step_at(k)

        def add(i, carry):
            j, r = i // (rows_n // 48), lax.rem(i, rows_n // 48)
            here = pl.ds(pl.multiple_of(r * 48, 16), 48)
            for m in range(number):
                value = (
                    part[buf, j, m, here, cols].astype(F32) + part[buf, j, number + m, here, cols].astype(F32)
                ).astype(BF)
                if k == steps - 1:
                    ws[h, j, place_o, place_p, here, cols] = value
                else:
                    part[buf, j, number + m, here, cols] = value
            return carry

        lax.fori_loop(0, 3 * (rows_n // 48), add, 0)
        if k == steps - 1:
            hand_back(kind, c, "start")
        else:
            stage_back(job, buf, "start")

    def stage_on(job, buf):
        kind, c, k = job
        if k < steps - 1:
            stage_back(job, buf, "end")
            step_send(kind, c, k + 1)

    def sums_of(jobs):
        for i, job in enumerate(jobs):
            if i == 0:
                stage_ask(job, 0, "start")
            if i >= 1:
                stage_on(jobs[i - 1], (i - 1) % 2)
            if i + 1 < len(jobs):
                stage_ask(jobs[i + 1], (i + 1) % 2, "start")
            stage_ask(job, i % 2, "end")
            stage_add(job, i % 2)
        stage_on(jobs[-1], (len(jobs) - 1) % 2)

    def out_slot(n):
        return (n // (2 * out_n), slice(None), lax.rem(n, 2 * out_n) // 2, lax.rem(n, 2))

    def hand_back(kind, c, op):
        _, n, _, cols = chunk_refs(kind, c)
        dst = (g_ff if kind == "f" else g_wi)
        if not direct:
            if op == "start":
                h, _, o2, p = out_slot(n)
                fetch(ws.at[h, :, o2, p, :, cols], dst.at[c], 1)
            return
        h, _, o2, p = out_slot(n)
        for q in range(group):
            src = ws.at[h, :, o2, p, pl.ds(q * block, block), cols]
            switch(
                (a == b) & (q == g),
                pltpu.make_async_copy(src, dst.at[t, c], back_rsem.at[n, t]),
                remote(src, dst.at[t, c], back_ssem.at[n, q], back_rsem.at[n, t], (2 * o + b, q)),
                op,
            )

    def hand_wait(kind, c):
        if direct:
            _, n, _, _ = chunk_refs(kind, c)
            for t2 in range(group):
                await_bytes((g_ff if kind == "f" else g_wi).at[t2, c], back_rsem.at[n, t2])

    half = out_n // 2

    def grad_rows(h):
        return pl.ds(pl.multiple_of(h * (D // 2), D // 2), D // 2), pl.ds(h * half, half)

    loop_pump = out_n + 3

    def d_normed_two(q):
        stage[q] = acc_n[any_span(q), :].astype(BF)

    def hidden_chunk(c, carry):
        s = lax.rem(c, 2)
        await_bytes(ws.at[s], wsem.at[s])
        hid, dgt, dup = (pl.ds(j * WIDTH, WIDTH) for j in range(3))

        def token_tile(m, carry):
            here = pl.ds(pl.multiple_of(m * (seq // 2), seq // 2), seq // 2)
            n2 = act[here, :]
            gate = dot(n2, ws[s, 0].reshape(D, WIDTH))
            upper = dot(n2, ws[s, 1].reshape(D, WIDTH))
            d_hidden = dot(bck[here, :], ws[s, 2].reshape(D, WIDTH))
            sigma = jax.nn.sigmoid(gate)
            active = gate * sigma
            dmix[here, hid] = (active * upper).astype(BF)
            dmix[here, dgt] = (d_hidden * upper * (sigma * (1.0 + gate * (1.0 - sigma)))).astype(BF)
            dmix[here, dup] = (d_hidden * active).astype(BF)
            acc_y[here, :] += dot_t(dmix[here, hid], ws[s, 2].reshape(D, WIDTH))
            acc_n[here, :] += dot_t(dmix[here, dgt], ws[s, 0].reshape(D, WIDTH))
            acc_n[here, :] += dot_t(dmix[here, dup], ws[s, 1].reshape(D, WIDTH))
            return carry

        lax.fori_loop(0, 2, token_tile, 0)

        @pl.when(c == chunks - 1)
        def _():
            scatter(staged, rs_n2, 1, d_normed_two)

        @pl.when(c >= 1)
        def _():
            pair_fetch("f", c - 1, "start")

        @pl.when(c >= 2)
        def _():
            first_send("f", c - 2)

        @pl.when(c >= 2)
        def _():
            pair_send("f", c - 2, "end")

        def grad_tile(h, carry):
            rows, os = grad_rows(h)
            shape = (half, 2, rows_n, WIDTH)
            grad[s, 0, os] = dot(act_t[rows, :], dmix[:, dgt]).astype(BF).reshape(shape)
            grad[s, 1, os] = dot(act_t[rows, :], dmix[:, dup]).astype(BF).reshape(shape)
            grad[s, 2, os] = dot(bck_t[rows, :], dmix[:, hid]).astype(BF).reshape(shape)
            return carry

        lax.fori_loop(0, 2, grad_tile, 0)
        pair_send("f", c, "start")

        @pl.when(c >= 1)
        def _():
            pair_add("f", c - 1)

        pump(c + loop_pump)

        @pl.when(c + 1 < chunks)
        def _():
            gather_wait(c + 3)
            pltpu.make_async_copy(wf_all.at[c + 1], ws.at[1 - s], wsem.at[1 - s]).start()

        return carry

    lax.fori_loop(0, chunks, hidden_chunk, 0)

    first_send("f", chunks - 2)
    pair_fetch("f", chunks - 1, "start")
    pair_add("f", chunks - 1)
    scatter_on(staged, rs_n2, 1)
    first_send("f", chunks - 1)
    for k in range(steps - 1):
        sums_of([("f", c, k) for c in range(chunks - 2)])
    scatter_wait(rs_n2, 1)
    scatter_end(staged, rs_n2, 1)
    spread(low, n2_all, 2, "end")
    fetch(rs_n2, stage.at[pl.ds(0, 3)], 0)
    fetch(bck_own, act.at[span(0)], 0)
    g_gains[...] = jnp.zeros_like(g_gains)

    def d_middle_rows(i, carry):
        here = rows16(i)
        dn = arrived(here)
        mi = mid[here, :]
        s2 = lax.rsqrt(jnp.mean(mi * mi, axis=-1, keepdims=True) + EPS_NORM)
        e2 = gains[1:2, :] * dn
        back = act[here, :].astype(F32)
        dm = back + s2 * e2 - mi * (s2 * s2 * s2) * jnp.mean(e2 * mi, axis=-1, keepdims=True)
        dmid[here, :] = dm
        low[here, :] = dm.astype(BF)
        g_gains[1] += jnp.sum((dn * mi * s2).reshape(ROW_TILE // 8, 8, D), axis=0)
        return carry

    lax.fori_loop(0, seg // ROW_TILE, d_middle_rows, 0)
    spread(low, dbr_all, 3, "start")

    for q in range(group):
        stage[q] = acc_y[span(q), :].astype(BF)
    spill_back = pltpu.make_async_copy(mixed_far, acc_y.at[:, pl.ds(0, 3 * ch)], lsem.at[2])
    spill_back.start()

    for q in range(group):
        bck_t[pl.ds(0, ch), span(q)] = gated[span(q), :].T
        fetch(nrm_far.at[span(q)], act.at[span(q)], 0)
        act_t[:, span(q)] = act[span(q), :].T
    spill_back.wait()
    spread_on(dbr_all, 3)
    for k in range(steps - 1):
        sums_of([("f", c, k) for c in range(chunks - 2, chunks)])
    sums_of([("f", c, steps - 1) for c in range(chunks - 3)])

    acc_n[pl.ds(seq, 8), pl.ds(0, ch)] = jnp.zeros((8, ch), F32)
    for q in arrivals:
        spread_wait(dbr_all, 3, q)
        fetch(dbr_all.at[q], bck.at[any_span(q)], 0)
        acc_n[any_span(q), pl.ds(ch, ch)] = dot_t(bck[any_span(q), :], wo[...].reshape(ch, D))
    for q in range(group):
        for k in range(blocks):
            col = pl.ds(k * 128, 128)
            d_gated = acc_n[span(q), pl.ds(ch + k * 128, 128)]
            acc_n[span(q), col] = d_gated * acc_y[span(q), lanes(k, 1)]
            dmix[span(q), lanes(k, 1)] = (d_gated * convolved(q, col)).astype(BF)
    scatter(staged, rs_y, 2, lambda q: None)
    g_taps[...] = jnp.zeros_like(g_taps)
    for q in range(group):
        for k in range(blocks):
            col = pl.ds(k * 128, 128)
            d0 = acc_n[span(q), col]
            for n in range(3):
                g_taps[n, :, col] += jnp.sum(
                    (d0 * prod[pl.ds(q * seg + 6 + n, seg), col]).reshape(seg // 8, 8, 128), axis=0
                )
            d_product = (
                taps[2:3, col] * d0
                + taps[1:2, col] * acc_n[pl.ds(q * seg + 1, seg), col]
                + taps[0:1, col] * acc_n[pl.ds(q * seg + 2, seg), col]
            )
            dmix[span(q), lanes(k, 0)] = (d_product * acc_y[span(q), lanes(k, 2)]).astype(BF)
            dmix[span(q), lanes(k, 2)] = (d_product * acc_y[span(q), lanes(k, 0)]).astype(BF)

    for k in range(blocks):
        s = (chunks + k) % 2
        if k < 2:
            pair_send("f", chunks - 2 + k, "end")
        else:
            pair_send("i", k - 2, "end")

        def intake_tile(h, carry, k=k, s=s):
            rows, os = grad_rows(h)
            value = dot(act_t[rows, :], dmix[:, pl.ds(k * 384, 384)]).astype(BF)
            for j in range(3):
                grad[s, j, os, :, :, pl.ds(0, 128)] = value[:, j * 128 : (j + 1) * 128].reshape(
                    half, 2, rows_n, 128
                )
            return carry

        lax.fori_loop(0, 2, intake_tile, 0)
        pair_send("i", k, "start")
        if k >= 1:
            pair_fetch("i", k - 1, "start")
            if k >= 2:
                first_send("i", k - 2)
            pair_add("i", k - 1)

    for n in range(4):
        col = pl.ds(n * 384, 384)
        wo[:, :, :, col] = dot(bck_t[pl.ds(0, ch), :], bck[:, col]).astype(BF).reshape(out_n, 2, cblk, 384)
    last = chunks + blocks
    pair_o = remote(wo.at[:, 1 - b], sib_o, gs_ssem.at[last], gs_rsem.at[last], mate)
    pair_o.start()
    if blocks >= 2:
        first_send("i", blocks - 2)
    pair_fetch("i", blocks - 1, "start")
    pair_add("i", blocks - 1)
    first_send("i", blocks - 1)

    await_bytes(sib_o, gs_rsem.at[last])
    fetch(sib_o, sibo, 1)

    def add_o(o2, carry):
        parto[o2] = (wo[o2, b].astype(F32) + sibo[o2].astype(F32)).astype(BF)
        return carry

    lax.fori_loop(0, out_n, add_o, 0)

    def part_o(op):
        def one(k, carry):
            o2, dev = peer(k)
            copy = remote(parto.at[o2], z_o.at[o], gz_ssem.at[last, k], come_sem.at[last, o], dev)
            if op == "start":
                copy.start()
            else:
                copy.wait_send()
            return carry

        lax.fori_loop(1, out_n, one, 0)
        keep = pltpu.make_async_copy(parto.at[o], z_o.at[o], osem.at[0])
        if op == "start":
            keep.start()
        else:
            keep.wait()

    part_o("start")

    def lent(q):
        return bck.at[any_span(q)]

    def d_normed(q):
        for n in range(4):
            bck[any_span(q), pl.ds(n * 384, 384)] = dot_t(
                dmix[any_span(q), :], wi[pl.ds(n * out_n // 4, out_n // 4)].reshape(384, 3 * ch)
            ).astype(BF)

    scatter(lent, rs_n1, 3, d_normed)
    scatter_on(staged, rs_y, 2)
    scatter_on(lent, rs_n1, 3)
    scatter_wait(rs_y, 2)
    scatter_end(staged, rs_y, 2)
    spread(low, dbr_all, 3, "end")
    for q in range(3):
        fetch(rs_y.at[q], act.at[span(q)], 0)

    def out_rows(i, carry):
        here = rows16(i)
        value = act[here, :].astype(F32)
        for q in range(1, 3):
            value = value + act[pl.ds(pl.multiple_of(q * seg + i * ROW_TILE, ROW_TILE), ROW_TILE), :].astype(F32)
        low[here, :] = (mid[here, :] + value).astype(BF)
        return carry

    lax.fori_loop(0, seg // ROW_TILE, out_rows, 0)
    fetch(low, block_out, 0)

    sums_of([("f", c, steps - 1) for c in range(chunks - 3, chunks)])
    scatter_wait(rs_n1, 3)
    scatter_end(lent, rs_n1, 3)
    fetch(rs_n1, stage.at[pl.ds(0, 3)], 0)

    def d_rows(i, carry):
        here = rows16(i)
        dn = arrived(here)
        row = tok[here, :].astype(F32)
        s1 = lax.rsqrt(jnp.mean(row * row, axis=-1, keepdims=True) + EPS_NORM)
        e1 = gains[0:1, :] * dn
        low[here, :] = (
            dmid[here, :] + s1 * e1 - row * (s1 * s1 * s1) * jnp.mean(e1 * row, axis=-1, keepdims=True)
        ).astype(BF)
        g_gains[0] += jnp.sum((dn * row * s1).reshape(ROW_TILE // 8, 8, D), axis=0)
        return carry

    lax.fori_loop(0, seg // ROW_TILE, d_rows, 0)
    fetch(low, input_grad, 0)

    sm_mine[...] = jnp.zeros_like(sm_mine)
    for i in range(2):
        value = jnp.sum(g_gains[i], axis=0, keepdims=True)
        for j in range(D // 128):
            row = i * (D // 128) + j
            sm_mine[row : row + 1, :] = value[:, j * 128 : (j + 1) * 128]
    for n in range(3):
        value = jnp.sum(g_taps[n], axis=0, keepdims=True)
        for k in range(blocks):
            for t2 in range(group):
                row = 2 * (D // 128) + (t2 * 3 + n) * blocks + k
                sm_mine[row : row + 1, :] = jnp.where(t == t2, value[:, k * 128 : (k + 1) * 128], 0.0)
    sm_plane[place] = sm_mine[...]
    plane(sm_mine, sm_plane.at[place], ta_ssem, ta_rsem, "start")

    for k in range(max(0, blocks - 2), blocks):
        pair_send("i", k, "end")

    for k in range(steps - 1):
        sums_of([("i", c, k) for c in range(blocks)])
    plane_wait(sm_mine, ta_rsem)
    value = sm_plane[0]
    for i in range(1, 2 * group):
        value = value + sm_plane[i]
    sm_sum[...] = value
    sm_z[o] = value
    far(sm_sum, sm_z.at[o], tz_ssem, tz_rsem, "start")
    sums_of([("i", c, steps - 1) for c in range(blocks)])
    part_o("end")
    pair_o.wait_send()

    def last_one(k, carry):
        await_bytes(z_o.at[o], come_sem.at[last, peer(k)[0]])
        return carry

    lax.fori_loop(1, out_n, last_one, 0)
    fetch(z_o, sibo, 1)
    value = sibo[0].astype(F32)
    for o2 in range(1, out_n):
        value = value + sibo[o2].astype(F32)
    outo = parto.at[0]
    outo[...] = value.astype(BF)

    def back_o(op):
        switch(
            a == b,
            pltpu.make_async_copy(outo, g_wo, back_rsem.at[last, 0]),
            remote(outo, g_wo, back_ssem.at[last, 0], back_rsem.at[last, 0], (2 * o + b, 2 * y + a)),
            op,
        )

    back_o("start")
    far_wait(sm_sum, tz_rsem)
    value = sm_z[0]
    for i in range(1, out_n):
        value = value + sm_z[i]
    g_small[...] = value

    plane(small_own, small_all.at[mine], sa_ssem, sa_rsem, "end")
    far(planes, planes, sz_ssem, sz_rsem, "end")
    plane(sm_mine, sm_plane.at[place], ta_ssem, ta_rsem, "end")
    far(sm_sum, sm_z.at[o], tz_ssem, tz_rsem, "end")
    spread(tok, tok_all, 0, "end")
    spread(bck_own, bck_all, 1, "end")
    gather_close(0)
    gather_close(1)

    def close(c, carry):
        gather_close(c + 2)
        for k in range(steps):
            step_send("f", c, k, "end")
        hand_back("f", c, "end")
        hand_wait("f", c)
        return carry

    lax.fori_loop(0, chunks, close, 0)
    for k in range(blocks):
        for step in range(steps):
            step_send("i", k, step, "end")
        hand_back("i", k, "end")
        hand_wait("i", k)
    back_o("end")
    await_bytes(g_wo, back_rsem.at[last, 0])


def forward_backward(sizes, tok, bck, wi_own, wo_own, ff_own, small_own):
    (out_n, group, rows_n, seg, ch, cblk, chunks) = sizes
    blocks = ch // 128
    seq = group * seg
    block = rows_n // group
    places = 2 * group
    small_rows = -(-(2 * D // 128 + group * 3 * blocks) // 8) * 8
    items = 2 + chunks
    sums = chunks + blocks + 1
    vm = pltpu.VMEM
    dma = pltpu.SemaphoreType.DMA

    def shape(*dims, dtype=BF):
        return jax.ShapeDtypeStruct(dims, dtype)

    any_spec = pl.BlockSpec(memory_space=pl.ANY)
    vmem_spec = pl.BlockSpec(memory_space=pltpu.VMEM)
    if block % 16 == 0:
        given = [shape(group, chunks, 3, block, WIDTH), shape(group, blocks, 3, block, 128)]
    else:
        given = [shape(chunks, 3, rows_n, WIDTH), shape(blocks, 3, rows_n, 128)]
    outs = [
        shape(seg, D), shape(seg, D), *given, shape(cblk, D), shape(small_rows, 128, dtype=F32),
        shape(chunks, 3, out_n, 2, rows_n, WIDTH), shape(out_n, 2, rows_n, 3 * ch), shape(out_n, 2, cblk, D),
        shape(group, seg, D), shape(seq, D), shape(group, seg, D), shape(group, seg, D), shape(group, seg, D),
        shape(3, seg, D), shape(3, seg, D), shape(3, seg, D), shape(3, seg, D), shape(4, 2, seg // 2, D),
        shape(chunks, 3, out_n, rows_n, WIDTH), shape(blocks, 3, out_n, rows_n, 128), shape(out_n, cblk, D),
        *[shape(chunks, 3, out_n, rows_n, WIDTH), shape(blocks, 3, out_n, rows_n, 128)] * 2, shape(out_n, cblk, D),
        shape(seq, 3 * ch, dtype=F32),
    ]
    out_specs = [any_spec] * 5 + [vmem_spec] + [any_spec] * (len(outs) - 6)
    scratch = [
        vm((2, 3, out_n, 2, rows_n, WIDTH), BF),
        vm((out_n, 2, rows_n, 3 * ch), BF),
        vm((out_n, 2, cblk, D), BF),
        vm((seq, D), BF), vm((D, seq), BF), vm((seq, D), BF), vm((D, seq), BF),
        vm((seq, D), F32), vm((seq + 8, D), F32),
        vm((2, 3, out_n, 2, rows_n, WIDTH), BF),
        vm((3, out_n, rows_n, WIDTH), BF),
        vm((2, 3, out_n, rows_n, WIDTH), BF),
        vm((group, seg, D), BF),
        vm((seq + 8, ch), F32), vm((seq, ch), BF), vm((seq, 3 * ch), BF),
        vm((seg, D), F32), vm((seg, D), F32), vm((seg, D), BF),
        vm((out_n, cblk, D), BF), vm((out_n, cblk, D), BF),
        vm((places * out_n, 8, 128), F32), vm((2, D), F32), vm((3, ch), F32),
        vm((2, 8, D), F32), vm((3, 8, ch), F32),
        vm((small_rows, 128), F32), vm((places, small_rows, 128), F32),
        vm((small_rows, 128), F32), vm((out_n, small_rows, 128), F32),
        vm((seg // 2, D), BF),
        dma((4, 3, 2)), dma((4, group, 2)), dma((4, 2)), dma((4, 4, 2)), dma((4, 3, 2)), dma((4, 2, 2)), dma((4, 2)),
        dma((items, 4, out_n)), dma((items, out_n)), dma((items,)), dma((items,)),
        dma((sums,)), dma((sums,)), dma((sums, out_n)), dma((sums, out_n)), dma((2,)), dma((2, out_n)),
        dma((items, group)), dma((items, group)), dma((sums, group)), dma((sums, group)), dma((1,)),
        dma((places,)), dma((places,)), dma((out_n,)), dma((out_n,)),
        dma((places,)), dma((places,)), dma((out_n,)), dma((out_n,)), dma((2,)), dma((5,)),
    ]
    results = pl.pallas_call(
        functools.partial(block_kernel, sizes),
        out_shape=outs,
        in_specs=[vmem_spec] + [any_spec] * 4 + [vmem_spec],
        out_specs=out_specs,
        scratch_shapes=scratch,
        compiler_params=pltpu.CompilerParams(
            collective_id=0, has_side_effects=True, vmem_limit_bytes=63 * 1024 * 1024
        ),
        cost_estimate=pl.CostEstimate(
            flops=6 * seq * D * (4 * ch + 3 * chunks * WIDTH),
            bytes_accessed=200_000_000,
            transcendentals=seq * chunks * WIDTH,
        ),
    )(tok, bck, wi_own, wo_own, ff_own, small_own)
    return results[:6]


def body(
    tokens,
    cotangent,
    lengths,
    intake_weight,
    intake_first,
    intake_second,
    output_weight,
    output_first,
    output_second,
    swiglu_weight,
    swiglu_first,
    swiglu_second,
    down_weight,
    down_first,
    down_second,
    norm_gains,
    gains_first,
    gains_second,
    conv_kernel,
    kernel_first,
    kernel_second,
):
    data_count = lax.axis_size("dp")
    group_count = lax.axis_size("group")
    dp = lax.axis_index("dp")
    member = lax.axis_index("group")
    block = D // (data_count * group_count)
    cblk = -(-block // 16) * 16
    ch = data_count * cblk
    blocks = ch // 128
    hidden_part = FF // group_count
    chunks = -(-hidden_part // WIDTH)
    hidden_full = chunks * WIDTH
    rows_n = D // data_count
    swap = []
    for one in range(data_count):
        for two in range(group_count):
            there = (2 * (one // 2) + two % 2) * group_count + 2 * (two // 2) + one % 2
            swap.append((one * group_count + two, there))

    def cross(value):
        return lax.ppermute(value, ("dp", "group"), swap)

    intake_local = (
        intake_weight.astype(BF)
        .reshape(block, 3, data_count, group_count, block)
        .transpose(3, 0, 1, 2, 4)
    )
    intake_local = jnp.pad(intake_local, ((0, 0),) * 4 + ((0, cblk - block),))
    intake_local = (
        intake_local.reshape(group_count, block, 3, blocks, 128)
        .transpose(0, 1, 3, 2, 4)
        .reshape(group_count, block, 3 * ch)
    )
    ff_local = jnp.concatenate(
        [
            swiglu_weight.astype(BF).reshape(block, 2, group_count, hidden_part),
            down_weight.astype(BF).reshape(block, 1, group_count, hidden_part),
        ],
        axis=1,
    )
    ff_local = jnp.pad(ff_local, ((0, 0),) * 3 + ((0, hidden_full - hidden_part),))
    ff_local = ff_local.reshape(block, 3, group_count, chunks, WIDTH).transpose(2, 3, 1, 0, 4)
    wo_own = jnp.pad(output_weight.astype(BF).reshape(block, D), ((0, cblk - block), (0, 0)))
    if block % 16 == 0:
        wi_own, ff_own = intake_local, ff_local
    else:
        wi_own = lax.all_to_all(intake_local, "group", split_axis=0, concat_axis=0, tiled=True)
        wi_own = cross(wi_own.reshape(rows_n, 3 * ch))
        ff_own = lax.all_to_all(ff_local, "group", split_axis=0, concat_axis=0, tiled=True)
        ff_own = cross(ff_own.transpose(1, 2, 0, 3, 4).reshape(chunks, 3, rows_n, WIDTH))

    number = dp * group_count + member
    share = norm_gains.shape[0]

    def placed(values, lane):
        line = lax.dynamic_update_slice(jnp.zeros((256,), F32), lax.reduce_precision(values, 8, 7), (lane,))
        return line.reshape(2, 128)

    runs = [placed(norm_gains, lax.rem(number * share, 128))]
    for piece in range(3):
        rest = lax.rem(3 * number + piece, data_count * group_count)
        lane = lax.rem(rest // group_count * cblk, 128)
        runs.append(placed(conv_kernel[piece * block : (piece + 1) * block], lane))
    small_own = jnp.concatenate(runs)

    seg_len = tokens.shape[1]
    positions = member * seg_len + lax.iota(jnp.int32, seg_len)
    valid = (positions < lengths[0]).astype(F32)[:, None]
    back_low = (cotangent[0].astype(F32) * valid).astype(BF)

    sizes = (data_count // 2, group_count, rows_n, seg_len, ch, cblk, chunks)
    block_out, input_grad, g_ff, g_wi, g_wo, g_small = forward_backward(
        sizes, tokens[0], back_low, wi_own, wo_own, ff_own, small_own
    )

    if block % 16:
        g_wi = cross(g_wi).reshape(blocks, 3, group_count, block, 128).transpose(2, 0, 1, 3, 4)
        g_wi = lax.all_to_all(g_wi, "group", split_axis=0, concat_axis=0, tiled=True)
        g_ff = cross(g_ff).reshape(chunks, 3, group_count, block, WIDTH).transpose(2, 0, 1, 3, 4)
        g_ff = lax.all_to_all(g_ff, "group", split_axis=0, concat_axis=0, tiled=True)
    g_wi = g_wi.transpose(0, 3, 2, 1, 4).reshape(group_count, block, 3, data_count, cblk)
    intake_grad_flat = g_wi[..., :block].transpose(1, 2, 3, 0, 4).reshape(-1).astype(F32)
    g_ff = g_ff.transpose(3, 2, 0, 1, 4).reshape(block, 3, group_count, hidden_full)
    g_ff = g_ff[..., :hidden_part]
    swiglu_grad_flat = g_ff[:, :2].reshape(-1).astype(F32)
    down_grad_flat = g_ff[:, 2].reshape(-1).astype(F32)
    output_grad_flat = g_wo[:block].reshape(-1).astype(F32)

    gain_rows = 2 * D // 128
    taps_grad = g_small[gain_rows : gain_rows + group_count * 3 * blocks]
    taps_grad = taps_grad.reshape(group_count, 3, data_count, cblk)[..., :block]
    taps_grad = taps_grad.transpose(1, 2, 0, 3).reshape(-1)
    small_shards = (
        lax.dynamic_slice(g_small[:gain_rows].reshape(-1), (number * share,), (share,)),
        lax.dynamic_slice(taps_grad, (number * 3 * block,), (3 * block,)),
    )
    intake_new = update(
        intake_weight, intake_first, intake_second, intake_grad_flat, RATE_MATRIX, DECAY
    )
    output_new = update(
        output_weight, output_first, output_second, output_grad_flat, RATE_MATRIX, DECAY
    )
    swiglu_new = update(
        swiglu_weight, swiglu_first, swiglu_second, swiglu_grad_flat, RATE_MATRIX, DECAY
    )
    down_new = update(down_weight, down_first, down_second, down_grad_flat, RATE_MATRIX, DECAY)
    gains_new = update(norm_gains, gains_first, gains_second, small_shards[0], RATE_VECTOR, 0.0)
    kernel_new = update(
        conv_kernel, kernel_first, kernel_second, small_shards[1], RATE_VECTOR, DECAY
    )
    return (
        block_out[None],
        input_grad[None],
        intake_new[0],
        intake_new[1],
        intake_new[2],
        output_new[0],
        output_new[1],
        output_new[2],
        swiglu_new[0],
        swiglu_new[1],
        swiglu_new[2],
        down_new[0],
        down_new[1],
        down_new[2],
        gains_new[0],
        gains_new[1],
        gains_new[2],
        kernel_new[0],
        kernel_new[1],
        kernel_new[2],
    )


def solution(mesh):
    in_specs = (
        P("dp", "group", None),
        P("dp", "group", None),
        P("dp"),
        P(("dp", "group")),
        P(("dp", "group")),
        P(("dp", "group")),
        P(("dp", "group")),
        P(("dp", "group")),
        P(("dp", "group")),
        P(("dp", "group")),
        P(("dp", "group")),
        P(("dp", "group")),
        P(("dp", "group")),
        P(("dp", "group")),
        P(("dp", "group")),
        P(("dp", "group")),
        P(("dp", "group")),
        P(("dp", "group")),
        P(("dp", "group")),
        P(("dp", "group")),
        P(("dp", "group")),
    )
    out_specs = (
        P("dp", "group", None),
        P("dp", "group", None),
        P(("dp", "group")),
        P(("dp", "group")),
        P(("dp", "group")),
        P(("dp", "group")),
        P(("dp", "group")),
        P(("dp", "group")),
        P(("dp", "group")),
        P(("dp", "group")),
        P(("dp", "group")),
        P(("dp", "group")),
        P(("dp", "group")),
        P(("dp", "group")),
        P(("dp", "group")),
        P(("dp", "group")),
        P(("dp", "group")),
        P(("dp", "group")),
        P(("dp", "group")),
        P(("dp", "group")),
    )
    return jax.shard_map(body, mesh=mesh, in_specs=in_specs, out_specs=out_specs, check_vma=False)
```

```python
import functools

import jax
import jax.numpy as jnp
from jax import lax
from jax.experimental import pallas as pl
from jax.experimental.pallas import tpu as pltpu
from jax.sharding import PartitionSpec as P

D = 1536
FF = 6912
STEP = 5
WIDTH = 256
ROW_TILE = 16

EPS_NORM = 1e-05
BETA_ONE = 0.5
BETA_TWO = 0.5
ADAM_EPS = 1e-08
RATE_MATRIX = 0.02
RATE_VECTOR = 0.2
DECAY = 0.1

MESH = pl.DeviceIdType.MESH
BF = jnp.bfloat16
F32 = jnp.float32


def update(weight, first, second, grad, rate, decay):
    first_new = BETA_ONE * first + (1.0 - BETA_ONE) * grad
    second_new = BETA_TWO * second + (1.0 - BETA_TWO) * grad * grad
    first_hat = first_new / (1.0 - BETA_ONE**STEP)
    second_hat = second_new / (1.0 - BETA_TWO**STEP)
    weight_new = weight - rate * (first_hat / (jnp.sqrt(second_hat) + ADAM_EPS) + decay * weight)
    return (first_new, second_new, weight_new)


def dot(left, right):
    return lax.dot_general(left, right, (((1,), (0,)), ((), ())), preferred_element_type=F32)


def dot_t(left, right):
    return lax.dot_general(left, right, (((1,), (1,)), ((), ())), preferred_element_type=F32)


def await_bytes(ref, sem):
    pltpu.make_async_copy(ref, ref, sem).wait()


def block_kernel(
    sizes,
    tok, bck_own, wi_own, wo_own, ff_own, small_own,
    block_out, input_grad, g_ff, g_wi, g_wo, g_small,
    wf_all, wi_all, wo_all, tok_all, nrm_far, bck_all, n2_all, dbr_all,
    rs_br, rs_y, rs_n2, rs_n1, via,
    sib_f, sib_i, sib_o, come_f, come_i, far_f, far_i, z_o, mixed_far,
    ws, wi, wo, act, act_t, bck, bck_t, acc_y, acc_n, grad, sibv, part, stage,
    prod, gated, dmix, mid, dmid, low, sibo, parto,
    small_all, gains, taps, g_gains, g_taps, sm_mine, sm_plane, sm_sum, sm_z,
    extra, ag_ssem, ag_rsem, ag_fsem, rs_ssem, rs_rsem, via_ssem, via_rsem, z_ssem, z_rsem, f_ssem, f_rsem,
    gs_ssem, gs_rsem, gz_ssem, come_sem, far_sem, buf_sem, own_ssem, own_rsem, back_ssem, back_rsem, osem,
    sa_ssem, sa_rsem, sz_ssem, sz_rsem, ta_ssem, ta_rsem, tz_ssem, tz_rsem, wsem, lsem,
):
    (out_n, group, rows_n, seg, ch, cblk, chunks) = sizes
    block = rows_n // group
    direct = block % 16 == 0
    count = 2 * out_n * group
    blocks = ch // 128
    seq = group * seg
    dp = lax.axis_index("dp")
    g = lax.axis_index("group")
    o, a = dp // 2, lax.rem(dp, 2)
    y, b = g // 2, lax.rem(g, 2)
    t = 2 * y + a
    mate = (dp, g + 1 - 2 * b)

    def peer(k):
        o2 = lax.rem(o + k, out_n)
        return o2, (2 * o2 + a, g)

    barrier = pltpu.get_barrier_semaphore()
    for x2 in range(2):
        for g2 in range(group):
            @pl.when((x2 != a) | (g2 != g))
            def _():
                pl.semaphore_signal(barrier, inc=1, device_id=(2 * o + x2, g2), device_id_type=MESH)

    def greet(k, carry):
        pl.semaphore_signal(barrier, inc=1, device_id=peer(k)[1], device_id_type=MESH)
        return carry

    lax.fori_loop(1, out_n, greet, 0)
    pl.semaphore_wait(barrier, 2 * group - 1 + out_n - 1)

    def remote(src, dst, ssem, rsem, dev):
        return pltpu.make_async_remote_copy(
            src_ref=src, dst_ref=dst, send_sem=ssem, recv_sem=rsem, device_id=dev, device_id_type=MESH
        )

    def switch(alone, local, copy, op):
        if op == "start":
            @pl.when(alone)
            def _():
                local.start()

            @pl.when(jnp.logical_not(alone))
            def _():
                copy.start()
        else:
            @pl.when(jnp.logical_not(alone))
            def _():
                copy.wait_send()

    odd = lax.rem(a + b, 2)
    size = seg // 2
    y_via = odd * y + (1 - odd) * (1 - y)
    h_via = 1 - odd
    partner = (2 * o + odd * a + (1 - odd) * (1 - a), 2 * (odd * (1 - y) + (1 - odd) * y) + b)

    def part_of(h):
        return pl.ds(h * size, size) if isinstance(h, int) else pl.ds(pl.multiple_of(h * size, size), size)

    def spread(src, dst, n, op):
        for d, h in ((1, 0), (2, 1), (1, 1), (2, 0), (0, 0), (0, 1)):
            x2, y2 = (1 - a if d == 1 else a), (1 - y if d == 2 else y)
            one, two = src.at[part_of(h)], dst.at[g, part_of(h)]
            copy = remote(one, two, ag_ssem.at[n, d, h], ag_rsem.at[n, g, h], (2 * o + x2, 2 * y2 + a))
            if d == 0:
                switch(a == b, pltpu.make_async_copy(one, two, ag_rsem.at[n, g, h]), copy, op)
            elif op == "start":
                copy.start()
            else:
                copy.wait_send()
        if op == "end":
            for k in range(2):
                ref = dst.at[2 * y_via + k, part_of(h_via)]
                await_bytes(ref, ag_fsem.at[n, k])

    def spread_on(dst, n):
        for k in range(2):
            q = 2 * y_via + k
            ref = dst.at[q, part_of(h_via)]
            await_bytes(ref, ag_rsem.at[n, q, h_via])
            remote(ref, ref, ag_fsem.at[n, k], ag_rsem.at[n, q, h_via], partner).start()

    def spread_wait(dst, n, q):
        for h in range(2):
            @pl.when((q // 2 != y_via) | (h != h_via))
            def _():
                await_bytes(dst.at[q, part_of(h)], ag_rsem.at[n, q, h])

    def give(terms, dst, n, at, q, h, slot, op="start"):
        one, two = terms(q).at[part_of(h)], dst.at[slot, part_of(h)]
        copy = remote(one, two, rs_ssem.at[n, at, h], rs_rsem.at[n, slot, h], (2 * o + b, q))
        if slot == 0:
            switch(q == g, pltpu.make_async_copy(one, two, rs_rsem.at[n, 0, h]), copy, op)
        elif op == "start":
            copy.start()
        else:
            copy.wait_send()

    def give_half(terms, n, k, h, op):
        q = 2 * (1 - y) + k
        dev = (2 * o + 1 - a, g) if h == 0 else (dp, 2 * (1 - y) + b)
        copy = remote(terms(q).at[part_of(h)], via.at[n, k], via_ssem.at[n, k, h], via_rsem.at[n, k], dev)
        if op == "start":
            copy.start()
        else:
            copy.wait_send()

    def scatter(terms, dst, n, produce):
        for k in range(2):
            q = 2 * (1 - y) + k
            produce(q)

            @pl.when(odd == 1)
            def _():
                give_half(terms, n, k, 0, "start")
                give_half(terms, n, k, 1, "start")

            @pl.when(odd == 0)
            def _():
                give(terms, dst, n, k, q, 1, 1)

        for k in range(2):
            q = 2 * y + k
            produce(q)

            @pl.when(odd == 1)
            def _():
                give(terms, dst, n, 2 + k, q, 0, 2)

            @pl.when(odd == 0)
            def _():
                give(terms, dst, n, 2 + k, q, 0, 0)
                give(terms, dst, n, 2 + k, q, 1, 0)

    def scatter_on(terms, dst, n):
        for k in range(2):
            q = 2 * y_via + k
            await_bytes(via.at[n, k], via_rsem.at[n, k])
            fetch(via.at[n, k], extra, 0)

            def add_rows(i, carry):
                here = pl.ds(pl.multiple_of(odd * size + i * ROW_TILE, ROW_TILE), ROW_TILE)
                ref = terms(q)
                ref[here, :] = (ref[here, :].astype(F32) + extra[rows16(i), :].astype(F32)).astype(BF)
                return carry

            lax.fori_loop(0, size // ROW_TILE, add_rows, 0)

            @pl.when(odd == 1)
            def _():
                give(terms, dst, n, 2 + k, q, 1, 2)

            @pl.when(odd == 0)
            def _():
                give(terms, dst, n, k, q, 0, 1)

    def scatter_end(terms, dst, n):
        @pl.when(odd == 1)
        def _():
            for k in range(2):
                for h in range(2):
                    give_half(terms, n, k, h, "end")
                    give(terms, dst, n, 2 + k, 2 * y + k, h, 2, "end")

        @pl.when(odd == 0)
        def _():
            for k in range(2):
                for h in range(2):
                    give(terms, dst, n, k, 2 * (1 - y) + k, h, 1, "end")
                    give(terms, dst, n, 2 + k, 2 * y + k, h, 0, "end")

    def scatter_wait(dst, n):
        for slot in range(3):
            for h in range(2):
                await_bytes(dst.at[slot, part_of(h)], rs_rsem.at[n, slot, h])

    def staged(q):
        return stage.at[q]

    def any_span(q):
        return pl.ds(pl.multiple_of(q * seg, seg), seg)

    def slot_of(i, o2, p):
        if isinstance(i, int) and i == 0:
            return wi_all.at[o2, p]
        if isinstance(i, int) and i == 1:
            return wo_all.at[o2, p]
        return wf_all.at[i - 2, :, o2, p]

    def half_of(i, p):
        if isinstance(i, int) and i == 0:
            return wi_all.at[:, p]
        if isinstance(i, int) and i == 1:
            return wo_all.at[:, p]
        return wf_all.at[i - 2, :, :, p]

    my_rows = pl.ds(pl.multiple_of(g * block, 4), block)

    def own_send(i, op):
        if isinstance(i, int) and i == 1:
            dst = wo_all.at[o, a]
            switch(
                a == b,
                pltpu.make_async_copy(wo_own, dst, own_rsem.at[1, 0]),
                remote(wo_own, dst, own_ssem.at[1, 0], own_rsem.at[1, 0], (2 * o + b, 2 * y + a)),
                op,
            )
            return
        if not direct:
            src = wi_own if isinstance(i, int) and i == 0 else ff_own.at[i - 2]
            if op == "start":
                pltpu.make_async_copy(src, slot_of(i, o, b), own_rsem.at[i, 0]).start()
            return
        for t2 in range(group):
            ty, tx = t2 // 2, t2 % 2
            if isinstance(i, int) and i == 0:
                src, dst = wi_own.at[t2], wi_all.at[o, a, my_rows]
            else:
                src, dst = ff_own.at[t2, i - 2], wf_all.at[i - 2, :, o, a, my_rows]
            switch(
                (tx == a) & (ty == y) & (a == b),
                pltpu.make_async_copy(src, dst, own_rsem.at[i, g]),
                remote(src, dst, own_ssem.at[i, t2], own_rsem.at[i, g], (2 * o + tx, 2 * ty + a)),
                op,
            )

    def own_wait(i):
        if not direct or isinstance(i, int) and i == 1:
            await_bytes(slot_of(i, o, b), own_rsem.at[i, 0])
            return
        for q in range(group):
            if isinstance(i, int) and i == 0:
                await_bytes(wi_all.at[o, b, pl.ds(q * block, block)], own_rsem.at[i, q])
            else:
                await_bytes(wf_all.at[i - 2, :, o, b, pl.ds(q * block, block)], own_rsem.at[i, q])

    first, final = o == 0, o == out_n - 1

    def piece_copy(i, src, side, far_by=1):
        ref = slot_of(i, src, b)
        dev = (2 * (o + far_by * (1 - 2 * side)) + a, g)
        return remote(ref, ref, z_ssem.at[i, 2 * side + far_by - 1, src], z_rsem.at[i, src], dev)

    def when(condition, call, *args):
        @pl.when(condition)
        def _():
            call(*args)

    def own_pieces(i, op):
        for side in range(2):
            for far_by in range(1, min(3, out_n)):
                copy = piece_copy(i, o, side, far_by)
                when((o >= far_by) if side else (o + far_by < out_n), copy.start if op == "start" else copy.wait_send)

    def pass_on(i, h, op="start"):
        for side in range(2):
            src = o + h if side else o - h
            there = (src < out_n) & (o > 0) if side else (src >= 0) & (o < out_n - 1)

            @pl.when((src < out_n) if side else (src >= 0))
            def _(src=src, side=side):
                if op == "start":
                    await_bytes(slot_of(i, src, b), z_rsem.at[i, src])

            @pl.when(there)
            def _(src=src, side=side):
                copy = piece_copy(i, src, side)
                copy.start() if op == "start" else copy.wait_send()

    def to_mate(i):
        for h in sorted({1, out_n - 1}):
            for side in range(2):
                src = o + h if side else o - h

                @pl.when((src < out_n) if side else (src >= 0))
                def _(src=src):
                    await_bytes(slot_of(i, src, b), z_rsem.at[i, src])

        remote(half_of(i, b), half_of(i, b), f_ssem.at[i], f_rsem.at[i], mate).start()

    items = 2 + chunks
    sent = set()

    def own_start(*which):
        for i in which:
            if i < items and i not in sent:
                sent.add(i)
                own_send(i, "start")

    def leave(i):
        own_wait(i)
        own_pieces(i, "start")

    def pump(time):
        work = [(time + 1, leave, ())]
        work += [(time - n, pass_on, (n + 1,)) for n in range(1, out_n - 2)]
        work += [(time - (out_n - 2), to_mate, ())]
        if isinstance(time, int):
            own_start(*range(time + 2))
        for i, call, args in work:
            if isinstance(i, int):
                if 0 <= i < items:
                    call(i, *args)
            else:
                when(i < items, call, i, *args)

    def gather_wait(i):
        await_bytes(half_of(i, 1 - b), f_rsem.at[i])

    def gather_close(i):
        own_pieces(i, "end")
        for h in range(2, out_n - 1):
            pass_on(i, h, "end")
        await_bytes(half_of(i, b), f_ssem.at[i])
        own_send(i, "end")

    def fetch(src, dst, n):
        copy = pltpu.make_async_copy(src, dst, lsem.at[n])
        copy.start()
        copy.wait()

    def span(q):
        return pl.ds(q * seg, seg)

    def rows16(i):
        return pl.ds(pl.multiple_of(i * ROW_TILE, ROW_TILE), ROW_TILE)

    def lanes(k, j):
        return pl.ds(k * 384 + j * 128, 128)

    place = a * group + g
    mine = o * (2 * group) + place

    def plane(src, dst, ssem, rsem, op):
        for x2 in range(2):
            for g2 in range(group):
                @pl.when((x2 != a) | (g2 != g))
                def _():
                    copy = remote(src, dst, ssem.at[x2 * group + g2], rsem.at[place], (2 * o + x2, g2))
                    if op == "start":
                        copy.start()
                    else:
                        copy.wait_send()

    def plane_wait(ref, rsem):
        for x2 in range(2):
            for g2 in range(group):
                @pl.when((x2 != a) | (g2 != g))
                def _():
                    await_bytes(ref, rsem.at[x2 * group + g2])

    def far(src, dst, ssem, rsem, op):
        def one(k, carry):
            copy = remote(src, dst, ssem.at[k], rsem.at[o], peer(k)[1])
            if op == "start":
                copy.start()
            else:
                copy.wait_send()
            return carry

        lax.fori_loop(1, out_n, one, 0)

    def far_wait(ref, rsem):
        def one(k, carry):
            await_bytes(ref, rsem.at[peer(k)[0]])
            return carry

        lax.fori_loop(1, out_n, one, 0)

    planes = small_all.at[pl.ds(o * 2 * group, 2 * group)]
    pltpu.make_async_copy(small_own, small_all.at[mine], lsem.at[2]).start()
    plane(small_own, small_all.at[mine], sa_ssem, sa_rsem, "start")

    def convolved(q, col):
        return (
            taps[0:1, col] * prod[pl.ds(q * seg + 6, seg), col]
            + taps[1:2, col] * prod[pl.ds(q * seg + 7, seg), col]
            + taps[2:3, col] * prod[pl.ds(q * seg + 8, seg), col]
        )

    own_start(0)
    own_start(1)
    own_start(2)
    spread(tok, tok_all, 0, "start")
    own_start(3)
    own_start(4)
    prod[pl.ds(0, 8), :] = jnp.zeros((8, ch), F32)
    leave(0)
    pump(0)
    await_bytes(small_own, lsem.at[2])
    plane_wait(small_own, sa_rsem)
    far(planes, planes, sz_ssem, sz_rsem, "start")
    pump(1)
    far_wait(planes, sz_rsem)
    spread_on(tok_all, 0)

    share = 2 * D // count
    rows_of = {}
    for n in range(count):
        row = n * share // 128
        rows_of.setdefault(row, []).append((n, 0))
        if (n * share + share - 1) // 128 > row:
            rows_of.setdefault(row + 1, []).append((n, 1))
    for tile, pieces in rows_of.items():
        value = sum(small_all[n, r : r + 1, :] for n, r in pieces)
        i, j = tile // (D // 128), tile % (D // 128)
        gains[i : i + 1, j * 128 : (j + 1) * 128] = value
    rows_of = {}
    for m in range(3 * count):
        n, piece = m // 3, m % 3
        tap, rest = m // count, m % count
        lane = rest // group * cblk
        rows_of.setdefault((tap, lane // 128), []).append((n, 2 + 2 * piece, rest % group))
        if (lane + block - 1) // 128 > lane // 128:
            rows_of.setdefault((tap, lane // 128 + 1), []).append((n, 3 + 2 * piece, rest % group))
    for (tap, tile), pieces in rows_of.items():
        value = jnp.zeros((1, 128), F32)
        for t2 in range(group):
            value = value + jnp.where(t == t2, sum(small_all[n, r : r + 1, :] for n, r, p in pieces if p == t2), 0.0)
        taps[tap : tap + 1, tile * 128 : (tile + 1) * 128] = value

    pump(2)
    for q in range(group):
        spread_wait(tok_all, 0, q)
        fetch(tok_all.at[q], act.at[span(q)], 0)

        def normed_rows(i, carry, q=q):
            here = pl.ds(pl.multiple_of(q * seg + i * ROW_TILE, ROW_TILE), ROW_TILE)
            row = act[here, :].astype(F32)
            s1 = lax.rsqrt(jnp.mean(row * row, axis=-1, keepdims=True) + EPS_NORM)
            act[here, :] = (row * s1 * gains[0:1, :]).astype(BF)
            return carry

        lax.fori_loop(0, seg // ROW_TILE, normed_rows, 0, unroll=2)
    spread(bck_own, bck_all, 1, "start")
    own_start(5)
    keep_normed = pltpu.make_async_copy(act, nrm_far, lsem.at[2])
    keep_normed.start()
    for time in range(3, out_n):
        pump(time)
    gather_wait(0)
    fetch(wi_all, wi, 0)
    keep_normed.wait()

    for q in range(group):
        for k in range(blocks):
            acc_y[span(q), pl.ds(k * 384, 384)] = dot(
                act[span(q), :], wi[:, :, :, pl.ds(k * 384, 384)].reshape(D, 384)
            )
        for k in range(blocks):
            col = pl.ds(k * 128, 128)
            prod[pl.ds(q * seg + 8, seg), col] = acc_y[span(q), lanes(k, 0)] * acc_y[span(q), lanes(k, 2)]
            gated[span(q), col] = (acc_y[span(q), lanes(k, 1)] * convolved(q, col)).astype(BF)
    spread_on(bck_all, 1)
    gather_wait(1)
    fetch(wo_all, wo, 0)

    def branch(q):
        for n in range(4):
            col = pl.ds(n * 384, 384)
            stage[q, :, col] = dot(gated[any_span(q), :], wo[:, :, :, col].reshape(ch, 384)).astype(BF)

    scatter(staged, rs_br, 0, branch)
    pump(out_n)
    scatter_on(staged, rs_br, 0)
    spill = pltpu.make_async_copy(acc_y.at[:, pl.ds(0, 3 * ch)], mixed_far, lsem.at[2])
    spill.start()
    own_start(6)
    for q in range(group):
        spread_wait(bck_all, 1, q)
        fetch(bck_all.at[q], bck.at[span(q)], 0)
        bck_t[:, span(q)] = bck[span(q), :].T

    pump(out_n + 1)
    scatter_wait(rs_br, 0)
    scatter_end(staged, rs_br, 0)
    fetch(rs_br, stage.at[pl.ds(0, 3)], 0)

    def arrived(here):
        total = stage[0, here, :].astype(F32)
        for q in range(1, 3):
            total = total + stage[q, here, :].astype(F32)
        return total

    def middle_rows(i, carry):
        here = rows16(i)
        mi = tok[here, :].astype(F32) + arrived(here)
        mid[here, :] = mi
        s2 = lax.rsqrt(jnp.mean(mi * mi, axis=-1, keepdims=True) + EPS_NORM)
        low[here, :] = (mi * s2 * gains[1:2, :]).astype(BF)
        return carry

    lax.fori_loop(0, seg // ROW_TILE, middle_rows, 0)
    spread(low, n2_all, 2, "start")
    own_start(*range(items))
    pump(out_n + 2)
    spread_on(n2_all, 2)
    gather_wait(2)
    pltpu.make_async_copy(wf_all.at[0], ws.at[0], wsem.at[0]).start()
    spill.wait()

    def clear(i, carry):
        here = rows16(i)
        acc_y[here, :] = jnp.zeros((ROW_TILE, D), F32)
        acc_n[here, :] = jnp.zeros((ROW_TILE, D), F32)
        return carry

    lax.fori_loop(0, seq // ROW_TILE, clear, 0)
    for q in range(group):
        spread_wait(n2_all, 2, q)
        fetch(n2_all.at[q], act.at[span(q)], 0)
        act_t[:, span(q)] = act[span(q), :].T


    def chunk_refs(kind, c):
        if kind == "f":
            return lax.rem(c, 2), c, sib_f.at[c], pl.ds(0, WIDTH)
        n = chunks + c
        return n % 2, n, sib_i.at[c], pl.ds(0, 128)

    def pair_send(kind, c, op):
        s, n, sib, cols = chunk_refs(kind, c)
        copy = remote(grad.at[s, :, :, 1 - b, :, cols], sib, gs_ssem.at[n], gs_rsem.at[n], mate)
        if op == "start":
            copy.start()
        else:
            copy.wait_send()

    steps = out_n.bit_length() - 1

    def halves_refs(kind, c):
        return (come_f if kind == "f" else come_i).at[c], (far_f if kind == "f" else far_i).at[c]

    def flipped(k):
        m = 1 << k
        return o + m - 2 * m * lax.rem(o // m, 2)

    def kept(device, k, i):
        return lax.rem(device, 2 << k) + (2 << k) * i

    def step_at(k):
        return out_n - (out_n >> k), out_n >> (k + 1)

    def step_send(kind, c, k, op="start"):
        _, n, _, _ = chunk_refs(kind, c)
        come, mine_far = halves_refs(kind, c)
        at, number = step_at(k)
        there = flipped(k)
        for i in range(number):
            copy = remote(
                mine_far.at[:, kept(there, k, i)], come.at[:, at + i],
                gz_ssem.at[n, at + i], come_sem.at[n, at + i], (2 * there + a, g),
            )
            if op == "start":
                copy.start()
            else:
                copy.wait_send()

    def pair_fetch(kind, c, op):
        s, n, sib, cols = chunk_refs(kind, c)
        if op == "start":
            await_bytes(sib, gs_rsem.at[n])
        copy = pltpu.make_async_copy(sib, sibv.at[:, :, :, cols], lsem.at[1])
        copy.start() if op == "start" else copy.wait()

    def pair_far(kind, c):
        s, n, _, cols = chunk_refs(kind, c)
        return pltpu.make_async_copy(part.at[s, :, :, :, cols], halves_refs(kind, c)[1], far_sem.at[s])

    def pair_add(kind, c):
        s, n, _, cols = chunk_refs(kind, c)
        pair_fetch(kind, c, "end")

        def one(i, carry):
            j, o2 = i // out_n, lax.rem(i, out_n)
            part[s, j, o2, :, cols] = (
                grad[s, j, o2, b, :, cols].astype(F32) + sibv[j, o2, :, cols].astype(F32)
            ).astype(BF)
            return carry

        lax.fori_loop(0, 3 * out_n, one, 0)
        pair_far(kind, c).start()

    def first_send(kind, c):
        pair_far(kind, c).wait()
        step_send(kind, c, 0)

    def stage_ask(job, buf, op):
        kind, c, k = job
        _, n, _, cols = chunk_refs(kind, c)
        come, mine_far = halves_refs(kind, c)
        at, number = step_at(k)
        for i in range(number):
            if op == "start":
                await_bytes(come.at[:, at + i], come_sem.at[n, at + i])
            for m, src in ((i, come.at[:, at + i]), (number + i, mine_far.at[:, kept(o, k, i)])):
                copy = pltpu.make_async_copy(src, part.at[buf, :, m, :, cols], buf_sem.at[buf, m])
                copy.start() if op == "start" else copy.wait()

    def stage_back(job, buf, op):
        kind, c, k = job
        _, n, _, cols = chunk_refs(kind, c)
        mine_far = halves_refs(kind, c)[1]
        at, number = step_at(k)
        for i in range(number):
            m = number + i
            copy = pltpu.make_async_copy(
                part.at[buf, :, m, :, cols], mine_far.at[:, kept(o, k, i)], buf_sem.at[buf, m]
            )
            copy.start() if op == "start" else copy.wait()

    def stage_add(job, buf):
        kind, c, k = job
        _, n, _, cols = chunk_refs(kind, c)
        h, _, place_o, place_p = out_slot(n)
        at, number = step_at(k)

        def add(i, carry):
            j, r = i // (rows_n // 48), lax.rem(i, rows_n // 48)
            here = pl.ds(pl.multiple_of(r * 48, 16), 48)
            for m in range(number):
                value = (
                    part[buf, j, m, here, cols].astype(F32) + part[buf, j, number + m, here, cols].astype(F32)
                ).astype(BF)
                if k == steps - 1:
                    ws[h, j, place_o, place_p, here, cols] = value
                else:
                    part[buf, j, number + m, here, cols] = value
            return carry

        lax.fori_loop(0, 3 * (rows_n // 48), add, 0)
        if k == steps - 1:
            hand_back(kind, c, "start")
        else:
            stage_back(job, buf, "start")

    def stage_on(job, buf):
        kind, c, k = job
        if k < steps - 1:
            stage_back(job, buf, "end")
            step_send(kind, c, k + 1)

    def sums_of(jobs):
        for i, job in enumerate(jobs):
            if i == 0:
                stage_ask(job, 0, "start")
            if i >= 1:
                stage_on(jobs[i - 1], (i - 1) % 2)
            if i + 1 < len(jobs):
                stage_ask(jobs[i + 1], (i + 1) % 2, "start")
            stage_ask(job, i % 2, "end")
            stage_add(job, i % 2)
        stage_on(jobs[-1], (len(jobs) - 1) % 2)

    def out_slot(n):
        return (n // (2 * out_n), slice(None), lax.rem(n, 2 * out_n) // 2, lax.rem(n, 2))

    def hand_back(kind, c, op):
        _, n, _, cols = chunk_refs(kind, c)
        dst = (g_ff if kind == "f" else g_wi)
        if not direct:
            if op == "start":
                h, _, o2, p = out_slot(n)
                fetch(ws.at[h, :, o2, p, :, cols], dst.at[c], 1)
            return
        h, _, o2, p = out_slot(n)
        for q in range(group):
            src = ws.at[h, :, o2, p, pl.ds(q * block, block), cols]
            switch(
                (a == b) & (q == g),
                pltpu.make_async_copy(src, dst.at[t, c], back_rsem.at[n, t]),
                remote(src, dst.at[t, c], back_ssem.at[n, q], back_rsem.at[n, t], (2 * o + b, q)),
                op,
            )

    def hand_wait(kind, c):
        if direct:
            _, n, _, _ = chunk_refs(kind, c)
            for t2 in range(group):
                await_bytes((g_ff if kind == "f" else g_wi).at[t2, c], back_rsem.at[n, t2])

    half = out_n // 2

    def grad_rows(h):
        return pl.ds(pl.multiple_of(h * (D // 2), D // 2), D // 2), pl.ds(h * half, half)

    loop_pump = out_n + 3

    def d_normed_two(q):
        stage[q] = acc_n[any_span(q), :].astype(BF)

    def hidden_chunk(c, carry):
        s = lax.rem(c, 2)
        await_bytes(ws.at[s], wsem.at[s])
        hid, dgt, dup = (pl.ds(j * WIDTH, WIDTH) for j in range(3))

        def token_tile(m, carry):
            here = pl.ds(pl.multiple_of(m * (seq // 2), seq // 2), seq // 2)
            n2 = act[here, :]
            gate = dot(n2, ws[s, 0].reshape(D, WIDTH))
            upper = dot(n2, ws[s, 1].reshape(D, WIDTH))
            d_hidden = dot(bck[here, :], ws[s, 2].reshape(D, WIDTH))
            sigma = jax.nn.sigmoid(gate)
            active = gate * sigma
            dmix[here, hid] = (active * upper).astype(BF)
            dmix[here, dgt] = (d_hidden * upper * (sigma * (1.0 + gate * (1.0 - sigma)))).astype(BF)
            dmix[here, dup] = (d_hidden * active).astype(BF)
            acc_y[here, :] += dot_t(dmix[here, hid], ws[s, 2].reshape(D, WIDTH))
            acc_n[here, :] += dot_t(dmix[here, dgt], ws[s, 0].reshape(D, WIDTH))
            acc_n[here, :] += dot_t(dmix[here, dup], ws[s, 1].reshape(D, WIDTH))
            return carry

        lax.fori_loop(0, 2, token_tile, 0)

        @pl.when(c >= 1)
        def _():
            pair_fetch("f", c - 1, "start")

        @pl.when(c >= 2)
        def _():
            first_send("f", c - 2)

        @pl.when(c >= 2)
        def _():
            pair_send("f", c - 2, "end")

        def grad_tile(h, carry):
            rows, os = grad_rows(h)
            shape = (half, 2, rows_n, WIDTH)
            grad[s, 0, os] = dot(act_t[rows, :], dmix[:, dgt]).astype(BF).reshape(shape)
            grad[s, 1, os] = dot(act_t[rows, :], dmix[:, dup]).astype(BF).reshape(shape)
            grad[s, 2, os] = dot(bck_t[rows, :], dmix[:, hid]).astype(BF).reshape(shape)
            return carry

        lax.fori_loop(0, 2, grad_tile, 0)
        pair_send("f", c, "start")

        @pl.when(c >= 1)
        def _():
            pair_add("f", c - 1)

        pump(c + loop_pump)

        @pl.when(c + 1 < chunks)
        def _():
            gather_wait(c + 3)
            pltpu.make_async_copy(wf_all.at[c + 1], ws.at[1 - s], wsem.at[1 - s]).start()

        return carry

    lax.fori_loop(0, chunks, hidden_chunk, 0)

    scatter(staged, rs_n2, 1, d_normed_two)
    first_send("f", chunks - 2)
    pair_fetch("f", chunks - 1, "start")
    pair_add("f", chunks - 1)
    scatter_on(staged, rs_n2, 1)
    first_send("f", chunks - 1)
    for k in range(steps - 1):
        sums_of([("f", c, k) for c in range(chunks - 2)])
    scatter_wait(rs_n2, 1)
    scatter_end(staged, rs_n2, 1)
    spread(low, n2_all, 2, "end")
    fetch(rs_n2, stage.at[pl.ds(0, 3)], 0)
    fetch(bck_own, act.at[span(0)], 0)
    g_gains[...] = jnp.zeros_like(g_gains)

    def d_middle_rows(i, carry):
        here = rows16(i)
        dn = arrived(here)
        mi = mid[here, :]
        s2 = lax.rsqrt(jnp.mean(mi * mi, axis=-1, keepdims=True) + EPS_NORM)
        e2 = gains[1:2, :] * dn
        back = act[here, :].astype(F32)
        dm = back + s2 * e2 - mi * (s2 * s2 * s2) * jnp.mean(e2 * mi, axis=-1, keepdims=True)
        dmid[here, :] = dm
        low[here, :] = dm.astype(BF)
        g_gains[1] += jnp.sum((dn * mi * s2).reshape(ROW_TILE // 8, 8, D), axis=0)
        return carry

    lax.fori_loop(0, seg // ROW_TILE, d_middle_rows, 0)
    spread(low, dbr_all, 3, "start")

    for q in range(group):
        stage[q] = acc_y[span(q), :].astype(BF)
    spill_back = pltpu.make_async_copy(mixed_far, acc_y.at[:, pl.ds(0, 3 * ch)], lsem.at[2])
    spill_back.start()

    for q in range(group):
        bck_t[pl.ds(0, ch), span(q)] = gated[span(q), :].T
        fetch(nrm_far.at[span(q)], act.at[span(q)], 0)
        act_t[:, span(q)] = act[span(q), :].T
    spill_back.wait()
    spread_on(dbr_all, 3)
    for k in range(steps - 1):
        sums_of([("f", c, k) for c in range(chunks - 2, chunks)])
    sums_of([("f", c, steps - 1) for c in range(chunks - 3)])

    acc_n[pl.ds(seq, 8), pl.ds(0, ch)] = jnp.zeros((8, ch), F32)
    for q in range(group):
        spread_wait(dbr_all, 3, q)
        fetch(dbr_all.at[q], bck.at[span(q)], 0)
        acc_n[span(q), pl.ds(ch, ch)] = dot_t(bck[span(q), :], wo[...].reshape(ch, D))
        for k in range(blocks):
            col = pl.ds(k * 128, 128)
            d_gated = acc_n[span(q), pl.ds(ch + k * 128, 128)]
            acc_n[span(q), col] = d_gated * acc_y[span(q), lanes(k, 1)]
            dmix[span(q), lanes(k, 1)] = (d_gated * convolved(q, col)).astype(BF)
    scatter(staged, rs_y, 2, lambda q: None)
    g_taps[...] = jnp.zeros_like(g_taps)
    for q in range(group):
        for k in range(blocks):
            col = pl.ds(k * 128, 128)
            d0 = acc_n[span(q), col]
            for n in range(3):
                g_taps[n, :, col] += jnp.sum(
                    (d0 * prod[pl.ds(q * seg + 6 + n, seg), col]).reshape(seg // 8, 8, 128), axis=0
                )
            d_product = (
                taps[2:3, col] * d0
                + taps[1:2, col] * acc_n[pl.ds(q * seg + 1, seg), col]
                + taps[0:1, col] * acc_n[pl.ds(q * seg + 2, seg), col]
            )
            dmix[span(q), lanes(k, 0)] = (d_product * acc_y[span(q), lanes(k, 2)]).astype(BF)
            dmix[span(q), lanes(k, 2)] = (d_product * acc_y[span(q), lanes(k, 0)]).astype(BF)

    for k in range(blocks):
        s = (chunks + k) % 2
        if k < 2:
            pair_send("f", chunks - 2 + k, "end")
        else:
            pair_send("i", k - 2, "end")

        def intake_tile(h, carry, k=k, s=s):
            rows, os = grad_rows(h)
            value = dot(act_t[rows, :], dmix[:, pl.ds(k * 384, 384)]).astype(BF)
            for j in range(3):
                grad[s, j, os, :, :, pl.ds(0, 128)] = value[:, j * 128 : (j + 1) * 128].reshape(
                    half, 2, rows_n, 128
                )
            return carry

        lax.fori_loop(0, 2, intake_tile, 0)
        pair_send("i", k, "start")
        if k >= 1:
            pair_fetch("i", k - 1, "start")
            if k >= 2:
                first_send("i", k - 2)
            pair_add("i", k - 1)

    for n in range(4):
        col = pl.ds(n * 384, 384)
        wo[:, :, :, col] = dot(bck_t[pl.ds(0, ch), :], bck[:, col]).astype(BF).reshape(out_n, 2, cblk, 384)
    last = chunks + blocks
    pair_o = remote(wo.at[:, 1 - b], sib_o, gs_ssem.at[last], gs_rsem.at[last], mate)
    pair_o.start()
    if blocks >= 2:
        first_send("i", blocks - 2)
    pair_fetch("i", blocks - 1, "start")
    pair_add("i", blocks - 1)
    first_send("i", blocks - 1)

    await_bytes(sib_o, gs_rsem.at[last])
    fetch(sib_o, sibo, 1)

    def add_o(o2, carry):
        parto[o2] = (wo[o2, b].astype(F32) + sibo[o2].astype(F32)).astype(BF)
        return carry

    lax.fori_loop(0, out_n, add_o, 0)

    def part_o(op):
        def one(k, carry):
            o2, dev = peer(k)
            copy = remote(parto.at[o2], z_o.at[o], gz_ssem.at[last, k], come_sem.at[last, o], dev)
            if op == "start":
                copy.start()
            else:
                copy.wait_send()
            return carry

        lax.fori_loop(1, out_n, one, 0)
        keep = pltpu.make_async_copy(parto.at[o], z_o.at[o], osem.at[0])
        if op == "start":
            keep.start()
        else:
            keep.wait()

    part_o("start")

    def lent(q):
        return bck.at[any_span(q)]

    def d_normed(q):
        for n in range(4):
            bck[any_span(q), pl.ds(n * 384, 384)] = dot_t(
                dmix[any_span(q), :], wi[pl.ds(n * out_n // 4, out_n // 4)].reshape(384, 3 * ch)
            ).astype(BF)

    scatter(lent, rs_n1, 3, d_normed)
    scatter_on(staged, rs_y, 2)
    scatter_on(lent, rs_n1, 3)
    scatter_wait(rs_y, 2)
    scatter_end(staged, rs_y, 2)
    spread(low, dbr_all, 3, "end")
    for q in range(3):
        fetch(rs_y.at[q], act.at[span(q)], 0)

    def out_rows(i, carry):
        here = rows16(i)
        value = act[here, :].astype(F32)
        for q in range(1, 3):
            value = value + act[pl.ds(pl.multiple_of(q * seg + i * ROW_TILE, ROW_TILE), ROW_TILE), :].astype(F32)
        low[here, :] = (mid[here, :] + value).astype(BF)
        return carry

    lax.fori_loop(0, seg // ROW_TILE, out_rows, 0)
    fetch(low, block_out, 0)

    sums_of([("f", c, steps - 1) for c in range(chunks - 3, chunks)])
    scatter_wait(rs_n1, 3)
    scatter_end(lent, rs_n1, 3)
    fetch(rs_n1, stage.at[pl.ds(0, 3)], 0)

    def d_rows(i, carry):
        here = rows16(i)
        dn = arrived(here)
        row = tok[here, :].astype(F32)
        s1 = lax.rsqrt(jnp.mean(row * row, axis=-1, keepdims=True) + EPS_NORM)
        e1 = gains[0:1, :] * dn
        low[here, :] = (
            dmid[here, :] + s1 * e1 - row * (s1 * s1 * s1) * jnp.mean(e1 * row, axis=-1, keepdims=True)
        ).astype(BF)
        g_gains[0] += jnp.sum((dn * row * s1).reshape(ROW_TILE // 8, 8, D), axis=0)
        return carry

    lax.fori_loop(0, seg // ROW_TILE, d_rows, 0)
    fetch(low, input_grad, 0)

    sm_mine[...] = jnp.zeros_like(sm_mine)
    for i in range(2):
        value = jnp.sum(g_gains[i], axis=0, keepdims=True)
        for j in range(D // 128):
            row = i * (D // 128) + j
            sm_mine[row : row + 1, :] = value[:, j * 128 : (j + 1) * 128]
    for n in range(3):
        value = jnp.sum(g_taps[n], axis=0, keepdims=True)
        for k in range(blocks):
            for t2 in range(group):
                row = 2 * (D // 128) + (t2 * 3 + n) * blocks + k
                sm_mine[row : row + 1, :] = jnp.where(t == t2, value[:, k * 128 : (k + 1) * 128], 0.0)
    sm_plane[place] = sm_mine[...]
    plane(sm_mine, sm_plane.at[place], ta_ssem, ta_rsem, "start")

    for k in range(max(0, blocks - 2), blocks):
        pair_send("i", k, "end")

    for k in range(steps - 1):
        sums_of([("i", c, k) for c in range(blocks)])
    plane_wait(sm_mine, ta_rsem)
    value = sm_plane[0]
    for i in range(1, 2 * group):
        value = value + sm_plane[i]
    sm_sum[...] = value
    sm_z[o] = value
    far(sm_sum, sm_z.at[o], tz_ssem, tz_rsem, "start")
    sums_of([("i", c, steps - 1) for c in range(blocks)])
    part_o("end")
    pair_o.wait_send()

    def last_one(k, carry):
        await_bytes(z_o.at[o], come_sem.at[last, peer(k)[0]])
        return carry

    lax.fori_loop(1, out_n, last_one, 0)
    fetch(z_o, sibo, 1)
    value = sibo[0].astype(F32)
    for o2 in range(1, out_n):
        value = value + sibo[o2].astype(F32)
    outo = parto.at[0]
    outo[...] = value.astype(BF)

    def back_o(op):
        switch(
            a == b,
            pltpu.make_async_copy(outo, g_wo, back_rsem.at[last, 0]),
            remote(outo, g_wo, back_ssem.at[last, 0], back_rsem.at[last, 0], (2 * o + b, 2 * y + a)),
            op,
        )

    back_o("start")
    far_wait(sm_sum, tz_rsem)
    value = sm_z[0]
    for i in range(1, out_n):
        value = value + sm_z[i]
    g_small[...] = value

    plane(small_own, small_all.at[mine], sa_ssem, sa_rsem, "end")
    far(planes, planes, sz_ssem, sz_rsem, "end")
    plane(sm_mine, sm_plane.at[place], ta_ssem, ta_rsem, "end")
    far(sm_sum, sm_z.at[o], tz_ssem, tz_rsem, "end")
    spread(tok, tok_all, 0, "end")
    spread(bck_own, bck_all, 1, "end")
    gather_close(0)
    gather_close(1)

    def close(c, carry):
        gather_close(c + 2)
        for k in range(steps):
            step_send("f", c, k, "end")
        hand_back("f", c, "end")
        hand_wait("f", c)
        return carry

    lax.fori_loop(0, chunks, close, 0)
    for k in range(blocks):
        for step in range(steps):
            step_send("i", k, step, "end")
        hand_back("i", k, "end")
        hand_wait("i", k)
    back_o("end")
    await_bytes(g_wo, back_rsem.at[last, 0])


def forward_backward(sizes, tok, bck, wi_own, wo_own, ff_own, small_own):
    (out_n, group, rows_n, seg, ch, cblk, chunks) = sizes
    blocks = ch // 128
    seq = group * seg
    block = rows_n // group
    places = 2 * group
    small_rows = -(-(2 * D // 128 + group * 3 * blocks) // 8) * 8
    items = 2 + chunks
    sums = chunks + blocks + 1
    vm = pltpu.VMEM
    dma = pltpu.SemaphoreType.DMA

    def shape(*dims, dtype=BF):
        return jax.ShapeDtypeStruct(dims, dtype)

    any_spec = pl.BlockSpec(memory_space=pl.ANY)
    vmem_spec = pl.BlockSpec(memory_space=pltpu.VMEM)
    if block % 16 == 0:
        given = [shape(group, chunks, 3, block, WIDTH), shape(group, blocks, 3, block, 128)]
    else:
        given = [shape(chunks, 3, rows_n, WIDTH), shape(blocks, 3, rows_n, 128)]
    outs = [
        shape(seg, D), shape(seg, D), *given, shape(cblk, D), shape(small_rows, 128, dtype=F32),
        shape(chunks, 3, out_n, 2, rows_n, WIDTH), shape(out_n, 2, rows_n, 3 * ch), shape(out_n, 2, cblk, D),
        shape(group, seg, D), shape(seq, D), shape(group, seg, D), shape(group, seg, D), shape(group, seg, D),
        shape(3, seg, D), shape(3, seg, D), shape(3, seg, D), shape(3, seg, D), shape(4, 2, seg // 2, D),
        shape(chunks, 3, out_n, rows_n, WIDTH), shape(blocks, 3, out_n, rows_n, 128), shape(out_n, cblk, D),
        *[shape(chunks, 3, out_n, rows_n, WIDTH), shape(blocks, 3, out_n, rows_n, 128)] * 2, shape(out_n, cblk, D),
        shape(seq, 3 * ch, dtype=F32),
    ]
    out_specs = [any_spec] * 5 + [vmem_spec] + [any_spec] * (len(outs) - 6)
    scratch = [
        vm((2, 3, out_n, 2, rows_n, WIDTH), BF),
        vm((out_n, 2, rows_n, 3 * ch), BF),
        vm((out_n, 2, cblk, D), BF),
        vm((seq, D), BF), vm((D, seq), BF), vm((seq, D), BF), vm((D, seq), BF),
        vm((seq, D), F32), vm((seq + 8, D), F32),
        vm((2, 3, out_n, 2, rows_n, WIDTH), BF),
        vm((3, out_n, rows_n, WIDTH), BF),
        vm((2, 3, out_n, rows_n, WIDTH), BF),
        vm((group, seg, D), BF),
        vm((seq + 8, ch), F32), vm((seq, ch), BF), vm((seq, 3 * ch), BF),
        vm((seg, D), F32), vm((seg, D), F32), vm((seg, D), BF),
        vm((out_n, cblk, D), BF), vm((out_n, cblk, D), BF),
        vm((places * out_n, 8, 128), F32), vm((2, D), F32), vm((3, ch), F32),
        vm((2, 8, D), F32), vm((3, 8, ch), F32),
        vm((small_rows, 128), F32), vm((places, small_rows, 128), F32),
        vm((small_rows, 128), F32), vm((out_n, small_rows, 128), F32),
        vm((seg // 2, D), BF),
        dma((4, 3, 2)), dma((4, group, 2)), dma((4, 2)), dma((4, 4, 2)), dma((4, 3, 2)), dma((4, 2, 2)), dma((4, 2)),
        dma((items, 4, out_n)), dma((items, out_n)), dma((items,)), dma((items,)),
        dma((sums,)), dma((sums,)), dma((sums, out_n)), dma((sums, out_n)), dma((2,)), dma((2, out_n)),
        dma((items, group)), dma((items, group)), dma((sums, group)), dma((sums, group)), dma((1,)),
        dma((places,)), dma((places,)), dma((out_n,)), dma((out_n,)),
        dma((places,)), dma((places,)), dma((out_n,)), dma((out_n,)), dma((2,)), dma((5,)),
    ]
    results = pl.pallas_call(
        functools.partial(block_kernel, sizes),
        out_shape=outs,
        in_specs=[vmem_spec] + [any_spec] * 4 + [vmem_spec],
        out_specs=out_specs,
        scratch_shapes=scratch,
        compiler_params=pltpu.CompilerParams(
            collective_id=0, has_side_effects=True, vmem_limit_bytes=63 * 1024 * 1024
        ),
        cost_estimate=pl.CostEstimate(
            flops=6 * seq * D * (4 * ch + 3 * chunks * WIDTH),
            bytes_accessed=200_000_000,
            transcendentals=seq * chunks * WIDTH,
        ),
    )(tok, bck, wi_own, wo_own, ff_own, small_own)
    return results[:6]


def body(
    tokens,
    cotangent,
    lengths,
    intake_weight,
    intake_first,
    intake_second,
    output_weight,
    output_first,
    output_second,
    swiglu_weight,
    swiglu_first,
    swiglu_second,
    down_weight,
    down_first,
    down_second,
    norm_gains,
    gains_first,
    gains_second,
    conv_kernel,
    kernel_first,
    kernel_second,
):
    data_count = lax.axis_size("dp")
    group_count = lax.axis_size("group")
    dp = lax.axis_index("dp")
    member = lax.axis_index("group")
    block = D // (data_count * group_count)
    cblk = -(-block // 16) * 16
    ch = data_count * cblk
    blocks = ch // 128
    hidden_part = FF // group_count
    chunks = -(-hidden_part // WIDTH)
    hidden_full = chunks * WIDTH
    rows_n = D // data_count
    swap = []
    for one in range(data_count):
        for two in range(group_count):
            there = (2 * (one // 2) + two % 2) * group_count + 2 * (two // 2) + one % 2
            swap.append((one * group_count + two, there))

    def cross(value):
        return lax.ppermute(value, ("dp", "group"), swap)

    intake_local = (
        intake_weight.astype(BF)
        .reshape(block, 3, data_count, group_count, block)
        .transpose(3, 0, 1, 2, 4)
    )
    intake_local = jnp.pad(intake_local, ((0, 0),) * 4 + ((0, cblk - block),))
    intake_local = (
        intake_local.reshape(group_count, block, 3, blocks, 128)
        .transpose(0, 1, 3, 2, 4)
        .reshape(group_count, block, 3 * ch)
    )
    ff_local = jnp.concatenate(
        [
            swiglu_weight.astype(BF).reshape(block, 2, group_count, hidden_part),
            down_weight.astype(BF).reshape(block, 1, group_count, hidden_part),
        ],
        axis=1,
    )
    ff_local = jnp.pad(ff_local, ((0, 0),) * 3 + ((0, hidden_full - hidden_part),))
    ff_local = ff_local.reshape(block, 3, group_count, chunks, WIDTH).transpose(2, 3, 1, 0, 4)
    wo_own = jnp.pad(output_weight.astype(BF).reshape(block, D), ((0, cblk - block), (0, 0)))
    if block % 16 == 0:
        wi_own, ff_own = intake_local, ff_local
    else:
        wi_own = lax.all_to_all(intake_local, "group", split_axis=0, concat_axis=0, tiled=True)
        wi_own = cross(wi_own.reshape(rows_n, 3 * ch))
        ff_own = lax.all_to_all(ff_local, "group", split_axis=0, concat_axis=0, tiled=True)
        ff_own = cross(ff_own.transpose(1, 2, 0, 3, 4).reshape(chunks, 3, rows_n, WIDTH))

    number = dp * group_count + member
    share = norm_gains.shape[0]

    def placed(values, lane):
        line = lax.dynamic_update_slice(jnp.zeros((256,), F32), lax.reduce_precision(values, 8, 7), (lane,))
        return line.reshape(2, 128)

    runs = [placed(norm_gains, lax.rem(number * share, 128))]
    for piece in range(3):
        rest = lax.rem(3 * number + piece, data_count * group_count)
        lane = lax.rem(rest // group_count * cblk, 128)
        runs.append(placed(conv_kernel[piece * block : (piece + 1) * block], lane))
    small_own = jnp.concatenate(runs)

    seg_len = tokens.shape[1]
    positions = member * seg_len + lax.iota(jnp.int32, seg_len)
    valid = (positions < lengths[0]).astype(F32)[:, None]
    back_low = (cotangent[0].astype(F32) * valid).astype(BF)

    sizes = (data_count // 2, group_count, rows_n, seg_len, ch, cblk, chunks)
    block_out, input_grad, g_ff, g_wi, g_wo, g_small = forward_backward(
        sizes, tokens[0], back_low, wi_own, wo_own, ff_own, small_own
    )

    if block % 16:
        g_wi = cross(g_wi).reshape(blocks, 3, group_count, block, 128).transpose(2, 0, 1, 3, 4)
        g_wi = lax.all_to_all(g_wi, "group", split_axis=0, concat_axis=0, tiled=True)
        g_ff = cross(g_ff).reshape(chunks, 3, group_count, block, WIDTH).transpose(2, 0, 1, 3, 4)
        g_ff = lax.all_to_all(g_ff, "group", split_axis=0, concat_axis=0, tiled=True)
    g_wi = g_wi.transpose(0, 3, 2, 1, 4).reshape(group_count, block, 3, data_count, cblk)
    intake_grad_flat = g_wi[..., :block].transpose(1, 2, 3, 0, 4).reshape(-1).astype(F32)
    g_ff = g_ff.transpose(3, 2, 0, 1, 4).reshape(block, 3, group_count, hidden_full)
    g_ff = g_ff[..., :hidden_part]
    swiglu_grad_flat = g_ff[:, :2].reshape(-1).astype(F32)
    down_grad_flat = g_ff[:, 2].reshape(-1).astype(F32)
    output_grad_flat = g_wo[:block].reshape(-1).astype(F32)

    gain_rows = 2 * D // 128
    taps_grad = g_small[gain_rows : gain_rows + group_count * 3 * blocks]
    taps_grad = taps_grad.reshape(group_count, 3, data_count, cblk)[..., :block]
    taps_grad = taps_grad.transpose(1, 2, 0, 3).reshape(-1)
    small_shards = (
        lax.dynamic_slice(g_small[:gain_rows].reshape(-1), (number * share,), (share,)),
        lax.dynamic_slice(taps_grad, (number * 3 * block,), (3 * block,)),
    )
    intake_new = update(
        intake_weight, intake_first, intake_second, intake_grad_flat, RATE_MATRIX, DECAY
    )
    output_new = update(
        output_weight, output_first, output_second, output_grad_flat, RATE_MATRIX, DECAY
    )
    swiglu_new = update(
        swiglu_weight, swiglu_first, swiglu_second, swiglu_grad_flat, RATE_MATRIX, DECAY
    )
    down_new = update(down_weight, down_first, down_second, down_grad_flat, RATE_MATRIX, DECAY)
    gains_new = update(norm_gains, gains_first, gains_second, small_shards[0], RATE_VECTOR, 0.0)
    kernel_new = update(
        conv_kernel, kernel_first, kernel_second, small_shards[1], RATE_VECTOR, DECAY
    )
    return (
        block_out[None],
        input_grad[None],
        intake_new[0],
        intake_new[1],
        intake_new[2],
        output_new[0],
        output_new[1],
        output_new[2],
        swiglu_new[0],
        swiglu_new[1],
        swiglu_new[2],
        down_new[0],
        down_new[1],
        down_new[2],
        gains_new[0],
        gains_new[1],
        gains_new[2],
        kernel_new[0],
        kernel_new[1],
        kernel_new[2],
    )


def solution(mesh):
    in_specs = (
        P("dp", "group", None),
        P("dp", "group", None),
        P("dp"),
        P(("dp", "group")),
        P(("dp", "group")),
        P(("dp", "group")),
        P(("dp", "group")),
        P(("dp", "group")),
        P(("dp", "group")),
        P(("dp", "group")),
        P(("dp", "group")),
        P(("dp", "group")),
        P(("dp", "group")),
        P(("dp", "group")),
        P(("dp", "group")),
        P(("dp", "group")),
        P(("dp", "group")),
        P(("dp", "group")),
        P(("dp", "group")),
        P(("dp", "group")),
        P(("dp", "group")),
    )
    out_specs = (
        P("dp", "group", None),
        P("dp", "group", None),
        P(("dp", "group")),
        P(("dp", "group")),
        P(("dp", "group")),
        P(("dp", "group")),
        P(("dp", "group")),
        P(("dp", "group")),
        P(("dp", "group")),
        P(("dp", "group")),
        P(("dp", "group")),
        P(("dp", "group")),
        P(("dp", "group")),
        P(("dp", "group")),
        P(("dp", "group")),
        P(("dp", "group")),
        P(("dp", "group")),
        P(("dp", "group")),
        P(("dp", "group")),
        P(("dp", "group")),
    )
    return jax.shard_map(body, mesh=mesh, in_specs=in_specs, out_specs=out_specs, check_vma=False)
```

```python
import functools

import jax
import jax.numpy as jnp
from jax import lax
from jax.experimental import pallas as pl
from jax.experimental.pallas import tpu as pltpu
from jax.sharding import PartitionSpec as P

D = 1536
FF = 6912
STEP = 5
WIDTH = 256
ROW_TILE = 16

EPS_NORM = 1e-05
BETA_ONE = 0.5
BETA_TWO = 0.5
ADAM_EPS = 1e-08
RATE_MATRIX = 0.02
RATE_VECTOR = 0.2
DECAY = 0.1

MESH = pl.DeviceIdType.MESH
BF = jnp.bfloat16
F32 = jnp.float32


def update(weight, first, second, grad, rate, decay):
    first_new = BETA_ONE * first + (1.0 - BETA_ONE) * grad
    second_new = BETA_TWO * second + (1.0 - BETA_TWO) * grad * grad
    first_hat = first_new / (1.0 - BETA_ONE**STEP)
    second_hat = second_new / (1.0 - BETA_TWO**STEP)
    weight_new = weight - rate * (first_hat / (jnp.sqrt(second_hat) + ADAM_EPS) + decay * weight)
    return (first_new, second_new, weight_new)


def dot(left, right):
    return lax.dot_general(left, right, (((1,), (0,)), ((), ())), preferred_element_type=F32)


def dot_t(left, right):
    return lax.dot_general(left, right, (((1,), (1,)), ((), ())), preferred_element_type=F32)


def await_bytes(ref, sem):
    pltpu.make_async_copy(ref, ref, sem).wait()


def block_kernel(
    sizes,
    tok, bck_own, wi_own, wo_own, ff_own, small_own,
    block_out, input_grad, g_ff, g_wi, g_wo, g_small,
    wf_all, wi_all, wo_all, tok_all, nrm_far, bck_all, n2_all, dbr_all,
    rs_br, rs_y, rs_n2, rs_n1, via,
    sib_f, sib_i, sib_o, come_f, come_i, far_f, far_i, z_o, mixed_far,
    ws, wi, wo, act, act_t, bck, bck_t, acc_y, acc_n, grad, sibv, part, stage,
    prod, gated, dmix, mid, dmid, low, sibo, parto,
    small_all, gains, taps, g_gains, g_taps, sm_mine, sm_plane, sm_sum, sm_z,
    extra, ag_ssem, ag_rsem, ag_fsem, rs_ssem, rs_rsem, via_ssem, via_rsem, z_ssem, z_rsem, f_ssem, f_rsem,
    gs_ssem, gs_rsem, gz_ssem, come_sem, far_sem, buf_sem, own_ssem, own_rsem, back_ssem, back_rsem, osem,
    sa_ssem, sa_rsem, sz_ssem, sz_rsem, ta_ssem, ta_rsem, tz_ssem, tz_rsem, wsem, lsem,
):
    (out_n, group, rows_n, seg, ch, cblk, chunks) = sizes
    block = rows_n // group
    direct = block % 16 == 0
    count = 2 * out_n * group
    blocks = ch // 128
    seq = group * seg
    dp = lax.axis_index("dp")
    g = lax.axis_index("group")
    o, a = dp // 2, lax.rem(dp, 2)
    y, b = g // 2, lax.rem(g, 2)
    t = 2 * y + a
    mate = (dp, g + 1 - 2 * b)

    def peer(k):
        o2 = lax.rem(o + k, out_n)
        return o2, (2 * o2 + a, g)

    barrier = pltpu.get_barrier_semaphore()
    for x2 in range(2):
        for g2 in range(group):
            @pl.when((x2 != a) | (g2 != g))
            def _():
                pl.semaphore_signal(barrier, inc=1, device_id=(2 * o + x2, g2), device_id_type=MESH)

    def greet(k, carry):
        pl.semaphore_signal(barrier, inc=1, device_id=peer(k)[1], device_id_type=MESH)
        return carry

    lax.fori_loop(1, out_n, greet, 0)
    pl.semaphore_wait(barrier, 2 * group - 1 + out_n - 1)

    def remote(src, dst, ssem, rsem, dev):
        return pltpu.make_async_remote_copy(
            src_ref=src, dst_ref=dst, send_sem=ssem, recv_sem=rsem, device_id=dev, device_id_type=MESH
        )

    def switch(alone, local, copy, op):
        if op == "start":
            @pl.when(alone)
            def _():
                local.start()

            @pl.when(jnp.logical_not(alone))
            def _():
                copy.start()
        else:
            @pl.when(jnp.logical_not(alone))
            def _():
                copy.wait_send()

    odd = lax.rem(a + b, 2)
    size = seg // 2
    y_via = odd * y + (1 - odd) * (1 - y)
    h_via = 1 - odd
    partner = (2 * o + odd * a + (1 - odd) * (1 - a), 2 * (odd * (1 - y) + (1 - odd) * y) + b)

    def part_of(h):
        return pl.ds(h * size, size) if isinstance(h, int) else pl.ds(pl.multiple_of(h * size, size), size)

    def spread(src, dst, n, op):
        for d, h in ((1, 0), (2, 1), (1, 1), (2, 0), (0, 0), (0, 1)):
            x2, y2 = (1 - a if d == 1 else a), (1 - y if d == 2 else y)
            one, two = src.at[part_of(h)], dst.at[g, part_of(h)]
            copy = remote(one, two, ag_ssem.at[n, d, h], ag_rsem.at[n, g, h], (2 * o + x2, 2 * y2 + a))
            if d == 0:
                switch(a == b, pltpu.make_async_copy(one, two, ag_rsem.at[n, g, h]), copy, op)
            elif op == "start":
                copy.start()
            else:
                copy.wait_send()
        if op == "end":
            for k in range(2):
                ref = dst.at[2 * y_via + k, part_of(h_via)]
                await_bytes(ref, ag_fsem.at[n, k])

    def spread_on(dst, n):
        for k in range(2):
            q = 2 * y_via + k
            ref = dst.at[q, part_of(h_via)]
            await_bytes(ref, ag_rsem.at[n, q, h_via])
            remote(ref, ref, ag_fsem.at[n, k], ag_rsem.at[n, q, h_via], partner).start()

    def spread_wait(dst, n, q):
        for h in range(2):
            @pl.when((q // 2 != y_via) | (h != h_via))
            def _():
                await_bytes(dst.at[q, part_of(h)], ag_rsem.at[n, q, h])

    def give(terms, dst, n, at, q, h, slot, op="start"):
        one, two = terms(q).at[part_of(h)], dst.at[slot, part_of(h)]
        copy = remote(one, two, rs_ssem.at[n, at, h], rs_rsem.at[n, slot, h], (2 * o + b, q))
        if slot == 0:
            switch(q == g, pltpu.make_async_copy(one, two, rs_rsem.at[n, 0, h]), copy, op)
        elif op == "start":
            copy.start()
        else:
            copy.wait_send()

    def give_half(terms, n, k, h, op):
        q = 2 * (1 - y) + k
        dev = (2 * o + 1 - a, g) if h == 0 else (dp, 2 * (1 - y) + b)
        copy = remote(terms(q).at[part_of(h)], via.at[n, k], via_ssem.at[n, k, h], via_rsem.at[n, k], dev)
        if op == "start":
            copy.start()
        else:
            copy.wait_send()

    def scatter(terms, dst, n, produce):
        for k in range(2):
            q = 2 * (1 - y) + k
            produce(q)

            @pl.when(odd == 1)
            def _():
                give_half(terms, n, k, 0, "start")
                give_half(terms, n, k, 1, "start")

            @pl.when(odd == 0)
            def _():
                give(terms, dst, n, k, q, 1, 1)

        for k in range(2):
            q = 2 * y + k
            produce(q)

            @pl.when(odd == 1)
            def _():
                give(terms, dst, n, 2 + k, q, 0, 2)

            @pl.when(odd == 0)
            def _():
                give(terms, dst, n, 2 + k, q, 0, 0)
                give(terms, dst, n, 2 + k, q, 1, 0)

    def scatter_on(terms, dst, n):
        for k in range(2):
            q = 2 * y_via + k
            await_bytes(via.at[n, k], via_rsem.at[n, k])
            fetch(via.at[n, k], extra, 0)

            def add_rows(i, carry):
                here = pl.ds(pl.multiple_of(odd * size + i * ROW_TILE, ROW_TILE), ROW_TILE)
                ref = terms(q)
                ref[here, :] = (ref[here, :].astype(F32) + extra[rows16(i), :].astype(F32)).astype(BF)
                return carry

            lax.fori_loop(0, size // ROW_TILE, add_rows, 0)

            @pl.when(odd == 1)
            def _():
                give(terms, dst, n, 2 + k, q, 1, 2)

            @pl.when(odd == 0)
            def _():
                give(terms, dst, n, k, q, 0, 1)

    def scatter_end(terms, dst, n):
        @pl.when(odd == 1)
        def _():
            for k in range(2):
                for h in range(2):
                    give_half(terms, n, k, h, "end")
                    give(terms, dst, n, 2 + k, 2 * y + k, h, 2, "end")

        @pl.when(odd == 0)
        def _():
            for k in range(2):
                for h in range(2):
                    give(terms, dst, n, k, 2 * (1 - y) + k, h, 1, "end")
                    give(terms, dst, n, 2 + k, 2 * y + k, h, 0, "end")

    def scatter_wait(dst, n):
        for slot in range(3):
            for h in range(2):
                await_bytes(dst.at[slot, part_of(h)], rs_rsem.at[n, slot, h])

    def staged(q):
        return stage.at[q]

    def any_span(q):
        return pl.ds(pl.multiple_of(q * seg, seg), seg)

    def slot_of(i, o2, p):
        if isinstance(i, int) and i == 0:
            return wi_all.at[o2, p]
        if isinstance(i, int) and i == 1:
            return wo_all.at[o2, p]
        return wf_all.at[i - 2, :, o2, p]

    def half_of(i, p):
        if isinstance(i, int) and i == 0:
            return wi_all.at[:, p]
        if isinstance(i, int) and i == 1:
            return wo_all.at[:, p]
        return wf_all.at[i - 2, :, :, p]

    my_rows = pl.ds(pl.multiple_of(g * block, 4), block)

    def own_send(i, op):
        if isinstance(i, int) and i == 1:
            dst = wo_all.at[o, a]
            switch(
                a == b,
                pltpu.make_async_copy(wo_own, dst, own_rsem.at[1, 0]),
                remote(wo_own, dst, own_ssem.at[1, 0], own_rsem.at[1, 0], (2 * o + b, 2 * y + a)),
                op,
            )
            return
        if not direct:
            src = wi_own if isinstance(i, int) and i == 0 else ff_own.at[i - 2]
            if op == "start":
                pltpu.make_async_copy(src, slot_of(i, o, b), own_rsem.at[i, 0]).start()
            return
        for t2 in range(group):
            ty, tx = t2 // 2, t2 % 2
            if isinstance(i, int) and i == 0:
                src, dst = wi_own.at[t2], wi_all.at[o, a, my_rows]
            else:
                src, dst = ff_own.at[t2, i - 2], wf_all.at[i - 2, :, o, a, my_rows]
            switch(
                (tx == a) & (ty == y) & (a == b),
                pltpu.make_async_copy(src, dst, own_rsem.at[i, g]),
                remote(src, dst, own_ssem.at[i, t2], own_rsem.at[i, g], (2 * o + tx, 2 * ty + a)),
                op,
            )

    def own_wait(i):
        if not direct or isinstance(i, int) and i == 1:
            await_bytes(slot_of(i, o, b), own_rsem.at[i, 0])
            return
        for q in range(group):
            if isinstance(i, int) and i == 0:
                await_bytes(wi_all.at[o, b, pl.ds(q * block, block)], own_rsem.at[i, q])
            else:
                await_bytes(wf_all.at[i - 2, :, o, b, pl.ds(q * block, block)], own_rsem.at[i, q])

    first, final = o == 0, o == out_n - 1

    def piece_copy(i, src, side, far_by=1):
        ref = slot_of(i, src, b)
        dev = (2 * (o + far_by * (1 - 2 * side)) + a, g)
        return remote(ref, ref, z_ssem.at[i, 2 * side + far_by - 1, src], z_rsem.at[i, src], dev)

    def when(condition, call, *args):
        @pl.when(condition)
        def _():
            call(*args)

    def own_pieces(i, op):
        for side in range(2):
            for far_by in range(1, min(3, out_n)):
                copy = piece_copy(i, o, side, far_by)
                when((o >= far_by) if side else (o + far_by < out_n), copy.start if op == "start" else copy.wait_send)

    def pass_on(i, h, op="start"):
        for side in range(2):
            src = o + h if side else o - h
            there = (src < out_n) & (o > 0) if side else (src >= 0) & (o < out_n - 1)

            @pl.when((src < out_n) if side else (src >= 0))
            def _(src=src, side=side):
                if op == "start":
                    await_bytes(slot_of(i, src, b), z_rsem.at[i, src])

            @pl.when(there)
            def _(src=src, side=side):
                copy = piece_copy(i, src, side)
                copy.start() if op == "start" else copy.wait_send()

    def to_mate(i):
        for h in sorted({1, out_n - 1}):
            for side in range(2):
                src = o + h if side else o - h

                @pl.when((src < out_n) if side else (src >= 0))
                def _(src=src):
                    await_bytes(slot_of(i, src, b), z_rsem.at[i, src])

        remote(half_of(i, b), half_of(i, b), f_ssem.at[i], f_rsem.at[i], mate).start()

    items = 2 + chunks
    sent = set()

    def own_start(*which):
        for i in which:
            if i < items and i not in sent:
                sent.add(i)
                own_send(i, "start")

    def leave(i):
        own_wait(i)
        own_pieces(i, "start")

    def pump(time, what="all"):
        work = []
        if what != "late":
            work += [(time - n, pass_on, (n + 1,)) for n in range(1, out_n - 2)]
        if what != "early":
            work += [(time - (out_n - 2), to_mate, ())]
        if what in ("all", "early"):
            work += [(time + 2, leave, ())]
        if isinstance(time, int):
            own_start(*range(time + 3))
        for i, call, args in work:
            if isinstance(i, int):
                if 0 <= i < items:
                    call(i, *args)
            else:
                when(i < items, call, i, *args)

    def gather_wait(i):
        await_bytes(half_of(i, 1 - b), f_rsem.at[i])

    def gather_close(i):
        own_pieces(i, "end")
        for h in range(2, out_n - 1):
            pass_on(i, h, "end")
        await_bytes(half_of(i, b), f_ssem.at[i])
        own_send(i, "end")

    def fetch(src, dst, n):
        copy = pltpu.make_async_copy(src, dst, lsem.at[n])
        copy.start()
        copy.wait()

    def span(q):
        return pl.ds(q * seg, seg)

    def rows16(i):
        return pl.ds(pl.multiple_of(i * ROW_TILE, ROW_TILE), ROW_TILE)

    def lanes(k, j):
        return pl.ds(k * 384 + j * 128, 128)

    place = a * group + g
    mine = o * (2 * group) + place

    def plane(src, dst, ssem, rsem, op):
        for x2 in range(2):
            for g2 in range(group):
                @pl.when((x2 != a) | (g2 != g))
                def _():
                    copy = remote(src, dst, ssem.at[x2 * group + g2], rsem.at[place], (2 * o + x2, g2))
                    if op == "start":
                        copy.start()
                    else:
                        copy.wait_send()

    def plane_wait(ref, rsem):
        for x2 in range(2):
            for g2 in range(group):
                @pl.when((x2 != a) | (g2 != g))
                def _():
                    await_bytes(ref, rsem.at[x2 * group + g2])

    def far(src, dst, ssem, rsem, op):
        def one(k, carry):
            copy = remote(src, dst, ssem.at[k], rsem.at[o], peer(k)[1])
            if op == "start":
                copy.start()
            else:
                copy.wait_send()
            return carry

        lax.fori_loop(1, out_n, one, 0)

    def far_wait(ref, rsem):
        def one(k, carry):
            await_bytes(ref, rsem.at[peer(k)[0]])
            return carry

        lax.fori_loop(1, out_n, one, 0)

    planes = small_all.at[pl.ds(o * 2 * group, 2 * group)]
    pltpu.make_async_copy(small_own, small_all.at[mine], lsem.at[2]).start()
    plane(small_own, small_all.at[mine], sa_ssem, sa_rsem, "start")

    def convolved(q, col):
        return (
            taps[0:1, col] * prod[pl.ds(q * seg + 6, seg), col]
            + taps[1:2, col] * prod[pl.ds(q * seg + 7, seg), col]
            + taps[2:3, col] * prod[pl.ds(q * seg + 8, seg), col]
        )

    own_start(0)
    own_start(1)
    own_start(2)
    own_start(3)
    spread(tok, tok_all, 0, "start")
    own_start(4)
    prod[pl.ds(0, 8), :] = jnp.zeros((8, ch), F32)
    leave(0)
    leave(1)
    pump(0)
    await_bytes(small_own, lsem.at[2])
    plane_wait(small_own, sa_rsem)
    far(planes, planes, sz_ssem, sz_rsem, "start")
    pump(1)
    far_wait(planes, sz_rsem)
    spread_on(tok_all, 0)

    share = 2 * D // count
    rows_of = {}
    for n in range(count):
        row = n * share // 128
        rows_of.setdefault(row, []).append((n, 0))
        if (n * share + share - 1) // 128 > row:
            rows_of.setdefault(row + 1, []).append((n, 1))
    for tile, pieces in rows_of.items():
        value = sum(small_all[n, r : r + 1, :] for n, r in pieces)
        i, j = tile // (D // 128), tile % (D // 128)
        gains[i : i + 1, j * 128 : (j + 1) * 128] = value
    rows_of = {}
    for m in range(3 * count):
        n, piece = m // 3, m % 3
        tap, rest = m // count, m % count
        lane = rest // group * cblk
        rows_of.setdefault((tap, lane // 128), []).append((n, 2 + 2 * piece, rest % group))
        if (lane + block - 1) // 128 > lane // 128:
            rows_of.setdefault((tap, lane // 128 + 1), []).append((n, 3 + 2 * piece, rest % group))
    for (tap, tile), pieces in rows_of.items():
        value = jnp.zeros((1, 128), F32)
        for t2 in range(group):
            value = value + jnp.where(t == t2, sum(small_all[n, r : r + 1, :] for n, r, p in pieces if p == t2), 0.0)
        taps[tap : tap + 1, tile * 128 : (tile + 1) * 128] = value

    pump(2, "stay")
    for q in range(group):
        spread_wait(tok_all, 0, q)
        fetch(tok_all.at[q], act.at[span(q)], 0)

        def normed_rows(i, carry, q=q):
            here = pl.ds(pl.multiple_of(q * seg + i * ROW_TILE, ROW_TILE), ROW_TILE)
            row = act[here, :].astype(F32)
            s1 = lax.rsqrt(jnp.mean(row * row, axis=-1, keepdims=True) + EPS_NORM)
            act[here, :] = (row * s1 * gains[0:1, :]).astype(BF)
            return carry

        lax.fori_loop(0, seg // ROW_TILE, normed_rows, 0, unroll=2)
    leave(4)
    spread(bck_own, bck_all, 1, "start")
    own_start(5)
    keep_normed = pltpu.make_async_copy(act, nrm_far, lsem.at[2])
    keep_normed.start()
    for time in range(3, out_n):
        pump(time)
    gather_wait(0)
    fetch(wi_all, wi, 0)
    keep_normed.wait()

    for q in range(group):
        for k in range(blocks):
            acc_y[span(q), pl.ds(k * 384, 384)] = dot(
                act[span(q), :], wi[:, :, :, pl.ds(k * 384, 384)].reshape(D, 384)
            )
        for k in range(blocks):
            col = pl.ds(k * 128, 128)
            prod[pl.ds(q * seg + 8, seg), col] = acc_y[span(q), lanes(k, 0)] * acc_y[span(q), lanes(k, 2)]
            gated[span(q), col] = (acc_y[span(q), lanes(k, 1)] * convolved(q, col)).astype(BF)
    spread_on(bck_all, 1)
    gather_wait(1)
    fetch(wo_all, wo, 0)

    def branch(q):
        for n in range(4):
            col = pl.ds(n * 384, 384)
            stage[q, :, col] = dot(gated[any_span(q), :], wo[:, :, :, col].reshape(ch, 384)).astype(BF)

    scatter(staged, rs_br, 0, branch)
    pump(out_n)
    scatter_on(staged, rs_br, 0)
    spill = pltpu.make_async_copy(acc_y.at[:, pl.ds(0, 3 * ch)], mixed_far, lsem.at[2])
    spill.start()
    own_start(6)
    for q in range(group):
        spread_wait(bck_all, 1, q)
        fetch(bck_all.at[q], bck.at[span(q)], 0)
        bck_t[:, span(q)] = bck[span(q), :].T

    pump(out_n + 1)
    scatter_wait(rs_br, 0)
    scatter_end(staged, rs_br, 0)
    fetch(rs_br, stage.at[pl.ds(0, 3)], 0)

    def arrived(here):
        total = stage[0, here, :].astype(F32)
        for q in range(1, 3):
            total = total + stage[q, here, :].astype(F32)
        return total

    def middle_rows(i, carry):
        here = rows16(i)
        mi = tok[here, :].astype(F32) + arrived(here)
        mid[here, :] = mi
        s2 = lax.rsqrt(jnp.mean(mi * mi, axis=-1, keepdims=True) + EPS_NORM)
        low[here, :] = (mi * s2 * gains[1:2, :]).astype(BF)
        return carry

    lax.fori_loop(0, seg // ROW_TILE, middle_rows, 0)
    spread(low, n2_all, 2, "start")
    own_start(*range(items))
    pump(out_n + 2)
    spread_on(n2_all, 2)
    pump(out_n + 3)
    gather_wait(2)
    pltpu.make_async_copy(wf_all.at[0], ws.at[0], wsem.at[0]).start()
    spill.wait()

    def clear(i, carry):
        here = rows16(i)
        acc_y[here, :] = jnp.zeros((ROW_TILE, D), F32)
        acc_n[here, :] = jnp.zeros((ROW_TILE, D), F32)
        return carry

    lax.fori_loop(0, seq // ROW_TILE, clear, 0)
    for q in range(group):
        spread_wait(n2_all, 2, q)
        fetch(n2_all.at[q], act.at[span(q)], 0)
        act_t[:, span(q)] = act[span(q), :].T


    def chunk_refs(kind, c):
        if kind == "f":
            return lax.rem(c, 2), c, sib_f.at[c], pl.ds(0, WIDTH)
        n = chunks + c
        return n % 2, n, sib_i.at[c], pl.ds(0, 128)

    def pair_send(kind, c, op):
        s, n, sib, cols = chunk_refs(kind, c)
        copy = remote(grad.at[s, :, :, 1 - b, :, cols], sib, gs_ssem.at[n], gs_rsem.at[n], mate)
        if op == "start":
            copy.start()
        else:
            copy.wait_send()

    steps = out_n.bit_length() - 1

    def halves_refs(kind, c):
        return (come_f if kind == "f" else come_i).at[c], (far_f if kind == "f" else far_i).at[c]

    def flipped(k):
        m = 1 << k
        return o + m - 2 * m * lax.rem(o // m, 2)

    def kept(device, k, i):
        return lax.rem(device, 2 << k) + (2 << k) * i

    def step_at(k):
        return out_n - (out_n >> k), out_n >> (k + 1)

    def step_send(kind, c, k, op="start"):
        _, n, _, _ = chunk_refs(kind, c)
        come, mine_far = halves_refs(kind, c)
        at, number = step_at(k)
        there = flipped(k)
        for i in range(number):
            copy = remote(
                mine_far.at[:, kept(there, k, i)], come.at[:, at + i],
                gz_ssem.at[n, at + i], come_sem.at[n, at + i], (2 * there + a, g),
            )
            if op == "start":
                copy.start()
            else:
                copy.wait_send()

    def pair_fetch(kind, c, op):
        s, n, sib, cols = chunk_refs(kind, c)
        if op == "start":
            await_bytes(sib, gs_rsem.at[n])
        copy = pltpu.make_async_copy(sib, sibv.at[:, :, :, cols], lsem.at[1])
        copy.start() if op == "start" else copy.wait()

    def pair_far(kind, c):
        s, n, _, cols = chunk_refs(kind, c)
        return pltpu.make_async_copy(part.at[s, :, :, :, cols], halves_refs(kind, c)[1], far_sem.at[s])

    def pair_add(kind, c):
        s, n, _, cols = chunk_refs(kind, c)
        pair_fetch(kind, c, "end")

        def one(i, carry):
            j, o2 = i // out_n, lax.rem(i, out_n)
            part[s, j, o2, :, cols] = (
                grad[s, j, o2, b, :, cols].astype(F32) + sibv[j, o2, :, cols].astype(F32)
            ).astype(BF)
            return carry

        lax.fori_loop(0, 3 * out_n, one, 0)
        pair_far(kind, c).start()

    def first_send(kind, c):
        pair_far(kind, c).wait()
        step_send(kind, c, 0)

    def stage_ask(job, buf, op):
        kind, c, k = job
        _, n, _, cols = chunk_refs(kind, c)
        come, mine_far = halves_refs(kind, c)
        at, number = step_at(k)
        for i in range(number):
            if op == "start":
                await_bytes(come.at[:, at + i], come_sem.at[n, at + i])
            for m, src in ((i, come.at[:, at + i]), (number + i, mine_far.at[:, kept(o, k, i)])):
                copy = pltpu.make_async_copy(src, part.at[buf, :, m, :, cols], buf_sem.at[buf, m])
                copy.start() if op == "start" else copy.wait()

    def stage_back(job, buf, op):
        kind, c, k = job
        _, n, _, cols = chunk_refs(kind, c)
        mine_far = halves_refs(kind, c)[1]
        at, number = step_at(k)
        for i in range(number):
            m = number + i
            copy = pltpu.make_async_copy(
                part.at[buf, :, m, :, cols], mine_far.at[:, kept(o, k, i)], buf_sem.at[buf, m]
            )
            copy.start() if op == "start" else copy.wait()

    def stage_add(job, buf):
        kind, c, k = job
        _, n, _, cols = chunk_refs(kind, c)
        h, _, place_o, place_p = out_slot(n)
        at, number = step_at(k)

        def add(i, carry):
            j, r = i // (rows_n // 48), lax.rem(i, rows_n // 48)
            here = pl.ds(pl.multiple_of(r * 48, 16), 48)
            for m in range(number):
                value = (
                    part[buf, j, m, here, cols].astype(F32) + part[buf, j, number + m, here, cols].astype(F32)
                ).astype(BF)
                if k == steps - 1:
                    ws[h, j, place_o, place_p, here, cols] = value
                else:
                    part[buf, j, number + m, here, cols] = value
            return carry

        lax.fori_loop(0, 3 * (rows_n // 48), add, 0)
        if k == steps - 1:
            hand_back(kind, c, "start")
        else:
            stage_back(job, buf, "start")

    def stage_on(job, buf):
        kind, c, k = job
        if k < steps - 1:
            stage_back(job, buf, "end")
            step_send(kind, c, k + 1)

    def sums_of(jobs):
        for i, job in enumerate(jobs):
            if i == 0:
                stage_ask(job, 0, "start")
            if i >= 1:
                stage_on(jobs[i - 1], (i - 1) % 2)
            if i + 1 < len(jobs):
                stage_ask(jobs[i + 1], (i + 1) % 2, "start")
            stage_ask(job, i % 2, "end")
            stage_add(job, i % 2)
        stage_on(jobs[-1], (len(jobs) - 1) % 2)

    def out_slot(n):
        return (n // (2 * out_n), slice(None), lax.rem(n, 2 * out_n) // 2, lax.rem(n, 2))

    def hand_back(kind, c, op):
        _, n, _, cols = chunk_refs(kind, c)
        dst = (g_ff if kind == "f" else g_wi)
        if not direct:
            if op == "start":
                h, _, o2, p = out_slot(n)
                fetch(ws.at[h, :, o2, p, :, cols], dst.at[c], 1)
            return
        h, _, o2, p = out_slot(n)
        for q in range(group):
            src = ws.at[h, :, o2, p, pl.ds(q * block, block), cols]
            switch(
                (a == b) & (q == g),
                pltpu.make_async_copy(src, dst.at[t, c], back_rsem.at[n, t]),
                remote(src, dst.at[t, c], back_ssem.at[n, q], back_rsem.at[n, t], (2 * o + b, q)),
                op,
            )

    def hand_wait(kind, c):
        if direct:
            _, n, _, _ = chunk_refs(kind, c)
            for t2 in range(group):
                await_bytes((g_ff if kind == "f" else g_wi).at[t2, c], back_rsem.at[n, t2])

    half = out_n // 2

    def grad_rows(h):
        return pl.ds(pl.multiple_of(h * (D // 2), D // 2), D // 2), pl.ds(h * half, half)

    loop_pump = out_n + 4

    def d_normed_two(q):
        stage[q] = acc_n[any_span(q), :].astype(BF)

    def hidden_chunk(c, carry):
        s = lax.rem(c, 2)
        await_bytes(ws.at[s], wsem.at[s])
        hid, dgt, dup = (pl.ds(j * WIDTH, WIDTH) for j in range(3))

        def token_tile(m, carry):
            here = pl.ds(pl.multiple_of(m * (seq // 2), seq // 2), seq // 2)
            n2 = act[here, :]
            gate = dot(n2, ws[s, 0].reshape(D, WIDTH))
            upper = dot(n2, ws[s, 1].reshape(D, WIDTH))
            d_hidden = dot(bck[here, :], ws[s, 2].reshape(D, WIDTH))
            sigma = jax.nn.sigmoid(gate)
            active = gate * sigma
            dmix[here, hid] = (active * upper).astype(BF)
            dmix[here, dgt] = (d_hidden * upper * (sigma * (1.0 + gate * (1.0 - sigma)))).astype(BF)
            dmix[here, dup] = (d_hidden * active).astype(BF)
            acc_y[here, :] += dot_t(dmix[here, hid], ws[s, 2].reshape(D, WIDTH))
            acc_n[here, :] += dot_t(dmix[here, dgt], ws[s, 0].reshape(D, WIDTH))
            acc_n[here, :] += dot_t(dmix[here, dup], ws[s, 1].reshape(D, WIDTH))
            return carry

        lax.fori_loop(0, 2, token_tile, 0)
        pump(c + loop_pump, "early")

        @pl.when(c == chunks - 1)
        def _():
            scatter(staged, rs_n2, 1, d_normed_two)

        @pl.when(c >= 1)
        def _():
            pair_fetch("f", c - 1, "start")

        @pl.when(c >= 2)
        def _():
            first_send("f", c - 2)

        @pl.when(c >= 2)
        def _():
            pair_send("f", c - 2, "end")

        def grad_tile(h, carry):
            rows, os = grad_rows(h)
            shape = (half, 2, rows_n, WIDTH)
            grad[s, 0, os] = dot(act_t[rows, :], dmix[:, dgt]).astype(BF).reshape(shape)
            grad[s, 1, os] = dot(act_t[rows, :], dmix[:, dup]).astype(BF).reshape(shape)
            grad[s, 2, os] = dot(bck_t[rows, :], dmix[:, hid]).astype(BF).reshape(shape)
            return carry

        lax.fori_loop(0, 2, grad_tile, 0)
        pair_send("f", c, "start")

        @pl.when(c >= 1)
        def _():
            pair_add("f", c - 1)

        pump(c + loop_pump, "late")

        @pl.when(c + 1 < chunks)
        def _():
            gather_wait(c + 3)
            pltpu.make_async_copy(wf_all.at[c + 1], ws.at[1 - s], wsem.at[1 - s]).start()

        return carry

    lax.fori_loop(0, chunks, hidden_chunk, 0)

    first_send("f", chunks - 2)
    pair_fetch("f", chunks - 1, "start")
    pair_add("f", chunks - 1)
    scatter_on(staged, rs_n2, 1)
    first_send("f", chunks - 1)
    for k in range(steps - 1):
        sums_of([("f", c, k) for c in range(chunks - 2)])
    scatter_wait(rs_n2, 1)
    scatter_end(staged, rs_n2, 1)
    spread(low, n2_all, 2, "end")
    fetch(rs_n2, stage.at[pl.ds(0, 3)], 0)
    fetch(bck_own, act.at[span(0)], 0)
    g_gains[...] = jnp.zeros_like(g_gains)

    def d_middle_rows(i, carry):
        here = rows16(i)
        dn = arrived(here)
        mi = mid[here, :]
        s2 = lax.rsqrt(jnp.mean(mi * mi, axis=-1, keepdims=True) + EPS_NORM)
        e2 = gains[1:2, :] * dn
        back = act[here, :].astype(F32)
        dm = back + s2 * e2 - mi * (s2 * s2 * s2) * jnp.mean(e2 * mi, axis=-1, keepdims=True)
        dmid[here, :] = dm
        low[here, :] = dm.astype(BF)
        g_gains[1] += jnp.sum((dn * mi * s2).reshape(ROW_TILE // 8, 8, D), axis=0)
        return carry

    lax.fori_loop(0, seg // ROW_TILE, d_middle_rows, 0)
    spread(low, dbr_all, 3, "start")

    for q in range(group):
        stage[q] = acc_y[span(q), :].astype(BF)
    spill_back = pltpu.make_async_copy(mixed_far, acc_y.at[:, pl.ds(0, 3 * ch)], lsem.at[2])
    spill_back.start()

    for q in range(group):
        bck_t[pl.ds(0, ch), span(q)] = gated[span(q), :].T
        fetch(nrm_far.at[span(q)], act.at[span(q)], 0)
        act_t[:, span(q)] = act[span(q), :].T
    spill_back.wait()
    spread_on(dbr_all, 3)
    for k in range(steps - 1):
        sums_of([("f", c, k) for c in range(chunks - 2, chunks)])
    sums_of([("f", c, steps - 1) for c in range(chunks - 3)])

    acc_n[pl.ds(seq, 8), pl.ds(0, ch)] = jnp.zeros((8, ch), F32)
    for q in range(group):
        spread_wait(dbr_all, 3, q)
        fetch(dbr_all.at[q], bck.at[span(q)], 0)
        acc_n[span(q), pl.ds(ch, ch)] = dot_t(bck[span(q), :], wo[...].reshape(ch, D))
        for k in range(blocks):
            col = pl.ds(k * 128, 128)
            d_gated = acc_n[span(q), pl.ds(ch + k * 128, 128)]
            acc_n[span(q), col] = d_gated * acc_y[span(q), lanes(k, 1)]
            dmix[span(q), lanes(k, 1)] = (d_gated * convolved(q, col)).astype(BF)
    scatter(staged, rs_y, 2, lambda q: None)
    g_taps[...] = jnp.zeros_like(g_taps)
    for q in range(group):
        for k in range(blocks):
            col = pl.ds(k * 128, 128)
            d0 = acc_n[span(q), col]
            for n in range(3):
                g_taps[n, :, col] += jnp.sum(
                    (d0 * prod[pl.ds(q * seg + 6 + n, seg), col]).reshape(seg // 8, 8, 128), axis=0
                )
            d_product = (
                taps[2:3, col] * d0
                + taps[1:2, col] * acc_n[pl.ds(q * seg + 1, seg), col]
                + taps[0:1, col] * acc_n[pl.ds(q * seg + 2, seg), col]
            )
            dmix[span(q), lanes(k, 0)] = (d_product * acc_y[span(q), lanes(k, 2)]).astype(BF)
            dmix[span(q), lanes(k, 2)] = (d_product * acc_y[span(q), lanes(k, 0)]).astype(BF)

    for k in range(blocks):
        s = (chunks + k) % 2
        if k < 2:
            pair_send("f", chunks - 2 + k, "end")
        else:
            pair_send("i", k - 2, "end")

        def intake_tile(h, carry, k=k, s=s):
            rows, os = grad_rows(h)
            value = dot(act_t[rows, :], dmix[:, pl.ds(k * 384, 384)]).astype(BF)
            for j in range(3):
                grad[s, j, os, :, :, pl.ds(0, 128)] = value[:, j * 128 : (j + 1) * 128].reshape(
                    half, 2, rows_n, 128
                )
            return carry

        lax.fori_loop(0, 2, intake_tile, 0)
        pair_send("i", k, "start")
        if k >= 1:
            pair_fetch("i", k - 1, "start")
            if k >= 2:
                first_send("i", k - 2)
            pair_add("i", k - 1)

    for n in range(4):
        col = pl.ds(n * 384, 384)
        wo[:, :, :, col] = dot(bck_t[pl.ds(0, ch), :], bck[:, col]).astype(BF).reshape(out_n, 2, cblk, 384)
    last = chunks + blocks
    pair_o = remote(wo.at[:, 1 - b], sib_o, gs_ssem.at[last], gs_rsem.at[last], mate)
    pair_o.start()
    if blocks >= 2:
        first_send("i", blocks - 2)
    pair_fetch("i", blocks - 1, "start")
    pair_add("i", blocks - 1)
    first_send("i", blocks - 1)

    await_bytes(sib_o, gs_rsem.at[last])
    fetch(sib_o, sibo, 1)

    def add_o(o2, carry):
        parto[o2] = (wo[o2, b].astype(F32) + sibo[o2].astype(F32)).astype(BF)
        return carry

    lax.fori_loop(0, out_n, add_o, 0)

    def part_o(op):
        def one(k, carry):
            o2, dev = peer(k)
            copy = remote(parto.at[o2], z_o.at[o], gz_ssem.at[last, k], come_sem.at[last, o], dev)
            if op == "start":
                copy.start()
            else:
                copy.wait_send()
            return carry

        lax.fori_loop(1, out_n, one, 0)
        keep = pltpu.make_async_copy(parto.at[o], z_o.at[o], osem.at[0])
        if op == "start":
            keep.start()
        else:
            keep.wait()

    part_o("start")

    def lent(q):
        return bck.at[any_span(q)]

    def d_normed(q):
        for n in range(4):
            bck[any_span(q), pl.ds(n * 384, 384)] = dot_t(
                dmix[any_span(q), :], wi[pl.ds(n * out_n // 4, out_n // 4)].reshape(384, 3 * ch)
            ).astype(BF)

    scatter(lent, rs_n1, 3, d_normed)
    scatter_on(staged, rs_y, 2)
    scatter_on(lent, rs_n1, 3)
    scatter_wait(rs_y, 2)
    scatter_end(staged, rs_y, 2)
    spread(low, dbr_all, 3, "end")
    for q in range(3):
        fetch(rs_y.at[q], act.at[span(q)], 0)

    def out_rows(i, carry):
        here = rows16(i)
        value = act[here, :].astype(F32)
        for q in range(1, 3):
            value = value + act[pl.ds(pl.multiple_of(q * seg + i * ROW_TILE, ROW_TILE), ROW_TILE), :].astype(F32)
        low[here, :] = (mid[here, :] + value).astype(BF)
        return carry

    lax.fori_loop(0, seg // ROW_TILE, out_rows, 0)
    fetch(low, block_out, 0)

    sums_of([("f", c, steps - 1) for c in range(chunks - 3, chunks)])
    scatter_wait(rs_n1, 3)
    scatter_end(lent, rs_n1, 3)
    fetch(rs_n1, stage.at[pl.ds(0, 3)], 0)

    def d_rows(i, carry):
        here = rows16(i)
        dn = arrived(here)
        row = tok[here, :].astype(F32)
        s1 = lax.rsqrt(jnp.mean(row * row, axis=-1, keepdims=True) + EPS_NORM)
        e1 = gains[0:1, :] * dn
        low[here, :] = (
            dmid[here, :] + s1 * e1 - row * (s1 * s1 * s1) * jnp.mean(e1 * row, axis=-1, keepdims=True)
        ).astype(BF)
        g_gains[0] += jnp.sum((dn * row * s1).reshape(ROW_TILE // 8, 8, D), axis=0)
        return carry

    lax.fori_loop(0, seg // ROW_TILE, d_rows, 0)
    fetch(low, input_grad, 0)

    sm_mine[...] = jnp.zeros_like(sm_mine)
    for i in range(2):
        value = jnp.sum(g_gains[i], axis=0, keepdims=True)
        for j in range(D // 128):
            row = i * (D // 128) + j
            sm_mine[row : row + 1, :] = value[:, j * 128 : (j + 1) * 128]
    for n in range(3):
        value = jnp.sum(g_taps[n], axis=0, keepdims=True)
        for k in range(blocks):
            for t2 in range(group):
                row = 2 * (D // 128) + (t2 * 3 + n) * blocks + k
                sm_mine[row : row + 1, :] = jnp.where(t == t2, value[:, k * 128 : (k + 1) * 128], 0.0)
    sm_plane[place] = sm_mine[...]
    plane(sm_mine, sm_plane.at[place], ta_ssem, ta_rsem, "start")

    for k in range(max(0, blocks - 2), blocks):
        pair_send("i", k, "end")

    for k in range(steps - 1):
        sums_of([("i", c, k) for c in range(blocks)])
    plane_wait(sm_mine, ta_rsem)
    value = sm_plane[0]
    for i in range(1, 2 * group):
        value = value + sm_plane[i]
    sm_sum[...] = value
    sm_z[o] = value
    far(sm_sum, sm_z.at[o], tz_ssem, tz_rsem, "start")
    sums_of([("i", c, steps - 1) for c in range(blocks)])
    part_o("end")
    pair_o.wait_send()

    def last_one(k, carry):
        await_bytes(z_o.at[o], come_sem.at[last, peer(k)[0]])
        return carry

    lax.fori_loop(1, out_n, last_one, 0)
    fetch(z_o, sibo, 1)
    value = sibo[0].astype(F32)
    for o2 in range(1, out_n):
        value = value + sibo[o2].astype(F32)
    outo = parto.at[0]
    outo[...] = value.astype(BF)

    def back_o(op):
        switch(
            a == b,
            pltpu.make_async_copy(outo, g_wo, back_rsem.at[last, 0]),
            remote(outo, g_wo, back_ssem.at[last, 0], back_rsem.at[last, 0], (2 * o + b, 2 * y + a)),
            op,
        )

    back_o("start")
    far_wait(sm_sum, tz_rsem)
    value = sm_z[0]
    for i in range(1, out_n):
        value = value + sm_z[i]
    g_small[...] = value

    plane(small_own, small_all.at[mine], sa_ssem, sa_rsem, "end")
    far(planes, planes, sz_ssem, sz_rsem, "end")
    plane(sm_mine, sm_plane.at[place], ta_ssem, ta_rsem, "end")
    far(sm_sum, sm_z.at[o], tz_ssem, tz_rsem, "end")
    spread(tok, tok_all, 0, "end")
    spread(bck_own, bck_all, 1, "end")
    gather_close(0)
    gather_close(1)

    def close(c, carry):
        gather_close(c + 2)
        for k in range(steps):
            step_send("f", c, k, "end")
        hand_back("f", c, "end")
        hand_wait("f", c)
        return carry

    lax.fori_loop(0, chunks, close, 0)
    for k in range(blocks):
        for step in range(steps):
            step_send("i", k, step, "end")
        hand_back("i", k, "end")
        hand_wait("i", k)
    back_o("end")
    await_bytes(g_wo, back_rsem.at[last, 0])


def forward_backward(sizes, tok, bck, wi_own, wo_own, ff_own, small_own):
    (out_n, group, rows_n, seg, ch, cblk, chunks) = sizes
    blocks = ch // 128
    seq = group * seg
    block = rows_n // group
    places = 2 * group
    small_rows = -(-(2 * D // 128 + group * 3 * blocks) // 8) * 8
    items = 2 + chunks
    sums = chunks + blocks + 1
    vm = pltpu.VMEM
    dma = pltpu.SemaphoreType.DMA

    def shape(*dims, dtype=BF):
        return jax.ShapeDtypeStruct(dims, dtype)

    any_spec = pl.BlockSpec(memory_space=pl.ANY)
    vmem_spec = pl.BlockSpec(memory_space=pltpu.VMEM)
    if block % 16 == 0:
        given = [shape(group, chunks, 3, block, WIDTH), shape(group, blocks, 3, block, 128)]
    else:
        given = [shape(chunks, 3, rows_n, WIDTH), shape(blocks, 3, rows_n, 128)]
    outs = [
        shape(seg, D), shape(seg, D), *given, shape(cblk, D), shape(small_rows, 128, dtype=F32),
        shape(chunks, 3, out_n, 2, rows_n, WIDTH), shape(out_n, 2, rows_n, 3 * ch), shape(out_n, 2, cblk, D),
        shape(group, seg, D), shape(seq, D), shape(group, seg, D), shape(group, seg, D), shape(group, seg, D),
        shape(3, seg, D), shape(3, seg, D), shape(3, seg, D), shape(3, seg, D), shape(4, 2, seg // 2, D),
        shape(chunks, 3, out_n, rows_n, WIDTH), shape(blocks, 3, out_n, rows_n, 128), shape(out_n, cblk, D),
        *[shape(chunks, 3, out_n, rows_n, WIDTH), shape(blocks, 3, out_n, rows_n, 128)] * 2, shape(out_n, cblk, D),
        shape(seq, 3 * ch, dtype=F32),
    ]
    out_specs = [any_spec] * 5 + [vmem_spec] + [any_spec] * (len(outs) - 6)
    scratch = [
        vm((2, 3, out_n, 2, rows_n, WIDTH), BF),
        vm((out_n, 2, rows_n, 3 * ch), BF),
        vm((out_n, 2, cblk, D), BF),
        vm((seq, D), BF), vm((D, seq), BF), vm((seq, D), BF), vm((D, seq), BF),
        vm((seq, D), F32), vm((seq + 8, D), F32),
        vm((2, 3, out_n, 2, rows_n, WIDTH), BF),
        vm((3, out_n, rows_n, WIDTH), BF),
        vm((2, 3, out_n, rows_n, WIDTH), BF),
        vm((group, seg, D), BF),
        vm((seq + 8, ch), F32), vm((seq, ch), BF), vm((seq, 3 * ch), BF),
        vm((seg, D), F32), vm((seg, D), F32), vm((seg, D), BF),
        vm((out_n, cblk, D), BF), vm((out_n, cblk, D), BF),
        vm((places * out_n, 8, 128), F32), vm((2, D), F32), vm((3, ch), F32),
        vm((2, 8, D), F32), vm((3, 8, ch), F32),
        vm((small_rows, 128), F32), vm((places, small_rows, 128), F32),
        vm((small_rows, 128), F32), vm((out_n, small_rows, 128), F32),
        vm((seg // 2, D), BF),
        dma((4, 3, 2)), dma((4, group, 2)), dma((4, 2)), dma((4, 4, 2)), dma((4, 3, 2)), dma((4, 2, 2)), dma((4, 2)),
        dma((items, 4, out_n)), dma((items, out_n)), dma((items,)), dma((items,)),
        dma((sums,)), dma((sums,)), dma((sums, out_n)), dma((sums, out_n)), dma((2,)), dma((2, out_n)),
        dma((items, group)), dma((items, group)), dma((sums, group)), dma((sums, group)), dma((1,)),
        dma((places,)), dma((places,)), dma((out_n,)), dma((out_n,)),
        dma((places,)), dma((places,)), dma((out_n,)), dma((out_n,)), dma((2,)), dma((5,)),
    ]
    results = pl.pallas_call(
        functools.partial(block_kernel, sizes),
        out_shape=outs,
        in_specs=[vmem_spec] + [any_spec] * 4 + [vmem_spec],
        out_specs=out_specs,
        scratch_shapes=scratch,
        compiler_params=pltpu.CompilerParams(
            collective_id=0, has_side_effects=True, vmem_limit_bytes=63 * 1024 * 1024
        ),
        cost_estimate=pl.CostEstimate(
            flops=6 * seq * D * (4 * ch + 3 * chunks * WIDTH),
            bytes_accessed=200_000_000,
            transcendentals=seq * chunks * WIDTH,
        ),
    )(tok, bck, wi_own, wo_own, ff_own, small_own)
    return results[:6]


def body(
    tokens,
    cotangent,
    lengths,
    intake_weight,
    intake_first,
    intake_second,
    output_weight,
    output_first,
    output_second,
    swiglu_weight,
    swiglu_first,
    swiglu_second,
    down_weight,
    down_first,
    down_second,
    norm_gains,
    gains_first,
    gains_second,
    conv_kernel,
    kernel_first,
    kernel_second,
):
    data_count = lax.axis_size("dp")
    group_count = lax.axis_size("group")
    dp = lax.axis_index("dp")
    member = lax.axis_index("group")
    block = D // (data_count * group_count)
    cblk = -(-block // 16) * 16
    ch = data_count * cblk
    blocks = ch // 128
    hidden_part = FF // group_count
    chunks = -(-hidden_part // WIDTH)
    hidden_full = chunks * WIDTH
    rows_n = D // data_count
    swap = []
    for one in range(data_count):
        for two in range(group_count):
            there = (2 * (one // 2) + two % 2) * group_count + 2 * (two // 2) + one % 2
            swap.append((one * group_count + two, there))

    def cross(value):
        return lax.ppermute(value, ("dp", "group"), swap)

    intake_local = (
        intake_weight.astype(BF)
        .reshape(block, 3, data_count, group_count, block)
        .transpose(3, 0, 1, 2, 4)
    )
    intake_local = jnp.pad(intake_local, ((0, 0),) * 4 + ((0, cblk - block),))
    intake_local = (
        intake_local.reshape(group_count, block, 3, blocks, 128)
        .transpose(0, 1, 3, 2, 4)
        .reshape(group_count, block, 3 * ch)
    )
    ff_local = jnp.concatenate(
        [
            swiglu_weight.astype(BF).reshape(block, 2, group_count, hidden_part),
            down_weight.astype(BF).reshape(block, 1, group_count, hidden_part),
        ],
        axis=1,
    )
    ff_local = jnp.pad(ff_local, ((0, 0),) * 3 + ((0, hidden_full - hidden_part),))
    ff_local = ff_local.reshape(block, 3, group_count, chunks, WIDTH).transpose(2, 3, 1, 0, 4)
    wo_own = jnp.pad(output_weight.astype(BF).reshape(block, D), ((0, cblk - block), (0, 0)))
    if block % 16 == 0:
        wi_own, ff_own = intake_local, ff_local
    else:
        wi_own = lax.all_to_all(intake_local, "group", split_axis=0, concat_axis=0, tiled=True)
        wi_own = cross(wi_own.reshape(rows_n, 3 * ch))
        ff_own = lax.all_to_all(ff_local, "group", split_axis=0, concat_axis=0, tiled=True)
        ff_own = cross(ff_own.transpose(1, 2, 0, 3, 4).reshape(chunks, 3, rows_n, WIDTH))

    number = dp * group_count + member
    share = norm_gains.shape[0]

    def placed(values, lane):
        line = lax.dynamic_update_slice(jnp.zeros((256,), F32), lax.reduce_precision(values, 8, 7), (lane,))
        return line.reshape(2, 128)

    runs = [placed(norm_gains, lax.rem(number * share, 128))]
    for piece in range(3):
        rest = lax.rem(3 * number + piece, data_count * group_count)
        lane = lax.rem(rest // group_count * cblk, 128)
        runs.append(placed(conv_kernel[piece * block : (piece + 1) * block], lane))
    small_own = jnp.concatenate(runs)

    seg_len = tokens.shape[1]
    positions = member * seg_len + lax.iota(jnp.int32, seg_len)
    valid = (positions < lengths[0]).astype(F32)[:, None]
    back_low = (cotangent[0].astype(F32) * valid).astype(BF)

    sizes = (data_count // 2, group_count, rows_n, seg_len, ch, cblk, chunks)
    block_out, input_grad, g_ff, g_wi, g_wo, g_small = forward_backward(
        sizes, tokens[0], back_low, wi_own, wo_own, ff_own, small_own
    )

    if block % 16:
        g_wi = cross(g_wi).reshape(blocks, 3, group_count, block, 128).transpose(2, 0, 1, 3, 4)
        g_wi = lax.all_to_all(g_wi, "group", split_axis=0, concat_axis=0, tiled=True)
        g_ff = cross(g_ff).reshape(chunks, 3, group_count, block, WIDTH).transpose(2, 0, 1, 3, 4)
        g_ff = lax.all_to_all(g_ff, "group", split_axis=0, concat_axis=0, tiled=True)
    g_wi = g_wi.transpose(0, 3, 2, 1, 4).reshape(group_count, block, 3, data_count, cblk)
    intake_grad_flat = g_wi[..., :block].transpose(1, 2, 3, 0, 4).reshape(-1).astype(F32)
    g_ff = g_ff.transpose(3, 2, 0, 1, 4).reshape(block, 3, group_count, hidden_full)
    g_ff = g_ff[..., :hidden_part]
    swiglu_grad_flat = g_ff[:, :2].reshape(-1).astype(F32)
    down_grad_flat = g_ff[:, 2].reshape(-1).astype(F32)
    output_grad_flat = g_wo[:block].reshape(-1).astype(F32)

    gain_rows = 2 * D // 128
    taps_grad = g_small[gain_rows : gain_rows + group_count * 3 * blocks]
    taps_grad = taps_grad.reshape(group_count, 3, data_count, cblk)[..., :block]
    taps_grad = taps_grad.transpose(1, 2, 0, 3).reshape(-1)
    small_shards = (
        lax.dynamic_slice(g_small[:gain_rows].reshape(-1), (number * share,), (share,)),
        lax.dynamic_slice(taps_grad, (number * 3 * block,), (3 * block,)),
    )
    intake_new = update(
        intake_weight, intake_first, intake_second, intake_grad_flat, RATE_MATRIX, DECAY
    )
    output_new = update(
        output_weight, output_first, output_second, output_grad_flat, RATE_MATRIX, DECAY
    )
    swiglu_new = update(
        swiglu_weight, swiglu_first, swiglu_second, swiglu_grad_flat, RATE_MATRIX, DECAY
    )
    down_new = update(down_weight, down_first, down_second, down_grad_flat, RATE_MATRIX, DECAY)
    gains_new = update(norm_gains, gains_first, gains_second, small_shards[0], RATE_VECTOR, 0.0)
    kernel_new = update(
        conv_kernel, kernel_first, kernel_second, small_shards[1], RATE_VECTOR, DECAY
    )
    return (
        block_out[None],
        input_grad[None],
        intake_new[0],
        intake_new[1],
        intake_new[2],
        output_new[0],
        output_new[1],
        output_new[2],
        swiglu_new[0],
        swiglu_new[1],
        swiglu_new[2],
        down_new[0],
        down_new[1],
        down_new[2],
        gains_new[0],
        gains_new[1],
        gains_new[2],
        kernel_new[0],
        kernel_new[1],
        kernel_new[2],
    )


def solution(mesh):
    in_specs = (
        P("dp", "group", None),
        P("dp", "group", None),
        P("dp"),
        P(("dp", "group")),
        P(("dp", "group")),
        P(("dp", "group")),
        P(("dp", "group")),
        P(("dp", "group")),
        P(("dp", "group")),
        P(("dp", "group")),
        P(("dp", "group")),
        P(("dp", "group")),
        P(("dp", "group")),
        P(("dp", "group")),
        P(("dp", "group")),
        P(("dp", "group")),
        P(("dp", "group")),
        P(("dp", "group")),
        P(("dp", "group")),
        P(("dp", "group")),
        P(("dp", "group")),
    )
    out_specs = (
        P("dp", "group", None),
        P("dp", "group", None),
        P(("dp", "group")),
        P(("dp", "group")),
        P(("dp", "group")),
        P(("dp", "group")),
        P(("dp", "group")),
        P(("dp", "group")),
        P(("dp", "group")),
        P(("dp", "group")),
        P(("dp", "group")),
        P(("dp", "group")),
        P(("dp", "group")),
        P(("dp", "group")),
        P(("dp", "group")),
        P(("dp", "group")),
        P(("dp", "group")),
        P(("dp", "group")),
        P(("dp", "group")),
        P(("dp", "group")),
    )
    return jax.shard_map(body, mesh=mesh, in_specs=in_specs, out_specs=out_specs, check_vma=False)
```

```python
import functools

import jax
import jax.numpy as jnp
from jax import lax
from jax.experimental import pallas as pl
from jax.experimental.pallas import tpu as pltpu
from jax.sharding import PartitionSpec as P

D = 1536
FF = 6912
STEP = 5
WIDTH = 256
ROW_TILE = 16

EPS_NORM = 1e-05
BETA_ONE = 0.5
BETA_TWO = 0.5
ADAM_EPS = 1e-08
RATE_MATRIX = 0.02
RATE_VECTOR = 0.2
DECAY = 0.1

MESH = pl.DeviceIdType.MESH
BF = jnp.bfloat16
F32 = jnp.float32


def update(weight, first, second, grad, rate, decay):
    first_new = BETA_ONE * first + (1.0 - BETA_ONE) * grad
    second_new = BETA_TWO * second + (1.0 - BETA_TWO) * grad * grad
    first_hat = first_new / (1.0 - BETA_ONE**STEP)
    second_hat = second_new / (1.0 - BETA_TWO**STEP)
    weight_new = weight - rate * (first_hat / (jnp.sqrt(second_hat) + ADAM_EPS) + decay * weight)
    return (first_new, second_new, weight_new)


def dot(left, right):
    return lax.dot_general(left, right, (((1,), (0,)), ((), ())), preferred_element_type=F32)


def dot_t(left, right):
    return lax.dot_general(left, right, (((1,), (1,)), ((), ())), preferred_element_type=F32)


def await_bytes(ref, sem):
    pltpu.make_async_copy(ref, ref, sem).wait()


def block_kernel(
    sizes,
    tok, bck_own, wi_own, wo_own, ff_own, small_own,
    block_out, input_grad, g_ff, g_wi, g_wo, g_small,
    wf_all, wi_all, wo_all, tok_all, nrm_far, bck_all, n2_all, dbr_all,
    rs_br, rs_y, rs_n2, rs_n1, via,
    sib_f, sib_i, sib_o, come_f, come_i, far_f, far_i, z_o, mixed_far,
    ws, wi, wo, act, act_t, bck, bck_t, acc_y, acc_n, grad, sibv, part, stage,
    prod, gated, dmix, mid, dmid, low, sibo, parto,
    small_all, gains, taps, g_gains, g_taps, sm_mine, sm_plane, sm_sum, sm_z,
    extra, ag_ssem, ag_rsem, ag_fsem, rs_ssem, rs_rsem, via_ssem, via_rsem, z_ssem, z_rsem, f_ssem, f_rsem,
    gs_ssem, gs_rsem, gz_ssem, come_sem, far_sem, buf_sem, own_ssem, own_rsem, back_ssem, back_rsem, osem,
    sa_ssem, sa_rsem, sz_ssem, sz_rsem, ta_ssem, ta_rsem, tz_ssem, tz_rsem, wsem, lsem,
):
    (out_n, group, rows_n, seg, ch, cblk, chunks) = sizes
    block = rows_n // group
    direct = block % 16 == 0
    count = 2 * out_n * group
    blocks = ch // 128
    seq = group * seg
    dp = lax.axis_index("dp")
    g = lax.axis_index("group")
    o, a = dp // 2, lax.rem(dp, 2)
    y, b = g // 2, lax.rem(g, 2)
    t = 2 * y + a
    mate = (dp, g + 1 - 2 * b)

    def peer(k):
        o2 = lax.rem(o + k, out_n)
        return o2, (2 * o2 + a, g)

    barrier = pltpu.get_barrier_semaphore()
    for x2 in range(2):
        for g2 in range(group):
            @pl.when((x2 != a) | (g2 != g))
            def _():
                pl.semaphore_signal(barrier, inc=1, device_id=(2 * o + x2, g2), device_id_type=MESH)

    def greet(k, carry):
        pl.semaphore_signal(barrier, inc=1, device_id=peer(k)[1], device_id_type=MESH)
        return carry

    lax.fori_loop(1, out_n, greet, 0)
    pl.semaphore_wait(barrier, 2 * group - 1 + out_n - 1)

    def remote(src, dst, ssem, rsem, dev):
        return pltpu.make_async_remote_copy(
            src_ref=src, dst_ref=dst, send_sem=ssem, recv_sem=rsem, device_id=dev, device_id_type=MESH
        )

    def switch(alone, local, copy, op):
        if op == "start":
            @pl.when(alone)
            def _():
                local.start()

            @pl.when(jnp.logical_not(alone))
            def _():
                copy.start()
        else:
            @pl.when(jnp.logical_not(alone))
            def _():
                copy.wait_send()

    odd = lax.rem(a + b, 2)
    size = seg // 2
    y_via = odd * y + (1 - odd) * (1 - y)
    h_via = 1 - odd
    partner = (2 * o + odd * a + (1 - odd) * (1 - a), 2 * (odd * (1 - y) + (1 - odd) * y) + b)

    def part_of(h):
        return pl.ds(h * size, size) if isinstance(h, int) else pl.ds(pl.multiple_of(h * size, size), size)

    def spread(src, dst, n, op):
        for d, h in ((1, 0), (2, 1), (1, 1), (2, 0), (0, 0), (0, 1)):
            x2, y2 = (1 - a if d == 1 else a), (1 - y if d == 2 else y)
            one, two = src.at[part_of(h)], dst.at[g, part_of(h)]
            copy = remote(one, two, ag_ssem.at[n, d, h], ag_rsem.at[n, g, h], (2 * o + x2, 2 * y2 + a))
            if d == 0:
                switch(a == b, pltpu.make_async_copy(one, two, ag_rsem.at[n, g, h]), copy, op)
            elif op == "start":
                copy.start()
            else:
                copy.wait_send()
        if op == "end":
            for k in range(2):
                ref = dst.at[2 * y_via + k, part_of(h_via)]
                await_bytes(ref, ag_fsem.at[n, k])

    def spread_on(dst, n):
        for k in range(2):
            q = 2 * y_via + k
            ref = dst.at[q, part_of(h_via)]
            await_bytes(ref, ag_rsem.at[n, q, h_via])
            remote(ref, ref, ag_fsem.at[n, k], ag_rsem.at[n, q, h_via], partner).start()

    def spread_wait(dst, n, q):
        for h in range(2):
            @pl.when((q // 2 != y_via) | (h != h_via))
            def _():
                await_bytes(dst.at[q, part_of(h)], ag_rsem.at[n, q, h])

    def give(terms, dst, n, at, q, h, slot, op="start"):
        one, two = terms(q).at[part_of(h)], dst.at[slot, part_of(h)]
        copy = remote(one, two, rs_ssem.at[n, at, h], rs_rsem.at[n, slot, h], (2 * o + b, q))
        if slot == 0:
            switch(q == g, pltpu.make_async_copy(one, two, rs_rsem.at[n, 0, h]), copy, op)
        elif op == "start":
            copy.start()
        else:
            copy.wait_send()

    def give_half(terms, n, k, h, op):
        q = 2 * (1 - y) + k
        dev = (2 * o + 1 - a, g) if h == 0 else (dp, 2 * (1 - y) + b)
        copy = remote(terms(q).at[part_of(h)], via.at[n, k], via_ssem.at[n, k, h], via_rsem.at[n, k], dev)
        if op == "start":
            copy.start()
        else:
            copy.wait_send()

    def scatter(terms, dst, n, produce):
        for k in range(2):
            q = 2 * (1 - y) + k
            produce(q)

            @pl.when(odd == 1)
            def _():
                give_half(terms, n, k, 0, "start")
                give_half(terms, n, k, 1, "start")

            @pl.when(odd == 0)
            def _():
                give(terms, dst, n, k, q, 1, 1)

        for k in range(2):
            q = 2 * y + k
            produce(q)

            @pl.when(odd == 1)
            def _():
                give(terms, dst, n, 2 + k, q, 0, 2)

            @pl.when(odd == 0)
            def _():
                give(terms, dst, n, 2 + k, q, 0, 0)
                give(terms, dst, n, 2 + k, q, 1, 0)

    def scatter_on(terms, dst, n):
        for k in range(2):
            q = 2 * y_via + k
            await_bytes(via.at[n, k], via_rsem.at[n, k])
            fetch(via.at[n, k], extra, 0)

            def add_rows(i, carry):
                here = pl.ds(pl.multiple_of(odd * size + i * ROW_TILE, ROW_TILE), ROW_TILE)
                ref = terms(q)
                ref[here, :] = (ref[here, :].astype(F32) + extra[rows16(i), :].astype(F32)).astype(BF)
                return carry

            lax.fori_loop(0, size // ROW_TILE, add_rows, 0)

            @pl.when(odd == 1)
            def _():
                give(terms, dst, n, 2 + k, q, 1, 2)

            @pl.when(odd == 0)
            def _():
                give(terms, dst, n, k, q, 0, 1)

    def scatter_end(terms, dst, n):
        @pl.when(odd == 1)
        def _():
            for k in range(2):
                for h in range(2):
                    give_half(terms, n, k, h, "end")
                    give(terms, dst, n, 2 + k, 2 * y + k, h, 2, "end")

        @pl.when(odd == 0)
        def _():
            for k in range(2):
                for h in range(2):
                    give(terms, dst, n, k, 2 * (1 - y) + k, h, 1, "end")
                    give(terms, dst, n, 2 + k, 2 * y + k, h, 0, "end")

    def scatter_wait(dst, n):
        for slot in range(3):
            for h in range(2):
                await_bytes(dst.at[slot, part_of(h)], rs_rsem.at[n, slot, h])

    def staged(q):
        return stage.at[q]

    def any_span(q):
        return pl.ds(pl.multiple_of(q * seg, seg), seg)

    def slot_of(i, o2, p):
        if isinstance(i, int) and i == 0:
            return wi_all.at[o2, p]
        if isinstance(i, int) and i == 1:
            return wo_all.at[o2, p]
        return wf_all.at[i - 2, :, o2, p]

    def half_of(i, p):
        if isinstance(i, int) and i == 0:
            return wi_all.at[:, p]
        if isinstance(i, int) and i == 1:
            return wo_all.at[:, p]
        return wf_all.at[i - 2, :, :, p]

    my_rows = pl.ds(pl.multiple_of(g * block, 4), block)

    def own_send(i, op):
        if isinstance(i, int) and i == 1:
            dst = wo_all.at[o, a]
            switch(
                a == b,
                pltpu.make_async_copy(wo_own, dst, own_rsem.at[1, 0]),
                remote(wo_own, dst, own_ssem.at[1, 0], own_rsem.at[1, 0], (2 * o + b, 2 * y + a)),
                op,
            )
            return
        if not direct:
            src = wi_own if isinstance(i, int) and i == 0 else ff_own.at[i - 2]
            if op == "start":
                pltpu.make_async_copy(src, slot_of(i, o, b), own_rsem.at[i, 0]).start()
            return
        for t2 in range(group):
            ty, tx = t2 // 2, t2 % 2
            if isinstance(i, int) and i == 0:
                src, dst = wi_own.at[t2], wi_all.at[o, a, my_rows]
            else:
                src, dst = ff_own.at[t2, i - 2], wf_all.at[i - 2, :, o, a, my_rows]
            switch(
                (tx == a) & (ty == y) & (a == b),
                pltpu.make_async_copy(src, dst, own_rsem.at[i, g]),
                remote(src, dst, own_ssem.at[i, t2], own_rsem.at[i, g], (2 * o + tx, 2 * ty + a)),
                op,
            )

    def own_wait(i):
        if not direct or isinstance(i, int) and i == 1:
            await_bytes(slot_of(i, o, b), own_rsem.at[i, 0])
            return
        for q in range(group):
            if isinstance(i, int) and i == 0:
                await_bytes(wi_all.at[o, b, pl.ds(q * block, block)], own_rsem.at[i, q])
            else:
                await_bytes(wf_all.at[i - 2, :, o, b, pl.ds(q * block, block)], own_rsem.at[i, q])

    first, final = o == 0, o == out_n - 1

    def piece_send(i, src, side):
        ref = slot_of(i, src, b)
        dev = (2 * (o + 1 - 2 * side) + a, g)
        remote(ref, ref, z_ssem.at[i, side, src], z_rsem.at[i, src], dev).start()

    def when(condition, call, *args):
        @pl.when(condition)
        def _():
            call(*args)

    def hop(i, h):
        if h == 0:
            own_wait(i)
            when(jnp.logical_not(final), piece_send, i, o, 0)
            when(jnp.logical_not(first), piece_send, i, o, 1)
            return

        @pl.when(o - h >= 0)
        def _():
            await_bytes(slot_of(i, o - h, b), z_rsem.at[i, o - h])
            when(jnp.logical_not(final), piece_send, i, o - h, 0)

        @pl.when(o + h < out_n)
        def _():
            await_bytes(slot_of(i, o + h, b), z_rsem.at[i, o + h])
            when(jnp.logical_not(first), piece_send, i, o + h, 1)

        if h == out_n - 1:
            remote(half_of(i, b), half_of(i, b), f_ssem.at[i], f_rsem.at[i], mate).start()

    items = 2 + chunks
    sent = set()

    def own_start(*which):
        for i in which:
            if i < items and i not in sent:
                sent.add(i)
                own_send(i, "start")

    def pump(time):
        if isinstance(time, int):
            own_start(*range(time + 1))
        for h in range(out_n - 1, -1, -1):
            if isinstance(time, int):
                if 0 <= time - h < items:
                    hop(time - h, h)
            else:
                when(time - h < items, hop, time - h, h)

    def gather_wait(i):
        await_bytes(half_of(i, 1 - b), f_rsem.at[i])

    def gather_close(i):
        def sent(src, side):
            await_bytes(slot_of(i, src, b), z_ssem.at[i, side, src])

        @pl.when(jnp.logical_not(final))
        def _():
            lax.fori_loop(0, o + 1, lambda src, carry: (sent(src, 0), carry)[1], 0)

        @pl.when(jnp.logical_not(first))
        def _():
            lax.fori_loop(o, out_n, lambda src, carry: (sent(src, 1), carry)[1], 0)

        await_bytes(half_of(i, b), f_ssem.at[i])
        own_send(i, "end")

    def fetch(src, dst, n):
        copy = pltpu.make_async_copy(src, dst, lsem.at[n])
        copy.start()
        copy.wait()

    def span(q):
        return pl.ds(q * seg, seg)

    def rows16(i):
        return pl.ds(pl.multiple_of(i * ROW_TILE, ROW_TILE), ROW_TILE)

    def lanes(k, j):
        return pl.ds(k * 384 + j * 128, 128)

    place = a * group + g
    mine = o * (2 * group) + place

    def plane(src, dst, ssem, rsem, op):
        for x2 in range(2):
            for g2 in range(group):
                @pl.when((x2 != a) | (g2 != g))
                def _():
                    copy = remote(src, dst, ssem.at[x2 * group + g2], rsem.at[place], (2 * o + x2, g2))
                    if op == "start":
                        copy.start()
                    else:
                        copy.wait_send()

    def plane_wait(ref, rsem):
        for x2 in range(2):
            for g2 in range(group):
                @pl.when((x2 != a) | (g2 != g))
                def _():
                    await_bytes(ref, rsem.at[x2 * group + g2])

    def far(src, dst, ssem, rsem, op):
        def one(k, carry):
            copy = remote(src, dst, ssem.at[k], rsem.at[o], peer(k)[1])
            if op == "start":
                copy.start()
            else:
                copy.wait_send()
            return carry

        lax.fori_loop(1, out_n, one, 0)

    def far_wait(ref, rsem):
        def one(k, carry):
            await_bytes(ref, rsem.at[peer(k)[0]])
            return carry

        lax.fori_loop(1, out_n, one, 0)

    planes = small_all.at[pl.ds(o * 2 * group, 2 * group)]
    pltpu.make_async_copy(small_own, small_all.at[mine], lsem.at[2]).start()
    plane(small_own, small_all.at[mine], sa_ssem, sa_rsem, "start")

    def convolved(q, col):
        return (
            taps[0:1, col] * prod[pl.ds(q * seg + 6, seg), col]
            + taps[1:2, col] * prod[pl.ds(q * seg + 7, seg), col]
            + taps[2:3, col] * prod[pl.ds(q * seg + 8, seg), col]
        )

    own_start(0)
    own_start(1)
    own_start(2)
    spread(tok, tok_all, 0, "start")
    own_start(3)
    prod[pl.ds(0, 8), :] = jnp.zeros((8, ch), F32)
    pump(0)
    await_bytes(small_own, lsem.at[2])
    plane_wait(small_own, sa_rsem)
    far(planes, planes, sz_ssem, sz_rsem, "start")
    pump(1)
    far_wait(planes, sz_rsem)
    spread_on(tok_all, 0)

    share = 2 * D // count
    rows_of = {}
    for n in range(count):
        row = n * share // 128
        rows_of.setdefault(row, []).append((n, 0))
        if (n * share + share - 1) // 128 > row:
            rows_of.setdefault(row + 1, []).append((n, 1))
    for tile, pieces in rows_of.items():
        value = sum(small_all[n, r : r + 1, :] for n, r in pieces)
        i, j = tile // (D // 128), tile % (D // 128)
        gains[i : i + 1, j * 128 : (j + 1) * 128] = value
    rows_of = {}
    for m in range(3 * count):
        n, piece = m // 3, m % 3
        tap, rest = m // count, m % count
        lane = rest // group * cblk
        rows_of.setdefault((tap, lane // 128), []).append((n, 2 + 2 * piece, rest % group))
        if (lane + block - 1) // 128 > lane // 128:
            rows_of.setdefault((tap, lane // 128 + 1), []).append((n, 3 + 2 * piece, rest % group))
    for (tap, tile), pieces in rows_of.items():
        value = jnp.zeros((1, 128), F32)
        for t2 in range(group):
            value = value + jnp.where(t == t2, sum(small_all[n, r : r + 1, :] for n, r, p in pieces if p == t2), 0.0)
        taps[tap : tap + 1, tile * 128 : (tile + 1) * 128] = value

    pump(2)
    for q in range(group):
        spread_wait(tok_all, 0, q)
        fetch(tok_all.at[q], act.at[span(q)], 0)

        def normed_rows(i, carry, q=q):
            here = pl.ds(pl.multiple_of(q * seg + i * ROW_TILE, ROW_TILE), ROW_TILE)
            row = act[here, :].astype(F32)
            s1 = lax.rsqrt(jnp.mean(row * row, axis=-1, keepdims=True) + EPS_NORM)
            act[here, :] = (row * s1 * gains[0:1, :]).astype(BF)
            return carry

        lax.fori_loop(0, seg // ROW_TILE, normed_rows, 0, unroll=2)
    own_start(4)
    spread(bck_own, bck_all, 1, "start")
    own_start(5)
    keep_normed = pltpu.make_async_copy(act, nrm_far, lsem.at[2])
    keep_normed.start()
    for time in range(3, out_n):
        pump(time)
    gather_wait(0)
    fetch(wi_all, wi, 0)
    keep_normed.wait()

    for q in range(group):
        for k in range(blocks):
            acc_y[span(q), pl.ds(k * 384, 384)] = dot(
                act[span(q), :], wi[:, :, :, pl.ds(k * 384, 384)].reshape(D, 384)
            )
        for k in range(blocks):
            col = pl.ds(k * 128, 128)
            prod[pl.ds(q * seg + 8, seg), col] = acc_y[span(q), lanes(k, 0)] * acc_y[span(q), lanes(k, 2)]
            gated[span(q), col] = (acc_y[span(q), lanes(k, 1)] * convolved(q, col)).astype(BF)
    spread_on(bck_all, 1)
    pump(out_n)
    gather_wait(1)
    fetch(wo_all, wo, 0)

    def branch(q):
        for n in range(4):
            col = pl.ds(n * 384, 384)
            stage[q, :, col] = dot(gated[any_span(q), :], wo[:, :, :, col].reshape(ch, 384)).astype(BF)

    scatter(staged, rs_br, 0, branch)
    scatter_on(staged, rs_br, 0)
    spill = pltpu.make_async_copy(acc_y.at[:, pl.ds(0, 3 * ch)], mixed_far, lsem.at[2])
    spill.start()
    own_start(6)
    pump(out_n + 1)
    for q in range(group):
        spread_wait(bck_all, 1, q)
        fetch(bck_all.at[q], bck.at[span(q)], 0)
        bck_t[:, span(q)] = bck[span(q), :].T

    pump(out_n + 2)
    scatter_wait(rs_br, 0)
    scatter_end(staged, rs_br, 0)
    fetch(rs_br, stage.at[pl.ds(0, 3)], 0)

    def arrived(here):
        total = stage[0, here, :].astype(F32)
        for q in range(1, 3):
            total = total + stage[q, here, :].astype(F32)
        return total

    def middle_rows(i, carry):
        here = rows16(i)
        mi = tok[here, :].astype(F32) + arrived(here)
        mid[here, :] = mi
        s2 = lax.rsqrt(jnp.mean(mi * mi, axis=-1, keepdims=True) + EPS_NORM)
        low[here, :] = (mi * s2 * gains[1:2, :]).astype(BF)
        return carry

    lax.fori_loop(0, seg // ROW_TILE, middle_rows, 0)
    spread(low, n2_all, 2, "start")
    own_start(*range(items))
    pump(out_n + 3)
    spread_on(n2_all, 2)
    pump(out_n + 4)
    gather_wait(2)
    pltpu.make_async_copy(wf_all.at[0], ws.at[0], wsem.at[0]).start()
    spill.wait()

    def clear(i, carry):
        here = rows16(i)
        acc_y[here, :] = jnp.zeros((ROW_TILE, D), F32)
        acc_n[here, :] = jnp.zeros((ROW_TILE, D), F32)
        return carry

    lax.fori_loop(0, seq // ROW_TILE, clear, 0)
    for q in range(group):
        spread_wait(n2_all, 2, q)
        fetch(n2_all.at[q], act.at[span(q)], 0)
        act_t[:, span(q)] = act[span(q), :].T

    def chunk_refs(kind, c):
        if kind == "f":
            return lax.rem(c, 2), c, sib_f.at[c], pl.ds(0, WIDTH)
        n = chunks + c
        return n % 2, n, sib_i.at[c], pl.ds(0, 128)

    def pair_send(kind, c, op):
        s, n, sib, cols = chunk_refs(kind, c)
        copy = remote(grad.at[s, :, :, 1 - b, :, cols], sib, gs_ssem.at[n], gs_rsem.at[n], mate)
        if op == "start":
            copy.start()
        else:
            copy.wait_send()

    steps = out_n.bit_length() - 1

    def halves_refs(kind, c):
        return (come_f if kind == "f" else come_i).at[c], (far_f if kind == "f" else far_i).at[c]

    def flipped(k):
        m = 1 << k
        return o + m - 2 * m * lax.rem(o // m, 2)

    def kept(device, k, i):
        return lax.rem(device, 2 << k) + (2 << k) * i

    def step_at(k):
        return out_n - (out_n >> k), out_n >> (k + 1)

    def step_send(kind, c, k, op="start"):
        _, n, _, _ = chunk_refs(kind, c)
        come, mine_far = halves_refs(kind, c)
        at, number = step_at(k)
        there = flipped(k)
        for i in range(number):
            copy = remote(
                mine_far.at[:, kept(there, k, i)], come.at[:, at + i],
                gz_ssem.at[n, at + i], come_sem.at[n, at + i], (2 * there + a, g),
            )
            if op == "start":
                copy.start()
            else:
                copy.wait_send()

    def pair_fetch(kind, c, op):
        s, n, sib, cols = chunk_refs(kind, c)
        if op == "start":
            await_bytes(sib, gs_rsem.at[n])
        copy = pltpu.make_async_copy(sib, sibv.at[:, :, :, cols], lsem.at[1])
        copy.start() if op == "start" else copy.wait()

    def pair_far(kind, c):
        s, n, _, cols = chunk_refs(kind, c)
        return pltpu.make_async_copy(part.at[s, :, :, :, cols], halves_refs(kind, c)[1], far_sem.at[s])

    def pair_add(kind, c):
        s, n, _, cols = chunk_refs(kind, c)
        pair_fetch(kind, c, "end")

        def one(i, carry):
            j, o2 = i // out_n, lax.rem(i, out_n)
            part[s, j, o2, :, cols] = (
                grad[s, j, o2, b, :, cols].astype(F32) + sibv[j, o2, :, cols].astype(F32)
            ).astype(BF)
            return carry

        lax.fori_loop(0, 3 * out_n, one, 0)
        pair_far(kind, c).start()

    def first_send(kind, c):
        pair_far(kind, c).wait()
        step_send(kind, c, 0)

    def stage_ask(job, buf, op):
        kind, c, k = job
        _, n, _, cols = chunk_refs(kind, c)
        come, mine_far = halves_refs(kind, c)
        at, number = step_at(k)
        for i in range(number):
            if op == "start":
                await_bytes(come.at[:, at + i], come_sem.at[n, at + i])
            for m, src in ((i, come.at[:, at + i]), (number + i, mine_far.at[:, kept(o, k, i)])):
                copy = pltpu.make_async_copy(src, part.at[buf, :, m, :, cols], buf_sem.at[buf, m])
                copy.start() if op == "start" else copy.wait()

    def stage_back(job, buf, op):
        kind, c, k = job
        _, n, _, cols = chunk_refs(kind, c)
        mine_far = halves_refs(kind, c)[1]
        at, number = step_at(k)
        for i in range(number):
            m = number + i
            copy = pltpu.make_async_copy(
                part.at[buf, :, m, :, cols], mine_far.at[:, kept(o, k, i)], buf_sem.at[buf, m]
            )
            copy.start() if op == "start" else copy.wait()

    def stage_add(job, buf):
        kind, c, k = job
        _, n, _, cols = chunk_refs(kind, c)
        h, _, place_o, place_p = out_slot(n)
        at, number = step_at(k)

        def add(i, carry):
            j, r = i // (rows_n // 48), lax.rem(i, rows_n // 48)
            here = pl.ds(pl.multiple_of(r * 48, 16), 48)
            for m in range(number):
                value = (
                    part[buf, j, m, here, cols].astype(F32) + part[buf, j, number + m, here, cols].astype(F32)
                ).astype(BF)
                if k == steps - 1:
                    ws[h, j, place_o, place_p, here, cols] = value
                else:
                    part[buf, j, number + m, here, cols] = value
            return carry

        lax.fori_loop(0, 3 * (rows_n // 48), add, 0)
        if k == steps - 1:
            hand_back(kind, c, "start")
        else:
            stage_back(job, buf, "start")

    def stage_on(job, buf):
        kind, c, k = job
        if k < steps - 1:
            stage_back(job, buf, "end")
            step_send(kind, c, k + 1)

    def sums_of(jobs):
        for i, job in enumerate(jobs):
            if i == 0:
                stage_ask(job, 0, "start")
            if i >= 1:
                stage_on(jobs[i - 1], (i - 1) % 2)
            if i + 1 < len(jobs):
                stage_ask(jobs[i + 1], (i + 1) % 2, "start")
            stage_ask(job, i % 2, "end")
            stage_add(job, i % 2)
        stage_on(jobs[-1], (len(jobs) - 1) % 2)

    def out_slot(n):
        return (n // (2 * out_n), slice(None), lax.rem(n, 2 * out_n) // 2, lax.rem(n, 2))

    def hand_back(kind, c, op):
        _, n, _, cols = chunk_refs(kind, c)
        dst = (g_ff if kind == "f" else g_wi)
        if not direct:
            if op == "start":
                h, _, o2, p = out_slot(n)
                fetch(ws.at[h, :, o2, p, :, cols], dst.at[c], 1)
            return
        h, _, o2, p = out_slot(n)
        for q in range(group):
            src = ws.at[h, :, o2, p, pl.ds(q * block, block), cols]
            switch(
                (a == b) & (q == g),
                pltpu.make_async_copy(src, dst.at[t, c], back_rsem.at[n, t]),
                remote(src, dst.at[t, c], back_ssem.at[n, q], back_rsem.at[n, t], (2 * o + b, q)),
                op,
            )

    def hand_wait(kind, c):
        if direct:
            _, n, _, _ = chunk_refs(kind, c)
            for t2 in range(group):
                await_bytes((g_ff if kind == "f" else g_wi).at[t2, c], back_rsem.at[n, t2])

    half = out_n // 2

    def grad_rows(h):
        return pl.ds(pl.multiple_of(h * (D // 2), D // 2), D // 2), pl.ds(h * half, half)

    loop_pump = out_n + 5

    def d_normed_two(q):
        stage[q] = acc_n[any_span(q), :].astype(BF)

    def hidden_chunk(c, carry):
        s = lax.rem(c, 2)
        await_bytes(ws.at[s], wsem.at[s])
        hid, dgt, dup = (pl.ds(j * WIDTH, WIDTH) for j in range(3))

        def token_tile(m, carry):
            here = pl.ds(pl.multiple_of(m * (seq // 2), seq // 2), seq // 2)
            n2 = act[here, :]
            gate = dot(n2, ws[s, 0].reshape(D, WIDTH))
            upper = dot(n2, ws[s, 1].reshape(D, WIDTH))
            d_hidden = dot(bck[here, :], ws[s, 2].reshape(D, WIDTH))
            sigma = jax.nn.sigmoid(gate)
            active = gate * sigma
            dmix[here, hid] = (active * upper).astype(BF)
            dmix[here, dgt] = (d_hidden * upper * (sigma * (1.0 + gate * (1.0 - sigma)))).astype(BF)
            dmix[here, dup] = (d_hidden * active).astype(BF)
            acc_y[here, :] += dot_t(dmix[here, hid], ws[s, 2].reshape(D, WIDTH))
            acc_n[here, :] += dot_t(dmix[here, dgt], ws[s, 0].reshape(D, WIDTH))
            acc_n[here, :] += dot_t(dmix[here, dup], ws[s, 1].reshape(D, WIDTH))
            return carry

        lax.fori_loop(0, 2, token_tile, 0)

        @pl.when(c == chunks - 1)
        def _():
            scatter(staged, rs_n2, 1, d_normed_two)

        @pl.when(c >= 1)
        def _():
            pair_fetch("f", c - 1, "start")

        @pl.when(c >= 2)
        def _():
            first_send("f", c - 2)

        @pl.when(c >= 2)
        def _():
            pair_send("f", c - 2, "end")

        def grad_tile(h, carry):
            rows, os = grad_rows(h)
            shape = (half, 2, rows_n, WIDTH)
            grad[s, 0, os] = dot(act_t[rows, :], dmix[:, dgt]).astype(BF).reshape(shape)
            grad[s, 1, os] = dot(act_t[rows, :], dmix[:, dup]).astype(BF).reshape(shape)
            grad[s, 2, os] = dot(bck_t[rows, :], dmix[:, hid]).astype(BF).reshape(shape)
            return carry

        lax.fori_loop(0, 2, grad_tile, 0)
        pair_send("f", c, "start")

        @pl.when(c >= 1)
        def _():
            pair_add("f", c - 1)

        pump(c + loop_pump)

        @pl.when(c + 1 < chunks)
        def _():
            gather_wait(c + 3)
            pltpu.make_async_copy(wf_all.at[c + 1], ws.at[1 - s], wsem.at[1 - s]).start()

        return carry

    lax.fori_loop(0, chunks, hidden_chunk, 0)

    first_send("f", chunks - 2)
    pair_fetch("f", chunks - 1, "start")
    pair_add("f", chunks - 1)
    scatter_on(staged, rs_n2, 1)
    first_send("f", chunks - 1)
    for k in range(steps - 1):
        sums_of([("f", c, k) for c in range(chunks - 2)])
    scatter_wait(rs_n2, 1)
    scatter_end(staged, rs_n2, 1)
    spread(low, n2_all, 2, "end")
    fetch(rs_n2, stage.at[pl.ds(0, 3)], 0)
    fetch(bck_own, act.at[span(0)], 0)
    g_gains[...] = jnp.zeros_like(g_gains)

    def d_middle_rows(i, carry):
        here = rows16(i)
        dn = arrived(here)
        mi = mid[here, :]
        s2 = lax.rsqrt(jnp.mean(mi * mi, axis=-1, keepdims=True) + EPS_NORM)
        e2 = gains[1:2, :] * dn
        back = act[here, :].astype(F32)
        dm = back + s2 * e2 - mi * (s2 * s2 * s2) * jnp.mean(e2 * mi, axis=-1, keepdims=True)
        dmid[here, :] = dm
        low[here, :] = dm.astype(BF)
        g_gains[1] += jnp.sum((dn * mi * s2).reshape(ROW_TILE // 8, 8, D), axis=0)
        return carry

    lax.fori_loop(0, seg // ROW_TILE, d_middle_rows, 0)
    spread(low, dbr_all, 3, "start")

    for q in range(group):
        stage[q] = acc_y[span(q), :].astype(BF)
    spill_back = pltpu.make_async_copy(mixed_far, acc_y.at[:, pl.ds(0, 3 * ch)], lsem.at[2])
    spill_back.start()

    for q in range(group):
        bck_t[pl.ds(0, ch), span(q)] = gated[span(q), :].T
        fetch(nrm_far.at[span(q)], act.at[span(q)], 0)
        act_t[:, span(q)] = act[span(q), :].T
        if q == 1:
            spread_on(dbr_all, 3)
    spill_back.wait()
    for k in range(steps - 1):
        sums_of([("f", c, k) for c in range(chunks - 2, chunks)])
    sums_of([("f", c, steps - 1) for c in range(chunks - 3)])

    acc_n[pl.ds(seq, 8), pl.ds(0, ch)] = jnp.zeros((8, ch), F32)
    for q in range(group):
        spread_wait(dbr_all, 3, q)
        fetch(dbr_all.at[q], bck.at[span(q)], 0)
        acc_n[span(q), pl.ds(ch, ch)] = dot_t(bck[span(q), :], wo[...].reshape(ch, D))
        for k in range(blocks):
            col = pl.ds(k * 128, 128)
            d_gated = acc_n[span(q), pl.ds(ch + k * 128, 128)]
            acc_n[span(q), col] = d_gated * acc_y[span(q), lanes(k, 1)]
            dmix[span(q), lanes(k, 1)] = (d_gated * convolved(q, col)).astype(BF)
    scatter(staged, rs_y, 2, lambda q: None)
    g_taps[...] = jnp.zeros_like(g_taps)
    for q in range(group):
        for k in range(blocks):
            col = pl.ds(k * 128, 128)
            d0 = acc_n[span(q), col]
            for n in range(3):
                g_taps[n, :, col] += jnp.sum(
                    (d0 * prod[pl.ds(q * seg + 6 + n, seg), col]).reshape(seg // 8, 8, 128), axis=0
                )
            d_product = (
                taps[2:3, col] * d0
                + taps[1:2, col] * acc_n[pl.ds(q * seg + 1, seg), col]
                + taps[0:1, col] * acc_n[pl.ds(q * seg + 2, seg), col]
            )
            dmix[span(q), lanes(k, 0)] = (d_product * acc_y[span(q), lanes(k, 2)]).astype(BF)
            dmix[span(q), lanes(k, 2)] = (d_product * acc_y[span(q), lanes(k, 0)]).astype(BF)

    for k in range(blocks):
        s = (chunks + k) % 2
        if k < 2:
            pair_send("f", chunks - 2 + k, "end")
        else:
            pair_send("i", k - 2, "end")

        def intake_tile(h, carry, k=k, s=s):
            rows, os = grad_rows(h)
            value = dot(act_t[rows, :], dmix[:, pl.ds(k * 384, 384)]).astype(BF)
            for j in range(3):
                grad[s, j, os, :, :, pl.ds(0, 128)] = value[:, j * 128 : (j + 1) * 128].reshape(
                    half, 2, rows_n, 128
                )
            return carry

        lax.fori_loop(0, 2, intake_tile, 0)
        pair_send("i", k, "start")
        if k >= 1:
            pair_fetch("i", k - 1, "start")
            if k >= 2:
                first_send("i", k - 2)
            pair_add("i", k - 1)

    for n in range(4):
        col = pl.ds(n * 384, 384)
        wo[:, :, :, col] = dot(bck_t[pl.ds(0, ch), :], bck[:, col]).astype(BF).reshape(out_n, 2, cblk, 384)
    last = chunks + blocks
    pair_o = remote(wo.at[:, 1 - b], sib_o, gs_ssem.at[last], gs_rsem.at[last], mate)
    pair_o.start()
    if blocks >= 2:
        first_send("i", blocks - 2)
    pair_fetch("i", blocks - 1, "start")
    pair_add("i", blocks - 1)
    first_send("i", blocks - 1)

    await_bytes(sib_o, gs_rsem.at[last])
    fetch(sib_o, sibo, 1)

    def add_o(o2, carry):
        parto[o2] = (wo[o2, b].astype(F32) + sibo[o2].astype(F32)).astype(BF)
        return carry

    lax.fori_loop(0, out_n, add_o, 0)

    def part_o(op):
        def one(k, carry):
            o2, dev = peer(k)
            copy = remote(parto.at[o2], z_o.at[o], gz_ssem.at[last, k], come_sem.at[last, o], dev)
            if op == "start":
                copy.start()
            else:
                copy.wait_send()
            return carry

        lax.fori_loop(1, out_n, one, 0)
        keep = pltpu.make_async_copy(parto.at[o], z_o.at[o], osem.at[0])
        if op == "start":
            keep.start()
        else:
            keep.wait()

    part_o("start")

    def lent(q):
        return bck.at[any_span(q)]

    def d_normed(q):
        for n in range(4):
            bck[any_span(q), pl.ds(n * 384, 384)] = dot_t(
                dmix[any_span(q), :], wi[pl.ds(n * out_n // 4, out_n // 4)].reshape(384, 3 * ch)
            ).astype(BF)

    scatter(lent, rs_n1, 3, d_normed)
    scatter_on(staged, rs_y, 2)
    scatter_on(lent, rs_n1, 3)
    scatter_wait(rs_y, 2)
    scatter_end(staged, rs_y, 2)
    spread(low, dbr_all, 3, "end")
    for q in range(3):
        fetch(rs_y.at[q], act.at[span(q)], 0)

    def out_rows(i, carry):
        here = rows16(i)
        value = act[here, :].astype(F32)
        for q in range(1, 3):
            value = value + act[pl.ds(pl.multiple_of(q * seg + i * ROW_TILE, ROW_TILE), ROW_TILE), :].astype(F32)
        low[here, :] = (mid[here, :] + value).astype(BF)
        return carry

    lax.fori_loop(0, seg // ROW_TILE, out_rows, 0)
    fetch(low, block_out, 0)

    sums_of([("f", c, steps - 1) for c in range(chunks - 3, chunks)])
    scatter_wait(rs_n1, 3)
    scatter_end(lent, rs_n1, 3)
    fetch(rs_n1, stage.at[pl.ds(0, 3)], 0)

    def d_rows(i, carry):
        here = rows16(i)
        dn = arrived(here)
        row = tok[here, :].astype(F32)
        s1 = lax.rsqrt(jnp.mean(row * row, axis=-1, keepdims=True) + EPS_NORM)
        e1 = gains[0:1, :] * dn
        low[here, :] = (
            dmid[here, :] + s1 * e1 - row * (s1 * s1 * s1) * jnp.mean(e1 * row, axis=-1, keepdims=True)
        ).astype(BF)
        g_gains[0] += jnp.sum((dn * row * s1).reshape(ROW_TILE // 8, 8, D), axis=0)
        return carry

    lax.fori_loop(0, seg // ROW_TILE, d_rows, 0)
    fetch(low, input_grad, 0)

    sm_mine[...] = jnp.zeros_like(sm_mine)
    for i in range(2):
        value = jnp.sum(g_gains[i], axis=0, keepdims=True)
        for j in range(D // 128):
            row = i * (D // 128) + j
            sm_mine[row : row + 1, :] = value[:, j * 128 : (j + 1) * 128]
    for n in range(3):
        value = jnp.sum(g_taps[n], axis=0, keepdims=True)
        for k in range(blocks):
            for t2 in range(group):
                row = 2 * (D // 128) + (t2 * 3 + n) * blocks + k
                sm_mine[row : row + 1, :] = jnp.where(t == t2, value[:, k * 128 : (k + 1) * 128], 0.0)
    sm_plane[place] = sm_mine[...]
    plane(sm_mine, sm_plane.at[place], ta_ssem, ta_rsem, "start")

    for k in range(max(0, blocks - 2), blocks):
        pair_send("i", k, "end")

    for k in range(steps - 1):
        sums_of([("i", c, k) for c in range(blocks)])
    plane_wait(sm_mine, ta_rsem)
    value = sm_plane[0]
    for i in range(1, 2 * group):
        value = value + sm_plane[i]
    sm_sum[...] = value
    sm_z[o] = value
    far(sm_sum, sm_z.at[o], tz_ssem, tz_rsem, "start")
    sums_of([("i", c, steps - 1) for c in range(blocks)])
    part_o("end")
    pair_o.wait_send()

    def last_one(k, carry):
        await_bytes(z_o.at[o], come_sem.at[last, peer(k)[0]])
        return carry

    lax.fori_loop(1, out_n, last_one, 0)
    fetch(z_o, sibo, 1)
    value = sibo[0].astype(F32)
    for o2 in range(1, out_n):
        value = value + sibo[o2].astype(F32)
    outo = parto.at[0]
    outo[...] = value.astype(BF)

    def back_o(op):
        switch(
            a == b,
            pltpu.make_async_copy(outo, g_wo, back_rsem.at[last, 0]),
            remote(outo, g_wo, back_ssem.at[last, 0], back_rsem.at[last, 0], (2 * o + b, 2 * y + a)),
            op,
        )

    back_o("start")
    far_wait(sm_sum, tz_rsem)
    value = sm_z[0]
    for i in range(1, out_n):
        value = value + sm_z[i]
    g_small[...] = value

    plane(small_own, small_all.at[mine], sa_ssem, sa_rsem, "end")
    far(planes, planes, sz_ssem, sz_rsem, "end")
    plane(sm_mine, sm_plane.at[place], ta_ssem, ta_rsem, "end")
    far(sm_sum, sm_z.at[o], tz_ssem, tz_rsem, "end")
    spread(tok, tok_all, 0, "end")
    spread(bck_own, bck_all, 1, "end")
    gather_close(0)
    gather_close(1)

    def close(c, carry):
        gather_close(c + 2)
        for k in range(steps):
            step_send("f", c, k, "end")
        hand_back("f", c, "end")
        hand_wait("f", c)
        return carry

    lax.fori_loop(0, chunks, close, 0)
    for k in range(blocks):
        for step in range(steps):
            step_send("i", k, step, "end")
        hand_back("i", k, "end")
        hand_wait("i", k)
    back_o("end")
    await_bytes(g_wo, back_rsem.at[last, 0])


def forward_backward(sizes, tok, bck, wi_own, wo_own, ff_own, small_own):
    (out_n, group, rows_n, seg, ch, cblk, chunks) = sizes
    blocks = ch // 128
    seq = group * seg
    block = rows_n // group
    places = 2 * group
    small_rows = -(-(2 * D // 128 + group * 3 * blocks) // 8) * 8
    items = 2 + chunks
    sums = chunks + blocks + 1
    vm = pltpu.VMEM
    dma = pltpu.SemaphoreType.DMA

    def shape(*dims, dtype=BF):
        return jax.ShapeDtypeStruct(dims, dtype)

    any_spec = pl.BlockSpec(memory_space=pl.ANY)
    vmem_spec = pl.BlockSpec(memory_space=pltpu.VMEM)
    if block % 16 == 0:
        given = [shape(group, chunks, 3, block, WIDTH), shape(group, blocks, 3, block, 128)]
    else:
        given = [shape(chunks, 3, rows_n, WIDTH), shape(blocks, 3, rows_n, 128)]
    outs = [
        shape(seg, D), shape(seg, D), *given, shape(cblk, D), shape(small_rows, 128, dtype=F32),
        shape(chunks, 3, out_n, 2, rows_n, WIDTH), shape(out_n, 2, rows_n, 3 * ch), shape(out_n, 2, cblk, D),
        shape(group, seg, D), shape(seq, D), shape(group, seg, D), shape(group, seg, D), shape(group, seg, D),
        shape(3, seg, D), shape(3, seg, D), shape(3, seg, D), shape(3, seg, D), shape(4, 2, seg // 2, D),
        shape(chunks, 3, out_n, rows_n, WIDTH), shape(blocks, 3, out_n, rows_n, 128), shape(out_n, cblk, D),
        *[shape(chunks, 3, out_n, rows_n, WIDTH), shape(blocks, 3, out_n, rows_n, 128)] * 2, shape(out_n, cblk, D),
        shape(seq, 3 * ch, dtype=F32),
    ]
    out_specs = [any_spec] * 5 + [vmem_spec] + [any_spec] * (len(outs) - 6)
    scratch = [
        vm((2, 3, out_n, 2, rows_n, WIDTH), BF),
        vm((out_n, 2, rows_n, 3 * ch), BF),
        vm((out_n, 2, cblk, D), BF),
        vm((seq, D), BF), vm((D, seq), BF), vm((seq, D), BF), vm((D, seq), BF),
        vm((seq, D), F32), vm((seq + 8, D), F32),
        vm((2, 3, out_n, 2, rows_n, WIDTH), BF),
        vm((3, out_n, rows_n, WIDTH), BF),
        vm((2, 3, out_n, rows_n, WIDTH), BF),
        vm((group, seg, D), BF),
        vm((seq + 8, ch), F32), vm((seq, ch), BF), vm((seq, 3 * ch), BF),
        vm((seg, D), F32), vm((seg, D), F32), vm((seg, D), BF),
        vm((out_n, cblk, D), BF), vm((out_n, cblk, D), BF),
        vm((places * out_n, 8, 128), F32), vm((2, D), F32), vm((3, ch), F32),
        vm((2, 8, D), F32), vm((3, 8, ch), F32),
        vm((small_rows, 128), F32), vm((places, small_rows, 128), F32),
        vm((small_rows, 128), F32), vm((out_n, small_rows, 128), F32),
        vm((seg // 2, D), BF),
        dma((4, 3, 2)), dma((4, group, 2)), dma((4, 2)), dma((4, 4, 2)), dma((4, 3, 2)), dma((4, 2, 2)), dma((4, 2)),
        dma((items, 2, out_n)), dma((items, out_n)), dma((items,)), dma((items,)),
        dma((sums,)), dma((sums,)), dma((sums, out_n)), dma((sums, out_n)), dma((2,)), dma((2, out_n)),
        dma((items, group)), dma((items, group)), dma((sums, group)), dma((sums, group)), dma((1,)),
        dma((places,)), dma((places,)), dma((out_n,)), dma((out_n,)),
        dma((places,)), dma((places,)), dma((out_n,)), dma((out_n,)), dma((2,)), dma((5,)),
    ]
    results = pl.pallas_call(
        functools.partial(block_kernel, sizes),
        out_shape=outs,
        in_specs=[vmem_spec] + [any_spec] * 4 + [vmem_spec],
        out_specs=out_specs,
        scratch_shapes=scratch,
        compiler_params=pltpu.CompilerParams(
            collective_id=0, has_side_effects=True, vmem_limit_bytes=63 * 1024 * 1024
        ),
        cost_estimate=pl.CostEstimate(
            flops=6 * seq * D * (4 * ch + 3 * chunks * WIDTH),
            bytes_accessed=200_000_000,
            transcendentals=seq * chunks * WIDTH,
        ),
    )(tok, bck, wi_own, wo_own, ff_own, small_own)
    return results[:6]


def body(
    tokens,
    cotangent,
    lengths,
    intake_weight,
    intake_first,
    intake_second,
    output_weight,
    output_first,
    output_second,
    swiglu_weight,
    swiglu_first,
    swiglu_second,
    down_weight,
    down_first,
    down_second,
    norm_gains,
    gains_first,
    gains_second,
    conv_kernel,
    kernel_first,
    kernel_second,
):
    data_count = lax.axis_size("dp")
    group_count = lax.axis_size("group")
    dp = lax.axis_index("dp")
    member = lax.axis_index("group")
    block = D // (data_count * group_count)
    cblk = -(-block // 16) * 16
    ch = data_count * cblk
    blocks = ch // 128
    hidden_part = FF // group_count
    chunks = -(-hidden_part // WIDTH)
    hidden_full = chunks * WIDTH
    rows_n = D // data_count
    swap = []
    for one in range(data_count):
        for two in range(group_count):
            there = (2 * (one // 2) + two % 2) * group_count + 2 * (two // 2) + one % 2
            swap.append((one * group_count + two, there))

    def cross(value):
        return lax.ppermute(value, ("dp", "group"), swap)

    intake_local = (
        intake_weight.astype(BF)
        .reshape(block, 3, data_count, group_count, block)
        .transpose(3, 0, 1, 2, 4)
    )
    intake_local = jnp.pad(intake_local, ((0, 0),) * 4 + ((0, cblk - block),))
    intake_local = (
        intake_local.reshape(group_count, block, 3, blocks, 128)
        .transpose(0, 1, 3, 2, 4)
        .reshape(group_count, block, 3 * ch)
    )
    ff_local = jnp.concatenate(
        [
            swiglu_weight.astype(BF).reshape(block, 2, group_count, hidden_part),
            down_weight.astype(BF).reshape(block, 1, group_count, hidden_part),
        ],
        axis=1,
    )
    ff_local = jnp.pad(ff_local, ((0, 0),) * 3 + ((0, hidden_full - hidden_part),))
    ff_local = ff_local.reshape(block, 3, group_count, chunks, WIDTH).transpose(2, 3, 1, 0, 4)
    wo_own = jnp.pad(output_weight.astype(BF).reshape(block, D), ((0, cblk - block), (0, 0)))
    if block % 16 == 0:
        wi_own, ff_own = intake_local, ff_local
    else:
        wi_own = lax.all_to_all(intake_local, "group", split_axis=0, concat_axis=0, tiled=True)
        wi_own = cross(wi_own.reshape(rows_n, 3 * ch))
        ff_own = lax.all_to_all(ff_local, "group", split_axis=0, concat_axis=0, tiled=True)
        ff_own = cross(ff_own.transpose(1, 2, 0, 3, 4).reshape(chunks, 3, rows_n, WIDTH))

    number = dp * group_count + member
    share = norm_gains.shape[0]

    def placed(values, lane):
        line = lax.dynamic_update_slice(jnp.zeros((256,), F32), lax.reduce_precision(values, 8, 7), (lane,))
        return line.reshape(2, 128)

    runs = [placed(norm_gains, lax.rem(number * share, 128))]
    for piece in range(3):
        rest = lax.rem(3 * number + piece, data_count * group_count)
        lane = lax.rem(rest // group_count * cblk, 128)
        runs.append(placed(conv_kernel[piece * block : (piece + 1) * block], lane))
    small_own = jnp.concatenate(runs)

    seg_len = tokens.shape[1]
    positions = member * seg_len + lax.iota(jnp.int32, seg_len)
    valid = (positions < lengths[0]).astype(F32)[:, None]
    back_low = (cotangent[0].astype(F32) * valid).astype(BF)

    sizes = (data_count // 2, group_count, rows_n, seg_len, ch, cblk, chunks)
    block_out, input_grad, g_ff, g_wi, g_wo, g_small = forward_backward(
        sizes, tokens[0], back_low, wi_own, wo_own, ff_own, small_own
    )

    if block % 16:
        g_wi = cross(g_wi).reshape(blocks, 3, group_count, block, 128).transpose(2, 0, 1, 3, 4)
        g_wi = lax.all_to_all(g_wi, "group", split_axis=0, concat_axis=0, tiled=True)
        g_ff = cross(g_ff).reshape(chunks, 3, group_count, block, WIDTH).transpose(2, 0, 1, 3, 4)
        g_ff = lax.all_to_all(g_ff, "group", split_axis=0, concat_axis=0, tiled=True)
    g_wi = g_wi.transpose(0, 3, 2, 1, 4).reshape(group_count, block, 3, data_count, cblk)
    intake_grad_flat = g_wi[..., :block].transpose(1, 2, 3, 0, 4).reshape(-1).astype(F32)
    g_ff = g_ff.transpose(3, 2, 0, 1, 4).reshape(block, 3, group_count, hidden_full)
    g_ff = g_ff[..., :hidden_part]
    swiglu_grad_flat = g_ff[:, :2].reshape(-1).astype(F32)
    down_grad_flat = g_ff[:, 2].reshape(-1).astype(F32)
    output_grad_flat = g_wo[:block].reshape(-1).astype(F32)

    gain_rows = 2 * D // 128
    taps_grad = g_small[gain_rows : gain_rows + group_count * 3 * blocks]
    taps_grad = taps_grad.reshape(group_count, 3, data_count, cblk)[..., :block]
    taps_grad = taps_grad.transpose(1, 2, 0, 3).reshape(-1)
    small_shards = (
        lax.dynamic_slice(g_small[:gain_rows].reshape(-1), (number * share,), (share,)),
        lax.dynamic_slice(taps_grad, (number * 3 * block,), (3 * block,)),
    )
    intake_new = update(
        intake_weight, intake_first, intake_second, intake_grad_flat, RATE_MATRIX, DECAY
    )
    output_new = update(
        output_weight, output_first, output_second, output_grad_flat, RATE_MATRIX, DECAY
    )
    swiglu_new = update(
        swiglu_weight, swiglu_first, swiglu_second, swiglu_grad_flat, RATE_MATRIX, DECAY
    )
    down_new = update(down_weight, down_first, down_second, down_grad_flat, RATE_MATRIX, DECAY)
    gains_new = update(norm_gains, gains_first, gains_second, small_shards[0], RATE_VECTOR, 0.0)
    kernel_new = update(
        conv_kernel, kernel_first, kernel_second, small_shards[1], RATE_VECTOR, DECAY
    )
    return (
        block_out[None],
        input_grad[None],
        intake_new[0],
        intake_new[1],
        intake_new[2],
        output_new[0],
        output_new[1],
        output_new[2],
        swiglu_new[0],
        swiglu_new[1],
        swiglu_new[2],
        down_new[0],
        down_new[1],
        down_new[2],
        gains_new[0],
        gains_new[1],
        gains_new[2],
        kernel_new[0],
        kernel_new[1],
        kernel_new[2],
    )


def solution(mesh):
    in_specs = (
        P("dp", "group", None),
        P("dp", "group", None),
        P("dp"),
        P(("dp", "group")),
        P(("dp", "group")),
        P(("dp", "group")),
        P(("dp", "group")),
        P(("dp", "group")),
        P(("dp", "group")),
        P(("dp", "group")),
        P(("dp", "group")),
        P(("dp", "group")),
        P(("dp", "group")),
        P(("dp", "group")),
        P(("dp", "group")),
        P(("dp", "group")),
        P(("dp", "group")),
        P(("dp", "group")),
        P(("dp", "group")),
        P(("dp", "group")),
        P(("dp", "group")),
    )
    out_specs = (
        P("dp", "group", None),
        P("dp", "group", None),
        P(("dp", "group")),
        P(("dp", "group")),
        P(("dp", "group")),
        P(("dp", "group")),
        P(("dp", "group")),
        P(("dp", "group")),
        P(("dp", "group")),
        P(("dp", "group")),
        P(("dp", "group")),
        P(("dp", "group")),
        P(("dp", "group")),
        P(("dp", "group")),
        P(("dp", "group")),
        P(("dp", "group")),
        P(("dp", "group")),
        P(("dp", "group")),
        P(("dp", "group")),
        P(("dp", "group")),
    )
    return jax.shard_map(body, mesh=mesh, in_specs=in_specs, out_specs=out_specs, check_vma=False)
```
